32 devices in a mesh: seq: 8 (over z, core), mod: 4 (over y, x).
Axes of the slice: x: 2, y: 2, z: 4, core: 2. Of those that a mesh axis runs over, the one named last changes fastest.
Arguments:
- tokens: bfloat16 [4096, 2048], P(('seq', 'mod')), may hold values from -6 to 6
- modality: int32 [4096], P('seq'), may hold values from 0 to 2, as said below
- lengths: int32 [2], replicated, may hold values from 256 to 3840, as said below
- norm_gain: bfloat16 [2048], replicated, may hold values from 0.5 to 1.5
- input_weight: bfloat16 [3, 2048, 2, 4096], P(None, 'seq', None, 'mod'), may hold values from -0.125 to 0.125
- param_weight: bfloat16 [3, 4096, 160], P(None, ('mod', 'seq')), may hold values from -0.09375 to 0.09375
- step_weight: bfloat16 [3, 128, 4096], P(None, None, ('mod', 'seq')), may hold values from -0.5 to 0.5
- step_bias: bfloat16 [3, 4096], P(None, ('mod', 'seq')), may hold values from -14 to -2
- output_weight: bfloat16 [3, 4096, 2048], P(None, 'mod', 'seq'), may hold values from -0.25 to 0.25
- conv_weight: bfloat16 [4, 4096], P(None, ('mod', 'seq')), may hold values from -3 to 3
- conv_bias: bfloat16 [4096], P(('mod', 'seq')), may hold values from -3 to 3
- decay_log: bfloat16 [16, 4096], P(None, ('mod', 'seq')), may hold values from 0 to 1.5
- skip_gain: bfloat16 [4096], P(('mod', 'seq')), may hold values from 0.5 to 1.5
- cotangent: bfloat16 [4096, 2048], P(('seq', 'mod')), may hold values from -6 to 6
Outputs:
- output: bfloat16 [4096, 2048], P(('seq', 'mod'))
- grad_tokens: float32 [4096, 2048], P(('seq', 'mod'))
- grad_norm_gain: float32 [2048], replicated
- grad_input_weight: float32 [3, 2048, 2, 4096], P(None, 'seq', None, 'mod')
- grad_param_weight: float32 [3, 4096, 160], P(None, ('mod', 'seq'))
- grad_step_weight: float32 [3, 128, 4096], P(None, None, ('mod', 'seq'))
- grad_output_weight: float32 [3, 4096, 2048], P(None, 'mod', 'seq')
- grad_conv_weight: float32 [4, 4096], P(None, ('mod', 'seq'))
- grad_conv_bias: float32 [4096], P(('mod', 'seq'))
- grad_decay_log: float32 [16, 4096], P(None, ('mod', 'seq'))
- grad_skip_gain: float32 [4096], P(('mod', 'seq'))
- grad_step_bias: float32 [3, 4096], P(None, ('mod', 'seq'))
The draws below stay inside these ranges and needn't reach their ends.
Inputs may be any that keep to these rules, and one draw needn't show every extreme that they name: In each aligned block of 128 tokens no modality has more than 48 tokens, and one modality has exactly 48. The two lengths sum to 4096; one of them is shorter than 512.
All inputs are finite; a program needn't handle non-finite values.
Results may differ from the reference program's by a relative error of at most 0.0078.
The reference program's roundings to bfloat16 on the way count: a program that leaves them out, or rounds other values in their place, can miss the bound.
Values may be sent and summed in bfloat16 or wider, within the bound.
No kernel may reach another device: no remote copies, remote signals or barrier semaphores. Data moves between devices by JAX's collectives and lax.ppermute only.
A program may use at most 576 MiB of HBM per device.

```python
import math
from functools import partial
import jax
import jax.numpy as jnp
from jax import lax

D = 2048
E = 4096
N = 16
KW = 4
R = 128
MODS = 3
TOK_DEV = 128
CAPD = 48
TB = 512
TOKENS = 4096


def draw_modality(key, part):
    key = jax.random.fold_in(key, 7)
    block_count = TOKENS // TOK_DEV
    key_major, key_second, key_turn, key_shuffle = jax.random.split(key, 4)
    major_kind = jax.random.randint(key_major, (block_count, 1), 0, MODS)
    second_count = jax.random.randint(key_second, (block_count, 1), TOK_DEV - 2 * CAPD, CAPD + 1)
    turn_step = jax.random.randint(key_turn, (block_count, 1), 1, MODS)
    slot_index = jnp.arange(TOK_DEV, dtype=jnp.int32)[None, :]
    labels = jnp.where(slot_index < CAPD, major_kind, jnp.where(slot_index < CAPD + second_count, (major_kind + turn_step) % MODS, (major_kind + MODS - turn_step) % MODS))
    shuffle_keys = jax.random.split(key_shuffle, block_count)
    shuffled = jax.vmap(lambda one_key, one_row: jax.random.permutation(one_key, one_row))(shuffle_keys, labels)
    return shuffled.reshape(TOKENS).astype(jnp.int32)


def draw_lengths(key, part):
    key = jax.random.fold_in(key, 11)
    key_short, key_order = jax.random.split(key)
    short_len = jax.random.randint(key_short, (), TB // 2, TB)
    long_len = TOKENS - short_len
    long_first = jax.random.randint(key_order, (), 0, 2)
    return jnp.where(long_first == 1, jnp.stack([long_len, short_len]), jnp.stack([short_len, long_len])).astype(jnp.int32)


def draw_step_bias(key, part):
    key = jax.random.fold_in(key, 13)
    key_kind, key_slow, key_fast, key_jitter = jax.random.split(key, 4)
    slow_share = 0.5
    slow_pick = jax.random.uniform(key_kind, (1, E)) < slow_share
    slow_value = jnp.log(0.25 / TOKENS) + jax.random.uniform(key_slow, (1, E), minval=-0.5, maxval=0.5)
    fast_value = jnp.log(jax.random.uniform(key_fast, (1, E), minval=0.02, maxval=0.06))
    jitter = jax.random.uniform(key_jitter, (MODS, E), minval=-0.3, maxval=0.3)
    return (jnp.where(slow_pick, slow_value, fast_value) + jitter).astype(jnp.bfloat16)


def steps_of(own_key, extent, shards, least, high):
    gain = 1.0
    for axis_at, blocks in shards:
        heights = jax.random.uniform(jax.random.fold_in(jax.random.fold_in(own_key, 6), axis_at), (blocks,), jnp.float32, least / len(shards), high / len(shards))
        gain = gain * jnp.repeat(jnp.exp(heights), extent[axis_at] // blocks).reshape((-1,) + (1,) * (len(extent) - 1 - axis_at))
    return gain


def centred(own_key, extent, deviation, reach, shards=(), held_as=jnp.bfloat16):
    result = deviation * jax.random.normal(own_key, extent, jnp.float32)
    if shards:
        result = result * steps_of(own_key, extent, shards, -0.22, 0.18)
    return jnp.clip(result, -reach, reach).astype(held_as)


def setup_inputs(seed: int = 0) -> dict:
    keys = jax.random.split(jax.random.key(seed), 15)
    return {
        "tokens": centred(keys[0], (TOKENS, D), 1.0, 6.0, ((0, 32),)),
        "modality": draw_modality(jax.random.fold_in(keys[14], 71), 0),
        "lengths": draw_lengths(jax.random.fold_in(keys[14], 71), 0),
        "norm_gain": jnp.clip(1.0 + 0.1 * jax.random.normal(keys[3], (D,), jnp.float32), 0.5, 1.5).astype(jnp.bfloat16),
        "input_weight": centred(keys[4], (MODS, D, 2, E), D ** -0.5, 0.125, ((1, 8), (3, 4))),
        "param_weight": centred(keys[5], (MODS, E, R + 2 * N), E ** -0.5, 0.09375, ((1, 32),)),
        "step_weight": centred(keys[6], (MODS, R, E), R ** -0.5, 0.5, ((2, 32),)),
        "step_bias": draw_step_bias(jax.random.fold_in(keys[14], 71), 0),
        "output_weight": centred(keys[8], (MODS, E, D), (E // 8) ** -0.5, 0.25, ((1, 4), (2, 8))),
        "conv_weight": centred(keys[9], (KW, E), KW ** -0.5, 3.0, ((1, 32),)),
        "conv_bias": centred(keys[10], (E,), 0.5, 3.0, ((0, 32),)),
        "decay_log": jnp.clip(1.5 * jax.random.uniform(keys[11], (N, E), jnp.float32) ** steps_of(keys[11], (N, E), ((1, 32),), -0.2, 0.2), 0.0, 1.5).astype(jnp.bfloat16),
        "skip_gain": jnp.clip(0.5 + 1.0 * jax.random.uniform(keys[12], (E,), jnp.float32) ** steps_of(keys[12], (E,), ((0, 32),), -0.2, 0.2), 0.5, 1.5).astype(jnp.bfloat16),
        "cotangent": centred(keys[13], (TOKENS, D), 1.0, 6.0, ((0, 32),)),
    }


@jax.custom_vjp
def low(v):
    return lax.optimization_barrier(v.astype(jnp.bfloat16)).astype(jnp.float32)

@jax.custom_vjp
def low_back(v):
    return v

def low_keep(v):
    return (low(v), None)

def low_pass(kept, grad):
    return (grad,)

def back_keep(v):
    return (v, None)

def back_low(kept, grad):
    return (low(grad),)
low.defvjp(low_keep, low_pass)
low_back.defvjp(back_keep, back_low)
EPSILON = 1e-05
HIGHEST = lax.Precision.HIGHEST

def modal_mix(values, weight, modal_ids):
    combined = jnp.zeros((values.shape[0], weight.shape[2]), jnp.float32)
    for modal_index in range(MODS):
        product = jnp.dot(values, weight[modal_index], precision=HIGHEST, preferred_element_type=jnp.float32)
        combined = combined + jnp.where((modal_ids == modal_index)[:, None], product, 0.0)
    return combined

def modal_select(table, modal_ids):
    picked = jnp.zeros((modal_ids.shape[0], table.shape[1]), jnp.float32)
    for modal_index in range(MODS):
        picked = picked + jnp.where((modal_ids == modal_index)[:, None], table[modal_index][None, :], 0.0)
    return picked

def selective_scan(keeping, step_size, activated, input_mix, output_mix, decay_rate):
    total_len = keeping.shape[0]
    span_rows = math.gcd(total_len, 256)

    def blocked(array_value):
        return array_value.reshape((total_len // span_rows, span_rows) + array_value.shape[1:])

    def run_block(state_now, inputs):

        def one_token(hidden, token_item):
            keep_t, step_t, act_t, in_t, out_t = token_item
            hidden = keep_t * jnp.exp(step_t[None, :] * decay_rate) * hidden + (step_t * act_t)[None, :] * in_t[:, None]
            return (hidden, lax.optimization_barrier(jnp.sum(out_t[:, None] * hidden, axis=0)))
        return lax.scan(one_token, state_now, inputs)
    blocks = (blocked(keeping), blocked(step_size), blocked(activated), blocked(input_mix), blocked(output_mix))
    _, scanned = lax.scan(jax.checkpoint(run_block), jnp.zeros(decay_rate.shape, jnp.float32), blocks)
    return scanned.reshape(total_len, decay_rate.shape[1])

def forward(tokens_f, norm_gain, input_weight, param_weight, step_weight, step_bias, output_weight, conv_weight, conv_bias, decay_log, skip_gain, modality, lengths):
    total_len = tokens_f.shape[0]
    inverse = lax.rsqrt(lax.optimization_barrier(jnp.mean(tokens_f * tokens_f, axis=1, keepdims=True)) + EPSILON)
    normed = low(tokens_f * inverse * norm_gain[None, :])
    inner_width = input_weight.shape[3]
    both = low_back(modal_mix(normed, input_weight.reshape(MODS, input_weight.shape[1], 2 * inner_width), modality))
    inner = both[:, :inner_width]
    gate_pre = both[:, inner_width:]
    places = jnp.arange(total_len, dtype=jnp.int32)
    split_place = lengths[0]
    begins = jnp.where(places >= split_place, split_place, 0)
    conv_pre = jnp.broadcast_to(conv_bias[None, :], inner.shape)
    for tap_index in range(KW):
        lag_rows = KW - 1 - tap_index
        shifted = jnp.concatenate([jnp.zeros((lag_rows, inner_width), inner.dtype), inner[:total_len - lag_rows]], axis=0)
        conv_pre = conv_pre + conv_weight[tap_index][None, :] * jnp.where((places - lag_rows >= begins)[:, None], shifted, 0.0)
    activated = jax.nn.silu(conv_pre)
    features = low_back(modal_mix(low(activated), param_weight, modality))
    step_low = low(features[:, :R])
    input_mix = features[:, R:R + N]
    output_mix = features[:, R + N:]
    step_pre = low_back(modal_mix(step_low, step_weight, modality)) + modal_select(step_bias, modality)
    step_size = jax.nn.softplus(step_pre)
    decay_rate = -jnp.exp(decay_log)
    keeping = (places != begins).astype(tokens_f.dtype)
    scan_out = selective_scan(keeping, step_size, activated, input_mix, output_mix, decay_rate) + skip_gain[None, :] * activated
    gated = low(scan_out * jax.nn.silu(gate_pre))
    branch = low_back(modal_mix(gated, output_weight, modality))
    return tokens_f + branch

def reference(tokens, modality, lengths, norm_gain, input_weight, param_weight, step_weight, step_bias, output_weight, conv_weight, conv_bias, decay_log, skip_gain, cotangent):
    arrays = [array_value.astype(jnp.float32) for array_value in (tokens, norm_gain, input_weight, param_weight, step_weight, step_bias, output_weight, conv_weight, conv_bias, decay_log, skip_gain)]
    output, pullback = jax.vjp(partial(forward, modality=modality, lengths=lengths), *arrays)
    grads = pullback(cotangent.astype(jnp.float32))
    return (output.astype(jnp.bfloat16), grads[0], grads[1], grads[2], grads[3], grads[4], grads[6], grads[7], grads[8], grads[9], grads[10], grads[5])
```

```python
import functools
import math

import jax
import jax.numpy as jnp
from jax import lax
from jax.experimental import pallas as pl
from jax.experimental.pallas import tpu as pltpu
from jax.sharding import PartitionSpec as P

N = 16
KW = 4
R = 128
MODS = 3
TOK_DEV = 128
CAPD = 48


EPSILON = 1e-05
SCAN_ROWS = 512

LANES = 128
SEGMENTS = 8
CHUNK = 32
UNROLL = 8
BACK = 4
COLUMNS = 4
FAR = 1e9
VMEM_BYTES = 60 * 1024 * 1024
f32 = jnp.float32
bf16 = jnp.bfloat16


def shifted_2(value, axis, by):
    size = lax.axis_size(axis)
    pairs = [(i, i + by) for i in range(size) if 0 <= i + by < size]
    return lax.ppermute(value, axis, pairs)


def carried_in(value, axis, combine, identity):
    size, here = (lax.axis_size(axis), lax.axis_index(axis))
    everything = jax.tree.map(
        lambda part, kind: lax.all_gather(part.astype(kind), axis),
        value,
        (jnp.bfloat16, jnp.bfloat16),
    )
    start = jax.tree.map(
        lambda part, zero: jnp.broadcast_to(jnp.asarray(zero, part.dtype), part.shape),
        value,
        identity,
    )

    def carried_hop(k, before):
        reached = k < here
        new = combine(
            before, jax.tree.map(lambda part, own: part[k].astype(own.dtype), everything, value)
        )
        return jax.tree.map(lambda a, b: jnp.where(reached, a, b), new, before)

    return lax.fori_loop(0, size, carried_hop, start)


def prefix(value, axis, combine, identity):
    size, here = (lax.axis_size(axis), lax.axis_index(axis))
    everything = jax.tree.map(lambda part: lax.all_gather(part, axis), value)
    start = jax.tree.map(
        lambda part, zero: jnp.broadcast_to(jnp.asarray(zero, part.dtype), part.shape),
        value,
        identity,
    )

    def prefix_hop(k, before):
        at = size - 1 - k
        reached = at > here
        new = combine(before, jax.tree.map(lambda part: part[at], everything))
        return jax.tree.map(lambda a, b: jnp.where(reached, a, b), new, before)

    return lax.fori_loop(0, size, prefix_hop, start)


def split_rows(count_rows):
    return (count_rows // TOK_DEV, TOK_DEV)


def slot_tables(modal_ids, capacity):
    sub_rows = modal_ids.shape[1]
    marked = (modal_ids[:, :, None] == jnp.arange(MODS, dtype=jnp.int32)[None, None, :]).astype(
        jnp.int32
    )
    ranking = jnp.sum((jnp.cumsum(marked, axis=1) - 1) * marked, axis=2)
    slot_ids = modal_ids * capacity + ranking
    positions = jnp.broadcast_to(jnp.arange(sub_rows, dtype=jnp.int32)[None, :], modal_ids.shape)
    unfilled = jnp.full((modal_ids.shape[0], MODS * capacity), sub_rows, jnp.int32)
    tables = jax.vmap(lambda table_row, slot_row, place_row: table_row.at[slot_row].set(place_row))(
        unfilled, slot_ids, positions
    )
    return (tables, slot_ids)


def group_rows(values, tables, capacity):
    padded = jnp.concatenate([values, jnp.zeros_like(values[:, :1])], axis=1)
    picked = jax.vmap(lambda block_values, block_table: block_values[block_table])(padded, tables)
    return picked.reshape(values.shape[0], MODS, capacity, values.shape[2])


def ungroup_rows(grouped, slot_ids):
    flattened = grouped.reshape(grouped.shape[0], MODS * grouped.shape[2], grouped.shape[3])
    return jax.vmap(lambda block_values, block_slots: block_values[block_slots])(
        flattened, slot_ids
    )


def modal_product(values, modal_ids, weight, transpose):
    count_rows = values.shape[0]
    sub_count, sub_rows = split_rows(count_rows)
    capacity = min(CAPD, sub_rows)
    tables, slot_ids = slot_tables(modal_ids.reshape(sub_count, sub_rows), capacity)
    grouped = group_rows(values.reshape(sub_count, sub_rows, values.shape[1]), tables, capacity)
    if transpose:
        result = jnp.einsum("gmcn,mkn->gmck", grouped, weight, preferred_element_type=jnp.float32)
    else:
        result = jnp.einsum("gmck,mkn->gmcn", grouped, weight, preferred_element_type=jnp.float32)
    return ungroup_rows(result, slot_ids).reshape(count_rows, result.shape[3])


def modal_outer(left, right, modal_ids):
    count_rows = left.shape[0]
    sub_count, sub_rows = split_rows(count_rows)
    capacity = min(CAPD, sub_rows)
    tables, slot_ids = slot_tables(modal_ids.reshape(sub_count, sub_rows), capacity)
    left_grouped = group_rows(left.reshape(sub_count, sub_rows, left.shape[1]), tables, capacity)
    right_grouped = group_rows(right.reshape(sub_count, sub_rows, right.shape[1]), tables, capacity)
    return jnp.einsum(
        "gmcl,gmcr->mlr", left_grouped, right_grouped, preferred_element_type=jnp.float32
    )


def modal_table(table, modal_ids):
    picked = jnp.zeros((modal_ids.shape[0], table.shape[1]), jnp.float32)
    for modal_index in range(MODS):
        picked = (
            picked
            + (modal_ids == modal_index).astype(jnp.float32)[:, None] * table[modal_index][None, :]
        )
    return picked


def modal_sums(values, modal_ids):
    return jnp.stack(
        [
            jnp.sum(values * (modal_ids == modal_index).astype(jnp.float32)[:, None], axis=0)
            for modal_index in range(MODS)
        ]
    )


def pair_combine(earlier, later):
    return (earlier[0] * later[0], later[0] * earlier[1] + later[1])


def back_combine(earlier, later):
    return (earlier[0] * later[0], later[1] + later[0] * earlier[1])


def silu_slope(values):
    sigmoid_part = jax.nn.sigmoid(values)
    return sigmoid_part * (1.0 + values * (1.0 - sigmoid_part))


def local(
    tokens,
    modality,
    lengths,
    norm_gain,
    input_weight,
    param_weight,
    step_weight,
    step_bias,
    output_weight,
    conv_weight,
    conv_bias,
    decay_log,
    skip_gain,
    cotangent,
):
    block_rows = modality.shape[0]
    gathered = (
        lax.all_gather(input_weight, "seq", axis=1, tiled=True),
        lax.all_gather(param_weight, "seq", axis=1, tiled=True),
        lax.all_gather(step_weight, "seq", axis=2, tiled=True),
        lax.all_gather(output_weight, "seq", axis=2, tiled=True),
        lax.all_gather(conv_weight, "seq", axis=1, tiled=True),
        lax.all_gather(conv_bias, "seq", axis=0, tiled=True),
        lax.all_gather(decay_log, "seq", axis=1, tiled=True),
        lax.all_gather(skip_gain, "seq", axis=0, tiled=True),
        lax.all_gather(step_bias, "seq", axis=1, tiled=True),
    )
    in_local = gathered[0]
    param_local = gathered[1]
    step_local = gathered[2]
    out_local = gathered[3]
    tap_weights = gathered[4].astype(jnp.float32)
    tap_bias = gathered[5].astype(jnp.float32)
    decay_rate = -jnp.exp(gathered[6].astype(jnp.float32))
    skip_local = gathered[7].astype(jnp.float32)
    bias_local = gathered[8].astype(jnp.float32)
    channels = in_local.shape[3]
    model_width = in_local.shape[1]
    in_flat = in_local.reshape(MODS, model_width, 2 * channels)
    token_vals = tokens.astype(jnp.float32)
    inverse = lax.rsqrt(jnp.mean(token_vals * token_vals, axis=1, keepdims=True) + EPSILON)
    normal_rows = token_vals * inverse
    gain_vals = norm_gain.astype(jnp.float32)
    normed = (normal_rows * gain_vals[None, :]).astype(jnp.bfloat16)
    piece = lax.all_gather(normed, "mod", axis=0, tiled=True)
    piece_ids = modality
    product = modal_product(piece, piece_ids, in_flat, False)
    filled = product
    folded = (filled, piece)
    expanded = folded[0].reshape(block_rows, 2, channels)
    inner = expanded[:, 0]
    gate_pre = expanded[:, 1]
    first_place = lax.axis_index("seq") * block_rows
    places = first_place + jnp.arange(block_rows, dtype=jnp.int32)
    split_place = lengths[0]
    begins = jnp.where(places >= split_place, split_place, 0)
    keeping = (places != begins).astype(jnp.float32)
    inherit = (begins < first_place).astype(jnp.float32)
    halo_rows = shifted_2(inner[block_rows - KW + 1 :], "seq", 1)
    extended = jnp.concatenate([halo_rows, inner], axis=0)
    valid_taps = [
        (places - (KW - 1 - tap_index) >= begins).astype(jnp.float32)[:, None]
        for tap_index in range(KW)
    ]
    conv_pre = jnp.broadcast_to(tap_bias[None, :], inner.shape)
    for tap_index in range(KW):
        conv_pre = (
            conv_pre
            + tap_weights[tap_index][None, :]
            * extended[tap_index : tap_index + block_rows]
            * valid_taps[tap_index]
        )
    activated = jax.nn.silu(conv_pre)
    act_low = activated.astype(jnp.bfloat16)
    feature_part = modal_product(act_low, modality, param_local, False)
    features = lax.psum(feature_part, "mod")
    step_low = features[:, :R].astype(jnp.bfloat16)
    input_mix = features[:, R : R + N]
    output_mix = features[:, R + N :]
    step_pre = modal_product(step_low, modality, step_local, False) + modal_table(
        bias_local, modality
    )
    step_size = jax.nn.softplus(step_pre)
    scan_rows = math.gcd(block_rows, SCAN_ROWS)
    scan_count = block_rows // scan_rows

    def blocked(values):
        return values.reshape((scan_count, scan_rows) + values.shape[1:])

    def block_mult(keep_block, step_block):
        return keep_block[:, None, None] * jnp.exp(step_block[:, None, :] * decay_rate[None])

    def local_step(state_now, inputs):
        keep_block, step_block, act_block, input_block, output_block = inputs
        multiplier = block_mult(keep_block, step_block)
        addition = (step_block * act_block)[:, None, :] * input_block[:, :, None]
        running = lax.associative_scan(pair_combine, (multiplier, addition), axis=0)
        states = running[0] * state_now[None] + running[1]
        return (
            states[-1],
            (jnp.sum(output_block[:, :, None] * states, axis=1), state_now, running[0], running[1]),
        )

    scan_inputs = (
        blocked(keeping),
        blocked(step_size),
        blocked(activated),
        blocked(input_mix),
        blocked(output_mix),
    )
    end_state, (local_out, local_starts, run_mult, run_add) = lax.scan(
        local_step, jnp.zeros((N, channels), jnp.float32), scan_inputs
    )
    device_decay = jnp.exp(decay_rate * jnp.sum(step_size, axis=0)[None, :]) * jnp.min(keeping)
    chained = carried_in(
        (device_decay, end_state),
        "seq",
        pair_combine,
        (jnp.ones_like(device_decay), jnp.zeros_like(end_state)),
    )
    state_in = chained[1]

    def fix_step(carried, inputs):
        total_step, alive = carried
        inherit_block, step_block, output_block = inputs
        start_factor = alive * jnp.exp(decay_rate * total_step[None, :])
        running_step = total_step[None, :] + jnp.cumsum(step_block, axis=0)
        reach = inherit_block[:, None, None] * jnp.exp(running_step[:, None, :] * decay_rate[None])
        extra = jnp.sum(output_block[:, :, None] * reach * state_in[None], axis=1)
        return ((running_step[-1], inherit_block[-1]), (extra, start_factor))

    reach_inputs = (blocked(inherit), blocked(step_size), blocked(output_mix))
    _, (extra_out, start_factors) = lax.scan(
        fix_step, (jnp.zeros((channels,), jnp.float32), jnp.float32(1.0)), reach_inputs
    )
    start_states = local_starts + start_factors * state_in[None]
    scan_out = (local_out + extra_out).reshape(block_rows, channels) + skip_local[
        None, :
    ] * activated
    gate_act = jax.nn.silu(gate_pre)
    gated = (scan_out * gate_act).astype(jnp.bfloat16)
    piece = gated
    piece_ids = modality
    branch = lax.psum_scatter(
        modal_product(piece, piece_ids, out_local, False), "mod", scatter_dimension=0, tiled=True
    )
    output = (token_vals + branch).astype(jnp.bfloat16)
    back_rows = cotangent.astype(jnp.float32)
    piece = lax.all_gather(cotangent, "mod", axis=0, tiled=True)
    piece_ids = modality
    product = modal_product(piece, piece_ids, out_local, True)
    grad_out = modal_outer(gated, piece, piece_ids)
    grad_scan = product * gate_act
    grad_gate = product * scan_out * silu_slope(gate_pre)
    grad_skip = jnp.sum(grad_scan * activated, axis=0)
    grad_act = grad_scan * skip_local[None, :]

    def lead_step(carried, inputs):
        total_step, lead_sum = carried
        inherit_block, step_block, output_block, grad_block = inputs
        running_step = total_step[None, :] + jnp.cumsum(step_block, axis=0)
        reach = inherit_block[:, None, None] * jnp.exp(running_step[:, None, :] * decay_rate[None])
        lead_sum = lead_sum + jnp.sum(
            reach * output_block[:, :, None] * grad_block[:, None, :], axis=0
        )
        return ((running_step[-1], lead_sum), None)

    (_, lead_local), _ = lax.scan(
        lead_step,
        (jnp.zeros((channels,), jnp.float32), jnp.zeros((N, channels), jnp.float32)),
        reach_inputs + (blocked(grad_scan),),
    )
    incoming = prefix(
        (device_decay, lead_local),
        "seq",
        back_combine,
        (jnp.ones_like(device_decay), jnp.zeros_like(lead_local)),
    )[1]

    def back_step(carried, inputs):
        after_block, rate_grad = carried
        (
            keep_block,
            step_block,
            act_block,
            input_block,
            output_block,
            grad_block,
            start_state,
            mult_block,
            add_block,
        ) = inputs
        multiplier = block_mult(keep_block, step_block)
        states = mult_block * start_state[None] + add_block
        previous = jnp.concatenate([start_state[None], states[:-1]], axis=0)
        pushed = output_block[:, :, None] * grad_block[:, None, :]
        pushed = pushed.at[-1].add(after_block)
        shifted = jnp.concatenate([multiplier[1:], jnp.ones_like(multiplier[:1])], axis=0)
        flipped = lax.associative_scan(pair_combine, (shifted[::-1], pushed[::-1]), axis=0)
        grad_state = flipped[1][::-1]
        mult_grad = grad_state * previous * multiplier
        state_input = jnp.sum(grad_state * input_block[:, :, None], axis=1)
        step_grad = jnp.sum(mult_grad * decay_rate[None], axis=1) + state_input * act_block
        rate_grad = rate_grad + jnp.sum(mult_grad * step_block[:, None, :], axis=0)
        input_grad = jnp.sum(grad_state * (step_block * act_block)[:, None, :], axis=2)
        act_grad = state_input * step_block
        output_grad = jnp.sum(states * grad_block[:, None, :], axis=2)
        return (
            (multiplier[0] * grad_state[0], rate_grad),
            (step_grad, input_grad, act_grad, output_grad),
        )

    back_inputs = scan_inputs[:5] + (blocked(grad_scan), start_states, run_mult, run_add)
    (_, rate_total), (step_grads, input_grads, act_grads, output_grads) = lax.scan(
        back_step, (incoming, jnp.zeros((N, channels), jnp.float32)), back_inputs, reverse=True
    )
    step_pre_grad = step_grads.reshape(block_rows, channels) * jax.nn.sigmoid(step_pre)
    grad_bias = modal_sums(step_pre_grad, modality)
    step_grad_low = step_pre_grad.astype(jnp.bfloat16)
    step_in_part = modal_product(step_grad_low, modality, step_local, True)
    grad_step = modal_outer(step_low, step_grad_low, modality)
    summed = lax.psum(
        (step_in_part, input_grads.reshape(block_rows, N), output_grads.reshape(block_rows, N)),
        "mod",
    )
    feature_grad = jnp.concatenate(summed, axis=1).astype(jnp.bfloat16)
    grad_param = modal_outer(act_low, feature_grad, modality)
    act_total = (
        grad_act
        + act_grads.reshape(block_rows, channels)
        + modal_product(feature_grad, modality, param_local, True)
    )
    conv_grad = act_total * silu_slope(conv_pre)
    tap_grads = []
    ext_grad = jnp.zeros((block_rows + KW - 1, channels), jnp.float32)
    for tap_index in range(KW):
        masked = conv_grad * valid_taps[tap_index]
        tap_grads.append(jnp.sum(masked * extended[tap_index : tap_index + block_rows], axis=0))
        ext_grad = ext_grad.at[tap_index : tap_index + block_rows].add(
            masked * tap_weights[tap_index][None, :]
        )
    grad_taps = jnp.stack(tap_grads)
    grad_tap_bias = jnp.sum(conv_grad, axis=0)
    spill = shifted_2(ext_grad[: KW - 1], "seq", -1)
    inner_grad = ext_grad[KW - 1 :].at[block_rows - KW + 1 :].add(spill)
    both_grad = (
        jnp.stack([inner_grad, grad_gate], axis=1)
        .astype(jnp.bfloat16)
        .reshape(block_rows, 2 * channels)
    )
    piece = both_grad
    piece_ids = modality
    normed_grad = lax.psum_scatter(
        modal_product(piece, piece_ids, in_flat, True), "mod", scatter_dimension=0, tiled=True
    )
    grad_in = modal_outer(folded[1], both_grad, modality)
    gain_part = jnp.sum(normed_grad * normal_rows, axis=0)
    hat_grad = normed_grad * gain_vals[None, :]
    token_grad = back_rows + inverse * (
        hat_grad - normal_rows * jnp.mean(hat_grad * normal_rows, axis=1, keepdims=True)
    )
    grad_gain = lax.psum(gain_part, ("seq", "mod"))
    grad_decay = rate_total * decay_rate
    weight_grads = (
        lax.psum_scatter(
            grad_in.reshape(MODS, model_width, 2, channels), "seq", scatter_dimension=1, tiled=True
        ),
        lax.psum_scatter(grad_param, "seq", scatter_dimension=1, tiled=True),
        lax.psum_scatter(grad_step, "seq", scatter_dimension=2, tiled=True),
        lax.psum_scatter(grad_out, "seq", scatter_dimension=2, tiled=True),
        lax.psum_scatter(grad_taps, "seq", scatter_dimension=1, tiled=True),
        lax.psum_scatter(grad_tap_bias, "seq", scatter_dimension=0, tiled=True),
        lax.psum_scatter(grad_decay, "seq", scatter_dimension=1, tiled=True),
        lax.psum_scatter(grad_skip, "seq", scatter_dimension=0, tiled=True),
        lax.psum_scatter(grad_bias, "seq", scatter_dimension=1, tiled=True),
    )
    return (
        output,
        token_grad,
        grad_gain,
        weight_grads[0],
        weight_grads[1],
        weight_grads[2],
        weight_grads[3],
        weight_grads[4],
        weight_grads[5],
        weight_grads[6],
        weight_grads[7],
        weight_grads[8],
    )


def pick(ids, parts):
    return jnp.where(ids == 0, parts[0], jnp.where(ids == 1, parts[1], parts[2]))


def silu(values):
    return values * jax.nn.sigmoid(values)


def softplus(values):
    small = jnp.exp(-jnp.abs(values))
    series = small * (
        1.0 + small * (-1 / 2 + small * (1 / 3 + small * (-1 / 4 + small * (1 / 5 - small / 6))))
    )
    return jnp.maximum(values, 0.0) + jnp.where(small < 0.05, series, jnp.log(1.0 + small))


def dot(left, right, left_dim=1, right_dim=0):
    return lax.dot_general(
        left, right, (((left_dim,), (right_dim,)), ((), ())), preferred_element_type=f32
    )


def row_places(first, rows):
    return first + lax.broadcasted_iota(jnp.int32, (rows, 1), 0)


def lane(values, at):
    return jnp.broadcast_to(values[:, at : at + 1], (SEGMENTS, LANES))


def tile(at):
    return pl.ds(at * LANES, LANES)


def whole(shape):
    return pl.BlockSpec(shape, lambda *_: (0,) * len(shape), pipeline_mode=pl.Buffered(1))


def cost(micros, flops=0):
    return pl.CostEstimate(flops=flops, bytes_accessed=int(micros * 3.69e6), transcendentals=0)


def modal_dot(values, ids, weight):
    part = values[0].shape[1]
    wide = sum(dot(v[...], weight[i * part : (i + 1) * part, :]) for i, v in enumerate(values))
    channels = wide.shape[1] // MODS
    return pick(ids, [wide[:, m * channels : (m + 1) * channels] for m in range(MODS)])


def put_masked(ref, rows, ids, values):
    channels = values.shape[1]
    for m in range(MODS):
        ref[rows, m * channels : (m + 1) * channels] = jnp.where(ids == m, values, 0.0).astype(
            ref.dtype
        )


def arrange(blocks, first, out):
    slab = out.shape[0] // blocks.shape[0]
    channels = blocks.shape[3]
    for at in range(blocks.shape[0]):
        for m in range(MODS):
            out[at * slab : (at + 1) * slab, m * channels : (m + 1) * channels] = blocks[
                at, first + m, 0:slab, :
            ]


def project_kernel(lengths, place, *refs):
    pieces, refs = refs[: 4 * COLUMNS], refs[4 * COLUMNS :]
    ids_ref, ids_rows, blocks, taps, bias, param_t = refs[:6]
    xs, refs = refs[6 : 6 + COLUMNS], refs[6 + COLUMNS :]
    w, w_gate, inner_ref, pre_ref, low_ref, feats, ext = refs
    step = pl.program_id(0)

    @pl.when(step == 0)
    def _():
        arrange(blocks, 0, w)
        arrange(blocks, MODS, w_gate)

    block_rows = pieces[0].shape[3]
    for which in (0, 1):

        @pl.when((place[0] == step % 2) == (which == 0))
        def _():
            for at in range(COLUMNS):
                own_line, other_line = pieces[4 * at + 2 * which : 4 * at + 2 * which + 2]
                here = place[1] if at % 2 == 0 else place[2]
                for near in (0, 1):
                    for line, value in ((here, own_line), (1 - here, other_line)):
                        block = line * 2 + near if at % 2 == 0 else near * 2 + line
                        row = pl.multiple_of(block * block_rows, block_rows)
                        xs[at][pl.ds(row, block_rows), :] = value[near, 0, 0]

    rows = xs[0].shape[0]
    channels = inner_ref.shape[1]
    ids = ids_ref[...]
    inner = modal_dot(xs, ids, w)
    inner_ref[...] = inner

    @pl.when(step == 0)
    def _():
        ext[0:8, :] = jnp.zeros((8, channels), f32)

    @pl.when(step > 0)
    def _():
        ext[0:8, :] = ext[rows : rows + 8, :]

    ext[8 : 8 + rows, :] = inner
    places = row_places(step * rows, rows)
    split = lengths[0]
    begins = jnp.where(places >= split, split, 0)
    pre = jnp.broadcast_to(bias[...], (rows, channels))
    for tap in range(KW):
        lag = KW - 1 - tap
        shifted = ext[8 - lag : 8 - lag + rows, :]
        pre = pre + taps[tap : tap + 1, :] * jnp.where(places - lag >= begins, shifted, 0.0)
    pre_ref[...] = pre
    low = silu(pre).astype(bf16)
    low_ref[...] = low
    across = feats.shape[2]
    ours = jnp.where(place[0] == step % 2, 1, 0)
    for j in range(across):
        block = low[j * block_rows : (j + 1) * block_rows]
        feats[ours, step // 2, j] = pick(
            ids_rows[pl.ds(step * across + j, 1), :],
            [dot(param_t[m], block, 1, 1) for m in range(MODS)],
        )


def project(lengths, place, pieces, ids, ids_rows, blocks, taps, bias, param_t):
    total = ids.shape[0]
    channels = taps.shape[1]
    chips, across = lax.axis_size("z"), lax.axis_size("mod")
    rows = total // (2 * chips)
    width = pieces[0].shape[4]
    by_rows = lambda i: (i, 0)
    feats = (2, chips, across, param_t.shape[1], rows // across)
    smem = pl.BlockSpec(memory_space=pltpu.SMEM)
    return pl.pallas_call(
        project_kernel,
        grid=(total // rows,),
        in_specs=[
            smem,
            smem,
            *[
                pl.BlockSpec((2, 1, 1) + piece.shape[3:], lambda i: (0, i // 2 % 2, i // 4, 0, 0))
                for piece in pieces
            ],
            pl.BlockSpec((rows, 1), by_rows),
            whole(ids_rows.shape),
            whole(blocks.shape),
            whole(taps.shape),
            whole(bias.shape),
            whole(param_t.shape),
        ],
        out_specs=[pl.BlockSpec((rows, width), by_rows)] * COLUMNS
        + [whole((COLUMNS * width, MODS * channels))] * 2
        + [pl.BlockSpec((rows, channels), by_rows)] * 3
        + [whole(feats)],
        out_shape=[jax.ShapeDtypeStruct((total, width), bf16)] * COLUMNS
        + [jax.ShapeDtypeStruct((COLUMNS * width, MODS * channels), bf16)] * 2
        + [jax.ShapeDtypeStruct((total, channels), f32)] * 2
        + [jax.ShapeDtypeStruct((total, channels), bf16)]
        + [jax.ShapeDtypeStruct(feats, f32)],
        scratch_shapes=[pltpu.VMEM((rows + 8, channels), f32)],
        compiler_params=pltpu.CompilerParams(vmem_limit_bytes=VMEM_BYTES),
        cost_estimate=cost(1),
        name="project",
    )(lengths, place, *pieces, ids, ids_rows, blocks, taps, bias, param_t)


def modal_kernel(*refs):
    *xs, ids_ref, w, out = refs
    out[...] = modal_dot(xs, ids_ref[...], w)


def modal_rows(values, ids, weight):
    total = values[0].shape[0]
    channels = weight.shape[1] // MODS
    rows = math.gcd(total, 512)
    by_rows = lambda i: (i, 0)
    return pl.pallas_call(
        modal_kernel,
        grid=(total // rows,),
        in_specs=[
            *[pl.BlockSpec((rows, part.shape[1]), by_rows) for part in values],
            pl.BlockSpec((rows, 1), by_rows),
            whole(weight.shape),
        ],
        out_specs=pl.BlockSpec((rows, channels), by_rows),
        out_shape=jax.ShapeDtypeStruct((total, channels), f32),
        compiler_params=pltpu.CompilerParams(vmem_limit_bytes=VMEM_BYTES),
        cost_estimate=cost(1),
        name="modal_rows",
    )(*values, ids, weight)


def side_kernel(*refs):
    out, columns = refs[-1], refs[0].shape[1]
    for at, part in enumerate(refs[:-1]):
        out[:, at * columns : (at + 1) * columns] = part[...]


def side_by_side(*parts):
    rows, columns = parts[0].shape
    step = math.gcd(rows, 512)
    by_rows = lambda i: (i, 0)
    return pl.pallas_call(
        side_kernel,
        grid=(rows // step,),
        in_specs=[pl.BlockSpec((step, columns), by_rows)] * len(parts),
        out_specs=pl.BlockSpec((step, columns * len(parts)), by_rows),
        out_shape=jax.ShapeDtypeStruct((rows, columns * len(parts)), parts[0].dtype),
        cost_estimate=cost(1),
        name="side_by_side",
    )(*parts)


def gates_kernel(
    cot, ids_ref, blocks, pre, out, w_out, grad_scan, gate_wide, gated_wide, gate_low, gated_low
):
    @pl.when(pl.program_id(0) == 0)
    def _():
        arrange(blocks, 0, w_out)

    ids = ids_ref[...]
    here = pre[...]
    grad = modal_dot([cot], ids, w_out)
    sig = jax.nn.sigmoid(here)
    scanned = out[...]
    grad_scan[...] = grad * (here * sig)
    gate_grad = grad * scanned * (sig * (1.0 + here * (1.0 - sig)))
    gated = scanned * (here * sig)
    gate_low[...] = gate_grad.astype(bf16)
    gated_low[...] = gated.astype(bf16)
    put_masked(gate_wide, slice(None), ids, gate_grad)
    put_masked(gated_wide, slice(None), ids, gated)


def gates(cotangents, ids, blocks, pre, out):
    total, channels = out.shape
    width = cotangents.shape[1]
    rows = total // size_of(SEQ)
    by_rows = lambda i: (i, 0)
    block = pl.BlockSpec((rows, channels), by_rows)
    wide = pl.BlockSpec((rows, MODS * channels), by_rows)
    return pl.pallas_call(
        gates_kernel,
        grid=(total // rows,),
        in_specs=[
            pl.BlockSpec((rows, width), by_rows),
            pl.BlockSpec((rows, 1), by_rows),
            whole(blocks.shape),
            block,
            block,
        ],
        out_specs=[whole((width, MODS * channels)), block, wide, wide, block, block],
        out_shape=[
            jax.ShapeDtypeStruct((width, MODS * channels), bf16),
            jax.ShapeDtypeStruct((total, channels), f32),
            jax.ShapeDtypeStruct((total, MODS * channels), bf16),
            jax.ShapeDtypeStruct((total, MODS * channels), bf16),
            jax.ShapeDtypeStruct((total, channels), bf16),
            jax.ShapeDtypeStruct((total, channels), bf16),
        ],
        compiler_params=pltpu.CompilerParams(vmem_limit_bytes=VMEM_BYTES),
        cost_estimate=cost(1),
        name="gates",
    )(cotangents, ids, blocks, pre, out)


def scan_kernel(
    lengths,
    ids_ref,
    feats,
    pre,
    step_w,
    step_b,
    rate,
    skip,
    states,
    enter,
    step_pre,
    mix,
    scan_out,
    s_turn,
    u_turn,
    mix_turn,
    y_turn,
    held,
):
    chunk = pl.program_id(0)
    total = pre.shape[0]
    length = total // SEGMENTS
    steps = states.shape[0] // SEGMENTS
    split = lengths[0]
    rows_on = UNROLL * SEGMENTS

    def rated(n):
        return jnp.broadcast_to(rate[n : n + 1, :], (SEGMENTS, LANES))

    def cut(values):
        return [values[j * SEGMENTS : (j + 1) * SEGMENTS] for j in range(UNROLL)]

    @pl.when(chunk == 0)
    def _():
        for seg in range(SEGMENTS):
            rows = pl.ds(seg * length, length)
            turned = pl.ds(seg, length, stride=SEGMENTS)
            ids = ids_ref[rows, :]
            block_rows = length // feats.shape[2]
            for j in range(feats.shape[2]):
                block = pl.ds(seg * length + j * block_rows, block_rows)
                block_ids = ids_ref[block, :]
                low = feats[seg % 2, seg // 2, j, 0:R, :]
                step_pre[block, :] = pick(
                    block_ids, [dot(low, step_w[m], 0, 0) for m in range(MODS)]
                ) + pick(block_ids, [step_b[m : m + 1, :] for m in range(MODS)])
                mixed = feats[seg % 2, seg // 2, j, R : R + 2 * N, :].astype(f32)
                mixed = mixed + feats[seg % 2, seg // 2, j, R + 2 * N :, :].astype(f32)
                blank = jnp.zeros((LANES - 2 * N, block_rows), f32)
                mix[block, :] = jnp.transpose(jnp.concatenate([mixed, blank], axis=0))
            step = softplus(step_pre[rows, :])
            places = row_places(seg * length, length)
            start = (places == 0) | (places == split)
            s_turn[turned, :] = jnp.where(start, FAR, step)
            u_turn[turned, :] = step * silu(pre[rows, :])
            mix_turn[turned, :] = mix[rows, :]

        def ahead(i, spent):
            at = pl.ds(pl.multiple_of(i * rows_on, rows_on), rows_on)
            s, u, bc = [cut(v[at, :]) for v in (s_turn, u_turn, mix_turn)]
            for n in range(N):
                rate_n, hidden = rated(n), held[:, tile(n)]
                for j in range(UNROLL):
                    hidden = jnp.exp2(s[j] * rate_n) * hidden + u[j] * lane(bc[j], n)
                held[:, tile(n)] = hidden
            return spent + sum(s)

        zero = jnp.zeros((SEGMENTS, LANES), f32)
        held[...] = jnp.zeros(held.shape, f32)
        spent = lax.fori_loop(0, length // UNROLL, ahead, zero)
        first = lax.broadcasted_iota(jnp.int32, (SEGMENTS, LANES), 0) == 0
        for n in range(N):
            through = jnp.exp2(spent * rated(n))
            end = held[:, tile(n)]
            inside = zero
            for _ in range(SEGMENTS - 1):
                inside = jnp.where(first, 0.0, pltpu.roll(end + through * inside, 1, 0))
            held[:, tile(n)] = inside
            enter[:, tile(n)] = inside

    base = chunk * steps

    def steps_on(i, carried):
        at = pl.ds(pl.multiple_of((base + i * UNROLL) * SEGMENTS, rows_on), rows_on)
        s, u, bc = [cut(v[at, :]) for v in (s_turn, u_turn, mix_turn)]
        result = [0.0] * UNROLL
        for n in range(N):
            rate_n, hidden = rated(n), held[:, tile(n)]
            for j in range(UNROLL):
                hidden = jnp.exp2(s[j] * rate_n) * hidden + u[j] * lane(bc[j], n)
                out = pl.ds(pl.multiple_of((i * UNROLL + j) * SEGMENTS, SEGMENTS), SEGMENTS)
                states[out, tile(n)] = hidden
                result[j] = result[j] + hidden * lane(bc[j], N + n)
            held[:, tile(n)] = hidden
        y_turn[at, :] = jnp.concatenate(result, axis=0)
        return carried

    lax.fori_loop(0, steps // UNROLL, steps_on, 0)

    @pl.when(chunk == pl.num_programs(0) - 1)
    def _():
        for seg in range(SEGMENTS):
            rows = pl.ds(seg * length, length)
            turned = pl.ds(seg, length, stride=SEGMENTS)
            scan_out[rows, :] = y_turn[turned, :] + skip[...] * silu(pre[rows, :])


def scan(lengths, ids, feats, pre, step_w, step_b, rate, skip):
    total, channels = pre.shape
    steps = math.gcd(total // SEGMENTS, CHUNK)
    rows = steps * SEGMENTS
    turn = pltpu.VMEM((total, channels), f32)
    ins = (ids, feats, pre, step_w, step_b, rate, skip)
    return pl.pallas_call(
        scan_kernel,
        grid=(total // rows,),
        in_specs=[pl.BlockSpec(memory_space=pltpu.SMEM)] + [whole(a.shape) for a in ins],
        out_specs=[
            pl.BlockSpec((rows, N * channels), lambda i: (i, 0)),
            whole((SEGMENTS, N * channels)),
            whole((total, channels)),
            whole((total, channels)),
            whole((total, channels)),
        ],
        out_shape=[
            jax.ShapeDtypeStruct((total, N * channels), f32),
            jax.ShapeDtypeStruct((SEGMENTS, N * channels), f32),
            jax.ShapeDtypeStruct((total, channels), f32),
            jax.ShapeDtypeStruct((total, channels), f32),
            jax.ShapeDtypeStruct((total, channels), f32),
        ],
        scratch_shapes=[turn, turn, turn, turn, pltpu.VMEM((SEGMENTS, N * channels), f32)],
        compiler_params=pltpu.CompilerParams(vmem_limit_bytes=VMEM_BYTES),
        cost_estimate=cost(1),
        name="scan",
    )(lengths, *ins)


def back_kernel(
    lengths,
    core,
    ids_ref,
    ids_rows,
    mix,
    pre,
    step_pre,
    grad,
    states,
    before,
    enter,
    step_w,
    rate,
    skip,
    gather_in,
    gather_out,
    act_part,
    step_grad_low,
    feat_part,
    sums,
    rate_out,
    s_turn,
    u_turn,
    g_turn,
    mix_turn,
    step_turn,
    in_turn,
    mix_grad,
    in_terms,
    out_terms,
    held,
    rate_sum,
):
    turn_at = pl.program_id(0)
    chunks = pl.num_programs(0)
    chunk = chunks - 1 - turn_at
    total = pre.shape[0]
    length = total // SEGMENTS
    steps = states.shape[0] // SEGMENTS
    split = lengths[0]
    zero = jnp.zeros((SEGMENTS, LANES), f32)

    def rated(n):
        return jnp.broadcast_to(rate[n : n + 1, :], (SEGMENTS, LANES))

    def cut(values):
        count = values.shape[0] // SEGMENTS
        return [values[j * SEGMENTS : (j + 1) * SEGMENTS] for j in range(count)]

    @pl.when(turn_at == 0)
    def _():
        for seg in range(SEGMENTS):
            rows = pl.ds(seg * length, length)
            turned = pl.ds(seg, length, stride=SEGMENTS)
            step = softplus(step_pre[rows, :])
            places = row_places(seg * length, length)
            start = (places == 0) | (places == split)
            s_turn[turned, :] = jnp.where(start, FAR, step)
            u_turn[turned, :] = step * silu(pre[rows, :])
            mix_turn[turned, :] = mix[rows, :]
            g_turn[turned, :] = grad[rows, :]

        def ahead(i, spent):
            rows_on = UNROLL * SEGMENTS
            first_row = total - (i + 1) * rows_on
            at = pl.ds(pl.multiple_of(first_row, rows_on), rows_on)
            s, g, bc = [cut(v[at, :]) for v in (s_turn, g_turn, mix_turn)]
            for n in range(N):
                rate_n, pulled = rated(n), held[:, tile(n)]
                for j in reversed(range(UNROLL)):
                    pulled = jnp.exp2(s[j] * rate_n) * (pulled + g[j] * lane(bc[j], N + n))
                held[:, tile(n)] = pulled
            return spent + sum(s)

        held[...] = jnp.zeros(held.shape, f32)
        spent = lax.fori_loop(0, length // UNROLL, ahead, zero)
        last = lax.broadcasted_iota(jnp.int32, (SEGMENTS, LANES), 0) == SEGMENTS - 1
        for n in range(N):
            through = jnp.exp2(spent * rated(n))
            end = held[:, tile(n)]
            inside = zero
            for _ in range(SEGMENTS - 1):
                inside = jnp.where(
                    last, 0.0, pltpu.roll(end + through * inside, SEGMENTS - 1, 0)
                )
            held[:, tile(n)] = inside
            rate_sum[:, tile(n)] = zero

    base = chunk * steps

    def steps_back(low_step, earlier):
        rows_on = BACK * SEGMENTS
        at = pl.ds(pl.multiple_of((base + low_step) * SEGMENTS, rows_on), rows_on)
        here = pl.ds(pl.multiple_of(low_step * SEGMENTS, rows_on), rows_on)
        s, u, g, bc = [cut(v[at, :]) for v in (s_turn, u_turn, g_turn, mix_turn)]
        step_sum, in_sum = [0.0] * BACK, [0.0] * BACK
        for n in range(N):
            rate_n, pull, rate_acc = rated(n), held[:, tile(n)], rate_sum[:, tile(n)]
            state = [earlier(n)] + cut(states[here, tile(n)])
            parts_in, parts_out = [None] * BACK, [None] * BACK
            for j in reversed(range(BACK)):
                grad_state = g[j] * lane(bc[j], N + n) + pull
                pull = jnp.exp2(s[j] * rate_n) * grad_state
                mult = pull * state[j]
                step_sum[j] = step_sum[j] + mult * rate_n
                rate_acc = rate_acc + mult * s[j]
                in_sum[j] = in_sum[j] + grad_state * lane(bc[j], n)
                parts_in[j] = grad_state * u[j]
                parts_out[j] = state[j + 1] * g[j]
            in_terms[here, tile(n)] = jnp.concatenate(parts_in, axis=0).astype(bf16)
            out_terms[here, tile(n)] = jnp.concatenate(parts_out, axis=0).astype(bf16)
            held[:, tile(n)] = pull
            rate_sum[:, tile(n)] = rate_acc
        step_turn[at, :] = jnp.concatenate(step_sum, axis=0)
        in_turn[at, :] = jnp.concatenate(in_sum, axis=0)

    def inside(i, carried):
        low_step = steps - BACK * (i + 1)
        prior = pl.ds(pl.multiple_of((low_step - 1) * SEGMENTS, SEGMENTS), SEGMENTS)
        steps_back(low_step, lambda n: states[prior, tile(n)])
        return carried

    def entering(n):
        return jnp.where(chunk == 0, enter[:, tile(n)], before[:, tile(n)])

    lax.fori_loop(0, steps // BACK - 1, inside, 0)
    steps_back(0, entering)
    mix_grad[pl.ds(pl.multiple_of(base * SEGMENTS, SEGMENTS), steps * SEGMENTS), :] = dot(
        in_terms[...], gather_in[...]
    ) + dot(out_terms[...], gather_out[...])

    @pl.when(turn_at == chunks - 1)
    def _():
        sums[...] = jnp.zeros(sums.shape, f32)
        for seg in range(SEGMENTS):
            rows = pl.ds(seg * length, length)
            turned = pl.ds(seg, length, stride=SEGMENTS)
            ids = ids_ref[rows, :]
            act = silu(pre[rows, :])
            step_in = step_pre[rows, :]
            state_in = in_turn[turned, :]
            grad_here = grad[rows, :]
            step_grad = step_turn[turned, :] * math.log(2.0) + state_in * act
            pre_grad = step_grad * jax.nn.sigmoid(step_in)
            low = pre_grad.astype(bf16)
            step_grad_low[rows, :] = low
            act_part[rows, :] = grad_here * skip[...] + state_in * softplus(step_in)
            block_rows = feat_part.shape[4]
            ours = jnp.where(core[0] == seg % 2, 1, 0)
            for j in range(length // block_rows):
                block = seg * (length // block_rows) + j
                block_low = low[j * block_rows : (j + 1) * block_rows]
                feat_part[ours, seg // 2, j, 0:R, :] = pick(
                    ids_rows[block : block + 1, :],
                    [dot(step_w[m], block_low, 1, 1) for m in range(MODS)],
                )
                part = pl.ds(j * block_rows * SEGMENTS + seg, block_rows, stride=SEGMENTS)
                turned_mix = jnp.transpose(mix_grad[part, :])
                feat_part[ours, seg // 2, j, R : R + 2 * N, :] = turned_mix[: 2 * N]
            for m in range(MODS):
                sums[m : m + 1, :] += jnp.sum(
                    jnp.where(ids == m, pre_grad, 0.0), axis=0, keepdims=True
                )
            sums[MODS : MODS + 1, :] += jnp.sum(grad_here * act, axis=0, keepdims=True)
        for n in range(N):
            rate_out[n : n + 1, :] = jnp.sum(rate_sum[:, tile(n)], axis=0, keepdims=True)


def scan_back(
    lengths, core, ids, ids_rows, mix, pre, step_pre, grad, states, enter, step_w, rate, skip
):
    total, channels = pre.shape
    steps = math.gcd(total // SEGMENTS, CHUNK)
    rows = steps * SEGMENTS
    chunks = total // rows
    turn = pltpu.VMEM((total, channels), f32)
    state_lane = jnp.arange(N * channels, dtype=jnp.int32)[:, None] // channels
    column = jnp.arange(LANES, dtype=jnp.int32)[None, :]
    gather_in = (state_lane == column).astype(bf16)
    gather_out = (state_lane + N == column).astype(bf16)
    across = lax.axis_size("mod")
    feats = (2, lax.axis_size("z"), across, R + 2 * N, ids_rows.shape[1])
    first = (ids, ids_rows, mix, pre, step_pre, grad)
    second = (enter, step_w, rate, skip, gather_in, gather_out)
    return pl.pallas_call(
        back_kernel,
        grid=(chunks,),
        in_specs=[pl.BlockSpec(memory_space=pltpu.SMEM)] * 2
        + [whole(a.shape) for a in first]
        + [
            pl.BlockSpec((rows, N * channels), lambda i: (chunks - 1 - i, 0)),
            pl.BlockSpec(
                (SEGMENTS, N * channels),
                lambda i: (jnp.maximum((chunks - 1 - i) * steps - 1, 0), 0),
            ),
        ]
        + [whole(a.shape) for a in second],
        out_specs=[
            whole((total, channels)),
            whole((total, channels)),
            whole(feats),
            whole((SEGMENTS, channels)),
            whole((N, channels)),
        ],
        out_shape=[
            jax.ShapeDtypeStruct((total, channels), f32),
            jax.ShapeDtypeStruct((total, channels), bf16),
            jax.ShapeDtypeStruct(feats, f32),
            jax.ShapeDtypeStruct((SEGMENTS, channels), f32),
            jax.ShapeDtypeStruct((N, channels), f32),
        ],
        scratch_shapes=[turn] * 7
        + [pltpu.VMEM((rows, N * channels), bf16)] * 2
        + [pltpu.VMEM((SEGMENTS, N * channels), f32)] * 2,
        compiler_params=pltpu.CompilerParams(vmem_limit_bytes=VMEM_BYTES),
        cost_estimate=cost(1),
        name="scan_back",
    )(lengths, core, *first, states, states, *second)


def conv_back_kernel(
    seqs,
    lengths,
    ids_ref,
    feat_grad,
    act_part,
    pre,
    inner,
    taps,
    param_t,
    inner_wide,
    inner_low,
    sums,
    ext,
):
    total, channels = pre.shape
    rows = total // seqs
    split = lengths[0]
    ext[total : total + 8, :] = jnp.zeros((8, channels), f32)
    sums[...] = jnp.zeros(sums.shape, f32)

    def through_silu(i, carried):
        at = pl.ds(pl.multiple_of(i * rows, rows), rows)
        for j in range(feat_grad.shape[2]):
            block_rows = feat_grad.shape[4]
            block = pl.ds(pl.multiple_of(i * rows + j * block_rows, block_rows), block_rows)
            low = feat_grad[i % 2, i // 2, j]
            ext[block, :] = pick(
                ids_ref[block, :], [dot(low, param_t[m], 0, 0) for m in range(MODS)]
            )
        act_grad = act_part[at, :] + ext[at, :]
        here = pre[at, :]
        sig = jax.nn.sigmoid(here)
        conv_grad = act_grad * (sig * (1.0 + here * (1.0 - sig)))
        ext[at, :] = conv_grad
        sums[KW : KW + 1, :] += jnp.sum(conv_grad, axis=0, keepdims=True)
        return carried

    lax.fori_loop(0, total // rows, through_silu, 0)

    for block in range(total // rows):
        first = block * rows
        at = pl.ds(first, rows)
        places = row_places(first, rows)
        here = inner[at, :]
        grad = jnp.zeros((rows, channels), f32)
        for tap in range(KW):
            lag = KW - 1 - tap
            kept = (places >= split) | (places + lag < split)
            later = jnp.where(kept, ext[pl.ds(first + lag, rows), :], 0.0)
            grad = grad + taps[tap : tap + 1, :] * later
            sums[tap : tap + 1, :] += jnp.sum(later * here, axis=0, keepdims=True)
        put_masked(inner_wide, at, ids_ref[at, :], grad)
        inner_low[at, :] = grad.astype(bf16)


def conv_back(seqs, lengths, ids, feat_grad, act_part, pre, inner, taps, param_t):
    total, channels = pre.shape
    ins = (ids, feat_grad, act_part, pre, inner, taps, param_t)
    vmem = pl.BlockSpec(memory_space=pltpu.VMEM)
    return pl.pallas_call(
        functools.partial(conv_back_kernel, seqs),
        in_specs=[pl.BlockSpec(memory_space=pltpu.SMEM)] + [vmem] * len(ins),
        out_specs=[vmem, vmem, vmem],
        out_shape=[
            jax.ShapeDtypeStruct((total, MODS * channels), bf16),
            jax.ShapeDtypeStruct((total, channels), bf16),
            jax.ShapeDtypeStruct((8, channels), f32),
        ],
        scratch_shapes=[pltpu.VMEM((total + 8, channels), f32)],
        compiler_params=pltpu.CompilerParams(vmem_limit_bytes=VMEM_BYTES),
        cost_estimate=cost(1),
        name="conv_back",
    )(lengths, *ins)


def flip(axis, bit):
    size = lax.axis_size(axis)
    return lambda value: lax.ppermute(value, axis, [(i, i ^ bit) for i in range(size)])


def taken(values, at, dim):
    return lax.dynamic_index_in_dim(values, at, dim, keepdims=False)


SEQ = ("z", "core")
SAME_CORE = ("z", "mod")


def size_of(axes):
    return math.prod(lax.axis_size(axis) for axis in axes)


def share(values, axes):
    size = size_of(axes)
    return lax.all_to_all(jnp.broadcast_to(values, (size,) + values.shape), axes, 0, 0)


def exchange(blocks, axes):
    return lax.all_to_all(blocks, axes, 0, 0)


def held_back(value, until):
    return lax.optimization_barrier((value, tuple(until)))[0] if until else value


def flip(axis, bit):
    size = lax.axis_size(axis)
    return lambda value: lax.ppermute(value, axis, [(i, i ^ bit) for i in range(size)])


def taken(values, at, dim):
    return lax.dynamic_index_in_dim(values, at, dim, keepdims=False)


def two(bit, mine, got):
    return jnp.where(bit == 0, jnp.stack([mine, got]), jnp.stack([got, mine]))


Z_HIGH, Z_LOW, CORE = ("z", 2), ("z", 1), ("core", 1)
Y, X = ("mod", 2), ("mod", 1)


def place_bit(place):
    axis, bit = place
    return lax.axis_index(axis) // bit % 2


def summed_features(feats, kind=f32):
    feats = (feats[1] + flip(*CORE)(feats[0])).astype(kind)
    feats = feats.reshape((-1,) + feats.shape[2:])
    return jnp.sum(exchange(feats, SAME_CORE).astype(f32), axis=0), feats


def shared_features(block, until=()):
    mine = share(block, SAME_CORE)
    every = two(place_bit(CORE), mine, flip(*CORE)(held_back(mine, until)))
    return every.reshape((2, lax.axis_size("z"), lax.axis_size("mod")) + block.shape)


def core_rows(values, which):
    blocks = values.reshape(lax.axis_size("z"), 2, -1, values.shape[1])
    return taken(blocks, which, 1).reshape(-1, values.shape[1])


def both_cores(low, ids_ours):
    core = place_bit(CORE)
    got = flip(*CORE)(core_rows(low, 1 - core))
    return [masked(core_rows(low, core), ids_ours), masked(got, ids_ours)]


def gathered_columns(shard, between):
    width = shard.shape[1] // COLUMNS
    lines, far = [], []
    for at in range(COLUMNS):
        part = shard[:, at * width : (at + 1) * width]
        far.append(flip(*Z_HIGH)(held_back(part, far[at - 1 : at] if at else ())))
        line = two(place_bit(Z_HIGH), part, far[at])
        given = held_back(line, lines[at - 1 : at] if at else ())
        lines.append(two(place_bit(Z_LOW), line, flip(*Z_LOW)(given)))
    until = between(lines[-1])
    pieces, arrived, halfway = [], [], []
    for at, line in enumerate(lines):
        near, next_ = (X, Y) if at % 2 == 0 else (Y, X)
        halfway.append(flip(*near)(held_back(line, halfway[at - 2 : at - 1] if at > 1 else ())))
        pair = two(place_bit(near), line, halfway[at])
        got = flip(*next_)(held_back(pair, until if at > 1 else ()))
        arrived.append(got)
        pieces += [pair, got, flip(*CORE)(pair), flip(*CORE)(got)]
    return pieces, arrived


def row_parts(left, right, count):
    width = right.shape[0] // count
    return [
        dot(left, right[at * width : (at + 1) * width], 1, 1)
        .astype(bf16)
        .reshape(2, 2, 2, 2, -1, width)
        for at in range(count)
    ]


class SummedRows:
    def __init__(self, parts):
        self.dims = [["zh", "zl", "y", "x"] for _ in parts]
        self.parts = [[part] for part in parts]

    def give(self, at, name, place):
        dim = self.dims[at].index(name)
        bit = place_bit(place)
        away = sum(taken(p, 1 - bit, dim).astype(f32) for p in self.parts[at]).astype(bf16)
        self.parts[at] = [taken(p, bit, dim) for p in self.parts[at]]
        self.dims[at].remove(name)
        return away

    def stage(self, names):
        places = {"x": X, "y": Y, "zl": Z_LOW, "zh": Z_HIGH}
        sent = []
        for at in range(len(self.parts)):
            name = names[at % 2]
            away = self.give(at, name, places[name])
            sent.append(away)
            self.parts[at].append(flip(*places[name])(away))
        return sent

    def merge(self):
        pairs = list(zip(self.parts[::2], self.parts[1::2]))
        self.parts = [
            [jnp.concatenate(both, axis=-1) for both in zip(even, odd)] for even, odd in pairs
        ]
        self.dims = self.dims[::2]

    def arrived(self):
        return [parts[-1] for parts in self.parts]

    def hold(self, until):
        for parts in self.parts:
            parts[-1] = held_back(parts[-1], until)

    def result(self):
        return jnp.concatenate([sum(p.astype(f32) for p in parts) for parts in self.parts], axis=1)


def masked(values, ids):
    return jnp.concatenate(
        [jnp.where(ids == m, values, jnp.zeros_like(values)) for m in range(MODS)], axis=1
    )


def channel_layout(
    tokens,
    modality,
    lengths,
    norm_gain,
    input_weight,
    param_weight,
    step_weight,
    step_bias,
    output_weight,
    conv_weight,
    conv_bias,
    decay_log,
    skip_gain,
    cotangent,
):
    seqs = size_of(SEQ)
    channels = conv_weight.shape[1]
    width = tokens.shape[1]
    features = param_weight.shape[2]
    slab = input_weight.shape[1]

    token_vals = tokens.astype(f32)
    inverse = lax.rsqrt(jnp.mean(token_vals * token_vals, axis=1, keepdims=True) + EPSILON)
    normal_rows = token_vals * inverse
    gain_vals = norm_gain.astype(f32)

    send_in = input_weight.reshape(MODS, slab, 2, seqs, channels)
    send_in = send_in.transpose(3, 2, 0, 1, 4).reshape(seqs, 2 * MODS, slab, channels)
    id_rows = 16
    send_ids = jnp.pad(modality.astype(bf16), (0, id_rows * channels - modality.shape[0]))
    send_ids = jnp.broadcast_to(
        send_ids.reshape(id_rows, channels), (seqs, 2 * MODS, id_rows, channels)
    )
    send_in = jnp.concatenate([send_in, send_ids], axis=2)
    made = []

    def send(line):
        made.append(exchange(held_back(send_in, [line]), SEQ))
        return made

    pieces, arrived = gathered_columns((normal_rows * gain_vals[None, :]).astype(bf16), send)
    inner_blocks = made[0]
    ids = inner_blocks[:, 0, slab:].reshape(seqs, -1)[:, : modality.shape[0]].astype(jnp.int32)
    ids_rows = ids.reshape(-1, tokens.shape[0])
    ids = ids.reshape(-1, 1)
    send_out = output_weight.reshape(MODS, seqs, channels, slab).transpose(1, 0, 3, 2)
    param_t = param_weight.transpose(0, 2, 1)
    core = place_bit(CORE)
    place = jnp.stack([place_bit(at) for at in (CORE, Y, X)]).astype(jnp.int32)
    taps = conv_weight.astype(f32)
    skip = skip_gain.astype(f32)[None, :]
    decay_rate = -jnp.exp(decay_log.astype(f32))
    rate = decay_rate * math.log2(math.e)

    *normed, own_inner, own_gate, inner, conv_pre, act_low, feats = project(
        lengths,
        place,
        pieces,
        ids,
        ids_rows,
        inner_blocks,
        taps,
        conv_bias.astype(f32)[None, :],
        param_t,
    )
    cotangents = lax.all_gather(
        held_back(cotangent, [inner]), SEQ + ("mod",), axis=0, tiled=True
    )
    feats, sent = summed_features(feats)
    gate_pre = modal_rows(normed, held_back(ids, [sent]), own_gate)
    feats = held_back(feats, [gate_pre])
    mix_high = feats[R:].astype(bf16)
    mix_rest = (feats[R:] - mix_high.astype(f32)).astype(bf16)
    feats = jnp.concatenate([feats[:R].astype(bf16), mix_high, mix_rest], axis=0)
    feats = shared_features(feats)

    out_blocks = exchange(held_back(send_out, [feats]), SEQ)
    states, enter, step_pre, mix, scan_out = scan(
        lengths, ids, feats, conv_pre, step_weight, step_bias.astype(f32), rate, skip
    )
    out_blocks, scan_out = lax.optimization_barrier((out_blocks, scan_out))
    own_out, grad_scan, gate_wide, gated_wide, gate_rows, gated_rows = gates(
        cotangents, ids, out_blocks, gate_pre, scan_out
    )

    def token_sums(wide, weight):
        lows, gains = [], []
        for at, part in enumerate(normed):
            rows = part.shape[1]
            grad = dot(part, wide, 0, 0)
            lows.append(grad.astype(bf16))
            gains.append(jnp.sum(grad * weight[at * rows : (at + 1) * rows].astype(f32), axis=1))
        return jnp.concatenate(lows, axis=0), jnp.concatenate(gains, axis=0)

    def by_holder(low):
        return low.reshape(seqs, slab, MODS * channels)

    ids_ours = core_rows(ids, core)
    gated_both = both_cores(gated_rows, ids_ours)
    other_out = flip(*CORE)(own_out)
    gate_low, gate_gain = token_sums(gate_wide, own_gate)
    gated_both, other_out, gated_wide = lax.optimization_barrier(
        (gated_both, other_out, gated_wide)
    )
    out_low = dot(cotangents, gated_wide, 0, 0).astype(bf16)
    gated_both = jnp.concatenate(gated_both, axis=1)
    branch = SummedRows(row_parts(gated_both, side_by_side(own_out, other_out), 2))
    branch_sent = branch.stage(("x", "y"))
    more_low = jnp.concatenate([by_holder(gate_low), by_holder(out_low)], axis=2)
    grad_scan = held_back(grad_scan, branch_sent + [more_low])
    more_low = exchange(more_low, SEQ).reshape(seqs, slab, 2, MODS, channels)
    grad_gate = more_low[:, :, 0].transpose(2, 1, 0, 3)
    grad_out = more_low[:, :, 1].transpose(2, 0, 3, 1)
    grad_out = grad_out.reshape(MODS, seqs * channels, slab).astype(f32)

    act_part, step_grad_low, feat_grad, sums, rate_sum = scan_back(
        lengths,
        place,
        ids,
        ids_rows,
        mix,
        conv_pre,
        step_pre,
        grad_scan,
        states,
        enter,
        step_weight,
        rate,
        skip,
    )

    feat_grad = held_back(feat_grad, [more_low] + branch.arrived())
    gate_rows = held_back(gate_rows, [feat_grad])
    gate_both = both_cores(gate_rows, ids_ours)
    feat_grad, sent = summed_features(feat_grad, bf16)
    own_inner, own_gate = held_back((own_inner, own_gate), [sent])
    pair_in = side_by_side(own_inner, flip(*CORE)(own_inner), own_gate, flip(*CORE)(own_gate))
    feat_grad = held_back(feat_grad.astype(bf16), branch.stage(("y", "x")) + [pair_in])
    feat_grad = shared_features(feat_grad)
    branch.hold([feat_grad])
    branch.merge()

    inner_wide, inner_rows, tap_sums = conv_back(
        seqs,
        lengths,
        ids,
        feat_grad,
        act_part,
        conv_pre,
        inner,
        taps,
        param_t,
    )
    both_wide = jnp.concatenate(both_cores(inner_rows, ids_ours) + gate_both, axis=1)
    products = row_parts(both_wide, pair_in, COLUMNS)
    normed_sums = SummedRows(products)
    sent = normed_sums.stage(("x", "y"))
    branch.hold(sent)
    branch.stage(("zl", "zl"))
    inner_low, inner_gain = token_sums(held_back(inner_wide, sent), own_inner)
    inner_low = exchange(by_holder(inner_low), SEQ).reshape(seqs, slab, MODS, channels)
    branch.stage(("zh", "zh"))
    sent = normed_sums.stage(("y", "x"))
    output = (token_vals + branch.result()).astype(bf16)
    gain_sum, inner_low = lax.optimization_barrier((inner_gain + gate_gain, inner_low))
    grad_gain = jnp.sum(share(gain_sum, SEQ + ("mod",)), axis=0) / gain_vals
    grad_in = jnp.stack([inner_low.transpose(2, 1, 0, 3), grad_gate], axis=2)
    grad_in = grad_in.reshape(MODS, slab, 2, seqs * channels).astype(f32)
    normed_sums.merge()
    normed_sums.stage(("zl", "zl"))
    normed_sums.hold([grad_in, grad_gain])
    normed_sums.stage(("zh", "zh"))
    normed_grad = normed_sums.result()
    step_grad_low, feat_late = held_back((step_grad_low, feat_grad), sent)
    step_t = feats[:, :, :, :R].transpose(3, 1, 0, 2, 4).reshape(R, -1)
    grad_step = dot(step_t, masked(step_grad_low, ids))
    grad_step = grad_step.reshape(R, MODS, channels).transpose(1, 0, 2)
    feat_late = feat_late.transpose(3, 1, 0, 2, 4).reshape(features, -1)
    feat_late = [
        jnp.where(ids_rows.reshape(1, -1) == m, feat_late, jnp.zeros_like(feat_late))
        for m in range(MODS)
    ]
    grad_param = dot(jnp.concatenate(feat_late, axis=0), act_low)
    grad_param = grad_param.reshape(MODS, features, channels).transpose(0, 2, 1)
    hat_grad = normed_grad * gain_vals[None, :]
    token_grad = cotangent.astype(f32) + inverse * (
        hat_grad - normal_rows * jnp.mean(hat_grad * normal_rows, axis=1, keepdims=True)
    )
    return (
        output,
        token_grad,
        grad_gain,
        grad_in,
        grad_param,
        grad_step,
        grad_out,
        tap_sums[:KW],
        tap_sums[KW],
        rate_sum * decay_rate,
        sums[MODS],
        sums[:MODS],
    )


def placed(spec, axes):
    entries = [
        sum((axes[name] for name in ((entry,) if isinstance(entry, str) else entry or ())), ())
        for entry in spec
    ]
    return P(*[entry or None for entry in entries])


def solution(mesh):
    token_rows = P(("seq", "mod"), None)
    in_weight = P(None, "seq", None, "mod")
    out_weight = P(None, "mod", "seq")
    row, column, depth = P(("mod", "seq")), P(None, ("mod", "seq")), P(None, None, ("mod", "seq"))
    middle = P(None, ("mod", "seq"), None)
    ins = (token_rows, P("seq"), P(), P(), in_weight, middle, depth, column, out_weight)
    ins += (column, row, column, row, token_rows)
    outs = (token_rows, token_rows, P(), in_weight, middle, depth, out_weight)
    outs += (column, row, column, row, column)

    def run(*args):
        sizes = (mesh.shape["seq"], mesh.shape["mod"])
        share_of_channels = args[12].shape[0] // (sizes[0] * sizes[1])
        if share_of_channels == LANES and sizes == (8, 4):
            part, over = channel_layout, jax.sharding.Mesh(
                mesh.devices.reshape(sizes[0] // 2, 2, sizes[1]), ("z", "core", "mod")
            )
            axes = {"seq": SEQ, "mod": ("mod",)}
        else:
            part, over = local, mesh
            axes = {"seq": ("seq",), "mod": ("mod",)}
        return jax.shard_map(
            part,
            mesh=over,
            in_specs=tuple(placed(spec, axes) for spec in ins),
            out_specs=tuple(placed(spec, axes) for spec in outs),
            check_vma=False,
        )(*args)

    return run
```

```python
import functools
import math

import jax
import jax.numpy as jnp
from jax import lax
from jax.experimental import pallas as pl
from jax.experimental.pallas import tpu as pltpu
from jax.sharding import PartitionSpec as P

N = 16
KW = 4
R = 128
MODS = 3
TOK_DEV = 128
CAPD = 48


EPSILON = 1e-05
SCAN_ROWS = 512

LANES = 128
SUB = 8
STEPS = 4
UNROLL = 4
COLUMNS = 4
FAR = 1e9
VMEM_BYTES = 60 * 1024 * 1024
f32 = jnp.float32
bf16 = jnp.bfloat16


def shifted_2(value, axis, by):
    size = lax.axis_size(axis)
    pairs = [(i, i + by) for i in range(size) if 0 <= i + by < size]
    return lax.ppermute(value, axis, pairs)


def carried_in(value, axis, combine, identity):
    size, here = (lax.axis_size(axis), lax.axis_index(axis))
    everything = jax.tree.map(
        lambda part, kind: lax.all_gather(part.astype(kind), axis),
        value,
        (jnp.bfloat16, jnp.bfloat16),
    )
    start = jax.tree.map(
        lambda part, zero: jnp.broadcast_to(jnp.asarray(zero, part.dtype), part.shape),
        value,
        identity,
    )

    def carried_hop(k, before):
        reached = k < here
        new = combine(
            before, jax.tree.map(lambda part, own: part[k].astype(own.dtype), everything, value)
        )
        return jax.tree.map(lambda a, b: jnp.where(reached, a, b), new, before)

    return lax.fori_loop(0, size, carried_hop, start)


def prefix(value, axis, combine, identity):
    size, here = (lax.axis_size(axis), lax.axis_index(axis))
    everything = jax.tree.map(lambda part: lax.all_gather(part, axis), value)
    start = jax.tree.map(
        lambda part, zero: jnp.broadcast_to(jnp.asarray(zero, part.dtype), part.shape),
        value,
        identity,
    )

    def prefix_hop(k, before):
        at = size - 1 - k
        reached = at > here
        new = combine(before, jax.tree.map(lambda part: part[at], everything))
        return jax.tree.map(lambda a, b: jnp.where(reached, a, b), new, before)

    return lax.fori_loop(0, size, prefix_hop, start)


def split_rows(count_rows):
    return (count_rows // TOK_DEV, TOK_DEV)


def slot_tables(modal_ids, capacity):
    sub_rows = modal_ids.shape[1]
    marked = (modal_ids[:, :, None] == jnp.arange(MODS, dtype=jnp.int32)[None, None, :]).astype(
        jnp.int32
    )
    ranking = jnp.sum((jnp.cumsum(marked, axis=1) - 1) * marked, axis=2)
    slot_ids = modal_ids * capacity + ranking
    positions = jnp.broadcast_to(jnp.arange(sub_rows, dtype=jnp.int32)[None, :], modal_ids.shape)
    unfilled = jnp.full((modal_ids.shape[0], MODS * capacity), sub_rows, jnp.int32)
    tables = jax.vmap(lambda table_row, slot_row, place_row: table_row.at[slot_row].set(place_row))(
        unfilled, slot_ids, positions
    )
    return (tables, slot_ids)


def group_rows(values, tables, capacity):
    padded = jnp.concatenate([values, jnp.zeros_like(values[:, :1])], axis=1)
    picked = jax.vmap(lambda block_values, block_table: block_values[block_table])(padded, tables)
    return picked.reshape(values.shape[0], MODS, capacity, values.shape[2])


def ungroup_rows(grouped, slot_ids):
    flattened = grouped.reshape(grouped.shape[0], MODS * grouped.shape[2], grouped.shape[3])
    return jax.vmap(lambda block_values, block_slots: block_values[block_slots])(
        flattened, slot_ids
    )


def modal_product(values, modal_ids, weight, transpose):
    count_rows = values.shape[0]
    sub_count, sub_rows = split_rows(count_rows)
    capacity = min(CAPD, sub_rows)
    tables, slot_ids = slot_tables(modal_ids.reshape(sub_count, sub_rows), capacity)
    grouped = group_rows(values.reshape(sub_count, sub_rows, values.shape[1]), tables, capacity)
    if transpose:
        result = jnp.einsum("gmcn,mkn->gmck", grouped, weight, preferred_element_type=jnp.float32)
    else:
        result = jnp.einsum("gmck,mkn->gmcn", grouped, weight, preferred_element_type=jnp.float32)
    return ungroup_rows(result, slot_ids).reshape(count_rows, result.shape[3])


def modal_outer(left, right, modal_ids):
    count_rows = left.shape[0]
    sub_count, sub_rows = split_rows(count_rows)
    capacity = min(CAPD, sub_rows)
    tables, slot_ids = slot_tables(modal_ids.reshape(sub_count, sub_rows), capacity)
    left_grouped = group_rows(left.reshape(sub_count, sub_rows, left.shape[1]), tables, capacity)
    right_grouped = group_rows(right.reshape(sub_count, sub_rows, right.shape[1]), tables, capacity)
    return jnp.einsum(
        "gmcl,gmcr->mlr", left_grouped, right_grouped, preferred_element_type=jnp.float32
    )


def modal_table(table, modal_ids):
    picked = jnp.zeros((modal_ids.shape[0], table.shape[1]), jnp.float32)
    for modal_index in range(MODS):
        picked = (
            picked
            + (modal_ids == modal_index).astype(jnp.float32)[:, None] * table[modal_index][None, :]
        )
    return picked


def modal_sums(values, modal_ids):
    return jnp.stack(
        [
            jnp.sum(values * (modal_ids == modal_index).astype(jnp.float32)[:, None], axis=0)
            for modal_index in range(MODS)
        ]
    )


def pair_combine(earlier, later):
    return (earlier[0] * later[0], later[0] * earlier[1] + later[1])


def back_combine(earlier, later):
    return (earlier[0] * later[0], later[1] + later[0] * earlier[1])


def silu_slope(values):
    sigmoid_part = jax.nn.sigmoid(values)
    return sigmoid_part * (1.0 + values * (1.0 - sigmoid_part))


def local(
    tokens,
    modality,
    lengths,
    norm_gain,
    input_weight,
    param_weight,
    step_weight,
    step_bias,
    output_weight,
    conv_weight,
    conv_bias,
    decay_log,
    skip_gain,
    cotangent,
):
    block_rows = modality.shape[0]
    gathered = (
        lax.all_gather(input_weight, "seq", axis=1, tiled=True),
        lax.all_gather(param_weight, "seq", axis=1, tiled=True),
        lax.all_gather(step_weight, "seq", axis=2, tiled=True),
        lax.all_gather(output_weight, "seq", axis=2, tiled=True),
        lax.all_gather(conv_weight, "seq", axis=1, tiled=True),
        lax.all_gather(conv_bias, "seq", axis=0, tiled=True),
        lax.all_gather(decay_log, "seq", axis=1, tiled=True),
        lax.all_gather(skip_gain, "seq", axis=0, tiled=True),
        lax.all_gather(step_bias, "seq", axis=1, tiled=True),
    )
    in_local = gathered[0]
    param_local = gathered[1]
    step_local = gathered[2]
    out_local = gathered[3]
    tap_weights = gathered[4].astype(jnp.float32)
    tap_bias = gathered[5].astype(jnp.float32)
    decay_rate = -jnp.exp(gathered[6].astype(jnp.float32))
    skip_local = gathered[7].astype(jnp.float32)
    bias_local = gathered[8].astype(jnp.float32)
    channels = in_local.shape[3]
    model_width = in_local.shape[1]
    in_flat = in_local.reshape(MODS, model_width, 2 * channels)
    token_vals = tokens.astype(jnp.float32)
    inverse = lax.rsqrt(jnp.mean(token_vals * token_vals, axis=1, keepdims=True) + EPSILON)
    normal_rows = token_vals * inverse
    gain_vals = norm_gain.astype(jnp.float32)
    normed = (normal_rows * gain_vals[None, :]).astype(jnp.bfloat16)
    piece = lax.all_gather(normed, "mod", axis=0, tiled=True)
    piece_ids = modality
    product = modal_product(piece, piece_ids, in_flat, False)
    filled = product
    folded = (filled, piece)
    expanded = folded[0].reshape(block_rows, 2, channels)
    inner = expanded[:, 0]
    gate_pre = expanded[:, 1]
    first_place = lax.axis_index("seq") * block_rows
    places = first_place + jnp.arange(block_rows, dtype=jnp.int32)
    split_place = lengths[0]
    begins = jnp.where(places >= split_place, split_place, 0)
    keeping = (places != begins).astype(jnp.float32)
    inherit = (begins < first_place).astype(jnp.float32)
    halo_rows = shifted_2(inner[block_rows - KW + 1 :], "seq", 1)
    extended = jnp.concatenate([halo_rows, inner], axis=0)
    valid_taps = [
        (places - (KW - 1 - tap_index) >= begins).astype(jnp.float32)[:, None]
        for tap_index in range(KW)
    ]
    conv_pre = jnp.broadcast_to(tap_bias[None, :], inner.shape)
    for tap_index in range(KW):
        conv_pre = (
            conv_pre
            + tap_weights[tap_index][None, :]
            * extended[tap_index : tap_index + block_rows]
            * valid_taps[tap_index]
        )
    activated = jax.nn.silu(conv_pre)
    act_low = activated.astype(jnp.bfloat16)
    feature_part = modal_product(act_low, modality, param_local, False)
    features = lax.psum(feature_part, "mod")
    step_low = features[:, :R].astype(jnp.bfloat16)
    input_mix = features[:, R : R + N]
    output_mix = features[:, R + N :]
    step_pre = modal_product(step_low, modality, step_local, False) + modal_table(
        bias_local, modality
    )
    step_size = jax.nn.softplus(step_pre)
    scan_rows = math.gcd(block_rows, SCAN_ROWS)
    scan_count = block_rows // scan_rows

    def blocked(values):
        return values.reshape((scan_count, scan_rows) + values.shape[1:])

    def block_mult(keep_block, step_block):
        return keep_block[:, None, None] * jnp.exp(step_block[:, None, :] * decay_rate[None])

    def local_step(state_now, inputs):
        keep_block, step_block, act_block, input_block, output_block = inputs
        multiplier = block_mult(keep_block, step_block)
        addition = (step_block * act_block)[:, None, :] * input_block[:, :, None]
        running = lax.associative_scan(pair_combine, (multiplier, addition), axis=0)
        states = running[0] * state_now[None] + running[1]
        return (
            states[-1],
            (jnp.sum(output_block[:, :, None] * states, axis=1), state_now, running[0], running[1]),
        )

    scan_inputs = (
        blocked(keeping),
        blocked(step_size),
        blocked(activated),
        blocked(input_mix),
        blocked(output_mix),
    )
    end_state, (local_out, local_starts, run_mult, run_add) = lax.scan(
        local_step, jnp.zeros((N, channels), jnp.float32), scan_inputs
    )
    device_decay = jnp.exp(decay_rate * jnp.sum(step_size, axis=0)[None, :]) * jnp.min(keeping)
    chained = carried_in(
        (device_decay, end_state),
        "seq",
        pair_combine,
        (jnp.ones_like(device_decay), jnp.zeros_like(end_state)),
    )
    state_in = chained[1]

    def fix_step(carried, inputs):
        total_step, alive = carried
        inherit_block, step_block, output_block = inputs
        start_factor = alive * jnp.exp(decay_rate * total_step[None, :])
        running_step = total_step[None, :] + jnp.cumsum(step_block, axis=0)
        reach = inherit_block[:, None, None] * jnp.exp(running_step[:, None, :] * decay_rate[None])
        extra = jnp.sum(output_block[:, :, None] * reach * state_in[None], axis=1)
        return ((running_step[-1], inherit_block[-1]), (extra, start_factor))

    reach_inputs = (blocked(inherit), blocked(step_size), blocked(output_mix))
    _, (extra_out, start_factors) = lax.scan(
        fix_step, (jnp.zeros((channels,), jnp.float32), jnp.float32(1.0)), reach_inputs
    )
    start_states = local_starts + start_factors * state_in[None]
    scan_out = (local_out + extra_out).reshape(block_rows, channels) + skip_local[
        None, :
    ] * activated
    gate_act = jax.nn.silu(gate_pre)
    gated = (scan_out * gate_act).astype(jnp.bfloat16)
    piece = gated
    piece_ids = modality
    branch = lax.psum_scatter(
        modal_product(piece, piece_ids, out_local, False), "mod", scatter_dimension=0, tiled=True
    )
    output = (token_vals + branch).astype(jnp.bfloat16)
    back_rows = cotangent.astype(jnp.float32)
    piece = lax.all_gather(cotangent, "mod", axis=0, tiled=True)
    piece_ids = modality
    product = modal_product(piece, piece_ids, out_local, True)
    grad_out = modal_outer(gated, piece, piece_ids)
    grad_scan = product * gate_act
    grad_gate = product * scan_out * silu_slope(gate_pre)
    grad_skip = jnp.sum(grad_scan * activated, axis=0)
    grad_act = grad_scan * skip_local[None, :]

    def lead_step(carried, inputs):
        total_step, lead_sum = carried
        inherit_block, step_block, output_block, grad_block = inputs
        running_step = total_step[None, :] + jnp.cumsum(step_block, axis=0)
        reach = inherit_block[:, None, None] * jnp.exp(running_step[:, None, :] * decay_rate[None])
        lead_sum = lead_sum + jnp.sum(
            reach * output_block[:, :, None] * grad_block[:, None, :], axis=0
        )
        return ((running_step[-1], lead_sum), None)

    (_, lead_local), _ = lax.scan(
        lead_step,
        (jnp.zeros((channels,), jnp.float32), jnp.zeros((N, channels), jnp.float32)),
        reach_inputs + (blocked(grad_scan),),
    )
    incoming = prefix(
        (device_decay, lead_local),
        "seq",
        back_combine,
        (jnp.ones_like(device_decay), jnp.zeros_like(lead_local)),
    )[1]

    def back_step(carried, inputs):
        after_block, rate_grad = carried
        (
            keep_block,
            step_block,
            act_block,
            input_block,
            output_block,
            grad_block,
            start_state,
            mult_block,
            add_block,
        ) = inputs
        multiplier = block_mult(keep_block, step_block)
        states = mult_block * start_state[None] + add_block
        previous = jnp.concatenate([start_state[None], states[:-1]], axis=0)
        pushed = output_block[:, :, None] * grad_block[:, None, :]
        pushed = pushed.at[-1].add(after_block)
        shifted = jnp.concatenate([multiplier[1:], jnp.ones_like(multiplier[:1])], axis=0)
        flipped = lax.associative_scan(pair_combine, (shifted[::-1], pushed[::-1]), axis=0)
        grad_state = flipped[1][::-1]
        mult_grad = grad_state * previous * multiplier
        state_input = jnp.sum(grad_state * input_block[:, :, None], axis=1)
        step_grad = jnp.sum(mult_grad * decay_rate[None], axis=1) + state_input * act_block
        rate_grad = rate_grad + jnp.sum(mult_grad * step_block[:, None, :], axis=0)
        input_grad = jnp.sum(grad_state * (step_block * act_block)[:, None, :], axis=2)
        act_grad = state_input * step_block
        output_grad = jnp.sum(states * grad_block[:, None, :], axis=2)
        return (
            (multiplier[0] * grad_state[0], rate_grad),
            (step_grad, input_grad, act_grad, output_grad),
        )

    back_inputs = scan_inputs[:5] + (blocked(grad_scan), start_states, run_mult, run_add)
    (_, rate_total), (step_grads, input_grads, act_grads, output_grads) = lax.scan(
        back_step, (incoming, jnp.zeros((N, channels), jnp.float32)), back_inputs, reverse=True
    )
    step_pre_grad = step_grads.reshape(block_rows, channels) * jax.nn.sigmoid(step_pre)
    grad_bias = modal_sums(step_pre_grad, modality)
    step_grad_low = step_pre_grad.astype(jnp.bfloat16)
    step_in_part = modal_product(step_grad_low, modality, step_local, True)
    grad_step = modal_outer(step_low, step_grad_low, modality)
    summed = lax.psum(
        (step_in_part, input_grads.reshape(block_rows, N), output_grads.reshape(block_rows, N)),
        "mod",
    )
    feature_grad = jnp.concatenate(summed, axis=1).astype(jnp.bfloat16)
    grad_param = modal_outer(act_low, feature_grad, modality)
    act_total = (
        grad_act
        + act_grads.reshape(block_rows, channels)
        + modal_product(feature_grad, modality, param_local, True)
    )
    conv_grad = act_total * silu_slope(conv_pre)
    tap_grads = []
    ext_grad = jnp.zeros((block_rows + KW - 1, channels), jnp.float32)
    for tap_index in range(KW):
        masked = conv_grad * valid_taps[tap_index]
        tap_grads.append(jnp.sum(masked * extended[tap_index : tap_index + block_rows], axis=0))
        ext_grad = ext_grad.at[tap_index : tap_index + block_rows].add(
            masked * tap_weights[tap_index][None, :]
        )
    grad_taps = jnp.stack(tap_grads)
    grad_tap_bias = jnp.sum(conv_grad, axis=0)
    spill = shifted_2(ext_grad[: KW - 1], "seq", -1)
    inner_grad = ext_grad[KW - 1 :].at[block_rows - KW + 1 :].add(spill)
    both_grad = (
        jnp.stack([inner_grad, grad_gate], axis=1)
        .astype(jnp.bfloat16)
        .reshape(block_rows, 2 * channels)
    )
    piece = both_grad
    piece_ids = modality
    normed_grad = lax.psum_scatter(
        modal_product(piece, piece_ids, in_flat, True), "mod", scatter_dimension=0, tiled=True
    )
    grad_in = modal_outer(folded[1], both_grad, modality)
    gain_part = jnp.sum(normed_grad * normal_rows, axis=0)
    hat_grad = normed_grad * gain_vals[None, :]
    token_grad = back_rows + inverse * (
        hat_grad - normal_rows * jnp.mean(hat_grad * normal_rows, axis=1, keepdims=True)
    )
    grad_gain = lax.psum(gain_part, ("seq", "mod"))
    grad_decay = rate_total * decay_rate
    weight_grads = (
        lax.psum_scatter(
            grad_in.reshape(MODS, model_width, 2, channels), "seq", scatter_dimension=1, tiled=True
        ),
        lax.psum_scatter(grad_param, "seq", scatter_dimension=1, tiled=True),
        lax.psum_scatter(grad_step, "seq", scatter_dimension=2, tiled=True),
        lax.psum_scatter(grad_out, "seq", scatter_dimension=2, tiled=True),
        lax.psum_scatter(grad_taps, "seq", scatter_dimension=1, tiled=True),
        lax.psum_scatter(grad_tap_bias, "seq", scatter_dimension=0, tiled=True),
        lax.psum_scatter(grad_decay, "seq", scatter_dimension=1, tiled=True),
        lax.psum_scatter(grad_skip, "seq", scatter_dimension=0, tiled=True),
        lax.psum_scatter(grad_bias, "seq", scatter_dimension=1, tiled=True),
    )
    return (
        output,
        token_grad,
        grad_gain,
        weight_grads[0],
        weight_grads[1],
        weight_grads[2],
        weight_grads[3],
        weight_grads[4],
        weight_grads[5],
        weight_grads[6],
        weight_grads[7],
        weight_grads[8],
    )


def pick(ids, parts):
    return jnp.where(ids == 0, parts[0], jnp.where(ids == 1, parts[1], parts[2]))


def silu(values):
    return values * jax.nn.sigmoid(values)


def softplus(values):
    small = jnp.exp(-jnp.abs(values))
    series = small * (
        1.0 + small * (-1 / 2 + small * (1 / 3 + small * (-1 / 4 + small * (1 / 5 - small / 6))))
    )
    return jnp.maximum(values, 0.0) + jnp.where(small < 0.05, series, jnp.log(1.0 + small))


def dot(left, right, left_dim=1, right_dim=0):
    return lax.dot_general(
        left, right, (((left_dim,), (right_dim,)), ((), ())), preferred_element_type=f32
    )


def row_places(first, rows):
    return first + lax.broadcasted_iota(jnp.int32, (rows, 1), 0)


def whole(shape):
    return pl.BlockSpec(shape, lambda *_: (0,) * len(shape), pipeline_mode=pl.Buffered(1))


def cost(micros, flops=0):
    return pl.CostEstimate(flops=flops, bytes_accessed=int(micros * 3.69e6), transcendentals=0)


def modal_dot(values, ids, weight):
    part = values[0].shape[1]
    wide = sum(dot(v[...], weight[i * part : (i + 1) * part, :]) for i, v in enumerate(values))
    channels = wide.shape[1] // MODS
    return pick(ids, [wide[:, m * channels : (m + 1) * channels] for m in range(MODS)])


def put_masked(ref, rows, ids, values):
    channels = values.shape[1]
    for m in range(MODS):
        ref[rows, m * channels : (m + 1) * channels] = jnp.where(ids == m, values, 0.0).astype(
            ref.dtype
        )


def arrange(blocks, first, out):
    slab = out.shape[0] // blocks.shape[0]
    channels = blocks.shape[3]
    for at in range(blocks.shape[0]):
        for m in range(MODS):
            out[at * slab : (at + 1) * slab, m * channels : (m + 1) * channels] = blocks[
                at, first + m, 0:slab, :
            ]


def project_kernel(lengths, place, *refs):
    pieces, refs = refs[: 4 * COLUMNS], refs[4 * COLUMNS :]
    ids_ref, ids_rows, blocks, taps, bias, param_t = refs[:6]
    xs, refs = refs[6 : 6 + COLUMNS], refs[6 + COLUMNS :]
    w, w_gate, inner_ref, pre_ref, low_ref, feats, ext = refs
    step = pl.program_id(0)

    @pl.when(step == 0)
    def _():
        arrange(blocks, 0, w)
        arrange(blocks, MODS, w_gate)

    block_rows = pieces[0].shape[3]
    for which in (0, 1):

        @pl.when((place[0] == step % 2) == (which == 0))
        def _():
            for at in range(COLUMNS):
                own_line, other_line = pieces[4 * at + 2 * which : 4 * at + 2 * which + 2]
                here = place[1] if at % 2 == 0 else place[2]
                for near in (0, 1):
                    for line, value in ((here, own_line), (1 - here, other_line)):
                        block = line * 2 + near if at % 2 == 0 else near * 2 + line
                        row = pl.multiple_of(block * block_rows, block_rows)
                        xs[at][pl.ds(row, block_rows), :] = value[near, 0, 0]

    rows = xs[0].shape[0]
    channels = inner_ref.shape[1]
    ids = ids_ref[...]
    inner = modal_dot(xs, ids, w)
    inner_ref[...] = inner

    @pl.when(step == 0)
    def _():
        ext[0:8, :] = jnp.zeros((8, channels), f32)

    @pl.when(step > 0)
    def _():
        ext[0:8, :] = ext[rows : rows + 8, :]

    ext[8 : 8 + rows, :] = inner
    places = row_places(step * rows, rows)
    split = lengths[0]
    begins = jnp.where(places >= split, split, 0)
    pre = jnp.broadcast_to(bias[...], (rows, channels))
    for tap in range(KW):
        lag = KW - 1 - tap
        shifted = ext[8 - lag : 8 - lag + rows, :]
        pre = pre + taps[tap : tap + 1, :] * jnp.where(places - lag >= begins, shifted, 0.0)
    pre_ref[...] = pre
    low = silu(pre).astype(bf16)
    low_ref[...] = low
    across = feats.shape[2]
    ours = jnp.where(place[0] == step % 2, 1, 0)
    for j in range(across):
        block = low[j * block_rows : (j + 1) * block_rows]
        feats[ours, step // 2, j] = pick(
            ids_rows[pl.ds(step * across + j, 1), :],
            [dot(param_t[m], block, 1, 1) for m in range(MODS)],
        )


def project(lengths, place, pieces, ids, ids_rows, blocks, taps, bias, param_t):
    total = ids.shape[0]
    channels = taps.shape[1]
    chips, across = lax.axis_size("z"), lax.axis_size("mod")
    rows = total // (2 * chips)
    width = pieces[0].shape[4]
    by_rows = lambda i: (i, 0)
    feats = (2, chips, across, param_t.shape[1], rows // across)
    smem = pl.BlockSpec(memory_space=pltpu.SMEM)
    return pl.pallas_call(
        project_kernel,
        grid=(total // rows,),
        in_specs=[
            smem,
            smem,
            *[
                pl.BlockSpec((2, 1, 1) + piece.shape[3:], lambda i: (0, i // 2 % 2, i // 4, 0, 0))
                for piece in pieces
            ],
            pl.BlockSpec((rows, 1), by_rows),
            whole(ids_rows.shape),
            whole(blocks.shape),
            whole(taps.shape),
            whole(bias.shape),
            whole(param_t.shape),
        ],
        out_specs=[pl.BlockSpec((rows, width), by_rows)] * COLUMNS
        + [whole((COLUMNS * width, MODS * channels))] * 2
        + [pl.BlockSpec((rows, channels), by_rows)] * 3
        + [whole(feats)],
        out_shape=[jax.ShapeDtypeStruct((total, width), bf16)] * COLUMNS
        + [jax.ShapeDtypeStruct((COLUMNS * width, MODS * channels), bf16)] * 2
        + [jax.ShapeDtypeStruct((total, channels), f32)] * 2
        + [jax.ShapeDtypeStruct((total, channels), bf16)]
        + [jax.ShapeDtypeStruct(feats, f32)],
        scratch_shapes=[pltpu.VMEM((rows + 8, channels), f32)],
        compiler_params=pltpu.CompilerParams(vmem_limit_bytes=VMEM_BYTES),
        cost_estimate=cost(1),
        name="project",
    )(lengths, place, *pieces, ids, ids_rows, blocks, taps, bias, param_t)


def modal_kernel(*refs):
    *xs, ids_ref, w, out = refs
    out[...] = modal_dot(xs, ids_ref[...], w)


def modal_rows(values, ids, weight):
    total = values[0].shape[0]
    channels = weight.shape[1] // MODS
    rows = math.gcd(total, 512)
    by_rows = lambda i: (i, 0)
    return pl.pallas_call(
        modal_kernel,
        grid=(total // rows,),
        in_specs=[
            *[pl.BlockSpec((rows, part.shape[1]), by_rows) for part in values],
            pl.BlockSpec((rows, 1), by_rows),
            whole(weight.shape),
        ],
        out_specs=pl.BlockSpec((rows, channels), by_rows),
        out_shape=jax.ShapeDtypeStruct((total, channels), f32),
        compiler_params=pltpu.CompilerParams(vmem_limit_bytes=VMEM_BYTES),
        cost_estimate=cost(1),
        name="modal_rows",
    )(*values, ids, weight)


def side_kernel(*refs):
    out, columns = refs[-1], refs[0].shape[1]
    for at, part in enumerate(refs[:-1]):
        out[:, at * columns : (at + 1) * columns] = part[...]


def side_by_side(*parts):
    rows, columns = parts[0].shape
    step = math.gcd(rows, 512)
    by_rows = lambda i: (i, 0)
    return pl.pallas_call(
        side_kernel,
        grid=(rows // step,),
        in_specs=[pl.BlockSpec((step, columns), by_rows)] * len(parts),
        out_specs=pl.BlockSpec((step, columns * len(parts)), by_rows),
        out_shape=jax.ShapeDtypeStruct((rows, columns * len(parts)), parts[0].dtype),
        cost_estimate=cost(1),
        name="side_by_side",
    )(*parts)


def gates_kernel(
    cot, ids_ref, blocks, pre, out, w_out, grad_scan, gate_wide, gated_wide, gate_low, gated_low
):
    @pl.when(pl.program_id(0) == 0)
    def _():
        arrange(blocks, 0, w_out)

    ids = ids_ref[...]
    here = pre[...]
    grad = modal_dot([cot], ids, w_out)
    sig = jax.nn.sigmoid(here)
    scanned = out[...]
    grad_scan[...] = grad * (here * sig)
    gate_grad = grad * scanned * (sig * (1.0 + here * (1.0 - sig)))
    gated = scanned * (here * sig)
    gate_low[...] = gate_grad.astype(bf16)
    gated_low[...] = gated.astype(bf16)
    put_masked(gate_wide, slice(None), ids, gate_grad)
    put_masked(gated_wide, slice(None), ids, gated)


def gates(cotangents, ids, blocks, pre, out):
    total, channels = out.shape
    width = cotangents.shape[1]
    rows = total // size_of(SEQ)
    by_rows = lambda i: (i, 0)
    block = pl.BlockSpec((rows, channels), by_rows)
    wide = pl.BlockSpec((rows, MODS * channels), by_rows)
    return pl.pallas_call(
        gates_kernel,
        grid=(total // rows,),
        in_specs=[
            pl.BlockSpec((rows, width), by_rows),
            pl.BlockSpec((rows, 1), by_rows),
            whole(blocks.shape),
            block,
            block,
        ],
        out_specs=[whole((width, MODS * channels)), block, wide, wide, block, block],
        out_shape=[
            jax.ShapeDtypeStruct((width, MODS * channels), bf16),
            jax.ShapeDtypeStruct((total, channels), f32),
            jax.ShapeDtypeStruct((total, MODS * channels), bf16),
            jax.ShapeDtypeStruct((total, MODS * channels), bf16),
            jax.ShapeDtypeStruct((total, channels), bf16),
            jax.ShapeDtypeStruct((total, channels), bf16),
        ],
        compiler_params=pltpu.CompilerParams(vmem_limit_bytes=VMEM_BYTES),
        cost_estimate=cost(1),
        name="gates",
    )(cotangents, ids, blocks, pre, out)


def spread_rates(rate_t, out):
    for group in range(rate_t.shape[0] // SUB):
        rows = rate_t[group * SUB : (group + 1) * SUB, :]
        for n in range(N):
            at = (group * N + n) * SUB
            out[at : at + SUB, :] = jnp.broadcast_to(rows[:, n : n + 1], (SUB, LANES))


def turned_rows(tau, length):
    return pl.ds(tau, LANES, stride=length)


def step_rows(tau, rows=LANES):
    return pl.ds(pl.multiple_of(tau * rows, rows), rows)


def over_segments(spent, ends, rates, backward):
    at = lax.broadcasted_iota(jnp.int32, (SUB, LANES), 1)
    ends = list(ends)
    reach = 1
    while reach < LANES:
        shift = LANES - reach if backward else reach
        inside = at < LANES - reach if backward else at >= reach
        for n in range(N):
            earlier = jnp.where(inside, pltpu.roll(ends[n], shift, 1), 0.0)
            ends[n] = ends[n] + jnp.exp2(spent * rates[n]) * earlier
        spent = spent + jnp.where(inside, pltpu.roll(spent, shift, 1), 0.0)
        reach *= 2
    shift = LANES - 1 if backward else 1
    inside = at < LANES - 1 if backward else at >= 1
    return [jnp.where(inside, pltpu.roll(end, shift, 1), 0.0) for end in ends]


def pieces_of(values, count):
    return [values[n * SUB : (n + 1) * SUB] for n in range(count)]


def scan_kernel(
    lengths,
    ids_ref,
    feats,
    pre,
    step_w,
    step_b,
    rate_t,
    skip,
    states,
    enter,
    step_pre,
    s_turn,
    u_turn,
    mix_turn,
    scan_out,
    s_flat,
    u_flat,
    mix_flat,
    y_turn,
    held,
    rates,
):
    chunk = pl.program_id(0)
    total, channels = pre.shape
    length = total // LANES
    steps = states.shape[0]
    groups = channels // SUB
    split = lengths[0]
    wide = N * SUB

    @pl.when(chunk == 0)
    def _():
        spread_rates(rate_t, rates)
        across = feats.shape[2]
        block_rows = feats.shape[4]
        for seq in range(2 * feats.shape[1]):
            for j in range(across):
                first = (seq * across + j) * block_rows
                block = pl.ds(first, block_rows)
                block_ids = ids_ref[block, :]
                low = feats[seq % 2, seq // 2, j, 0:R, :]
                here = pick(block_ids, [dot(low, step_w[m], 0, 0) for m in range(MODS)]) + pick(
                    block_ids, [step_b[m : m + 1, :] for m in range(MODS)]
                )
                step_pre[block, :] = here
                step = softplus(here)
                places = row_places(first, block_rows)
                start = (places == 0) | (places == split)
                s_flat[block, :] = jnp.where(start, FAR, step)
                u_flat[block, :] = step * silu(pre[block, :])
                mixed = feats[seq % 2, seq // 2, j, R : R + 2 * N, :].astype(f32)
                mixed = mixed + feats[seq % 2, seq // 2, j, R + 2 * N :, :].astype(f32)
                blank = jnp.zeros((LANES - 2 * N, block_rows), f32)
                mix_flat[block, :] = jnp.transpose(jnp.concatenate([mixed, blank], axis=0))

        def turn(tau, carried):
            rows = turned_rows(tau, length)
            s_turn[step_rows(tau), :] = jnp.transpose(s_flat[rows, :])
            u_turn[step_rows(tau), :] = jnp.transpose(u_flat[rows, :])
            mixed = jnp.transpose(mix_flat[rows, :])
            spread = [jnp.broadcast_to(mixed[n : n + 1, :], (SUB, LANES)) for n in range(2 * N)]
            mix_turn[step_rows(tau, 2 * wide), :] = jnp.concatenate(spread, axis=0)
            return carried

        lax.fori_loop(0, length, turn, 0)

        def ahead(group, carried):
            rate = pieces_of(rates[step_rows(group, wide), :], N)

            def some(i, carried):
                hidden, spent = list(carried[0]), carried[1]
                for j in range(UNROLL):
                    tau = i * UNROLL + j
                    at = pl.ds(pl.multiple_of(tau * channels + group * SUB, SUB), SUB)
                    s, u = s_turn[at, :], u_turn[at, :]
                    for n in range(N):
                        row = pl.ds(pl.multiple_of((tau * 2 * N + n) * SUB, SUB), SUB)
                        hidden[n] = jnp.exp2(s * rate[n]) * hidden[n] + u * mix_turn[row, :]
                    spent = spent + s
                return hidden, spent

            zero = jnp.zeros((SUB, LANES), f32)
            ends, spent = lax.fori_loop(0, length // UNROLL, some, ([zero] * N, zero))
            inside = jnp.concatenate(over_segments(spent, ends, rate, False), axis=0)
            held[step_rows(group, wide), :] = inside
            enter[step_rows(group, wide), :] = inside
            return carried

        lax.fori_loop(0, groups, ahead, 0)

    def advance(group, carried):
        own = step_rows(group, wide)
        rate = pieces_of(rates[own, :], N)
        hidden = pieces_of(held[own, :], N)
        for j in range(steps):
            tau = chunk * steps + j
            at = pl.ds(pl.multiple_of(tau * channels + group * SUB, SUB), SUB)
            s, u = s_turn[at, :], u_turn[at, :]
            terms = []
            for n in range(N):
                row = pl.ds(pl.multiple_of((tau * 2 * N + n) * SUB, SUB), SUB)
                other = pl.ds(pl.multiple_of((tau * 2 * N + N + n) * SUB, SUB), SUB)
                hidden[n] = jnp.exp2(s * rate[n]) * hidden[n] + u * mix_turn[row, :]
                states[j, pl.ds(pl.multiple_of((group * N + n) * SUB, SUB), SUB), :] = hidden[n]
                terms.append(hidden[n] * mix_turn[other, :])
            while len(terms) > 1:
                terms = [a + b for a, b in zip(terms[::2], terms[1::2])]
            y_turn[at, :] = terms[0]
        held[own, :] = jnp.concatenate(hidden, axis=0)
        return carried

    lax.fori_loop(0, groups, advance, 0)

    @pl.when(chunk == pl.num_programs(0) - 1)
    def _():
        def turn_back(tau, carried):
            s_flat[turned_rows(tau, length), :] = jnp.transpose(y_turn[step_rows(tau), :])
            return carried

        lax.fori_loop(0, length, turn_back, 0)
        for block in range(total // 512):
            rows = pl.ds(block * 512, 512)
            scan_out[rows, :] = s_flat[rows, :] + skip[...] * silu(pre[rows, :])


def scan(lengths, ids, feats, pre, step_w, step_b, rate_t, skip):
    total, channels = pre.shape
    length = total // LANES
    steps = math.gcd(length, STEPS)
    wide = N * channels
    flat = pltpu.VMEM((total, channels), f32)
    ins = (ids, feats, pre, step_w, step_b, rate_t, skip)
    shapes = [
        (wide, LANES),
        (total, channels),
        (length * channels, LANES),
        (length * channels, LANES),
        (length * 2 * N * SUB, LANES),
        (total, channels),
    ]
    return pl.pallas_call(
        scan_kernel,
        grid=(length // steps,),
        in_specs=[pl.BlockSpec(memory_space=pltpu.SMEM)] + [whole(a.shape) for a in ins],
        out_specs=[pl.BlockSpec((steps, wide, LANES), lambda i: (i, 0, 0))]
        + [whole(shape) for shape in shapes],
        out_shape=[jax.ShapeDtypeStruct((length, wide, LANES), f32)]
        + [jax.ShapeDtypeStruct(shape, f32) for shape in shapes],
        scratch_shapes=[flat, flat, flat, pltpu.VMEM((length * channels, LANES), f32)]
        + [pltpu.VMEM((wide, LANES), f32)] * 2,
        compiler_params=pltpu.CompilerParams(vmem_limit_bytes=VMEM_BYTES),
        cost_estimate=cost(1),
        name="scan",
    )(lengths, *ins)


def back_kernel(
    core,
    ids_ref,
    ids_rows,
    s_turn,
    u_turn,
    mix_turn,
    pre,
    step_pre,
    grad,
    states,
    before,
    enter,
    step_w,
    rate_t,
    skip,
    act_part,
    step_grad_low,
    feat_part,
    sums,
    rate_out,
    g_turn,
    step_turn,
    in_turn,
    mix_grad,
    step_flat,
    in_flat,
    mix_flat,
    in_terms,
    out_terms,
    held,
    rate_sum,
    rates,
):
    turn_at = pl.program_id(0)
    chunks = pl.num_programs(0)
    chunk = chunks - 1 - turn_at
    total, channels = pre.shape
    length = total // LANES
    steps = states.shape[0]
    groups = channels // SUB
    wide = N * SUB

    @pl.when(turn_at == 0)
    def _():
        spread_rates(rate_t, rates)
        rate_sum[...] = jnp.zeros(rate_sum.shape, f32)

        def turn(tau, carried):
            g_turn[step_rows(tau), :] = jnp.transpose(grad[turned_rows(tau, length), :])
            return carried

        lax.fori_loop(0, length, turn, 0)

        def ahead(group, carried):
            rate = pieces_of(rates[step_rows(group, wide), :], N)

            def some(i, carried):
                pulled, spent = list(carried[0]), carried[1]
                for j in range(UNROLL):
                    tau = length - 1 - (i * UNROLL + j)
                    at = pl.ds(pl.multiple_of(tau * channels + group * SUB, SUB), SUB)
                    s, g = s_turn[at, :], g_turn[at, :]
                    for n in range(N):
                        row = pl.ds(pl.multiple_of((tau * 2 * N + N + n) * SUB, SUB), SUB)
                        pulled[n] = jnp.exp2(s * rate[n]) * (pulled[n] + g * mix_turn[row, :])
                    spent = spent + s
                return pulled, spent

            zero = jnp.zeros((SUB, LANES), f32)
            ends, spent = lax.fori_loop(0, length // UNROLL, some, ([zero] * N, zero))
            inside = jnp.concatenate(over_segments(spent, ends, rate, True), axis=0)
            held[step_rows(group, wide), :] = inside
            return carried

        lax.fori_loop(0, groups, ahead, 0)

    in_terms[...] = jnp.zeros(in_terms.shape, f32)
    out_terms[...] = jnp.zeros(out_terms.shape, f32)

    def retreat(group, carried):
        ats = [
            pl.ds(pl.multiple_of((chunk * steps + j) * channels + group * SUB, SUB), SUB)
            for j in range(steps)
        ]
        s, u, g = [[v[at, :] for at in ats] for v in (s_turn, u_turn, g_turn)]
        step_sum, in_sum = [0.0] * steps, [0.0] * steps
        for n in range(N):
            own = pl.ds(pl.multiple_of((group * N + n) * SUB, SUB), SUB)
            rate, pull, rate_acc = rates[own, :], held[own, :], rate_sum[own, :]
            first = jnp.where(chunk == 0, enter[own, :], before[0, own, :])
            state = [first] + [states[j, own, :] for j in range(steps)]
            for j in reversed(range(steps)):
                tau = chunk * steps + j
                b_row = pl.ds(pl.multiple_of((tau * 2 * N + n) * SUB, SUB), SUB)
                c_row = pl.ds(pl.multiple_of((tau * 2 * N + N + n) * SUB, SUB), SUB)
                term = pl.ds((j * N + n) * SUB, SUB)
                grad_state = g[j] * mix_turn[c_row, :] + pull
                pull = jnp.exp2(s[j] * rate) * grad_state
                mult = pull * state[j]
                step_sum[j] = step_sum[j] + mult * rate
                rate_acc = rate_acc + mult * s[j]
                in_sum[j] = in_sum[j] + grad_state * mix_turn[b_row, :]
                in_terms[term, :] += grad_state * u[j]
                out_terms[term, :] += state[j + 1] * g[j]
            held[own, :] = pull
            rate_sum[own, :] = rate_acc
        for j, at in enumerate(ats):
            step_turn[at, :] = step_sum[j]
            in_turn[at, :] = in_sum[j]
        return carried

    lax.fori_loop(0, groups, retreat, 0)
    for j in range(steps):
        rows = []
        for terms in (in_terms, out_terms):
            for n in range(N):
                at = (j * N + n) * SUB
                rows.append(jnp.sum(terms[at : at + SUB, :], axis=0, keepdims=True))
        mix_grad[step_rows(chunk * steps + j, 2 * N), :] = jnp.concatenate(rows, axis=0)

    @pl.when(turn_at == chunks - 1)
    def _():
        def turn_back(tau, carried):
            rows = turned_rows(tau, length)
            step_flat[rows, :] = jnp.transpose(step_turn[step_rows(tau), :])
            in_flat[rows, :] = jnp.transpose(in_turn[step_rows(tau), :])
            mixed = mix_grad[step_rows(tau, 2 * N), :]
            blank = jnp.zeros((LANES - 2 * N, LANES), f32)
            mix_flat[rows, :] = jnp.transpose(jnp.concatenate([mixed, blank], axis=0))
            return carried

        lax.fori_loop(0, length, turn_back, 0)
        sums[...] = jnp.zeros(sums.shape, f32)
        across, block_rows = feat_part.shape[2], feat_part.shape[4]
        for seq in range(2 * feat_part.shape[1]):
            rows = pl.ds(seq * across * block_rows, across * block_rows)
            ids = ids_ref[rows, :]
            act = silu(pre[rows, :])
            step_in = step_pre[rows, :]
            state_in = in_flat[rows, :]
            grad_here = grad[rows, :]
            step_grad = step_flat[rows, :] * math.log(2.0) + state_in * act
            pre_grad = step_grad * jax.nn.sigmoid(step_in)
            low = pre_grad.astype(bf16)
            step_grad_low[rows, :] = low
            act_part[rows, :] = grad_here * skip[...] + state_in * softplus(step_in)
            ours = jnp.where(core[0] == seq % 2, 1, 0)
            for j in range(across):
                block = seq * across + j
                block_low = low[j * block_rows : (j + 1) * block_rows]
                feat_part[ours, seq // 2, j, 0:R, :] = pick(
                    ids_rows[block : block + 1, :],
                    [dot(step_w[m], block_low, 1, 1) for m in range(MODS)],
                )
                turned = jnp.transpose(mix_flat[pl.ds(block * block_rows, block_rows), :])
                feat_part[ours, seq // 2, j, R : R + 2 * N, :] = turned[: 2 * N]
            for m in range(MODS):
                sums[m : m + 1, :] += jnp.sum(
                    jnp.where(ids == m, pre_grad, 0.0), axis=0, keepdims=True
                )
            sums[MODS : MODS + 1, :] += jnp.sum(grad_here * act, axis=0, keepdims=True)
        lane_at = lax.broadcasted_iota(jnp.int32, (SUB, LANES), 1)
        for group in range(groups):
            found = jnp.zeros((SUB, LANES), f32)
            for n in range(N):
                at = (group * N + n) * SUB
                total_rate = jnp.sum(rate_sum[at : at + SUB, :], axis=1, keepdims=True)
                found = jnp.where(lane_at == n, total_rate, found)
            rate_out[group * SUB : (group + 1) * SUB, :] = found


def scan_back(
    core, ids, ids_rows, turned, pre, step_pre, grad, states, enter, step_w, rate_t, skip
):
    total, channels = pre.shape
    length = total // LANES
    steps = math.gcd(length, STEPS)
    chunks = length // steps
    wide = N * channels
    feats = (2, lax.axis_size("z"), lax.axis_size("mod"), R + 2 * N, ids_rows.shape[1])
    first = (ids, ids_rows) + turned + (pre, step_pre, grad)
    second = (enter, step_w, rate_t, skip)
    turn = pltpu.VMEM((length * channels, LANES), f32)
    flat = pltpu.VMEM((total, channels), f32)
    terms = pltpu.VMEM((steps * N * SUB, LANES), f32)
    states_row = pltpu.VMEM((wide, LANES), f32)
    return pl.pallas_call(
        back_kernel,
        grid=(chunks,),
        in_specs=[pl.BlockSpec(memory_space=pltpu.SMEM)]
        + [whole(a.shape) for a in first]
        + [
            pl.BlockSpec((steps, wide, LANES), lambda i: (chunks - 1 - i, 0, 0)),
            pl.BlockSpec(
                (1, wide, LANES), lambda i: (jnp.maximum((chunks - 1 - i) * steps - 1, 0), 0, 0)
            ),
        ]
        + [whole(a.shape) for a in second],
        out_specs=[
            whole((total, channels)),
            whole((total, channels)),
            whole(feats),
            whole((SUB, channels)),
            whole((channels, LANES)),
        ],
        out_shape=[
            jax.ShapeDtypeStruct((total, channels), f32),
            jax.ShapeDtypeStruct((total, channels), bf16),
            jax.ShapeDtypeStruct(feats, f32),
            jax.ShapeDtypeStruct((SUB, channels), f32),
            jax.ShapeDtypeStruct((channels, LANES), f32),
        ],
        scratch_shapes=[turn, turn, turn, pltpu.VMEM((length * 2 * N, LANES), f32)]
        + [flat, flat, flat, terms, terms, states_row, states_row, states_row],
        compiler_params=pltpu.CompilerParams(vmem_limit_bytes=VMEM_BYTES),
        cost_estimate=cost(1),
        name="scan_back",
    )(core, *first, states, states, *second)


def conv_back_kernel(
    seqs,
    lengths,
    ids_ref,
    feat_grad,
    act_part,
    pre,
    inner,
    taps,
    param_t,
    inner_wide,
    inner_low,
    sums,
    ext,
):
    total, channels = pre.shape
    rows = total // seqs
    split = lengths[0]
    ext[total : total + 8, :] = jnp.zeros((8, channels), f32)
    sums[...] = jnp.zeros(sums.shape, f32)

    def through_silu(i, carried):
        at = pl.ds(pl.multiple_of(i * rows, rows), rows)
        for j in range(feat_grad.shape[2]):
            block_rows = feat_grad.shape[4]
            block = pl.ds(pl.multiple_of(i * rows + j * block_rows, block_rows), block_rows)
            low = feat_grad[i % 2, i // 2, j]
            ext[block, :] = pick(
                ids_ref[block, :], [dot(low, param_t[m], 0, 0) for m in range(MODS)]
            )
        act_grad = act_part[at, :] + ext[at, :]
        here = pre[at, :]
        sig = jax.nn.sigmoid(here)
        conv_grad = act_grad * (sig * (1.0 + here * (1.0 - sig)))
        ext[at, :] = conv_grad
        sums[KW : KW + 1, :] += jnp.sum(conv_grad, axis=0, keepdims=True)
        return carried

    lax.fori_loop(0, total // rows, through_silu, 0)

    for block in range(total // rows):
        first = block * rows
        at = pl.ds(first, rows)
        places = row_places(first, rows)
        here = inner[at, :]
        grad = jnp.zeros((rows, channels), f32)
        for tap in range(KW):
            lag = KW - 1 - tap
            kept = (places >= split) | (places + lag < split)
            later = jnp.where(kept, ext[pl.ds(first + lag, rows), :], 0.0)
            grad = grad + taps[tap : tap + 1, :] * later
            sums[tap : tap + 1, :] += jnp.sum(later * here, axis=0, keepdims=True)
        put_masked(inner_wide, at, ids_ref[at, :], grad)
        inner_low[at, :] = grad.astype(bf16)


def conv_back(seqs, lengths, ids, feat_grad, act_part, pre, inner, taps, param_t):
    total, channels = pre.shape
    ins = (ids, feat_grad, act_part, pre, inner, taps, param_t)
    vmem = pl.BlockSpec(memory_space=pltpu.VMEM)
    return pl.pallas_call(
        functools.partial(conv_back_kernel, seqs),
        in_specs=[pl.BlockSpec(memory_space=pltpu.SMEM)] + [vmem] * len(ins),
        out_specs=[vmem, vmem, vmem],
        out_shape=[
            jax.ShapeDtypeStruct((total, MODS * channels), bf16),
            jax.ShapeDtypeStruct((total, channels), bf16),
            jax.ShapeDtypeStruct((8, channels), f32),
        ],
        scratch_shapes=[pltpu.VMEM((total + 8, channels), f32)],
        compiler_params=pltpu.CompilerParams(vmem_limit_bytes=VMEM_BYTES),
        cost_estimate=cost(1),
        name="conv_back",
    )(lengths, *ins)


def flip(axis, bit):
    size = lax.axis_size(axis)
    return lambda value: lax.ppermute(value, axis, [(i, i ^ bit) for i in range(size)])


def taken(values, at, dim):
    return lax.dynamic_index_in_dim(values, at, dim, keepdims=False)


SEQ = ("z", "core")
SAME_CORE = ("z", "mod")


def size_of(axes):
    return math.prod(lax.axis_size(axis) for axis in axes)


def share(values, axes):
    size = size_of(axes)
    return lax.all_to_all(jnp.broadcast_to(values, (size,) + values.shape), axes, 0, 0)


def exchange(blocks, axes):
    return lax.all_to_all(blocks, axes, 0, 0)


def held_back(value, until):
    return lax.optimization_barrier((value, tuple(until)))[0] if until else value


def flip(axis, bit):
    size = lax.axis_size(axis)
    return lambda value: lax.ppermute(value, axis, [(i, i ^ bit) for i in range(size)])


def taken(values, at, dim):
    return lax.dynamic_index_in_dim(values, at, dim, keepdims=False)


def two(bit, mine, got):
    return jnp.where(bit == 0, jnp.stack([mine, got]), jnp.stack([got, mine]))


Z_HIGH, Z_LOW, CORE = ("z", 2), ("z", 1), ("core", 1)
Y, X = ("mod", 2), ("mod", 1)


def place_bit(place):
    axis, bit = place
    return lax.axis_index(axis) // bit % 2


def summed_features(feats, kind=f32):
    feats = (feats[1] + flip(*CORE)(feats[0])).astype(kind)
    feats = feats.reshape((-1,) + feats.shape[2:])
    return jnp.sum(exchange(feats, SAME_CORE).astype(f32), axis=0), feats


def shared_features(block, until=()):
    mine = share(block, SAME_CORE)
    every = two(place_bit(CORE), mine, flip(*CORE)(held_back(mine, until)))
    return every.reshape((2, lax.axis_size("z"), lax.axis_size("mod")) + block.shape)


def core_rows(values, which):
    blocks = values.reshape(lax.axis_size("z"), 2, -1, values.shape[1])
    return taken(blocks, which, 1).reshape(-1, values.shape[1])


def both_cores(low, ids_ours):
    core = place_bit(CORE)
    got = flip(*CORE)(core_rows(low, 1 - core))
    return [masked(core_rows(low, core), ids_ours), masked(got, ids_ours)]


def gathered_columns(shard, between):
    width = shard.shape[1] // COLUMNS
    lines, far = [], []
    for at in range(COLUMNS):
        part = shard[:, at * width : (at + 1) * width]
        far.append(flip(*Z_HIGH)(held_back(part, far[at - 1 : at] if at else ())))
        line = two(place_bit(Z_HIGH), part, far[at])
        given = held_back(line, lines[at - 1 : at] if at else ())
        lines.append(two(place_bit(Z_LOW), line, flip(*Z_LOW)(given)))
    until = between(lines[-1])
    pieces, arrived, halfway = [], [], []
    for at, line in enumerate(lines):
        near, next_ = (X, Y) if at % 2 == 0 else (Y, X)
        halfway.append(flip(*near)(held_back(line, halfway[at - 2 : at - 1] if at > 1 else ())))
        pair = two(place_bit(near), line, halfway[at])
        got = flip(*next_)(held_back(pair, until if at > 1 else ()))
        arrived.append(got)
        pieces += [pair, got, flip(*CORE)(pair), flip(*CORE)(got)]
    return pieces, arrived


def row_parts(left, right, count):
    width = right.shape[0] // count
    return [
        dot(left, right[at * width : (at + 1) * width], 1, 1)
        .astype(bf16)
        .reshape(2, 2, 2, 2, -1, width)
        for at in range(count)
    ]


class SummedRows:
    def __init__(self, parts):
        self.dims = [["zh", "zl", "y", "x"] for _ in parts]
        self.parts = [[part] for part in parts]

    def give(self, at, name, place):
        dim = self.dims[at].index(name)
        bit = place_bit(place)
        away = sum(taken(p, 1 - bit, dim).astype(f32) for p in self.parts[at]).astype(bf16)
        self.parts[at] = [taken(p, bit, dim) for p in self.parts[at]]
        self.dims[at].remove(name)
        return away

    def stage(self, names):
        places = {"x": X, "y": Y, "zl": Z_LOW, "zh": Z_HIGH}
        sent = []
        for at in range(len(self.parts)):
            name = names[at % 2]
            away = self.give(at, name, places[name])
            sent.append(away)
            self.parts[at].append(flip(*places[name])(away))
        return sent

    def merge(self):
        pairs = list(zip(self.parts[::2], self.parts[1::2]))
        self.parts = [
            [jnp.concatenate(both, axis=-1) for both in zip(even, odd)] for even, odd in pairs
        ]
        self.dims = self.dims[::2]

    def arrived(self):
        return [parts[-1] for parts in self.parts]

    def hold(self, until):
        for parts in self.parts:
            parts[-1] = held_back(parts[-1], until)

    def result(self):
        return jnp.concatenate([sum(p.astype(f32) for p in parts) for parts in self.parts], axis=1)


def masked(values, ids):
    return jnp.concatenate(
        [jnp.where(ids == m, values, jnp.zeros_like(values)) for m in range(MODS)], axis=1
    )


def channel_layout(
    tokens,
    modality,
    lengths,
    norm_gain,
    input_weight,
    param_weight,
    step_weight,
    step_bias,
    output_weight,
    conv_weight,
    conv_bias,
    decay_log,
    skip_gain,
    cotangent,
):
    seqs = size_of(SEQ)
    channels = conv_weight.shape[1]
    width = tokens.shape[1]
    features = param_weight.shape[2]
    slab = input_weight.shape[1]

    token_vals = tokens.astype(f32)
    inverse = lax.rsqrt(jnp.mean(token_vals * token_vals, axis=1, keepdims=True) + EPSILON)
    normal_rows = token_vals * inverse
    gain_vals = norm_gain.astype(f32)

    send_in = input_weight.reshape(MODS, slab, 2, seqs, channels)
    send_in = send_in.transpose(3, 2, 0, 1, 4).reshape(seqs, 2 * MODS, slab, channels)
    id_rows = 16
    send_ids = jnp.pad(modality.astype(bf16), (0, id_rows * channels - modality.shape[0]))
    send_ids = jnp.broadcast_to(
        send_ids.reshape(id_rows, channels), (seqs, 2 * MODS, id_rows, channels)
    )
    send_in = jnp.concatenate([send_in, send_ids], axis=2)
    made = []

    def send(line):
        made.append(exchange(held_back(send_in, [line]), SEQ))
        return made

    pieces, arrived = gathered_columns((normal_rows * gain_vals[None, :]).astype(bf16), send)
    inner_blocks = made[0]
    ids = inner_blocks[:, 0, slab:].reshape(seqs, -1)[:, : modality.shape[0]].astype(jnp.int32)
    ids_rows = ids.reshape(-1, tokens.shape[0])
    ids = ids.reshape(-1, 1)
    send_out = output_weight.reshape(MODS, seqs, channels, slab).transpose(1, 0, 3, 2)
    param_t = param_weight.transpose(0, 2, 1)
    core = place_bit(CORE)
    place = jnp.stack([place_bit(at) for at in (CORE, Y, X)]).astype(jnp.int32)
    taps = conv_weight.astype(f32)
    skip = skip_gain.astype(f32)[None, :]
    decay_rate = -jnp.exp(decay_log.astype(f32))
    rate_t = jnp.pad((decay_rate * math.log2(math.e)).T, ((0, 0), (0, LANES - N)))

    *normed, own_inner, own_gate, inner, conv_pre, act_low, feats = project(
        lengths,
        place,
        pieces,
        ids,
        ids_rows,
        inner_blocks,
        taps,
        conv_bias.astype(f32)[None, :],
        param_t,
    )
    cotangents = lax.all_gather(
        held_back(cotangent, [inner]), SEQ + ("mod",), axis=0, tiled=True
    )
    feats, sent = summed_features(feats)
    gate_pre = modal_rows(normed, held_back(ids, [sent]), own_gate)
    feats = held_back(feats, [gate_pre])
    mix_high = feats[R:].astype(bf16)
    mix_rest = (feats[R:] - mix_high.astype(f32)).astype(bf16)
    feats = jnp.concatenate([feats[:R].astype(bf16), mix_high, mix_rest], axis=0)
    feats = shared_features(feats)

    out_blocks = exchange(held_back(send_out, [feats]), SEQ)
    states, enter, step_pre, *turned, scan_out = scan(
        lengths, ids, feats, conv_pre, step_weight, step_bias.astype(f32), rate_t, skip
    )
    out_blocks, scan_out = lax.optimization_barrier((out_blocks, scan_out))
    own_out, grad_scan, gate_wide, gated_wide, gate_rows, gated_rows = gates(
        cotangents, ids, out_blocks, gate_pre, scan_out
    )

    def token_sums(wide, weight):
        lows, gains = [], []
        for at, part in enumerate(normed):
            rows = part.shape[1]
            grad = dot(part, wide, 0, 0)
            lows.append(grad.astype(bf16))
            gains.append(jnp.sum(grad * weight[at * rows : (at + 1) * rows].astype(f32), axis=1))
        return jnp.concatenate(lows, axis=0), jnp.concatenate(gains, axis=0)

    def by_holder(low):
        return low.reshape(seqs, slab, MODS * channels)

    ids_ours = core_rows(ids, core)
    gated_both = both_cores(gated_rows, ids_ours)
    other_out = flip(*CORE)(own_out)
    gate_low, gate_gain = token_sums(gate_wide, own_gate)
    gated_both, other_out, gated_wide = lax.optimization_barrier(
        (gated_both, other_out, gated_wide)
    )
    out_low = dot(cotangents, gated_wide, 0, 0).astype(bf16)
    gated_both = jnp.concatenate(gated_both, axis=1)
    branch = SummedRows(row_parts(gated_both, side_by_side(own_out, other_out), 2))
    branch_sent = branch.stage(("x", "y"))
    more_low = jnp.concatenate([by_holder(gate_low), by_holder(out_low)], axis=2)
    grad_scan = held_back(grad_scan, branch_sent + [more_low])
    more_low = exchange(more_low, SEQ).reshape(seqs, slab, 2, MODS, channels)
    grad_gate = more_low[:, :, 0].transpose(2, 1, 0, 3)
    grad_out = more_low[:, :, 1].transpose(2, 0, 3, 1)
    grad_out = grad_out.reshape(MODS, seqs * channels, slab).astype(f32)

    act_part, step_grad_low, feat_grad, sums, rate_sum = scan_back(
        place,
        ids,
        ids_rows,
        tuple(turned),
        conv_pre,
        step_pre,
        grad_scan,
        states,
        enter,
        step_weight,
        rate_t,
        skip,
    )
    feat_grad = held_back(feat_grad, [more_low] + branch.arrived())
    gate_rows = held_back(gate_rows, [feat_grad])
    gate_both = both_cores(gate_rows, ids_ours)
    feat_grad, sent = summed_features(feat_grad, bf16)
    own_inner, own_gate = held_back((own_inner, own_gate), [sent])
    pair_in = side_by_side(own_inner, flip(*CORE)(own_inner), own_gate, flip(*CORE)(own_gate))
    feat_grad = held_back(feat_grad.astype(bf16), branch.stage(("y", "x")) + [pair_in])
    feat_grad = shared_features(feat_grad)
    branch.hold([feat_grad])
    branch.merge()

    inner_wide, inner_rows, tap_sums = conv_back(
        seqs,
        lengths,
        ids,
        feat_grad,
        act_part,
        conv_pre,
        inner,
        taps,
        param_t,
    )
    both_wide = jnp.concatenate(both_cores(inner_rows, ids_ours) + gate_both, axis=1)
    products = row_parts(both_wide, pair_in, COLUMNS)
    normed_sums = SummedRows(products)
    sent = normed_sums.stage(("x", "y"))
    branch.hold(sent)
    branch.stage(("zl", "zl"))
    inner_low, inner_gain = token_sums(held_back(inner_wide, sent), own_inner)
    inner_low = exchange(by_holder(inner_low), SEQ).reshape(seqs, slab, MODS, channels)
    branch.stage(("zh", "zh"))
    sent = normed_sums.stage(("y", "x"))
    output = (token_vals + branch.result()).astype(bf16)
    gain_sum, inner_low = lax.optimization_barrier((inner_gain + gate_gain, inner_low))
    grad_gain = jnp.sum(share(gain_sum, SEQ + ("mod",)), axis=0) / gain_vals
    grad_in = jnp.stack([inner_low.transpose(2, 1, 0, 3), grad_gate], axis=2)
    grad_in = grad_in.reshape(MODS, slab, 2, seqs * channels).astype(f32)
    normed_sums.merge()
    normed_sums.stage(("zl", "zl"))
    normed_sums.hold([grad_in, grad_gain])
    normed_sums.stage(("zh", "zh"))
    normed_grad = normed_sums.result()
    step_grad_low, feat_late = held_back((step_grad_low, feat_grad), sent)
    step_t = feats[:, :, :, :R].transpose(3, 1, 0, 2, 4).reshape(R, -1)
    grad_step = dot(step_t, masked(step_grad_low, ids))
    grad_step = grad_step.reshape(R, MODS, channels).transpose(1, 0, 2)
    feat_late = feat_late.transpose(3, 1, 0, 2, 4).reshape(features, -1)
    feat_late = [
        jnp.where(ids_rows.reshape(1, -1) == m, feat_late, jnp.zeros_like(feat_late))
        for m in range(MODS)
    ]
    grad_param = dot(jnp.concatenate(feat_late, axis=0), act_low)
    grad_param = grad_param.reshape(MODS, features, channels).transpose(0, 2, 1)
    hat_grad = normed_grad * gain_vals[None, :]
    token_grad = cotangent.astype(f32) + inverse * (
        hat_grad - normal_rows * jnp.mean(hat_grad * normal_rows, axis=1, keepdims=True)
    )
    return (
        output,
        token_grad,
        grad_gain,
        grad_in,
        grad_param,
        grad_step,
        grad_out,
        tap_sums[:KW],
        tap_sums[KW],
        rate_sum[:, :N].T * decay_rate,
        sums[MODS],
        sums[:MODS],
    )


def placed(spec, axes):
    entries = [
        sum((axes[name] for name in ((entry,) if isinstance(entry, str) else entry or ())), ())
        for entry in spec
    ]
    return P(*[entry or None for entry in entries])


def solution(mesh):
    token_rows = P(("seq", "mod"), None)
    in_weight = P(None, "seq", None, "mod")
    out_weight = P(None, "mod", "seq")
    row, column, depth = P(("mod", "seq")), P(None, ("mod", "seq")), P(None, None, ("mod", "seq"))
    middle = P(None, ("mod", "seq"), None)
    ins = (token_rows, P("seq"), P(), P(), in_weight, middle, depth, column, out_weight)
    ins += (column, row, column, row, token_rows)
    outs = (token_rows, token_rows, P(), in_weight, middle, depth, out_weight)
    outs += (column, row, column, row, column)

    def run(*args):
        sizes = (mesh.shape["seq"], mesh.shape["mod"])
        share_of_channels = args[12].shape[0] // (sizes[0] * sizes[1])
        if share_of_channels == LANES and sizes == (8, 4):
            part, over = channel_layout, jax.sharding.Mesh(
                mesh.devices.reshape(sizes[0] // 2, 2, sizes[1]), ("z", "core", "mod")
            )
            axes = {"seq": SEQ, "mod": ("mod",)}
        else:
            part, over = local, mesh
            axes = {"seq": ("seq",), "mod": ("mod",)}
        return jax.shard_map(
            part,
            mesh=over,
            in_specs=tuple(placed(spec, axes) for spec in ins),
            out_specs=tuple(placed(spec, axes) for spec in outs),
            check_vma=False,
        )(*args)

    return run
```

```python
import functools
import math

import jax
import jax.numpy as jnp
from jax import lax
from jax.experimental import pallas as pl
from jax.experimental.pallas import tpu as pltpu
from jax.sharding import PartitionSpec as P

N = 16
KW = 4
R = 128
MODS = 3
TOK_DEV = 128
CAPD = 48


EPSILON = 1e-05
SCAN_ROWS = 512

LANES = 128
SUB = 8
STEPS = 4
UNROLL = 4
COLUMNS = 4
FAR = 1e9
VMEM_BYTES = 60 * 1024 * 1024
f32 = jnp.float32
bf16 = jnp.bfloat16


def shifted_2(value, axis, by):
    size = lax.axis_size(axis)
    pairs = [(i, i + by) for i in range(size) if 0 <= i + by < size]
    return lax.ppermute(value, axis, pairs)


def carried_in(value, axis, combine, identity):
    size, here = (lax.axis_size(axis), lax.axis_index(axis))
    everything = jax.tree.map(
        lambda part, kind: lax.all_gather(part.astype(kind), axis),
        value,
        (jnp.bfloat16, jnp.bfloat16),
    )
    start = jax.tree.map(
        lambda part, zero: jnp.broadcast_to(jnp.asarray(zero, part.dtype), part.shape),
        value,
        identity,
    )

    def carried_hop(k, before):
        reached = k < here
        new = combine(
            before, jax.tree.map(lambda part, own: part[k].astype(own.dtype), everything, value)
        )
        return jax.tree.map(lambda a, b: jnp.where(reached, a, b), new, before)

    return lax.fori_loop(0, size, carried_hop, start)


def prefix(value, axis, combine, identity):
    size, here = (lax.axis_size(axis), lax.axis_index(axis))
    everything = jax.tree.map(lambda part: lax.all_gather(part, axis), value)
    start = jax.tree.map(
        lambda part, zero: jnp.broadcast_to(jnp.asarray(zero, part.dtype), part.shape),
        value,
        identity,
    )

    def prefix_hop(k, before):
        at = size - 1 - k
        reached = at > here
        new = combine(before, jax.tree.map(lambda part: part[at], everything))
        return jax.tree.map(lambda a, b: jnp.where(reached, a, b), new, before)

    return lax.fori_loop(0, size, prefix_hop, start)


def split_rows(count_rows):
    return (count_rows // TOK_DEV, TOK_DEV)


def slot_tables(modal_ids, capacity):
    sub_rows = modal_ids.shape[1]
    marked = (modal_ids[:, :, None] == jnp.arange(MODS, dtype=jnp.int32)[None, None, :]).astype(
        jnp.int32
    )
    ranking = jnp.sum((jnp.cumsum(marked, axis=1) - 1) * marked, axis=2)
    slot_ids = modal_ids * capacity + ranking
    positions = jnp.broadcast_to(jnp.arange(sub_rows, dtype=jnp.int32)[None, :], modal_ids.shape)
    unfilled = jnp.full((modal_ids.shape[0], MODS * capacity), sub_rows, jnp.int32)
    tables = jax.vmap(lambda table_row, slot_row, place_row: table_row.at[slot_row].set(place_row))(
        unfilled, slot_ids, positions
    )
    return (tables, slot_ids)


def group_rows(values, tables, capacity):
    padded = jnp.concatenate([values, jnp.zeros_like(values[:, :1])], axis=1)
    picked = jax.vmap(lambda block_values, block_table: block_values[block_table])(padded, tables)
    return picked.reshape(values.shape[0], MODS, capacity, values.shape[2])


def ungroup_rows(grouped, slot_ids):
    flattened = grouped.reshape(grouped.shape[0], MODS * grouped.shape[2], grouped.shape[3])
    return jax.vmap(lambda block_values, block_slots: block_values[block_slots])(
        flattened, slot_ids
    )


def modal_product(values, modal_ids, weight, transpose):
    count_rows = values.shape[0]
    sub_count, sub_rows = split_rows(count_rows)
    capacity = min(CAPD, sub_rows)
    tables, slot_ids = slot_tables(modal_ids.reshape(sub_count, sub_rows), capacity)
    grouped = group_rows(values.reshape(sub_count, sub_rows, values.shape[1]), tables, capacity)
    if transpose:
        result = jnp.einsum("gmcn,mkn->gmck", grouped, weight, preferred_element_type=jnp.float32)
    else:
        result = jnp.einsum("gmck,mkn->gmcn", grouped, weight, preferred_element_type=jnp.float32)
    return ungroup_rows(result, slot_ids).reshape(count_rows, result.shape[3])


def modal_outer(left, right, modal_ids):
    count_rows = left.shape[0]
    sub_count, sub_rows = split_rows(count_rows)
    capacity = min(CAPD, sub_rows)
    tables, slot_ids = slot_tables(modal_ids.reshape(sub_count, sub_rows), capacity)
    left_grouped = group_rows(left.reshape(sub_count, sub_rows, left.shape[1]), tables, capacity)
    right_grouped = group_rows(right.reshape(sub_count, sub_rows, right.shape[1]), tables, capacity)
    return jnp.einsum(
        "gmcl,gmcr->mlr", left_grouped, right_grouped, preferred_element_type=jnp.float32
    )


def modal_table(table, modal_ids):
    picked = jnp.zeros((modal_ids.shape[0], table.shape[1]), jnp.float32)
    for modal_index in range(MODS):
        picked = (
            picked
            + (modal_ids == modal_index).astype(jnp.float32)[:, None] * table[modal_index][None, :]
        )
    return picked


def modal_sums(values, modal_ids):
    return jnp.stack(
        [
            jnp.sum(values * (modal_ids == modal_index).astype(jnp.float32)[:, None], axis=0)
            for modal_index in range(MODS)
        ]
    )


def pair_combine(earlier, later):
    return (earlier[0] * later[0], later[0] * earlier[1] + later[1])


def back_combine(earlier, later):
    return (earlier[0] * later[0], later[1] + later[0] * earlier[1])


def silu_slope(values):
    sigmoid_part = jax.nn.sigmoid(values)
    return sigmoid_part * (1.0 + values * (1.0 - sigmoid_part))


def local(
    tokens,
    modality,
    lengths,
    norm_gain,
    input_weight,
    param_weight,
    step_weight,
    step_bias,
    output_weight,
    conv_weight,
    conv_bias,
    decay_log,
    skip_gain,
    cotangent,
):
    block_rows = modality.shape[0]
    gathered = (
        lax.all_gather(input_weight, "seq", axis=1, tiled=True),
        lax.all_gather(param_weight, "seq", axis=1, tiled=True),
        lax.all_gather(step_weight, "seq", axis=2, tiled=True),
        lax.all_gather(output_weight, "seq", axis=2, tiled=True),
        lax.all_gather(conv_weight, "seq", axis=1, tiled=True),
        lax.all_gather(conv_bias, "seq", axis=0, tiled=True),
        lax.all_gather(decay_log, "seq", axis=1, tiled=True),
        lax.all_gather(skip_gain, "seq", axis=0, tiled=True),
        lax.all_gather(step_bias, "seq", axis=1, tiled=True),
    )
    in_local = gathered[0]
    param_local = gathered[1]
    step_local = gathered[2]
    out_local = gathered[3]
    tap_weights = gathered[4].astype(jnp.float32)
    tap_bias = gathered[5].astype(jnp.float32)
    decay_rate = -jnp.exp(gathered[6].astype(jnp.float32))
    skip_local = gathered[7].astype(jnp.float32)
    bias_local = gathered[8].astype(jnp.float32)
    channels = in_local.shape[3]
    model_width = in_local.shape[1]
    in_flat = in_local.reshape(MODS, model_width, 2 * channels)
    token_vals = tokens.astype(jnp.float32)
    inverse = lax.rsqrt(jnp.mean(token_vals * token_vals, axis=1, keepdims=True) + EPSILON)
    normal_rows = token_vals * inverse
    gain_vals = norm_gain.astype(jnp.float32)
    normed = (normal_rows * gain_vals[None, :]).astype(jnp.bfloat16)
    piece = lax.all_gather(normed, "mod", axis=0, tiled=True)
    piece_ids = modality
    product = modal_product(piece, piece_ids, in_flat, False)
    filled = product
    folded = (filled, piece)
    expanded = folded[0].reshape(block_rows, 2, channels)
    inner = expanded[:, 0]
    gate_pre = expanded[:, 1]
    first_place = lax.axis_index("seq") * block_rows
    places = first_place + jnp.arange(block_rows, dtype=jnp.int32)
    split_place = lengths[0]
    begins = jnp.where(places >= split_place, split_place, 0)
    keeping = (places != begins).astype(jnp.float32)
    inherit = (begins < first_place).astype(jnp.float32)
    halo_rows = shifted_2(inner[block_rows - KW + 1 :], "seq", 1)
    extended = jnp.concatenate([halo_rows, inner], axis=0)
    valid_taps = [
        (places - (KW - 1 - tap_index) >= begins).astype(jnp.float32)[:, None]
        for tap_index in range(KW)
    ]
    conv_pre = jnp.broadcast_to(tap_bias[None, :], inner.shape)
    for tap_index in range(KW):
        conv_pre = (
            conv_pre
            + tap_weights[tap_index][None, :]
            * extended[tap_index : tap_index + block_rows]
            * valid_taps[tap_index]
        )
    activated = jax.nn.silu(conv_pre)
    act_low = activated.astype(jnp.bfloat16)
    feature_part = modal_product(act_low, modality, param_local, False)
    features = lax.psum(feature_part, "mod")
    step_low = features[:, :R].astype(jnp.bfloat16)
    input_mix = features[:, R : R + N]
    output_mix = features[:, R + N :]
    step_pre = modal_product(step_low, modality, step_local, False) + modal_table(
        bias_local, modality
    )
    step_size = jax.nn.softplus(step_pre)
    scan_rows = math.gcd(block_rows, SCAN_ROWS)
    scan_count = block_rows // scan_rows

    def blocked(values):
        return values.reshape((scan_count, scan_rows) + values.shape[1:])

    def block_mult(keep_block, step_block):
        return keep_block[:, None, None] * jnp.exp(step_block[:, None, :] * decay_rate[None])

    def local_step(state_now, inputs):
        keep_block, step_block, act_block, input_block, output_block = inputs
        multiplier = block_mult(keep_block, step_block)
        addition = (step_block * act_block)[:, None, :] * input_block[:, :, None]
        running = lax.associative_scan(pair_combine, (multiplier, addition), axis=0)
        states = running[0] * state_now[None] + running[1]
        return (
            states[-1],
            (jnp.sum(output_block[:, :, None] * states, axis=1), state_now, running[0], running[1]),
        )

    scan_inputs = (
        blocked(keeping),
        blocked(step_size),
        blocked(activated),
        blocked(input_mix),
        blocked(output_mix),
    )
    end_state, (local_out, local_starts, run_mult, run_add) = lax.scan(
        local_step, jnp.zeros((N, channels), jnp.float32), scan_inputs
    )
    device_decay = jnp.exp(decay_rate * jnp.sum(step_size, axis=0)[None, :]) * jnp.min(keeping)
    chained = carried_in(
        (device_decay, end_state),
        "seq",
        pair_combine,
        (jnp.ones_like(device_decay), jnp.zeros_like(end_state)),
    )
    state_in = chained[1]

    def fix_step(carried, inputs):
        total_step, alive = carried
        inherit_block, step_block, output_block = inputs
        start_factor = alive * jnp.exp(decay_rate * total_step[None, :])
        running_step = total_step[None, :] + jnp.cumsum(step_block, axis=0)
        reach = inherit_block[:, None, None] * jnp.exp(running_step[:, None, :] * decay_rate[None])
        extra = jnp.sum(output_block[:, :, None] * reach * state_in[None], axis=1)
        return ((running_step[-1], inherit_block[-1]), (extra, start_factor))

    reach_inputs = (blocked(inherit), blocked(step_size), blocked(output_mix))
    _, (extra_out, start_factors) = lax.scan(
        fix_step, (jnp.zeros((channels,), jnp.float32), jnp.float32(1.0)), reach_inputs
    )
    start_states = local_starts + start_factors * state_in[None]
    scan_out = (local_out + extra_out).reshape(block_rows, channels) + skip_local[
        None, :
    ] * activated
    gate_act = jax.nn.silu(gate_pre)
    gated = (scan_out * gate_act).astype(jnp.bfloat16)
    piece = gated
    piece_ids = modality
    branch = lax.psum_scatter(
        modal_product(piece, piece_ids, out_local, False), "mod", scatter_dimension=0, tiled=True
    )
    output = (token_vals + branch).astype(jnp.bfloat16)
    back_rows = cotangent.astype(jnp.float32)
    piece = lax.all_gather(cotangent, "mod", axis=0, tiled=True)
    piece_ids = modality
    product = modal_product(piece, piece_ids, out_local, True)
    grad_out = modal_outer(gated, piece, piece_ids)
    grad_scan = product * gate_act
    grad_gate = product * scan_out * silu_slope(gate_pre)
    grad_skip = jnp.sum(grad_scan * activated, axis=0)
    grad_act = grad_scan * skip_local[None, :]

    def lead_step(carried, inputs):
        total_step, lead_sum = carried
        inherit_block, step_block, output_block, grad_block = inputs
        running_step = total_step[None, :] + jnp.cumsum(step_block, axis=0)
        reach = inherit_block[:, None, None] * jnp.exp(running_step[:, None, :] * decay_rate[None])
        lead_sum = lead_sum + jnp.sum(
            reach * output_block[:, :, None] * grad_block[:, None, :], axis=0
        )
        return ((running_step[-1], lead_sum), None)

    (_, lead_local), _ = lax.scan(
        lead_step,
        (jnp.zeros((channels,), jnp.float32), jnp.zeros((N, channels), jnp.float32)),
        reach_inputs + (blocked(grad_scan),),
    )
    incoming = prefix(
        (device_decay, lead_local),
        "seq",
        back_combine,
        (jnp.ones_like(device_decay), jnp.zeros_like(lead_local)),
    )[1]

    def back_step(carried, inputs):
        after_block, rate_grad = carried
        (
            keep_block,
            step_block,
            act_block,
            input_block,
            output_block,
            grad_block,
            start_state,
            mult_block,
            add_block,
        ) = inputs
        multiplier = block_mult(keep_block, step_block)
        states = mult_block * start_state[None] + add_block
        previous = jnp.concatenate([start_state[None], states[:-1]], axis=0)
        pushed = output_block[:, :, None] * grad_block[:, None, :]
        pushed = pushed.at[-1].add(after_block)
        shifted = jnp.concatenate([multiplier[1:], jnp.ones_like(multiplier[:1])], axis=0)
        flipped = lax.associative_scan(pair_combine, (shifted[::-1], pushed[::-1]), axis=0)
        grad_state = flipped[1][::-1]
        mult_grad = grad_state * previous * multiplier
        state_input = jnp.sum(grad_state * input_block[:, :, None], axis=1)
        step_grad = jnp.sum(mult_grad * decay_rate[None], axis=1) + state_input * act_block
        rate_grad = rate_grad + jnp.sum(mult_grad * step_block[:, None, :], axis=0)
        input_grad = jnp.sum(grad_state * (step_block * act_block)[:, None, :], axis=2)
        act_grad = state_input * step_block
        output_grad = jnp.sum(states * grad_block[:, None, :], axis=2)
        return (
            (multiplier[0] * grad_state[0], rate_grad),
            (step_grad, input_grad, act_grad, output_grad),
        )

    back_inputs = scan_inputs[:5] + (blocked(grad_scan), start_states, run_mult, run_add)
    (_, rate_total), (step_grads, input_grads, act_grads, output_grads) = lax.scan(
        back_step, (incoming, jnp.zeros((N, channels), jnp.float32)), back_inputs, reverse=True
    )
    step_pre_grad = step_grads.reshape(block_rows, channels) * jax.nn.sigmoid(step_pre)
    grad_bias = modal_sums(step_pre_grad, modality)
    step_grad_low = step_pre_grad.astype(jnp.bfloat16)
    step_in_part = modal_product(step_grad_low, modality, step_local, True)
    grad_step = modal_outer(step_low, step_grad_low, modality)
    summed = lax.psum(
        (step_in_part, input_grads.reshape(block_rows, N), output_grads.reshape(block_rows, N)),
        "mod",
    )
    feature_grad = jnp.concatenate(summed, axis=1).astype(jnp.bfloat16)
    grad_param = modal_outer(act_low, feature_grad, modality)
    act_total = (
        grad_act
        + act_grads.reshape(block_rows, channels)
        + modal_product(feature_grad, modality, param_local, True)
    )
    conv_grad = act_total * silu_slope(conv_pre)
    tap_grads = []
    ext_grad = jnp.zeros((block_rows + KW - 1, channels), jnp.float32)
    for tap_index in range(KW):
        masked = conv_grad * valid_taps[tap_index]
        tap_grads.append(jnp.sum(masked * extended[tap_index : tap_index + block_rows], axis=0))
        ext_grad = ext_grad.at[tap_index : tap_index + block_rows].add(
            masked * tap_weights[tap_index][None, :]
        )
    grad_taps = jnp.stack(tap_grads)
    grad_tap_bias = jnp.sum(conv_grad, axis=0)
    spill = shifted_2(ext_grad[: KW - 1], "seq", -1)
    inner_grad = ext_grad[KW - 1 :].at[block_rows - KW + 1 :].add(spill)
    both_grad = (
        jnp.stack([inner_grad, grad_gate], axis=1)
        .astype(jnp.bfloat16)
        .reshape(block_rows, 2 * channels)
    )
    piece = both_grad
    piece_ids = modality
    normed_grad = lax.psum_scatter(
        modal_product(piece, piece_ids, in_flat, True), "mod", scatter_dimension=0, tiled=True
    )
    grad_in = modal_outer(folded[1], both_grad, modality)
    gain_part = jnp.sum(normed_grad * normal_rows, axis=0)
    hat_grad = normed_grad * gain_vals[None, :]
    token_grad = back_rows + inverse * (
        hat_grad - normal_rows * jnp.mean(hat_grad * normal_rows, axis=1, keepdims=True)
    )
    grad_gain = lax.psum(gain_part, ("seq", "mod"))
    grad_decay = rate_total * decay_rate
    weight_grads = (
        lax.psum_scatter(
            grad_in.reshape(MODS, model_width, 2, channels), "seq", scatter_dimension=1, tiled=True
        ),
        lax.psum_scatter(grad_param, "seq", scatter_dimension=1, tiled=True),
        lax.psum_scatter(grad_step, "seq", scatter_dimension=2, tiled=True),
        lax.psum_scatter(grad_out, "seq", scatter_dimension=2, tiled=True),
        lax.psum_scatter(grad_taps, "seq", scatter_dimension=1, tiled=True),
        lax.psum_scatter(grad_tap_bias, "seq", scatter_dimension=0, tiled=True),
        lax.psum_scatter(grad_decay, "seq", scatter_dimension=1, tiled=True),
        lax.psum_scatter(grad_skip, "seq", scatter_dimension=0, tiled=True),
        lax.psum_scatter(grad_bias, "seq", scatter_dimension=1, tiled=True),
    )
    return (
        output,
        token_grad,
        grad_gain,
        weight_grads[0],
        weight_grads[1],
        weight_grads[2],
        weight_grads[3],
        weight_grads[4],
        weight_grads[5],
        weight_grads[6],
        weight_grads[7],
        weight_grads[8],
    )


def pick(ids, parts):
    return jnp.where(ids == 0, parts[0], jnp.where(ids == 1, parts[1], parts[2]))


def silu(values):
    return values * jax.nn.sigmoid(values)


def softplus(values):
    small = jnp.exp(-jnp.abs(values))
    series = small * (
        1.0 + small * (-1 / 2 + small * (1 / 3 + small * (-1 / 4 + small * (1 / 5 - small / 6))))
    )
    return jnp.maximum(values, 0.0) + jnp.where(small < 0.05, series, jnp.log(1.0 + small))


def dot(left, right, left_dim=1, right_dim=0):
    return lax.dot_general(
        left, right, (((left_dim,), (right_dim,)), ((), ())), preferred_element_type=f32
    )


def row_places(first, rows):
    return first + lax.broadcasted_iota(jnp.int32, (rows, 1), 0)


def whole(shape):
    return pl.BlockSpec(shape, lambda *_: (0,) * len(shape), pipeline_mode=pl.Buffered(1))


def cost(micros, flops=0):
    return pl.CostEstimate(flops=flops, bytes_accessed=int(micros * 3.69e6), transcendentals=0)


def modal_dot(values, ids, weight):
    part = values[0].shape[1]
    wide = sum(dot(v[...], weight[i * part : (i + 1) * part, :]) for i, v in enumerate(values))
    channels = wide.shape[1] // MODS
    return pick(ids, [wide[:, m * channels : (m + 1) * channels] for m in range(MODS)])


def modal_rows_of(weight, values, ids_row):
    stacked = dot(weight, values, 1, 1)
    height = stacked.shape[0] // MODS
    return pick(ids_row, [stacked[m * height : (m + 1) * height] for m in range(MODS)])


def put_masked(ref, rows, ids, values):
    channels = values.shape[1]
    for m in range(MODS):
        ref[rows, m * channels : (m + 1) * channels] = jnp.where(ids == m, values, 0.0).astype(
            ref.dtype
        )


def arrange(blocks, first, out):
    slab = out.shape[0] // blocks.shape[0]
    channels = blocks.shape[2]
    for at in range(blocks.shape[0]):
        for m in range(MODS):
            out[at * slab : (at + 1) * slab, m * channels : (m + 1) * channels] = blocks[
                at, (first + m) * slab : (first + m + 1) * slab, :
            ]


def project_kernel(lengths, place, *refs):
    pieces, refs = refs[: 4 * COLUMNS], refs[4 * COLUMNS :]
    ids_ref, ids_rows, blocks, taps, bias, param_t = refs[:6]
    xs, refs = refs[6 : 6 + COLUMNS], refs[6 + COLUMNS :]
    w, w_gate, inner_ref, pre_ref, low_ref, feats, ext = refs
    step = pl.program_id(0)

    @pl.when(step == 0)
    def _():
        arrange(blocks, 0, w)
        arrange(blocks, MODS, w_gate)

    block_rows = pieces[0].shape[3]
    for which in (0, 1):

        @pl.when((place[0] == step % 2) == (which == 0))
        def _():
            for at in range(COLUMNS):
                own_line, other_line = pieces[4 * at + 2 * which : 4 * at + 2 * which + 2]
                here = place[1] if at % 2 == 0 else place[2]
                for near in (0, 1):
                    for line, value in ((here, own_line), (1 - here, other_line)):
                        block = line * 2 + near if at % 2 == 0 else near * 2 + line
                        row = pl.multiple_of(block * block_rows, block_rows)
                        xs[at][pl.ds(row, block_rows), :] = value[near, 0, 0]

    rows = xs[0].shape[0]
    channels = inner_ref.shape[1]
    ids = ids_ref[...]
    inner = modal_dot(xs, ids, w)
    inner_ref[...] = inner

    @pl.when(step == 0)
    def _():
        ext[0:8, :] = jnp.zeros((8, channels), f32)

    @pl.when(step > 0)
    def _():
        ext[0:8, :] = ext[rows : rows + 8, :]

    ext[8 : 8 + rows, :] = inner
    places = row_places(step * rows, rows)
    split = lengths[0]
    begins = jnp.where(places >= split, split, 0)
    pre = jnp.broadcast_to(bias[...], (rows, channels))
    for tap in range(KW):
        lag = KW - 1 - tap
        shifted = ext[8 - lag : 8 - lag + rows, :]
        pre = pre + taps[tap : tap + 1, :] * jnp.where(places - lag >= begins, shifted, 0.0)
    pre_ref[...] = pre
    low = silu(pre).astype(bf16)
    low_ref[...] = low
    across = feats.shape[2]
    ours = jnp.where(place[0] == step % 2, 1, 0)
    for j in range(across):
        block = low[j * block_rows : (j + 1) * block_rows]
        feats[ours, step // 2, j] = modal_rows_of(
            param_t[...], block, ids_rows[pl.ds(step * across + j, 1), :]
        )


def project(lengths, place, pieces, ids, ids_rows, blocks, taps, bias, param_t):
    total = ids.shape[0]
    channels = taps.shape[1]
    chips, across = lax.axis_size("z"), lax.axis_size("mod")
    rows = total // (2 * chips)
    width = pieces[0].shape[4]
    by_rows = lambda i: (i, 0)
    feats = (2, chips, across, param_t.shape[0] // MODS, rows // across)
    smem = pl.BlockSpec(memory_space=pltpu.SMEM)
    return pl.pallas_call(
        project_kernel,
        grid=(total // rows,),
        in_specs=[
            smem,
            smem,
            *[
                pl.BlockSpec((2, 1, 1) + piece.shape[3:], lambda i: (0, i // 2 % 2, i // 4, 0, 0))
                for piece in pieces
            ],
            pl.BlockSpec((rows, 1), by_rows),
            whole(ids_rows.shape),
            whole(blocks.shape),
            whole(taps.shape),
            whole(bias.shape),
            whole(param_t.shape),
        ],
        out_specs=[pl.BlockSpec((rows, width), by_rows)] * COLUMNS
        + [whole((COLUMNS * width, MODS * channels))] * 2
        + [pl.BlockSpec((rows, channels), by_rows)] * 3
        + [whole(feats)],
        out_shape=[jax.ShapeDtypeStruct((total, width), bf16)] * COLUMNS
        + [jax.ShapeDtypeStruct((COLUMNS * width, MODS * channels), bf16)] * 2
        + [jax.ShapeDtypeStruct((total, channels), f32)] * 2
        + [jax.ShapeDtypeStruct((total, channels), bf16)]
        + [jax.ShapeDtypeStruct(feats, f32)],
        scratch_shapes=[pltpu.VMEM((rows + 8, channels), f32)],
        compiler_params=pltpu.CompilerParams(vmem_limit_bytes=VMEM_BYTES),
        cost_estimate=cost(1),
        name="project",
    )(lengths, place, *pieces, ids, ids_rows, blocks, taps, bias, param_t)


def modal_kernel(*refs):
    *xs, ids_ref, w, out = refs
    out[...] = modal_dot(xs, ids_ref[...], w)


def modal_rows(values, ids, weight):
    total = values[0].shape[0]
    channels = weight.shape[1] // MODS
    rows = math.gcd(total, 512)
    by_rows = lambda i: (i, 0)
    return pl.pallas_call(
        modal_kernel,
        grid=(total // rows,),
        in_specs=[
            *[pl.BlockSpec((rows, part.shape[1]), by_rows) for part in values],
            pl.BlockSpec((rows, 1), by_rows),
            whole(weight.shape),
        ],
        out_specs=pl.BlockSpec((rows, channels), by_rows),
        out_shape=jax.ShapeDtypeStruct((total, channels), f32),
        compiler_params=pltpu.CompilerParams(vmem_limit_bytes=VMEM_BYTES),
        cost_estimate=cost(1),
        name="modal_rows",
    )(*values, ids, weight)


def side_kernel(*refs):
    out, columns = refs[-1], refs[0].shape[1]
    for at, part in enumerate(refs[:-1]):
        out[:, at * columns : (at + 1) * columns] = part[...]


def side_by_side(*parts):
    rows, columns = parts[0].shape
    step = math.gcd(rows, 512)
    by_rows = lambda i: (i, 0)
    return pl.pallas_call(
        side_kernel,
        grid=(rows // step,),
        in_specs=[pl.BlockSpec((step, columns), by_rows)] * len(parts),
        out_specs=pl.BlockSpec((step, columns * len(parts)), by_rows),
        out_shape=jax.ShapeDtypeStruct((rows, columns * len(parts)), parts[0].dtype),
        cost_estimate=cost(1),
        name="side_by_side",
    )(*parts)


def gates_kernel(
    cot, ids_ref, blocks, pre, out, w_out, grad_scan, gate_wide, gated_wide, gate_low, gated_low
):
    @pl.when(pl.program_id(0) == 0)
    def _():
        arrange(blocks, 0, w_out)

    ids = ids_ref[...]
    here = pre[...]
    grad = modal_dot([cot], ids, w_out)
    sig = jax.nn.sigmoid(here)
    scanned = out[...]
    grad_scan[...] = grad * (here * sig)
    gate_grad = grad * scanned * (sig * (1.0 + here * (1.0 - sig)))
    gated = scanned * (here * sig)
    gate_low[...] = gate_grad.astype(bf16)
    gated_low[...] = gated.astype(bf16)
    put_masked(gate_wide, slice(None), ids, gate_grad)
    put_masked(gated_wide, slice(None), ids, gated)


def gates(cotangents, ids, blocks, pre, out):
    total, channels = out.shape
    width = cotangents.shape[1]
    rows = total // size_of(SEQ)
    by_rows = lambda i: (i, 0)
    block = pl.BlockSpec((rows, channels), by_rows)
    wide = pl.BlockSpec((rows, MODS * channels), by_rows)
    return pl.pallas_call(
        gates_kernel,
        grid=(total // rows,),
        in_specs=[
            pl.BlockSpec((rows, width), by_rows),
            pl.BlockSpec((rows, 1), by_rows),
            whole(blocks.shape),
            block,
            block,
        ],
        out_specs=[whole((width, MODS * channels)), block, wide, wide, block, block],
        out_shape=[
            jax.ShapeDtypeStruct((width, MODS * channels), bf16),
            jax.ShapeDtypeStruct((total, channels), f32),
            jax.ShapeDtypeStruct((total, MODS * channels), bf16),
            jax.ShapeDtypeStruct((total, MODS * channels), bf16),
            jax.ShapeDtypeStruct((total, channels), bf16),
            jax.ShapeDtypeStruct((total, channels), bf16),
        ],
        compiler_params=pltpu.CompilerParams(vmem_limit_bytes=VMEM_BYTES),
        cost_estimate=cost(1),
        name="gates",
    )(cotangents, ids, blocks, pre, out)


def spread_rates(rate_t, out):
    for group in range(rate_t.shape[0] // SUB):
        rows = rate_t[group * SUB : (group + 1) * SUB, :]
        for n in range(N):
            at = (group * N + n) * SUB
            out[at : at + SUB, :] = jnp.broadcast_to(rows[:, n : n + 1], (SUB, LANES))


def spread_mix(mixed, out, tau):
    spread = [jnp.broadcast_to(mixed[n : n + 1, :], (SUB, LANES)) for n in range(2 * N)]
    out[step_rows(tau, 2 * N * SUB), :] = jnp.concatenate(spread, axis=0)


def turned_rows(tau, length):
    return pl.ds(tau, LANES, stride=length)


def step_rows(tau, rows=LANES):
    return pl.ds(pl.multiple_of(tau * rows, rows), rows)


def over_segments(spent, ends, rates, backward):
    at = lax.broadcasted_iota(jnp.int32, (SUB, LANES), 1)
    ends = list(ends)
    reach = 1
    while reach < LANES:
        shift = LANES - reach if backward else reach
        inside = at < LANES - reach if backward else at >= reach
        for n in range(N):
            earlier = jnp.where(inside, pltpu.roll(ends[n], shift, 1), 0.0)
            ends[n] = ends[n] + jnp.exp(spent * rates[n]) * earlier
        spent = spent + jnp.where(inside, pltpu.roll(spent, shift, 1), 0.0)
        reach *= 2
    shift = LANES - 1 if backward else 1
    inside = at < LANES - 1 if backward else at >= 1
    return [jnp.where(inside, pltpu.roll(end, shift, 1), 0.0) for end in ends]


def row_of(at):
    return slice(at * SUB, (at + 1) * SUB)


def group_view(ref, first, count, group):
    start = pl.multiple_of(first * (count * LANES) + group * SUB, SUB)
    return ref.at[pl.ds(start, (count - 1) * LANES + SUB)]


def pieces_of(values, count):
    return [values[n * SUB : (n + 1) * SUB] for n in range(count)]


def scan_kernel(
    lengths,
    ids_ref,
    feats,
    pre,
    step_w,
    step_b,
    rate_t,
    skip,
    states,
    enter,
    step_pre,
    s_turn,
    u_turn,
    mix_rows,
    scan_out,
    s_flat,
    u_flat,
    mix_flat,
    y_turn,
    held,
    rates,
    mix_turn,
):
    chunk = pl.program_id(0)
    total, channels = pre.shape
    length = total // LANES
    steps = states.shape[0]
    groups = channels // SUB
    split = lengths[0]
    wide = N * SUB

    @pl.when(chunk == 0)
    def _():
        spread_rates(rate_t, rates)
        across = feats.shape[2]
        block_rows = feats.shape[4]
        for seq in range(2 * feats.shape[1]):
            for j in range(across):
                first = (seq * across + j) * block_rows
                block = pl.ds(first, block_rows)
                block_ids = ids_ref[block, :]
                low = feats[seq % 2, seq // 2, j, 0:R, :]
                stacked = dot(low, step_w[...], 0, 0) + step_b[...]
                here = pick(
                    block_ids, [stacked[:, m * channels : (m + 1) * channels] for m in range(MODS)]
                )
                step_pre[block, :] = here
                step = softplus(here)
                places = row_places(first, block_rows)
                start = (places == 0) | (places == split)
                s_flat[block, :] = jnp.where(start, FAR, step)
                u_flat[block, :] = step * silu(pre[block, :])
                mixed = feats[seq % 2, seq // 2, j, R : R + 2 * N, :].astype(f32)
                mixed = mixed + feats[seq % 2, seq // 2, j, R + 2 * N :, :].astype(f32)
                blank = jnp.zeros((LANES - 2 * N, block_rows), f32)
                mix_flat[block, :] = jnp.transpose(jnp.concatenate([mixed, blank], axis=0))

        def turn(tau, carried):
            rows = turned_rows(tau, length)
            s_turn[step_rows(tau), :] = jnp.transpose(s_flat[rows, :])
            u_turn[step_rows(tau), :] = jnp.transpose(u_flat[rows, :])
            mixed = jnp.transpose(mix_flat[rows, :])[: 2 * N]
            mix_rows[step_rows(tau, 2 * N), :] = mixed
            spread_mix(mixed, mix_turn, tau)
            return carried

        lax.fori_loop(0, length, turn, 0)

        def ahead(group, carried):
            rate = pieces_of(rates[step_rows(group, wide), :], N)

            def some(i, carried):
                hidden, spent = list(carried[0]), carried[1]
                s_here, u_here = [group_view(v, i, UNROLL, group) for v in (s_turn, u_turn)]
                mix_here = mix_turn.at[step_rows(i, UNROLL * 2 * wide)]
                for j in range(UNROLL):
                    s, u = s_here[row_of(j * groups), :], u_here[row_of(j * groups), :]
                    for n in range(N):
                        b = mix_here[row_of(j * 2 * N + n), :]
                        hidden[n] = jnp.exp(s * rate[n]) * hidden[n] + u * b
                    spent = spent + s
                return hidden, spent

            zero = jnp.zeros((SUB, LANES), f32)
            ends, spent = lax.fori_loop(0, length // UNROLL, some, ([zero] * N, zero))
            inside = jnp.concatenate(over_segments(spent, ends, rate, False), axis=0)
            held[step_rows(group, wide), :] = inside
            enter[step_rows(group, wide), :] = inside
            return carried

        lax.fori_loop(0, groups, ahead, 0)

    def advance(group, carried):
        own = step_rows(group, wide)
        rate = pieces_of(rates[own, :], N)
        hidden = pieces_of(held[own, :], N)
        s_here, u_here, y_here = [
            group_view(v, chunk, steps, group) for v in (s_turn, u_turn, y_turn)
        ]
        mix_here = mix_turn.at[step_rows(chunk, steps * 2 * wide)]
        for j in range(steps):
            s, u = s_here[row_of(j * groups), :], u_here[row_of(j * groups), :]
            out = states.at[j, own]
            terms = []
            for n in range(N):
                b = mix_here[row_of(j * 2 * N + n), :]
                hidden[n] = jnp.exp(s * rate[n]) * hidden[n] + u * b
                out[row_of(n), :] = hidden[n]
                terms.append(hidden[n] * mix_here[row_of(j * 2 * N + N + n), :])
            while len(terms) > 1:
                terms = [a + b for a, b in zip(terms[::2], terms[1::2])]
            y_here[row_of(j * groups), :] = terms[0]
        held[own, :] = jnp.concatenate(hidden, axis=0)
        return carried

    lax.fori_loop(0, groups, advance, 0)

    @pl.when(chunk == pl.num_programs(0) - 1)
    def _():
        def turn_back(tau, carried):
            s_flat[turned_rows(tau, length), :] = jnp.transpose(y_turn[step_rows(tau), :])
            return carried

        lax.fori_loop(0, length, turn_back, 0)
        for block in range(total // 512):
            rows = pl.ds(block * 512, 512)
            scan_out[rows, :] = s_flat[rows, :] + skip[...] * silu(pre[rows, :])


def scan(lengths, ids, feats, pre, step_w, step_b, rate_t, skip):
    total, channels = pre.shape
    length = total // LANES
    steps = math.gcd(length, STEPS)
    wide = N * channels
    flat = pltpu.VMEM((total, channels), f32)
    ins = (ids, feats, pre, step_w, step_b, rate_t, skip)
    shapes = [
        (wide, LANES),
        (total, channels),
        (length * channels, LANES),
        (length * channels, LANES),
        (length * 2 * N, LANES),
        (total, channels),
    ]
    return pl.pallas_call(
        scan_kernel,
        grid=(length // steps,),
        in_specs=[pl.BlockSpec(memory_space=pltpu.SMEM)] + [whole(a.shape) for a in ins],
        out_specs=[pl.BlockSpec((steps, wide, LANES), lambda i: (i, 0, 0))]
        + [whole(shape) for shape in shapes],
        out_shape=[jax.ShapeDtypeStruct((length, wide, LANES), f32)]
        + [jax.ShapeDtypeStruct(shape, f32) for shape in shapes],
        scratch_shapes=[flat, flat, flat, pltpu.VMEM((length * channels, LANES), f32)]
        + [pltpu.VMEM((wide, LANES), f32)] * 2
        + [pltpu.VMEM((length * 2 * N * SUB, LANES), f32)],
        compiler_params=pltpu.CompilerParams(vmem_limit_bytes=VMEM_BYTES),
        cost_estimate=cost(1),
        name="scan",
    )(lengths, *ins)


def back_kernel(
    core,
    ids_ref,
    ids_rows,
    s_turn,
    u_turn,
    mix_rows,
    pre,
    step_pre,
    grad,
    states,
    before,
    enter,
    step_w,
    rate_t,
    skip,
    act_part,
    step_grad_low,
    feat_part,
    sums,
    rate_out,
    g_turn,
    step_turn,
    in_turn,
    mix_grad,
    step_flat,
    in_flat,
    mix_flat,
    in_terms,
    out_terms,
    held,
    rate_sum,
    rates,
    mix_turn,
):
    turn_at = pl.program_id(0)
    chunks = pl.num_programs(0)
    chunk = chunks - 1 - turn_at
    total, channels = pre.shape
    length = total // LANES
    steps = states.shape[0]
    groups = channels // SUB
    wide = N * SUB

    @pl.when(turn_at == 0)
    def _():
        spread_rates(rate_t, rates)
        rate_sum[...] = jnp.zeros(rate_sum.shape, f32)

        def turn(tau, carried):
            g_turn[step_rows(tau), :] = jnp.transpose(grad[turned_rows(tau, length), :])
            spread_mix(mix_rows[step_rows(tau, 2 * N), :], mix_turn, tau)
            return carried

        lax.fori_loop(0, length, turn, 0)

        def ahead(group, carried):
            rate = pieces_of(rates[step_rows(group, wide), :], N)

            def some(i, carried):
                pulled, spent = list(carried[0]), carried[1]
                block = length // UNROLL - 1 - i
                s_here, g_here = [group_view(v, block, UNROLL, group) for v in (s_turn, g_turn)]
                mix_here = mix_turn.at[step_rows(block, UNROLL * 2 * wide)]
                for j in reversed(range(UNROLL)):
                    s, g = s_here[row_of(j * groups), :], g_here[row_of(j * groups), :]
                    for n in range(N):
                        c = mix_here[row_of(j * 2 * N + N + n), :]
                        pulled[n] = jnp.exp(s * rate[n]) * (pulled[n] + g * c)
                    spent = spent + s
                return pulled, spent

            zero = jnp.zeros((SUB, LANES), f32)
            ends, spent = lax.fori_loop(0, length // UNROLL, some, ([zero] * N, zero))
            inside = jnp.concatenate(over_segments(spent, ends, rate, True), axis=0)
            held[step_rows(group, wide), :] = inside
            return carried

        lax.fori_loop(0, groups, ahead, 0)

    in_terms[...] = jnp.zeros(in_terms.shape, f32)
    out_terms[...] = jnp.zeros(out_terms.shape, f32)

    def retreat(group, carried):
        own = step_rows(group, wide)
        views = [
            group_view(v, chunk, steps, group)
            for v in (s_turn, u_turn, g_turn, step_turn, in_turn)
        ]
        s, u, g = [[view[row_of(j * groups), :] for j in range(steps)] for view in views[:3]]
        mix_here = mix_turn.at[step_rows(chunk, steps * 2 * wide)]
        states_here = [states.at[j, own] for j in range(steps)]
        enter_here, before_here = enter.at[own], before.at[0, own]
        rate_here, held_here, sum_here = rates.at[own], held.at[own], rate_sum.at[own]
        step_sum, in_sum = [0.0] * steps, [0.0] * steps
        for n in range(N):
            at = row_of(n)
            rate, pull, rate_acc = rate_here[at, :], held_here[at, :], sum_here[at, :]
            first = jnp.where(chunk == 0, enter_here[at, :], before_here[at, :])
            state = [first] + [view[at, :] for view in states_here]
            for j in reversed(range(steps)):
                term = row_of(j * N + n)
                grad_state = g[j] * mix_here[row_of(j * 2 * N + N + n), :] + pull
                pull = jnp.exp(s[j] * rate) * grad_state
                mult = pull * state[j]
                step_sum[j] = step_sum[j] + mult * rate
                rate_acc = rate_acc + mult * s[j]
                in_sum[j] = in_sum[j] + grad_state * mix_here[row_of(j * 2 * N + n), :]
                in_terms[term, :] += grad_state * u[j]
                out_terms[term, :] += state[j + 1] * g[j]
            held_here[at, :] = pull
            sum_here[at, :] = rate_acc
        for j in range(steps):
            views[3][row_of(j * groups), :] = step_sum[j]
            views[4][row_of(j * groups), :] = in_sum[j]
        return carried

    lax.fori_loop(0, groups, retreat, 0)
    for j in range(steps):
        rows = []
        for terms in (in_terms, out_terms):
            for n in range(N):
                at = (j * N + n) * SUB
                rows.append(jnp.sum(terms[at : at + SUB, :], axis=0, keepdims=True))
        mix_grad[step_rows(chunk * steps + j, 2 * N), :] = jnp.concatenate(rows, axis=0)

    @pl.when(turn_at == chunks - 1)
    def _():
        def turn_back(tau, carried):
            rows = turned_rows(tau, length)
            step_flat[rows, :] = jnp.transpose(step_turn[step_rows(tau), :])
            in_flat[rows, :] = jnp.transpose(in_turn[step_rows(tau), :])
            mixed = mix_grad[step_rows(tau, 2 * N), :]
            blank = jnp.zeros((LANES - 2 * N, LANES), f32)
            mix_flat[rows, :] = jnp.transpose(jnp.concatenate([mixed, blank], axis=0))
            return carried

        lax.fori_loop(0, length, turn_back, 0)
        sums[...] = jnp.zeros(sums.shape, f32)
        across, block_rows = feat_part.shape[2], feat_part.shape[4]
        for seq in range(2 * feat_part.shape[1]):
            rows = pl.ds(seq * across * block_rows, across * block_rows)
            ids = ids_ref[rows, :]
            act = silu(pre[rows, :])
            step_in = step_pre[rows, :]
            state_in = in_flat[rows, :]
            grad_here = grad[rows, :]
            step_grad = step_flat[rows, :] + state_in * act
            pre_grad = step_grad * jax.nn.sigmoid(step_in)
            low = pre_grad.astype(bf16)
            step_grad_low[rows, :] = low
            act_part[rows, :] = grad_here * skip[...] + state_in * softplus(step_in)
            ours = jnp.where(core[0] == seq % 2, 1, 0)
            for j in range(across):
                block = seq * across + j
                block_low = low[j * block_rows : (j + 1) * block_rows]
                feat_part[ours, seq // 2, j, 0:R, :] = modal_rows_of(
                    step_w[...], block_low, ids_rows[block : block + 1, :]
                )
                turned = jnp.transpose(mix_flat[pl.ds(block * block_rows, block_rows), :])
                feat_part[ours, seq // 2, j, R : R + 2 * N, :] = turned[: 2 * N]
            for m in range(MODS):
                sums[m : m + 1, :] += jnp.sum(
                    jnp.where(ids == m, pre_grad, 0.0), axis=0, keepdims=True
                )
            sums[MODS : MODS + 1, :] += jnp.sum(grad_here * act, axis=0, keepdims=True)
        lane_at = lax.broadcasted_iota(jnp.int32, (SUB, LANES), 1)
        for group in range(groups):
            found = jnp.zeros((SUB, LANES), f32)
            for n in range(N):
                at = (group * N + n) * SUB
                total_rate = jnp.sum(rate_sum[at : at + SUB, :], axis=1, keepdims=True)
                found = jnp.where(lane_at == n, total_rate, found)
            rate_out[group * SUB : (group + 1) * SUB, :] = found


def scan_back(
    core, ids, ids_rows, turned, pre, step_pre, grad, states, enter, step_w, rate_t, skip
):
    total, channels = pre.shape
    length = total // LANES
    steps = math.gcd(length, STEPS)
    chunks = length // steps
    wide = N * channels
    feats = (2, lax.axis_size("z"), lax.axis_size("mod"), R + 2 * N, ids_rows.shape[1])
    first = (ids, ids_rows) + turned + (pre, step_pre, grad)
    second = (enter, step_w, rate_t, skip)
    turn = pltpu.VMEM((length * channels, LANES), f32)
    flat = pltpu.VMEM((total, channels), f32)
    terms = pltpu.VMEM((steps * N * SUB, LANES), f32)
    states_row = pltpu.VMEM((wide, LANES), f32)
    return pl.pallas_call(
        back_kernel,
        grid=(chunks,),
        in_specs=[pl.BlockSpec(memory_space=pltpu.SMEM)]
        + [whole(a.shape) for a in first]
        + [
            pl.BlockSpec((steps, wide, LANES), lambda i: (chunks - 1 - i, 0, 0)),
            pl.BlockSpec(
                (1, wide, LANES), lambda i: (jnp.maximum((chunks - 1 - i) * steps - 1, 0), 0, 0)
            ),
        ]
        + [whole(a.shape) for a in second],
        out_specs=[
            whole((total, channels)),
            whole((total, channels)),
            whole(feats),
            whole((SUB, channels)),
            whole((channels, LANES)),
        ],
        out_shape=[
            jax.ShapeDtypeStruct((total, channels), f32),
            jax.ShapeDtypeStruct((total, channels), bf16),
            jax.ShapeDtypeStruct(feats, f32),
            jax.ShapeDtypeStruct((SUB, channels), f32),
            jax.ShapeDtypeStruct((channels, LANES), f32),
        ],
        scratch_shapes=[turn, turn, turn, pltpu.VMEM((length * 2 * N, LANES), f32)]
        + [flat, flat, flat, terms, terms, states_row, states_row, states_row]
        + [pltpu.VMEM((length * 2 * N * SUB, LANES), f32)],
        compiler_params=pltpu.CompilerParams(vmem_limit_bytes=VMEM_BYTES),
        cost_estimate=cost(1),
        name="scan_back",
    )(core, *first, states, states, *second)


def conv_back_kernel(
    seqs,
    lengths,
    ids_ref,
    feat_grad,
    act_part,
    pre,
    inner,
    taps,
    param_w,
    inner_wide,
    inner_low,
    sums,
    ext,
):
    total, channels = pre.shape
    rows = total // seqs
    split = lengths[0]
    ext[total : total + 8, :] = jnp.zeros((8, channels), f32)
    sums[...] = jnp.zeros(sums.shape, f32)

    def through_silu(i, carried):
        at = pl.ds(pl.multiple_of(i * rows, rows), rows)
        for j in range(feat_grad.shape[2]):
            block_rows = feat_grad.shape[4]
            block = pl.ds(pl.multiple_of(i * rows + j * block_rows, block_rows), block_rows)
            low = feat_grad[i % 2, i // 2, j]
            stacked = dot(low, param_w[...], 0, 0)
            ext[block, :] = pick(
                ids_ref[block, :], [stacked[:, m * channels : (m + 1) * channels] for m in range(MODS)]
            )
        act_grad = act_part[at, :] + ext[at, :]
        here = pre[at, :]
        sig = jax.nn.sigmoid(here)
        conv_grad = act_grad * (sig * (1.0 + here * (1.0 - sig)))
        ext[at, :] = conv_grad
        sums[KW : KW + 1, :] += jnp.sum(conv_grad, axis=0, keepdims=True)
        return carried

    lax.fori_loop(0, total // rows, through_silu, 0)

    for block in range(total // rows):
        first = block * rows
        at = pl.ds(first, rows)
        places = row_places(first, rows)
        here = inner[at, :]
        grad = jnp.zeros((rows, channels), f32)
        for tap in range(KW):
            lag = KW - 1 - tap
            kept = (places >= split) | (places + lag < split)
            later = jnp.where(kept, ext[pl.ds(first + lag, rows), :], 0.0)
            grad = grad + taps[tap : tap + 1, :] * later
            sums[tap : tap + 1, :] += jnp.sum(later * here, axis=0, keepdims=True)
        put_masked(inner_wide, at, ids_ref[at, :], grad)
        inner_low[at, :] = grad.astype(bf16)


def conv_back(seqs, lengths, ids, feat_grad, act_part, pre, inner, taps, param_w):
    total, channels = pre.shape
    ins = (ids, feat_grad, act_part, pre, inner, taps, param_w)
    vmem = pl.BlockSpec(memory_space=pltpu.VMEM)
    return pl.pallas_call(
        functools.partial(conv_back_kernel, seqs),
        in_specs=[pl.BlockSpec(memory_space=pltpu.SMEM)] + [vmem] * len(ins),
        out_specs=[vmem, vmem, vmem],
        out_shape=[
            jax.ShapeDtypeStruct((total, MODS * channels), bf16),
            jax.ShapeDtypeStruct((total, channels), bf16),
            jax.ShapeDtypeStruct((8, channels), f32),
        ],
        scratch_shapes=[pltpu.VMEM((total + 8, channels), f32)],
        compiler_params=pltpu.CompilerParams(vmem_limit_bytes=VMEM_BYTES),
        cost_estimate=cost(1),
        name="conv_back",
    )(lengths, *ins)


def flip(axis, bit):
    size = lax.axis_size(axis)
    return lambda value: lax.ppermute(value, axis, [(i, i ^ bit) for i in range(size)])


def taken(values, at, dim):
    return lax.dynamic_index_in_dim(values, at, dim, keepdims=False)


SEQ = ("z", "core")
SAME_CORE = ("z", "mod")


def size_of(axes):
    return math.prod(lax.axis_size(axis) for axis in axes)


def share(values, axes):
    size = size_of(axes)
    return lax.all_to_all(jnp.broadcast_to(values, (size,) + values.shape), axes, 0, 0)


def exchange(blocks, axes):
    return lax.all_to_all(blocks, axes, 0, 0)


def held_back(value, until):
    return lax.optimization_barrier((value, tuple(until)))[0] if until else value


def flip(axis, bit):
    size = lax.axis_size(axis)
    return lambda value: lax.ppermute(value, axis, [(i, i ^ bit) for i in range(size)])


def taken(values, at, dim):
    return lax.dynamic_index_in_dim(values, at, dim, keepdims=False)


def two(bit, mine, got):
    return jnp.where(bit == 0, jnp.stack([mine, got]), jnp.stack([got, mine]))


Z_HIGH, Z_LOW, CORE = ("z", 2), ("z", 1), ("core", 1)
Y, X = ("mod", 2), ("mod", 1)


def place_bit(place):
    axis, bit = place
    return lax.axis_index(axis) // bit % 2


def summed_features(feats, kind=f32):
    feats = (feats[1] + flip(*CORE)(feats[0])).astype(kind)
    feats = feats.reshape((-1,) + feats.shape[2:])
    return jnp.sum(exchange(feats, SAME_CORE).astype(f32), axis=0), feats


def shared_features(block, until=()):
    mine = share(block, SAME_CORE)
    every = two(place_bit(CORE), mine, flip(*CORE)(held_back(mine, until)))
    return every.reshape((2, lax.axis_size("z"), lax.axis_size("mod")) + block.shape)


def core_rows(values, which):
    blocks = values.reshape(lax.axis_size("z"), 2, -1, values.shape[1])
    return taken(blocks, which, 1).reshape(-1, values.shape[1])


def both_cores(low, ids_ours):
    core = place_bit(CORE)
    got = flip(*CORE)(core_rows(low, 1 - core))
    return [masked(core_rows(low, core), ids_ours), masked(got, ids_ours)]


def gathered_columns(shard, between):
    width = shard.shape[1] // COLUMNS
    lines, far = [], []
    for at in range(COLUMNS):
        part = shard[:, at * width : (at + 1) * width]
        far.append(flip(*Z_HIGH)(held_back(part, far[at - 1 : at] if at else ())))
        line = two(place_bit(Z_HIGH), part, far[at])
        given = held_back(line, lines[at - 1 : at] if at else ())
        lines.append(two(place_bit(Z_LOW), line, flip(*Z_LOW)(given)))
    until = between(lines[-1])
    pieces, arrived, halfway = [], [], []
    for at, line in enumerate(lines):
        near, next_ = (X, Y) if at % 2 == 0 else (Y, X)
        halfway.append(flip(*near)(held_back(line, halfway[at - 2 : at - 1] if at > 1 else ())))
        pair = two(place_bit(near), line, halfway[at])
        got = flip(*next_)(held_back(pair, until if at > 1 else ()))
        arrived.append(got)
        pieces += [pair, got, flip(*CORE)(pair), flip(*CORE)(got)]
    return pieces, arrived


def row_parts(left, right, count):
    width = right.shape[0] // count
    return [
        dot(left, right[at * width : (at + 1) * width], 1, 1)
        .astype(bf16)
        .reshape(2, 2, 2, 2, -1, width)
        for at in range(count)
    ]


class SummedRows:
    def __init__(self, parts):
        self.dims = [["zh", "zl", "y", "x"] for _ in parts]
        self.parts = [[part] for part in parts]

    def give(self, at, name, place):
        dim = self.dims[at].index(name)
        bit = place_bit(place)
        away = sum(taken(p, 1 - bit, dim).astype(f32) for p in self.parts[at]).astype(bf16)
        self.parts[at] = [taken(p, bit, dim) for p in self.parts[at]]
        self.dims[at].remove(name)
        return away

    def stage(self, names):
        places = {"x": X, "y": Y, "zl": Z_LOW, "zh": Z_HIGH}
        sent = []
        for at in range(len(self.parts)):
            name = names[at % 2]
            away = self.give(at, name, places[name])
            sent.append(away)
            self.parts[at].append(flip(*places[name])(away))
        return sent

    def merge(self):
        pairs = list(zip(self.parts[::2], self.parts[1::2]))
        self.parts = [
            [jnp.concatenate(both, axis=-1) for both in zip(even, odd)] for even, odd in pairs
        ]
        self.dims = self.dims[::2]

    def arrived(self):
        return [parts[-1] for parts in self.parts]

    def hold(self, until):
        for parts in self.parts:
            parts[-1] = held_back(parts[-1], until)

    def result(self):
        return jnp.concatenate([sum(p.astype(f32) for p in parts) for parts in self.parts], axis=1)


def masked(values, ids):
    return jnp.concatenate(
        [jnp.where(ids == m, values, jnp.zeros_like(values)) for m in range(MODS)], axis=1
    )


def channel_layout(
    tokens,
    modality,
    lengths,
    norm_gain,
    input_weight,
    param_weight,
    step_weight,
    step_bias,
    output_weight,
    conv_weight,
    conv_bias,
    decay_log,
    skip_gain,
    cotangent,
):
    seqs = size_of(SEQ)
    channels = conv_weight.shape[1]
    width = tokens.shape[1]
    features = param_weight.shape[2]
    slab = input_weight.shape[1]

    token_vals = tokens.astype(f32)
    inverse = lax.rsqrt(jnp.mean(token_vals * token_vals, axis=1, keepdims=True) + EPSILON)
    normal_rows = token_vals * inverse
    gain_vals = norm_gain.astype(f32)

    send_in = input_weight.reshape(MODS, slab, 2, seqs, channels)
    send_in = send_in.transpose(3, 2, 0, 1, 4).reshape(seqs, 2 * MODS * slab, channels)
    id_rows = 16
    send_ids = jnp.pad(modality.astype(bf16), (0, id_rows * channels - modality.shape[0]))
    send_ids = jnp.broadcast_to(send_ids.reshape(id_rows, channels), (seqs, id_rows, channels))
    send_in = jnp.concatenate([send_in, send_ids], axis=1)
    made = []

    def send(line):
        made.append(exchange(held_back(send_in, [line]), SEQ))
        return made

    pieces, arrived = gathered_columns((normal_rows * gain_vals[None, :]).astype(bf16), send)
    inner_blocks = made[0]
    ids = inner_blocks[:, 2 * MODS * slab :].reshape(seqs, -1)[:, : modality.shape[0]].astype(jnp.int32)
    ids_rows = ids.reshape(-1, tokens.shape[0])
    ids = ids.reshape(-1, 1)
    send_out = output_weight.reshape(MODS, seqs, channels, slab).transpose(1, 0, 3, 2)
    send_out = send_out.reshape(seqs, MODS * slab, channels)
    param_rows = param_weight.transpose(0, 2, 1).reshape(MODS * features, channels)
    param_columns = param_weight.transpose(2, 0, 1).reshape(features, MODS * channels)
    step_rows_w = step_weight.reshape(MODS * R, channels)
    step_columns = step_weight.transpose(1, 0, 2).reshape(R, MODS * channels)
    core = place_bit(CORE)
    place = jnp.stack([place_bit(at) for at in (CORE, Y, X)]).astype(jnp.int32)
    taps = conv_weight.astype(f32)
    skip = skip_gain.astype(f32)[None, :]
    decay_rate = -jnp.exp(decay_log.astype(f32))
    rate_t = jnp.pad(decay_rate.T, ((0, 0), (0, LANES - N)))

    *normed, own_inner, own_gate, inner, conv_pre, act_low, feats = project(
        lengths,
        place,
        pieces,
        ids,
        ids_rows,
        inner_blocks,
        taps,
        conv_bias.astype(f32)[None, :],
        param_rows,
    )
    cotangents = lax.all_gather(
        held_back(cotangent, [inner]), SEQ + ("mod",), axis=0, tiled=True
    )
    feats, sent = summed_features(feats)
    gate_pre = modal_rows(normed, held_back(ids, [sent]), own_gate)
    pair_in = side_by_side(own_inner, flip(*CORE)(own_inner), own_gate, flip(*CORE)(own_gate))
    feats = held_back(feats, [gate_pre, pair_in])
    mix_high = feats[R:].astype(bf16)
    mix_rest = (feats[R:] - mix_high.astype(f32)).astype(bf16)
    feats = jnp.concatenate([feats[:R].astype(bf16), mix_high, mix_rest], axis=0)
    feats = shared_features(feats)

    out_blocks = exchange(held_back(send_out, [feats]), SEQ)
    states, enter, step_pre, *turned, scan_out = scan(
        lengths,
        ids,
        feats,
        conv_pre,
        step_columns,
        step_bias.astype(f32).reshape(1, MODS * channels),
        rate_t,
        skip,
    )
    out_blocks, scan_out = lax.optimization_barrier((out_blocks, scan_out))
    own_out, grad_scan, gate_wide, gated_wide, gate_rows, gated_rows = gates(
        cotangents, ids, out_blocks, gate_pre, scan_out
    )

    def token_sums(wide, weight):
        lows, gains = [], []
        for at, part in enumerate(normed):
            rows = part.shape[1]
            grad = dot(part, wide, 0, 0)
            lows.append(grad.astype(bf16))
            gains.append(jnp.sum(grad * weight[at * rows : (at + 1) * rows].astype(f32), axis=1))
        return jnp.concatenate(lows, axis=0), jnp.concatenate(gains, axis=0)

    def by_holder(low):
        return low.reshape(seqs, slab, MODS * channels)

    ids_ours = core_rows(ids, core)
    gated_both = jnp.concatenate(both_cores(gated_rows, ids_ours), axis=1)
    pair_out = side_by_side(own_out, flip(*CORE)(own_out))
    branch = SummedRows(row_parts(gated_both, pair_out, 2))
    branch_sent = branch.stage(("x", "y"))
    grad_scan = held_back(grad_scan, branch_sent)

    act_part, step_grad_low, feat_grad, sums, rate_sum = scan_back(
        place,
        ids,
        ids_rows,
        tuple(turned),
        conv_pre,
        step_pre,
        grad_scan,
        states,
        enter,
        step_rows_w,
        rate_t,
        skip,
    )
    feat_grad = held_back(feat_grad, branch.arrived())
    gate_rows, gate_wide, gated_wide = held_back((gate_rows, gate_wide, gated_wide), [feat_grad])
    gate_both = both_cores(gate_rows, ids_ours)
    feat_grad, sent = summed_features(feat_grad, bf16)
    feat_grad = held_back(feat_grad.astype(bf16), branch.stage(("y", "x")))
    gate_wide, gated_wide = held_back((gate_wide, gated_wide), [sent])
    gate_low, gate_gain = token_sums(gate_wide, own_gate)
    out_low = dot(cotangents, gated_wide, 0, 0).astype(bf16)
    more_low = jnp.concatenate([by_holder(gate_low), by_holder(out_low)], axis=2)
    feat_grad = shared_features(feat_grad, [more_low])
    more_low = exchange(held_back(more_low, [feat_grad]), SEQ)
    branch.hold([feat_grad])
    branch.merge()

    inner_wide, inner_rows, tap_sums = conv_back(
        seqs,
        lengths,
        ids,
        feat_grad,
        act_part,
        conv_pre,
        inner,
        taps,
        param_columns,
    )
    both_wide = jnp.concatenate(both_cores(inner_rows, ids_ours) + gate_both, axis=1)
    products = row_parts(both_wide, pair_in, COLUMNS)
    normed_sums = SummedRows(products)
    sent = normed_sums.stage(("x", "y"))
    branch.hold(sent)
    branch.stage(("zl", "zl"))
    inner_low, inner_gain = token_sums(held_back(inner_wide, sent), own_inner)
    inner_low, more_low = lax.optimization_barrier((by_holder(inner_low), more_low))
    inner_low = exchange(inner_low, SEQ).reshape(seqs, slab, MODS, channels)
    more_low = more_low.reshape(seqs, slab, 2, MODS, channels)
    grad_gate = more_low[:, :, 0].transpose(2, 1, 0, 3)
    grad_out = more_low[:, :, 1].transpose(2, 0, 3, 1)
    grad_out = grad_out.reshape(MODS, seqs * channels, slab).astype(f32)
    branch.stage(("zh", "zh"))
    sent = normed_sums.stage(("y", "x"))
    output = (token_vals + branch.result()).astype(bf16)
    gain_sum, inner_low = lax.optimization_barrier((inner_gain + gate_gain, inner_low))
    grad_gain = jnp.sum(share(gain_sum, SEQ + ("mod",)), axis=0) / gain_vals
    grad_in = jnp.stack([inner_low.transpose(2, 1, 0, 3), grad_gate], axis=2)
    grad_in = grad_in.reshape(MODS, slab, 2, seqs * channels).astype(f32)
    normed_sums.merge()
    normed_sums.stage(("zl", "zl"))
    normed_sums.hold([grad_in, grad_gain])
    normed_sums.stage(("zh", "zh"))
    normed_grad = normed_sums.result()
    step_grad_low, feat_late = held_back((step_grad_low, feat_grad), sent)
    step_t = feats[:, :, :, :R].transpose(3, 1, 0, 2, 4).reshape(R, -1)
    grad_step = dot(step_t, masked(step_grad_low, ids))
    grad_step = grad_step.reshape(R, MODS, channels).transpose(1, 0, 2)
    feat_late = feat_late.transpose(3, 1, 0, 2, 4).reshape(features, -1)
    feat_late = [
        jnp.where(ids_rows.reshape(1, -1) == m, feat_late, jnp.zeros_like(feat_late))
        for m in range(MODS)
    ]
    grad_param = dot(jnp.concatenate(feat_late, axis=0), act_low)
    grad_param = grad_param.reshape(MODS, features, channels).transpose(0, 2, 1)
    hat_grad = normed_grad * gain_vals[None, :]
    token_grad = cotangent.astype(f32) + inverse * (
        hat_grad - normal_rows * jnp.mean(hat_grad * normal_rows, axis=1, keepdims=True)
    )
    return (
        output,
        token_grad,
        grad_gain,
        grad_in,
        grad_param,
        grad_step,
        grad_out,
        tap_sums[:KW],
        tap_sums[KW],
        rate_sum[:, :N].T * decay_rate,
        sums[MODS],
        sums[:MODS],
    )


def placed(spec, axes):
    entries = [
        sum((axes[name] for name in ((entry,) if isinstance(entry, str) else entry or ())), ())
        for entry in spec
    ]
    return P(*[entry or None for entry in entries])


def solution(mesh):
    token_rows = P(("seq", "mod"), None)
    in_weight = P(None, "seq", None, "mod")
    out_weight = P(None, "mod", "seq")
    row, column, depth = P(("mod", "seq")), P(None, ("mod", "seq")), P(None, None, ("mod", "seq"))
    middle = P(None, ("mod", "seq"), None)
    ins = (token_rows, P("seq"), P(), P(), in_weight, middle, depth, column, out_weight)
    ins += (column, row, column, row, token_rows)
    outs = (token_rows, token_rows, P(), in_weight, middle, depth, out_weight)
    outs += (column, row, column, row, column)

    def run(*args):
        sizes = (mesh.shape["seq"], mesh.shape["mod"])
        share_of_channels = args[12].shape[0] // (sizes[0] * sizes[1])
        if share_of_channels == LANES and sizes == (8, 4):
            part, over = channel_layout, jax.sharding.Mesh(
                mesh.devices.reshape(sizes[0] // 2, 2, sizes[1]), ("z", "core", "mod")
            )
            axes = {"seq": SEQ, "mod": ("mod",)}
        else:
            part, over = local, mesh
            axes = {"seq": ("seq",), "mod": ("mod",)}
        return jax.shard_map(
            part,
            mesh=over,
            in_specs=tuple(placed(spec, axes) for spec in ins),
            out_specs=tuple(placed(spec, axes) for spec in outs),
            check_vma=False,
        )(*args)

    return run
```

```python
import functools
import math

import jax
import jax.numpy as jnp
from jax import lax
from jax.experimental import pallas as pl
from jax.experimental.pallas import tpu as pltpu
from jax.sharding import PartitionSpec as P

N = 16
KW = 4
R = 128
MODS = 3
TOK_DEV = 128
CAPD = 48


EPSILON = 1e-05
SCAN_ROWS = 512

LANES = 128
SUB = 8
STEPS = 4
UNROLL = 4
COLUMNS = 4
FAR = 1e9
VMEM_BYTES = 60 * 1024 * 1024
f32 = jnp.float32
bf16 = jnp.bfloat16


def shifted_2(value, axis, by):
    size = lax.axis_size(axis)
    pairs = [(i, i + by) for i in range(size) if 0 <= i + by < size]
    return lax.ppermute(value, axis, pairs)


def carried_in(value, axis, combine, identity):
    size, here = (lax.axis_size(axis), lax.axis_index(axis))
    everything = jax.tree.map(
        lambda part, kind: lax.all_gather(part.astype(kind), axis),
        value,
        (jnp.bfloat16, jnp.bfloat16),
    )
    start = jax.tree.map(
        lambda part, zero: jnp.broadcast_to(jnp.asarray(zero, part.dtype), part.shape),
        value,
        identity,
    )

    def carried_hop(k, before):
        reached = k < here
        new = combine(
            before, jax.tree.map(lambda part, own: part[k].astype(own.dtype), everything, value)
        )
        return jax.tree.map(lambda a, b: jnp.where(reached, a, b), new, before)

    return lax.fori_loop(0, size, carried_hop, start)


def prefix(value, axis, combine, identity):
    size, here = (lax.axis_size(axis), lax.axis_index(axis))
    everything = jax.tree.map(lambda part: lax.all_gather(part, axis), value)
    start = jax.tree.map(
        lambda part, zero: jnp.broadcast_to(jnp.asarray(zero, part.dtype), part.shape),
        value,
        identity,
    )

    def prefix_hop(k, before):
        at = size - 1 - k
        reached = at > here
        new = combine(before, jax.tree.map(lambda part: part[at], everything))
        return jax.tree.map(lambda a, b: jnp.where(reached, a, b), new, before)

    return lax.fori_loop(0, size, prefix_hop, start)


def split_rows(count_rows):
    return (count_rows // TOK_DEV, TOK_DEV)


def slot_tables(modal_ids, capacity):
    sub_rows = modal_ids.shape[1]
    marked = (modal_ids[:, :, None] == jnp.arange(MODS, dtype=jnp.int32)[None, None, :]).astype(
        jnp.int32
    )
    ranking = jnp.sum((jnp.cumsum(marked, axis=1) - 1) * marked, axis=2)
    slot_ids = modal_ids * capacity + ranking
    positions = jnp.broadcast_to(jnp.arange(sub_rows, dtype=jnp.int32)[None, :], modal_ids.shape)
    unfilled = jnp.full((modal_ids.shape[0], MODS * capacity), sub_rows, jnp.int32)
    tables = jax.vmap(lambda table_row, slot_row, place_row: table_row.at[slot_row].set(place_row))(
        unfilled, slot_ids, positions
    )
    return (tables, slot_ids)


def group_rows(values, tables, capacity):
    padded = jnp.concatenate([values, jnp.zeros_like(values[:, :1])], axis=1)
    picked = jax.vmap(lambda block_values, block_table: block_values[block_table])(padded, tables)
    return picked.reshape(values.shape[0], MODS, capacity, values.shape[2])


def ungroup_rows(grouped, slot_ids):
    flattened = grouped.reshape(grouped.shape[0], MODS * grouped.shape[2], grouped.shape[3])
    return jax.vmap(lambda block_values, block_slots: block_values[block_slots])(
        flattened, slot_ids
    )


def modal_product(values, modal_ids, weight, transpose):
    count_rows = values.shape[0]
    sub_count, sub_rows = split_rows(count_rows)
    capacity = min(CAPD, sub_rows)
    tables, slot_ids = slot_tables(modal_ids.reshape(sub_count, sub_rows), capacity)
    grouped = group_rows(values.reshape(sub_count, sub_rows, values.shape[1]), tables, capacity)
    if transpose:
        result = jnp.einsum("gmcn,mkn->gmck", grouped, weight, preferred_element_type=jnp.float32)
    else:
        result = jnp.einsum("gmck,mkn->gmcn", grouped, weight, preferred_element_type=jnp.float32)
    return ungroup_rows(result, slot_ids).reshape(count_rows, result.shape[3])


def modal_outer(left, right, modal_ids):
    count_rows = left.shape[0]
    sub_count, sub_rows = split_rows(count_rows)
    capacity = min(CAPD, sub_rows)
    tables, slot_ids = slot_tables(modal_ids.reshape(sub_count, sub_rows), capacity)
    left_grouped = group_rows(left.reshape(sub_count, sub_rows, left.shape[1]), tables, capacity)
    right_grouped = group_rows(right.reshape(sub_count, sub_rows, right.shape[1]), tables, capacity)
    return jnp.einsum(
        "gmcl,gmcr->mlr", left_grouped, right_grouped, preferred_element_type=jnp.float32
    )


def modal_table(table, modal_ids):
    picked = jnp.zeros((modal_ids.shape[0], table.shape[1]), jnp.float32)
    for modal_index in range(MODS):
        picked = (
            picked
            + (modal_ids == modal_index).astype(jnp.float32)[:, None] * table[modal_index][None, :]
        )
    return picked


def modal_sums(values, modal_ids):
    return jnp.stack(
        [
            jnp.sum(values * (modal_ids == modal_index).astype(jnp.float32)[:, None], axis=0)
            for modal_index in range(MODS)
        ]
    )


def pair_combine(earlier, later):
    return (earlier[0] * later[0], later[0] * earlier[1] + later[1])


def back_combine(earlier, later):
    return (earlier[0] * later[0], later[1] + later[0] * earlier[1])


def silu_slope(values):
    sigmoid_part = jax.nn.sigmoid(values)
    return sigmoid_part * (1.0 + values * (1.0 - sigmoid_part))


def local(
    tokens,
    modality,
    lengths,
    norm_gain,
    input_weight,
    param_weight,
    step_weight,
    step_bias,
    output_weight,
    conv_weight,
    conv_bias,
    decay_log,
    skip_gain,
    cotangent,
):
    block_rows = modality.shape[0]
    gathered = (
        lax.all_gather(input_weight, "seq", axis=1, tiled=True),
        lax.all_gather(param_weight, "seq", axis=1, tiled=True),
        lax.all_gather(step_weight, "seq", axis=2, tiled=True),
        lax.all_gather(output_weight, "seq", axis=2, tiled=True),
        lax.all_gather(conv_weight, "seq", axis=1, tiled=True),
        lax.all_gather(conv_bias, "seq", axis=0, tiled=True),
        lax.all_gather(decay_log, "seq", axis=1, tiled=True),
        lax.all_gather(skip_gain, "seq", axis=0, tiled=True),
        lax.all_gather(step_bias, "seq", axis=1, tiled=True),
    )
    in_local = gathered[0]
    param_local = gathered[1]
    step_local = gathered[2]
    out_local = gathered[3]
    tap_weights = gathered[4].astype(jnp.float32)
    tap_bias = gathered[5].astype(jnp.float32)
    decay_rate = -jnp.exp(gathered[6].astype(jnp.float32))
    skip_local = gathered[7].astype(jnp.float32)
    bias_local = gathered[8].astype(jnp.float32)
    channels = in_local.shape[3]
    model_width = in_local.shape[1]
    in_flat = in_local.reshape(MODS, model_width, 2 * channels)
    token_vals = tokens.astype(jnp.float32)
    inverse = lax.rsqrt(jnp.mean(token_vals * token_vals, axis=1, keepdims=True) + EPSILON)
    normal_rows = token_vals * inverse
    gain_vals = norm_gain.astype(jnp.float32)
    normed = (normal_rows * gain_vals[None, :]).astype(jnp.bfloat16)
    piece = lax.all_gather(normed, "mod", axis=0, tiled=True)
    piece_ids = modality
    product = modal_product(piece, piece_ids, in_flat, False)
    filled = product
    folded = (filled, piece)
    expanded = folded[0].reshape(block_rows, 2, channels)
    inner = expanded[:, 0]
    gate_pre = expanded[:, 1]
    first_place = lax.axis_index("seq") * block_rows
    places = first_place + jnp.arange(block_rows, dtype=jnp.int32)
    split_place = lengths[0]
    begins = jnp.where(places >= split_place, split_place, 0)
    keeping = (places != begins).astype(jnp.float32)
    inherit = (begins < first_place).astype(jnp.float32)
    halo_rows = shifted_2(inner[block_rows - KW + 1 :], "seq", 1)
    extended = jnp.concatenate([halo_rows, inner], axis=0)
    valid_taps = [
        (places - (KW - 1 - tap_index) >= begins).astype(jnp.float32)[:, None]
        for tap_index in range(KW)
    ]
    conv_pre = jnp.broadcast_to(tap_bias[None, :], inner.shape)
    for tap_index in range(KW):
        conv_pre = (
            conv_pre
            + tap_weights[tap_index][None, :]
            * extended[tap_index : tap_index + block_rows]
            * valid_taps[tap_index]
        )
    activated = jax.nn.silu(conv_pre)
    act_low = activated.astype(jnp.bfloat16)
    feature_part = modal_product(act_low, modality, param_local, False)
    features = lax.psum(feature_part, "mod")
    step_low = features[:, :R].astype(jnp.bfloat16)
    input_mix = features[:, R : R + N]
    output_mix = features[:, R + N :]
    step_pre = modal_product(step_low, modality, step_local, False) + modal_table(
        bias_local, modality
    )
    step_size = jax.nn.softplus(step_pre)
    scan_rows = math.gcd(block_rows, SCAN_ROWS)
    scan_count = block_rows // scan_rows

    def blocked(values):
        return values.reshape((scan_count, scan_rows) + values.shape[1:])

    def block_mult(keep_block, step_block):
        return keep_block[:, None, None] * jnp.exp(step_block[:, None, :] * decay_rate[None])

    def local_step(state_now, inputs):
        keep_block, step_block, act_block, input_block, output_block = inputs
        multiplier = block_mult(keep_block, step_block)
        addition = (step_block * act_block)[:, None, :] * input_block[:, :, None]
        running = lax.associative_scan(pair_combine, (multiplier, addition), axis=0)
        states = running[0] * state_now[None] + running[1]
        return (
            states[-1],
            (jnp.sum(output_block[:, :, None] * states, axis=1), state_now, running[0], running[1]),
        )

    scan_inputs = (
        blocked(keeping),
        blocked(step_size),
        blocked(activated),
        blocked(input_mix),
        blocked(output_mix),
    )
    end_state, (local_out, local_starts, run_mult, run_add) = lax.scan(
        local_step, jnp.zeros((N, channels), jnp.float32), scan_inputs
    )
    device_decay = jnp.exp(decay_rate * jnp.sum(step_size, axis=0)[None, :]) * jnp.min(keeping)
    chained = carried_in(
        (device_decay, end_state),
        "seq",
        pair_combine,
        (jnp.ones_like(device_decay), jnp.zeros_like(end_state)),
    )
    state_in = chained[1]

    def fix_step(carried, inputs):
        total_step, alive = carried
        inherit_block, step_block, output_block = inputs
        start_factor = alive * jnp.exp(decay_rate * total_step[None, :])
        running_step = total_step[None, :] + jnp.cumsum(step_block, axis=0)
        reach = inherit_block[:, None, None] * jnp.exp(running_step[:, None, :] * decay_rate[None])
        extra = jnp.sum(output_block[:, :, None] * reach * state_in[None], axis=1)
        return ((running_step[-1], inherit_block[-1]), (extra, start_factor))

    reach_inputs = (blocked(inherit), blocked(step_size), blocked(output_mix))
    _, (extra_out, start_factors) = lax.scan(
        fix_step, (jnp.zeros((channels,), jnp.float32), jnp.float32(1.0)), reach_inputs
    )
    start_states = local_starts + start_factors * state_in[None]
    scan_out = (local_out + extra_out).reshape(block_rows, channels) + skip_local[
        None, :
    ] * activated
    gate_act = jax.nn.silu(gate_pre)
    gated = (scan_out * gate_act).astype(jnp.bfloat16)
    piece = gated
    piece_ids = modality
    branch = lax.psum_scatter(
        modal_product(piece, piece_ids, out_local, False), "mod", scatter_dimension=0, tiled=True
    )
    output = (token_vals + branch).astype(jnp.bfloat16)
    back_rows = cotangent.astype(jnp.float32)
    piece = lax.all_gather(cotangent, "mod", axis=0, tiled=True)
    piece_ids = modality
    product = modal_product(piece, piece_ids, out_local, True)
    grad_out = modal_outer(gated, piece, piece_ids)
    grad_scan = product * gate_act
    grad_gate = product * scan_out * silu_slope(gate_pre)
    grad_skip = jnp.sum(grad_scan * activated, axis=0)
    grad_act = grad_scan * skip_local[None, :]

    def lead_step(carried, inputs):
        total_step, lead_sum = carried
        inherit_block, step_block, output_block, grad_block = inputs
        running_step = total_step[None, :] + jnp.cumsum(step_block, axis=0)
        reach = inherit_block[:, None, None] * jnp.exp(running_step[:, None, :] * decay_rate[None])
        lead_sum = lead_sum + jnp.sum(
            reach * output_block[:, :, None] * grad_block[:, None, :], axis=0
        )
        return ((running_step[-1], lead_sum), None)

    (_, lead_local), _ = lax.scan(
        lead_step,
        (jnp.zeros((channels,), jnp.float32), jnp.zeros((N, channels), jnp.float32)),
        reach_inputs + (blocked(grad_scan),),
    )
    incoming = prefix(
        (device_decay, lead_local),
        "seq",
        back_combine,
        (jnp.ones_like(device_decay), jnp.zeros_like(lead_local)),
    )[1]

    def back_step(carried, inputs):
        after_block, rate_grad = carried
        (
            keep_block,
            step_block,
            act_block,
            input_block,
            output_block,
            grad_block,
            start_state,
            mult_block,
            add_block,
        ) = inputs
        multiplier = block_mult(keep_block, step_block)
        states = mult_block * start_state[None] + add_block
        previous = jnp.concatenate([start_state[None], states[:-1]], axis=0)
        pushed = output_block[:, :, None] * grad_block[:, None, :]
        pushed = pushed.at[-1].add(after_block)
        shifted = jnp.concatenate([multiplier[1:], jnp.ones_like(multiplier[:1])], axis=0)
        flipped = lax.associative_scan(pair_combine, (shifted[::-1], pushed[::-1]), axis=0)
        grad_state = flipped[1][::-1]
        mult_grad = grad_state * previous * multiplier
        state_input = jnp.sum(grad_state * input_block[:, :, None], axis=1)
        step_grad = jnp.sum(mult_grad * decay_rate[None], axis=1) + state_input * act_block
        rate_grad = rate_grad + jnp.sum(mult_grad * step_block[:, None, :], axis=0)
        input_grad = jnp.sum(grad_state * (step_block * act_block)[:, None, :], axis=2)
        act_grad = state_input * step_block
        output_grad = jnp.sum(states * grad_block[:, None, :], axis=2)
        return (
            (multiplier[0] * grad_state[0], rate_grad),
            (step_grad, input_grad, act_grad, output_grad),
        )

    back_inputs = scan_inputs[:5] + (blocked(grad_scan), start_states, run_mult, run_add)
    (_, rate_total), (step_grads, input_grads, act_grads, output_grads) = lax.scan(
        back_step, (incoming, jnp.zeros((N, channels), jnp.float32)), back_inputs, reverse=True
    )
    step_pre_grad = step_grads.reshape(block_rows, channels) * jax.nn.sigmoid(step_pre)
    grad_bias = modal_sums(step_pre_grad, modality)
    step_grad_low = step_pre_grad.astype(jnp.bfloat16)
    step_in_part = modal_product(step_grad_low, modality, step_local, True)
    grad_step = modal_outer(step_low, step_grad_low, modality)
    summed = lax.psum(
        (step_in_part, input_grads.reshape(block_rows, N), output_grads.reshape(block_rows, N)),
        "mod",
    )
    feature_grad = jnp.concatenate(summed, axis=1).astype(jnp.bfloat16)
    grad_param = modal_outer(act_low, feature_grad, modality)
    act_total = (
        grad_act
        + act_grads.reshape(block_rows, channels)
        + modal_product(feature_grad, modality, param_local, True)
    )
    conv_grad = act_total * silu_slope(conv_pre)
    tap_grads = []
    ext_grad = jnp.zeros((block_rows + KW - 1, channels), jnp.float32)
    for tap_index in range(KW):
        masked = conv_grad * valid_taps[tap_index]
        tap_grads.append(jnp.sum(masked * extended[tap_index : tap_index + block_rows], axis=0))
        ext_grad = ext_grad.at[tap_index : tap_index + block_rows].add(
            masked * tap_weights[tap_index][None, :]
        )
    grad_taps = jnp.stack(tap_grads)
    grad_tap_bias = jnp.sum(conv_grad, axis=0)
    spill = shifted_2(ext_grad[: KW - 1], "seq", -1)
    inner_grad = ext_grad[KW - 1 :].at[block_rows - KW + 1 :].add(spill)
    both_grad = (
        jnp.stack([inner_grad, grad_gate], axis=1)
        .astype(jnp.bfloat16)
        .reshape(block_rows, 2 * channels)
    )
    piece = both_grad
    piece_ids = modality
    normed_grad = lax.psum_scatter(
        modal_product(piece, piece_ids, in_flat, True), "mod", scatter_dimension=0, tiled=True
    )
    grad_in = modal_outer(folded[1], both_grad, modality)
    gain_part = jnp.sum(normed_grad * normal_rows, axis=0)
    hat_grad = normed_grad * gain_vals[None, :]
    token_grad = back_rows + inverse * (
        hat_grad - normal_rows * jnp.mean(hat_grad * normal_rows, axis=1, keepdims=True)
    )
    grad_gain = lax.psum(gain_part, ("seq", "mod"))
    grad_decay = rate_total * decay_rate
    weight_grads = (
        lax.psum_scatter(
            grad_in.reshape(MODS, model_width, 2, channels), "seq", scatter_dimension=1, tiled=True
        ),
        lax.psum_scatter(grad_param, "seq", scatter_dimension=1, tiled=True),
        lax.psum_scatter(grad_step, "seq", scatter_dimension=2, tiled=True),
        lax.psum_scatter(grad_out, "seq", scatter_dimension=2, tiled=True),
        lax.psum_scatter(grad_taps, "seq", scatter_dimension=1, tiled=True),
        lax.psum_scatter(grad_tap_bias, "seq", scatter_dimension=0, tiled=True),
        lax.psum_scatter(grad_decay, "seq", scatter_dimension=1, tiled=True),
        lax.psum_scatter(grad_skip, "seq", scatter_dimension=0, tiled=True),
        lax.psum_scatter(grad_bias, "seq", scatter_dimension=1, tiled=True),
    )
    return (
        output,
        token_grad,
        grad_gain,
        weight_grads[0],
        weight_grads[1],
        weight_grads[2],
        weight_grads[3],
        weight_grads[4],
        weight_grads[5],
        weight_grads[6],
        weight_grads[7],
        weight_grads[8],
    )


def pick(ids, parts):
    return jnp.where(ids == 0, parts[0], jnp.where(ids == 1, parts[1], parts[2]))


def silu(values):
    return values * jax.nn.sigmoid(values)


def softplus(values):
    small = jnp.exp(-jnp.abs(values))
    series = small * (
        1.0 + small * (-1 / 2 + small * (1 / 3 + small * (-1 / 4 + small * (1 / 5 - small / 6))))
    )
    return jnp.maximum(values, 0.0) + jnp.where(small < 0.05, series, jnp.log(1.0 + small))


def dot(left, right, left_dim=1, right_dim=0):
    return lax.dot_general(
        left, right, (((left_dim,), (right_dim,)), ((), ())), preferred_element_type=f32
    )


def row_places(first, rows):
    return first + lax.broadcasted_iota(jnp.int32, (rows, 1), 0)


def whole(shape):
    return pl.BlockSpec(shape, lambda *_: (0,) * len(shape), pipeline_mode=pl.Buffered(1))


def cost(micros, flops=0):
    return pl.CostEstimate(flops=flops, bytes_accessed=int(micros * 3.69e6), transcendentals=0)


def modal_dot(values, ids, weight):
    part = values[0].shape[1]
    wide = sum(dot(v[...], weight[i * part : (i + 1) * part, :]) for i, v in enumerate(values))
    channels = wide.shape[1] // MODS
    return pick(ids, [wide[:, m * channels : (m + 1) * channels] for m in range(MODS)])


def modal_rows_of(weight, values, ids_row):
    stacked = dot(weight, values, 1, 1)
    height = stacked.shape[0] // MODS
    return pick(ids_row, [stacked[m * height : (m + 1) * height] for m in range(MODS)])


def put_masked(ref, rows, ids, values):
    channels = values.shape[1]
    for m in range(MODS):
        ref[rows, m * channels : (m + 1) * channels] = jnp.where(ids == m, values, 0.0).astype(
            ref.dtype
        )


def arrange(blocks, first, out):
    slab = out.shape[0] // blocks.shape[0]
    channels = blocks.shape[2]
    for at in range(blocks.shape[0]):
        for m in range(MODS):
            out[at * slab : (at + 1) * slab, m * channels : (m + 1) * channels] = blocks[
                at, (first + m) * slab : (first + m + 1) * slab, :
            ]


def project_kernel(lengths, place, *refs):
    pieces, refs = refs[: 4 * COLUMNS], refs[4 * COLUMNS :]
    ids_ref, ids_rows, blocks, taps, bias, param_t = refs[:6]
    xs, refs = refs[6 : 6 + COLUMNS], refs[6 + COLUMNS :]
    w, w_gate, inner_ref, pre_ref, low_ref, feats, ext = refs
    step = pl.program_id(0)

    @pl.when(step == 0)
    def _():
        arrange(blocks, 0, w)
        arrange(blocks, MODS, w_gate)

    block_rows = pieces[0].shape[3]
    for which in (0, 1):

        @pl.when((place[0] == step % 2) == (which == 0))
        def _():
            for at in range(COLUMNS):
                own_line, other_line = pieces[4 * at + 2 * which : 4 * at + 2 * which + 2]
                here = place[1] if at % 2 == 0 else place[2]
                for near in (0, 1):
                    for line, value in ((here, own_line), (1 - here, other_line)):
                        block = line * 2 + near if at % 2 == 0 else near * 2 + line
                        row = pl.multiple_of(block * block_rows, block_rows)
                        xs[at][pl.ds(row, block_rows), :] = value[near, 0, 0]

    rows = xs[0].shape[0]
    channels = inner_ref.shape[1]
    ids = ids_ref[...]
    inner = modal_dot(xs, ids, w)
    inner_ref[...] = inner

    @pl.when(step == 0)
    def _():
        ext[0:8, :] = jnp.zeros((8, channels), f32)

    @pl.when(step > 0)
    def _():
        ext[0:8, :] = ext[rows : rows + 8, :]

    ext[8 : 8 + rows, :] = inner
    places = row_places(step * rows, rows)
    split = lengths[0]
    begins = jnp.where(places >= split, split, 0)
    pre = jnp.broadcast_to(bias[...], (rows, channels))
    for tap in range(KW):
        lag = KW - 1 - tap
        shifted = ext[8 - lag : 8 - lag + rows, :]
        pre = pre + taps[tap : tap + 1, :] * jnp.where(places - lag >= begins, shifted, 0.0)
    pre_ref[...] = pre
    low = silu(pre).astype(bf16)
    low_ref[...] = low
    across = feats.shape[2]
    ours = jnp.where(place[0] == step % 2, 1, 0)
    for j in range(across):
        block = low[j * block_rows : (j + 1) * block_rows]
        feats[ours, step // 2, j] = modal_rows_of(
            param_t[...], block, ids_rows[pl.ds(step * across + j, 1), :]
        )


def project(lengths, place, pieces, ids, ids_rows, blocks, taps, bias, param_t):
    total = ids.shape[0]
    channels = taps.shape[1]
    chips, across = lax.axis_size("z"), lax.axis_size("mod")
    rows = total // (2 * chips)
    width = pieces[0].shape[4]
    by_rows = lambda i: (i, 0)
    feats = (2, chips, across, param_t.shape[0] // MODS, rows // across)
    smem = pl.BlockSpec(memory_space=pltpu.SMEM)
    return pl.pallas_call(
        project_kernel,
        grid=(total // rows,),
        in_specs=[
            smem,
            smem,
            *[
                pl.BlockSpec((2, 1, 1) + piece.shape[3:], lambda i: (0, i // 2 % 2, i // 4, 0, 0))
                for piece in pieces
            ],
            pl.BlockSpec((rows, 1), by_rows),
            whole(ids_rows.shape),
            whole(blocks.shape),
            whole(taps.shape),
            whole(bias.shape),
            whole(param_t.shape),
        ],
        out_specs=[pl.BlockSpec((rows, width), by_rows)] * COLUMNS
        + [whole((COLUMNS * width, MODS * channels))] * 2
        + [pl.BlockSpec((rows, channels), by_rows)] * 3
        + [whole(feats)],
        out_shape=[jax.ShapeDtypeStruct((total, width), bf16)] * COLUMNS
        + [jax.ShapeDtypeStruct((COLUMNS * width, MODS * channels), bf16)] * 2
        + [jax.ShapeDtypeStruct((total, channels), f32)] * 2
        + [jax.ShapeDtypeStruct((total, channels), bf16)]
        + [jax.ShapeDtypeStruct(feats, f32)],
        scratch_shapes=[pltpu.VMEM((rows + 8, channels), f32)],
        compiler_params=pltpu.CompilerParams(vmem_limit_bytes=VMEM_BYTES),
        cost_estimate=cost(1),
        name="project",
    )(lengths, place, *pieces, ids, ids_rows, blocks, taps, bias, param_t)


def modal_kernel(*refs):
    *xs, ids_ref, w, out = refs
    out[...] = modal_dot(xs, ids_ref[...], w)


def modal_rows(values, ids, weight):
    total = values[0].shape[0]
    channels = weight.shape[1] // MODS
    rows = math.gcd(total, 512)
    by_rows = lambda i: (i, 0)
    return pl.pallas_call(
        modal_kernel,
        grid=(total // rows,),
        in_specs=[
            *[pl.BlockSpec((rows, part.shape[1]), by_rows) for part in values],
            pl.BlockSpec((rows, 1), by_rows),
            whole(weight.shape),
        ],
        out_specs=pl.BlockSpec((rows, channels), by_rows),
        out_shape=jax.ShapeDtypeStruct((total, channels), f32),
        compiler_params=pltpu.CompilerParams(vmem_limit_bytes=VMEM_BYTES),
        cost_estimate=cost(1),
        name="modal_rows",
    )(*values, ids, weight)


def side_kernel(*refs):
    out, columns = refs[-1], refs[0].shape[1]
    for at, part in enumerate(refs[:-1]):
        out[:, at * columns : (at + 1) * columns] = part[...]


def side_by_side(*parts):
    rows, columns = parts[0].shape
    step = math.gcd(rows, 512)
    by_rows = lambda i: (i, 0)
    return pl.pallas_call(
        side_kernel,
        grid=(rows // step,),
        in_specs=[pl.BlockSpec((step, columns), by_rows)] * len(parts),
        out_specs=pl.BlockSpec((step, columns * len(parts)), by_rows),
        out_shape=jax.ShapeDtypeStruct((rows, columns * len(parts)), parts[0].dtype),
        cost_estimate=cost(1),
        name="side_by_side",
    )(*parts)


def gates_kernel(
    cot, ids_ref, blocks, pre, out, w_out, grad_scan, gate_wide, gated_wide, gate_low, gated_low
):
    @pl.when(pl.program_id(0) == 0)
    def _():
        arrange(blocks, 0, w_out)

    ids = ids_ref[...]
    here = pre[...]
    grad = modal_dot([cot], ids, w_out)
    sig = jax.nn.sigmoid(here)
    scanned = out[...]
    grad_scan[...] = grad * (here * sig)
    gate_grad = grad * scanned * (sig * (1.0 + here * (1.0 - sig)))
    gated = scanned * (here * sig)
    gate_low[...] = gate_grad.astype(bf16)
    gated_low[...] = gated.astype(bf16)
    put_masked(gate_wide, slice(None), ids, gate_grad)
    put_masked(gated_wide, slice(None), ids, gated)


def gates(cotangents, ids, blocks, pre, out):
    total, channels = out.shape
    width = cotangents.shape[1]
    rows = total // size_of(SEQ)
    by_rows = lambda i: (i, 0)
    block = pl.BlockSpec((rows, channels), by_rows)
    wide = pl.BlockSpec((rows, MODS * channels), by_rows)
    return pl.pallas_call(
        gates_kernel,
        grid=(total // rows,),
        in_specs=[
            pl.BlockSpec((rows, width), by_rows),
            pl.BlockSpec((rows, 1), by_rows),
            whole(blocks.shape),
            block,
            block,
        ],
        out_specs=[whole((width, MODS * channels)), block, wide, wide, block, block],
        out_shape=[
            jax.ShapeDtypeStruct((width, MODS * channels), bf16),
            jax.ShapeDtypeStruct((total, channels), f32),
            jax.ShapeDtypeStruct((total, MODS * channels), bf16),
            jax.ShapeDtypeStruct((total, MODS * channels), bf16),
            jax.ShapeDtypeStruct((total, channels), bf16),
            jax.ShapeDtypeStruct((total, channels), bf16),
        ],
        compiler_params=pltpu.CompilerParams(vmem_limit_bytes=VMEM_BYTES),
        cost_estimate=cost(1),
        name="gates",
    )(cotangents, ids, blocks, pre, out)


def spread_rates(rate_t, out):
    for group in range(rate_t.shape[0] // SUB):
        rows = rate_t[group * SUB : (group + 1) * SUB, :]
        for n in range(N):
            at = (group * N + n) * SUB
            out[at : at + SUB, :] = jnp.broadcast_to(rows[:, n : n + 1], (SUB, LANES))


def spread_mix(mixed, out, tau):
    spread = [jnp.broadcast_to(mixed[n : n + 1, :], (SUB, LANES)) for n in range(2 * N)]
    out[step_rows(tau, 2 * N * SUB), :] = jnp.concatenate(spread, axis=0)


def turned_rows(tau, length):
    return pl.ds(tau, LANES, stride=length)


def step_rows(tau, rows=LANES):
    return pl.ds(pl.multiple_of(tau * rows, rows), rows)


def over_segments(spent, ends, rates, backward):
    at = lax.broadcasted_iota(jnp.int32, (SUB, LANES), 1)
    ends = list(ends)
    reach = 1
    while reach < LANES:
        shift = LANES - reach if backward else reach
        inside = at < LANES - reach if backward else at >= reach
        for n in range(N):
            earlier = jnp.where(inside, pltpu.roll(ends[n], shift, 1), 0.0)
            ends[n] = ends[n] + jnp.exp(spent * rates[n]) * earlier
        spent = spent + jnp.where(inside, pltpu.roll(spent, shift, 1), 0.0)
        reach *= 2
    shift = LANES - 1 if backward else 1
    inside = at < LANES - 1 if backward else at >= 1
    return [jnp.where(inside, pltpu.roll(end, shift, 1), 0.0) for end in ends]


def row_of(at):
    return slice(at * SUB, (at + 1) * SUB)


def group_view(ref, first, count, group):
    start = pl.multiple_of(first * (count * LANES) + group * SUB, SUB)
    return ref.at[pl.ds(start, (count - 1) * LANES + SUB)]


def pieces_of(values, count):
    return [values[n * SUB : (n + 1) * SUB] for n in range(count)]


def scan_kernel(
    lengths,
    ids_ref,
    feats,
    pre,
    step_w,
    step_b,
    rate_t,
    skip,
    states,
    enter,
    step_pre,
    s_turn,
    u_turn,
    mix_rows,
    scan_out,
    s_flat,
    u_flat,
    mix_flat,
    y_turn,
    held,
    rates,
    mix_turn,
):
    chunk = pl.program_id(0)
    total, channels = pre.shape
    length = total // LANES
    steps = states.shape[0]
    groups = channels // SUB
    split = lengths[0]
    wide = N * SUB

    @pl.when(chunk == 0)
    def _():
        spread_rates(rate_t, rates)
        across = feats.shape[2]
        block_rows = feats.shape[4]
        for seq in range(2 * feats.shape[1]):
            for j in range(across):
                first = (seq * across + j) * block_rows
                block = pl.ds(first, block_rows)
                block_ids = ids_ref[block, :]
                low = feats[seq % 2, seq // 2, j, 0:R, :]
                stacked = dot(low, step_w[...], 0, 0) + step_b[...]
                here = pick(
                    block_ids, [stacked[:, m * channels : (m + 1) * channels] for m in range(MODS)]
                )
                step_pre[block, :] = here
                step = softplus(here)
                places = row_places(first, block_rows)
                start = (places == 0) | (places == split)
                s_flat[block, :] = jnp.where(start, FAR, step)
                u_flat[block, :] = step * silu(pre[block, :])
                mixed = feats[seq % 2, seq // 2, j, R : R + 2 * N, :].astype(f32)
                mixed = mixed + feats[seq % 2, seq // 2, j, R + 2 * N :, :].astype(f32)
                blank = jnp.zeros((LANES - 2 * N, block_rows), f32)
                mix_flat[block, :] = jnp.transpose(jnp.concatenate([mixed, blank], axis=0))

        def turn(tau, carried):
            rows = turned_rows(tau, length)
            s_turn[step_rows(tau), :] = jnp.transpose(s_flat[rows, :])
            u_turn[step_rows(tau), :] = jnp.transpose(u_flat[rows, :])
            mixed = jnp.transpose(mix_flat[rows, :])[: 2 * N]
            mix_rows[step_rows(tau, 2 * N), :] = mixed
            spread_mix(mixed, mix_turn, tau)
            return carried

        lax.fori_loop(0, length, turn, 0)

        def ahead(group, carried):
            rate = pieces_of(rates[step_rows(group, wide), :], N)

            def some(i, carried):
                hidden, spent = list(carried[0]), carried[1]
                s_here, u_here = [group_view(v, i, UNROLL, group) for v in (s_turn, u_turn)]
                mix_here = mix_turn.at[step_rows(i, UNROLL * 2 * wide)]
                for j in range(UNROLL):
                    s, u = s_here[row_of(j * groups), :], u_here[row_of(j * groups), :]
                    for n in range(N):
                        b = mix_here[row_of(j * 2 * N + n), :]
                        hidden[n] = jnp.exp(s * rate[n]) * hidden[n] + u * b
                    spent = spent + s
                return hidden, spent

            zero = jnp.zeros((SUB, LANES), f32)
            ends, spent = lax.fori_loop(0, length // UNROLL, some, ([zero] * N, zero))
            inside = jnp.concatenate(over_segments(spent, ends, rate, False), axis=0)
            held[step_rows(group, wide), :] = inside
            enter[step_rows(group, wide), :] = inside
            return carried

        lax.fori_loop(0, groups, ahead, 0)

    def advance(group, carried):
        own = step_rows(group, wide)
        rate = pieces_of(rates[own, :], N)
        hidden = pieces_of(held[own, :], N)
        s_here, u_here, y_here = [
            group_view(v, chunk, steps, group) for v in (s_turn, u_turn, y_turn)
        ]
        mix_here = mix_turn.at[step_rows(chunk, steps * 2 * wide)]
        for j in range(steps):
            s, u = s_here[row_of(j * groups), :], u_here[row_of(j * groups), :]
            out = states.at[j, own]
            terms = []
            for n in range(N):
                b = mix_here[row_of(j * 2 * N + n), :]
                hidden[n] = jnp.exp(s * rate[n]) * hidden[n] + u * b
                out[row_of(n), :] = hidden[n]
                terms.append(hidden[n] * mix_here[row_of(j * 2 * N + N + n), :])
            while len(terms) > 1:
                terms = [a + b for a, b in zip(terms[::2], terms[1::2])]
            y_here[row_of(j * groups), :] = terms[0]
        held[own, :] = jnp.concatenate(hidden, axis=0)
        return carried

    lax.fori_loop(0, groups, advance, 0)

    @pl.when(chunk == pl.num_programs(0) - 1)
    def _():
        def turn_back(tau, carried):
            s_flat[turned_rows(tau, length), :] = jnp.transpose(y_turn[step_rows(tau), :])
            return carried

        lax.fori_loop(0, length, turn_back, 0)
        for block in range(total // 512):
            rows = pl.ds(block * 512, 512)
            scan_out[rows, :] = s_flat[rows, :] + skip[...] * silu(pre[rows, :])


def scan(lengths, ids, feats, pre, step_w, step_b, rate_t, skip):
    total, channels = pre.shape
    length = total // LANES
    steps = math.gcd(length, STEPS)
    wide = N * channels
    flat = pltpu.VMEM((total, channels), f32)
    ins = (ids, feats, pre, step_w, step_b, rate_t, skip)
    shapes = [
        (wide, LANES),
        (total, channels),
        (length * channels, LANES),
        (length * channels, LANES),
        (length * 2 * N, LANES),
        (total, channels),
    ]
    return pl.pallas_call(
        scan_kernel,
        grid=(length // steps,),
        in_specs=[pl.BlockSpec(memory_space=pltpu.SMEM)] + [whole(a.shape) for a in ins],
        out_specs=[pl.BlockSpec((steps, wide, LANES), lambda i: (i, 0, 0))]
        + [whole(shape) for shape in shapes],
        out_shape=[jax.ShapeDtypeStruct((length, wide, LANES), f32)]
        + [jax.ShapeDtypeStruct(shape, f32) for shape in shapes],
        scratch_shapes=[flat, flat, flat, pltpu.VMEM((length * channels, LANES), f32)]
        + [pltpu.VMEM((wide, LANES), f32)] * 2
        + [pltpu.VMEM((length * 2 * N * SUB, LANES), f32)],
        compiler_params=pltpu.CompilerParams(vmem_limit_bytes=VMEM_BYTES),
        cost_estimate=cost(1),
        name="scan",
    )(lengths, *ins)


def back_kernel(
    core,
    ids_ref,
    ids_rows,
    s_turn,
    u_turn,
    mix_rows,
    pre,
    step_pre,
    grad,
    states,
    before,
    enter,
    step_w,
    rate_t,
    skip,
    act_part,
    step_grad_low,
    feat_part,
    sums,
    rate_out,
    g_turn,
    step_turn,
    in_turn,
    mix_grad,
    step_flat,
    in_flat,
    mix_flat,
    in_terms,
    out_terms,
    held,
    rate_sum,
    rates,
    mix_turn,
):
    turn_at = pl.program_id(0)
    chunks = pl.num_programs(0)
    chunk = chunks - 1 - turn_at
    total, channels = pre.shape
    length = total // LANES
    steps = states.shape[0]
    groups = channels // SUB
    wide = N * SUB

    @pl.when(turn_at == 0)
    def _():
        spread_rates(rate_t, rates)
        rate_sum[...] = jnp.zeros(rate_sum.shape, f32)

        def turn(tau, carried):
            g_turn[step_rows(tau), :] = jnp.transpose(grad[turned_rows(tau, length), :])
            spread_mix(mix_rows[step_rows(tau, 2 * N), :], mix_turn, tau)
            return carried

        lax.fori_loop(0, length, turn, 0)

        def ahead(group, carried):
            rate = pieces_of(rates[step_rows(group, wide), :], N)

            def some(i, carried):
                pulled, spent = list(carried[0]), carried[1]
                block = length // UNROLL - 1 - i
                s_here, g_here = [group_view(v, block, UNROLL, group) for v in (s_turn, g_turn)]
                mix_here = mix_turn.at[step_rows(block, UNROLL * 2 * wide)]
                for j in reversed(range(UNROLL)):
                    s, g = s_here[row_of(j * groups), :], g_here[row_of(j * groups), :]
                    for n in range(N):
                        c = mix_here[row_of(j * 2 * N + N + n), :]
                        pulled[n] = jnp.exp(s * rate[n]) * (pulled[n] + g * c)
                    spent = spent + s
                return pulled, spent

            zero = jnp.zeros((SUB, LANES), f32)
            ends, spent = lax.fori_loop(0, length // UNROLL, some, ([zero] * N, zero))
            inside = jnp.concatenate(over_segments(spent, ends, rate, True), axis=0)
            held[step_rows(group, wide), :] = inside
            return carried

        lax.fori_loop(0, groups, ahead, 0)

    in_terms[...] = jnp.zeros(in_terms.shape, f32)
    out_terms[...] = jnp.zeros(out_terms.shape, f32)

    def retreat(group, carried):
        own = step_rows(group, wide)
        views = [
            group_view(v, chunk, steps, group)
            for v in (s_turn, u_turn, g_turn, step_turn, in_turn)
        ]
        s, u, g = [[view[row_of(j * groups), :] for j in range(steps)] for view in views[:3]]
        mix_here = mix_turn.at[step_rows(chunk, steps * 2 * wide)]
        states_here = [states.at[j, own] for j in range(steps)]
        enter_here, before_here = enter.at[own], before.at[0, own]
        rate_here, held_here, sum_here = rates.at[own], held.at[own], rate_sum.at[own]
        step_sum, in_sum = [0.0] * steps, [0.0] * steps
        for n in range(N):
            at = row_of(n)
            rate, pull, rate_acc = rate_here[at, :], held_here[at, :], sum_here[at, :]
            first = jnp.where(chunk == 0, enter_here[at, :], before_here[at, :])
            state = [first] + [view[at, :] for view in states_here]
            for j in reversed(range(steps)):
                term = row_of(j * N + n)
                grad_state = g[j] * mix_here[row_of(j * 2 * N + N + n), :] + pull
                pull = jnp.exp(s[j] * rate) * grad_state
                mult = pull * state[j]
                step_sum[j] = step_sum[j] + mult * rate
                rate_acc = rate_acc + mult * s[j]
                in_sum[j] = in_sum[j] + grad_state * mix_here[row_of(j * 2 * N + n), :]
                in_terms[term, :] += grad_state * u[j]
                out_terms[term, :] += state[j + 1] * g[j]
            held_here[at, :] = pull
            sum_here[at, :] = rate_acc
        for j in range(steps):
            views[3][row_of(j * groups), :] = step_sum[j]
            views[4][row_of(j * groups), :] = in_sum[j]
        return carried

    lax.fori_loop(0, groups, retreat, 0)
    for j in range(steps):
        rows = []
        for terms in (in_terms, out_terms):
            for n in range(N):
                at = (j * N + n) * SUB
                rows.append(jnp.sum(terms[at : at + SUB, :], axis=0, keepdims=True))
        mix_grad[step_rows(chunk * steps + j, 2 * N), :] = jnp.concatenate(rows, axis=0)

    @pl.when(turn_at == chunks - 1)
    def _():
        def turn_back(tau, carried):
            rows = turned_rows(tau, length)
            step_flat[rows, :] = jnp.transpose(step_turn[step_rows(tau), :])
            in_flat[rows, :] = jnp.transpose(in_turn[step_rows(tau), :])
            mixed = mix_grad[step_rows(tau, 2 * N), :]
            blank = jnp.zeros((LANES - 2 * N, LANES), f32)
            mix_flat[rows, :] = jnp.transpose(jnp.concatenate([mixed, blank], axis=0))
            return carried

        lax.fori_loop(0, length, turn_back, 0)
        sums[...] = jnp.zeros(sums.shape, f32)
        across, block_rows = feat_part.shape[2], feat_part.shape[4]
        for seq in range(2 * feat_part.shape[1]):
            rows = pl.ds(seq * across * block_rows, across * block_rows)
            ids = ids_ref[rows, :]
            act = silu(pre[rows, :])
            step_in = step_pre[rows, :]
            state_in = in_flat[rows, :]
            grad_here = grad[rows, :]
            step_grad = step_flat[rows, :] + state_in * act
            pre_grad = step_grad * jax.nn.sigmoid(step_in)
            low = pre_grad.astype(bf16)
            step_grad_low[rows, :] = low
            act_part[rows, :] = grad_here * skip[...] + state_in * softplus(step_in)
            ours = jnp.where(core[0] == seq % 2, 1, 0)
            for j in range(across):
                block = seq * across + j
                block_low = low[j * block_rows : (j + 1) * block_rows]
                feat_part[ours, seq // 2, j, 0:R, :] = modal_rows_of(
                    step_w[...], block_low, ids_rows[block : block + 1, :]
                )
                turned = jnp.transpose(mix_flat[pl.ds(block * block_rows, block_rows), :])
                feat_part[ours, seq // 2, j, R : R + 2 * N, :] = turned[: 2 * N]
            for m in range(MODS):
                sums[m : m + 1, :] += jnp.sum(
                    jnp.where(ids == m, pre_grad, 0.0), axis=0, keepdims=True
                )
            sums[MODS : MODS + 1, :] += jnp.sum(grad_here * act, axis=0, keepdims=True)
        lane_at = lax.broadcasted_iota(jnp.int32, (SUB, LANES), 1)
        for group in range(groups):
            found = jnp.zeros((SUB, LANES), f32)
            for n in range(N):
                at = (group * N + n) * SUB
                total_rate = jnp.sum(rate_sum[at : at + SUB, :], axis=1, keepdims=True)
                found = jnp.where(lane_at == n, total_rate, found)
            rate_out[group * SUB : (group + 1) * SUB, :] = found


def scan_back(
    core, ids, ids_rows, turned, pre, step_pre, grad, states, enter, step_w, rate_t, skip
):
    total, channels = pre.shape
    length = total // LANES
    steps = math.gcd(length, STEPS)
    chunks = length // steps
    wide = N * channels
    feats = (2, lax.axis_size("z"), lax.axis_size("mod"), R + 2 * N, ids_rows.shape[1])
    first = (ids, ids_rows) + turned + (pre, step_pre, grad)
    second = (enter, step_w, rate_t, skip)
    turn = pltpu.VMEM((length * channels, LANES), f32)
    flat = pltpu.VMEM((total, channels), f32)
    terms = pltpu.VMEM((steps * N * SUB, LANES), f32)
    states_row = pltpu.VMEM((wide, LANES), f32)
    return pl.pallas_call(
        back_kernel,
        grid=(chunks,),
        in_specs=[pl.BlockSpec(memory_space=pltpu.SMEM)]
        + [whole(a.shape) for a in first]
        + [
            pl.BlockSpec((steps, wide, LANES), lambda i: (chunks - 1 - i, 0, 0)),
            pl.BlockSpec(
                (1, wide, LANES), lambda i: (jnp.maximum((chunks - 1 - i) * steps - 1, 0), 0, 0)
            ),
        ]
        + [whole(a.shape) for a in second],
        out_specs=[
            whole((total, channels)),
            whole((total, channels)),
            whole(feats),
            whole((SUB, channels)),
            whole((channels, LANES)),
        ],
        out_shape=[
            jax.ShapeDtypeStruct((total, channels), f32),
            jax.ShapeDtypeStruct((total, channels), bf16),
            jax.ShapeDtypeStruct(feats, f32),
            jax.ShapeDtypeStruct((SUB, channels), f32),
            jax.ShapeDtypeStruct((channels, LANES), f32),
        ],
        scratch_shapes=[turn, turn, turn, pltpu.VMEM((length * 2 * N, LANES), f32)]
        + [flat, flat, flat, terms, terms, states_row, states_row, states_row]
        + [pltpu.VMEM((length * 2 * N * SUB, LANES), f32)],
        compiler_params=pltpu.CompilerParams(vmem_limit_bytes=VMEM_BYTES),
        cost_estimate=cost(1),
        name="scan_back",
    )(core, *first, states, states, *second)


def conv_back_kernel(
    seqs,
    lengths,
    ids_ref,
    feat_grad,
    act_part,
    pre,
    inner,
    taps,
    param_w,
    inner_wide,
    inner_low,
    sums,
    ext,
):
    total, channels = pre.shape
    rows = total // seqs
    split = lengths[0]
    ext[total : total + 8, :] = jnp.zeros((8, channels), f32)
    sums[...] = jnp.zeros(sums.shape, f32)

    def through_silu(i, carried):
        at = pl.ds(pl.multiple_of(i * rows, rows), rows)
        for j in range(feat_grad.shape[2]):
            block_rows = feat_grad.shape[4]
            block = pl.ds(pl.multiple_of(i * rows + j * block_rows, block_rows), block_rows)
            low = feat_grad[i % 2, i // 2, j]
            stacked = dot(low, param_w[...], 0, 0)
            ext[block, :] = pick(
                ids_ref[block, :], [stacked[:, m * channels : (m + 1) * channels] for m in range(MODS)]
            )
        act_grad = act_part[at, :] + ext[at, :]
        here = pre[at, :]
        sig = jax.nn.sigmoid(here)
        conv_grad = act_grad * (sig * (1.0 + here * (1.0 - sig)))
        ext[at, :] = conv_grad
        sums[KW : KW + 1, :] += jnp.sum(conv_grad, axis=0, keepdims=True)
        return carried

    lax.fori_loop(0, total // rows, through_silu, 0)

    for block in range(total // rows):
        first = block * rows
        at = pl.ds(first, rows)
        places = row_places(first, rows)
        here = inner[at, :]
        grad = jnp.zeros((rows, channels), f32)
        for tap in range(KW):
            lag = KW - 1 - tap
            kept = (places >= split) | (places + lag < split)
            later = jnp.where(kept, ext[pl.ds(first + lag, rows), :], 0.0)
            grad = grad + taps[tap : tap + 1, :] * later
            sums[tap : tap + 1, :] += jnp.sum(later * here, axis=0, keepdims=True)
        put_masked(inner_wide, at, ids_ref[at, :], grad)
        inner_low[at, :] = grad.astype(bf16)


def conv_back(seqs, lengths, ids, feat_grad, act_part, pre, inner, taps, param_w):
    total, channels = pre.shape
    ins = (ids, feat_grad, act_part, pre, inner, taps, param_w)
    vmem = pl.BlockSpec(memory_space=pltpu.VMEM)
    return pl.pallas_call(
        functools.partial(conv_back_kernel, seqs),
        in_specs=[pl.BlockSpec(memory_space=pltpu.SMEM)] + [vmem] * len(ins),
        out_specs=[vmem, vmem, vmem],
        out_shape=[
            jax.ShapeDtypeStruct((total, MODS * channels), bf16),
            jax.ShapeDtypeStruct((total, channels), bf16),
            jax.ShapeDtypeStruct((8, channels), f32),
        ],
        scratch_shapes=[pltpu.VMEM((total + 8, channels), f32)],
        compiler_params=pltpu.CompilerParams(vmem_limit_bytes=VMEM_BYTES),
        cost_estimate=cost(1),
        name="conv_back",
    )(lengths, *ins)


def flip(axis, bit):
    size = lax.axis_size(axis)
    return lambda value: lax.ppermute(value, axis, [(i, i ^ bit) for i in range(size)])


def taken(values, at, dim):
    return lax.dynamic_index_in_dim(values, at, dim, keepdims=False)


SEQ = ("z", "core")
SAME_CORE = ("z", "mod")


def size_of(axes):
    return math.prod(lax.axis_size(axis) for axis in axes)


def share(values, axes):
    size = size_of(axes)
    return lax.all_to_all(jnp.broadcast_to(values, (size,) + values.shape), axes, 0, 0)


def exchange(blocks, axes):
    return lax.all_to_all(blocks, axes, 0, 0)


def held_back(value, until):
    return lax.optimization_barrier((value, tuple(until)))[0] if until else value


def flip(axis, bit):
    size = lax.axis_size(axis)
    return lambda value: lax.ppermute(value, axis, [(i, i ^ bit) for i in range(size)])


def taken(values, at, dim):
    return lax.dynamic_index_in_dim(values, at, dim, keepdims=False)


def two(bit, mine, got):
    return jnp.where(bit == 0, jnp.stack([mine, got]), jnp.stack([got, mine]))


Z_HIGH, Z_LOW, CORE = ("z", 2), ("z", 1), ("core", 1)
Y, X = ("mod", 2), ("mod", 1)


def place_bit(place):
    axis, bit = place
    return lax.axis_index(axis) // bit % 2


def summed_features(feats, kind=f32):
    feats = (feats[1] + flip(*CORE)(feats[0])).astype(kind)
    feats = feats.reshape((-1,) + feats.shape[2:])
    return jnp.sum(exchange(feats, SAME_CORE).astype(f32), axis=0), feats


def shared_features(block, until=()):
    mine = share(block, SAME_CORE)
    every = two(place_bit(CORE), mine, flip(*CORE)(held_back(mine, until)))
    return every.reshape((2, lax.axis_size("z"), lax.axis_size("mod")) + block.shape)


def core_rows(values, which):
    blocks = values.reshape(lax.axis_size("z"), 2, -1, values.shape[1])
    return taken(blocks, which, 1).reshape(-1, values.shape[1])


def both_cores(low, ids_ours):
    core = place_bit(CORE)
    got = flip(*CORE)(core_rows(low, 1 - core))
    return [masked(core_rows(low, core), ids_ours), masked(got, ids_ours)]


def gathered_columns(shard, between):
    width = shard.shape[1] // COLUMNS
    lines, far = [], []
    for at in range(COLUMNS):
        part = shard[:, at * width : (at + 1) * width]
        far.append(flip(*Z_HIGH)(held_back(part, far[at - 1 : at] if at else ())))
        line = two(place_bit(Z_HIGH), part, far[at])
        given = held_back(line, lines[at - 1 : at] if at else ())
        lines.append(two(place_bit(Z_LOW), line, flip(*Z_LOW)(given)))
    until = between(lines[-1])
    pieces, arrived, halfway = [], [], []
    for at, line in enumerate(lines):
        near, next_ = (X, Y) if at % 2 == 0 else (Y, X)
        halfway.append(flip(*near)(held_back(line, halfway[at - 2 : at - 1] if at > 1 else ())))
        pair = two(place_bit(near), line, halfway[at])
        got = flip(*next_)(held_back(pair, until if at > 1 else ()))
        arrived.append(got)
        pieces += [pair, got, flip(*CORE)(pair), flip(*CORE)(got)]
    return pieces, arrived


def row_parts(left, right, count):
    width = right.shape[0] // count
    return [
        dot(left, right[at * width : (at + 1) * width], 1, 1)
        .astype(bf16)
        .reshape(2, 2, 2, 2, -1, width)
        for at in range(count)
    ]


class SummedRows:
    def __init__(self, parts):
        self.dims = [["zh", "zl", "y", "x"] for _ in parts]
        self.parts = [[part] for part in parts]

    def give(self, at, name, place):
        dim = self.dims[at].index(name)
        bit = place_bit(place)
        away = sum(taken(p, 1 - bit, dim).astype(f32) for p in self.parts[at]).astype(bf16)
        self.parts[at] = [taken(p, bit, dim) for p in self.parts[at]]
        self.dims[at].remove(name)
        return away

    def stage(self, names):
        places = {"x": X, "y": Y, "zl": Z_LOW, "zh": Z_HIGH}
        sent = []
        for at in range(len(self.parts)):
            name = names[at % 2]
            away = self.give(at, name, places[name])
            sent.append(away)
            self.parts[at].append(flip(*places[name])(away))
        return sent

    def merge(self):
        pairs = list(zip(self.parts[::2], self.parts[1::2]))
        self.parts = [
            [jnp.concatenate(both, axis=-1) for both in zip(even, odd)] for even, odd in pairs
        ]
        self.dims = self.dims[::2]

    def arrived(self):
        return [parts[-1] for parts in self.parts]

    def hold(self, until):
        for parts in self.parts:
            parts[-1] = held_back(parts[-1], until)

    def result(self):
        return jnp.concatenate([sum(p.astype(f32) for p in parts) for parts in self.parts], axis=1)


def masked(values, ids):
    return jnp.concatenate(
        [jnp.where(ids == m, values, jnp.zeros_like(values)) for m in range(MODS)], axis=1
    )


def channel_layout(
    tokens,
    modality,
    lengths,
    norm_gain,
    input_weight,
    param_weight,
    step_weight,
    step_bias,
    output_weight,
    conv_weight,
    conv_bias,
    decay_log,
    skip_gain,
    cotangent,
):
    seqs = size_of(SEQ)
    channels = conv_weight.shape[1]
    width = tokens.shape[1]
    features = param_weight.shape[2]
    slab = input_weight.shape[1]

    token_vals = tokens.astype(f32)
    inverse = lax.rsqrt(jnp.mean(token_vals * token_vals, axis=1, keepdims=True) + EPSILON)
    normal_rows = token_vals * inverse
    gain_vals = norm_gain.astype(f32)

    send_in = input_weight.reshape(MODS, slab, 2, seqs, channels)
    send_in = send_in.transpose(3, 2, 0, 1, 4).reshape(seqs, 2 * MODS * slab, channels)
    id_rows = 16
    send_ids = jnp.pad(modality.astype(bf16), (0, id_rows * channels - modality.shape[0]))
    send_ids = jnp.broadcast_to(send_ids.reshape(id_rows, channels), (seqs, id_rows, channels))
    send_in = jnp.concatenate([send_in, send_ids], axis=1)
    made = []

    def send(line):
        made.append(exchange(held_back(send_in, [line]), SEQ))
        return made

    pieces, arrived = gathered_columns((normal_rows * gain_vals[None, :]).astype(bf16), send)
    inner_blocks = made[0]
    ids = inner_blocks[:, 2 * MODS * slab :].reshape(seqs, -1)[:, : modality.shape[0]].astype(jnp.int32)
    ids_rows = ids.reshape(-1, tokens.shape[0])
    ids = ids.reshape(-1, 1)
    send_out = output_weight.reshape(MODS, seqs, channels, slab).transpose(1, 0, 3, 2)
    send_out = send_out.reshape(seqs, MODS * slab, channels)
    param_rows = param_weight.transpose(0, 2, 1).reshape(MODS * features, channels)
    param_columns = param_weight.transpose(2, 0, 1).reshape(features, MODS * channels)
    step_rows_w = step_weight.reshape(MODS * R, channels)
    step_columns = step_weight.transpose(1, 0, 2).reshape(R, MODS * channels)
    core = place_bit(CORE)
    place = jnp.stack([place_bit(at) for at in (CORE, Y, X)]).astype(jnp.int32)
    taps = conv_weight.astype(f32)
    skip = skip_gain.astype(f32)[None, :]
    decay_rate = -jnp.exp(decay_log.astype(f32))
    rate_t = jnp.pad(decay_rate.T, ((0, 0), (0, LANES - N)))

    *normed, own_inner, own_gate, inner, conv_pre, act_low, feats = project(
        lengths,
        place,
        pieces,
        ids,
        ids_rows,
        inner_blocks,
        taps,
        conv_bias.astype(f32)[None, :],
        param_rows,
    )
    cotangents = lax.all_gather(
        held_back(cotangent, [inner]), SEQ + ("mod",), axis=0, tiled=True
    )
    feats, sent = summed_features(feats)
    gate_pre = modal_rows(normed, held_back(ids, [sent]), own_gate)
    pair_in = side_by_side(own_inner, flip(*CORE)(own_inner), own_gate, flip(*CORE)(own_gate))
    feats = held_back(feats, [gate_pre, pair_in])
    mix_high = feats[R:].astype(bf16)
    mix_rest = (feats[R:] - mix_high.astype(f32)).astype(bf16)
    feats = jnp.concatenate([feats[:R].astype(bf16), mix_high, mix_rest], axis=0)
    feats = shared_features(feats)

    out_blocks = exchange(held_back(send_out, [feats]), SEQ)
    states, enter, step_pre, *turned, scan_out = scan(
        lengths,
        ids,
        feats,
        conv_pre,
        step_columns,
        step_bias.astype(f32).reshape(1, MODS * channels),
        rate_t,
        skip,
    )
    out_blocks, scan_out = lax.optimization_barrier((out_blocks, scan_out))
    own_out, grad_scan, gate_wide, gated_wide, gate_rows, gated_rows = gates(
        cotangents, ids, out_blocks, gate_pre, scan_out
    )

    def token_sums(wide, weight):
        lows, gains = [], []
        for at, part in enumerate(normed):
            rows = part.shape[1]
            grad = dot(part, wide, 0, 0)
            lows.append(grad.astype(bf16))
            gains.append(jnp.sum(grad * weight[at * rows : (at + 1) * rows].astype(f32), axis=1))
        return jnp.concatenate(lows, axis=0), jnp.concatenate(gains, axis=0)

    def by_holder(low):
        return low.reshape(seqs, slab, MODS * channels)

    ids_ours = core_rows(ids, core)
    gated_both = jnp.concatenate(both_cores(gated_rows, ids_ours), axis=1)
    pair_out = side_by_side(own_out, flip(*CORE)(own_out))
    branch = SummedRows(row_parts(gated_both, pair_out, 2))
    branch_sent = branch.stage(("x", "y"))
    grad_scan = held_back(grad_scan, branch_sent)

    act_part, step_grad_low, feat_grad, sums, rate_sum = scan_back(
        place,
        ids,
        ids_rows,
        tuple(turned),
        conv_pre,
        step_pre,
        grad_scan,
        states,
        enter,
        step_rows_w,
        rate_t,
        skip,
    )
    feat_grad = held_back(feat_grad, branch.arrived())
    gate_rows, gate_wide, gated_wide = held_back((gate_rows, gate_wide, gated_wide), [feat_grad])
    gate_both = both_cores(gate_rows, ids_ours)
    feat_grad, sent = summed_features(feat_grad, bf16)
    feat_grad = held_back(feat_grad.astype(bf16), branch.stage(("y", "x")))
    gate_wide, gated_wide = held_back((gate_wide, gated_wide), [sent])
    gate_low, gate_gain = token_sums(gate_wide, own_gate)
    out_low = dot(cotangents, gated_wide, 0, 0).astype(bf16)
    more_low = jnp.concatenate([by_holder(gate_low), by_holder(out_low)], axis=2)
    feat_grad = shared_features(feat_grad, [more_low])
    more_low = exchange(held_back(more_low, [feat_grad]), SEQ)
    branch.hold([feat_grad])
    branch.merge()

    inner_wide, inner_rows, tap_sums = conv_back(
        seqs,
        lengths,
        ids,
        feat_grad,
        act_part,
        conv_pre,
        inner,
        taps,
        param_columns,
    )
    both_wide = jnp.concatenate(both_cores(inner_rows, ids_ours) + gate_both, axis=1)
    products = row_parts(both_wide, pair_in, COLUMNS)
    normed_sums = SummedRows(products)
    sent = normed_sums.stage(("x", "y"))
    branch.hold(sent)
    branch.stage(("zl", "zl"))
    inner_low, inner_gain = token_sums(held_back(inner_wide, sent), own_inner)
    gain_sum, more_low = lax.optimization_barrier((inner_gain + gate_gain, more_low))
    gain_sum = jnp.sum(share(gain_sum, SEQ + ("mod",)), axis=0)
    inner_low, gain_sum = lax.optimization_barrier((by_holder(inner_low), gain_sum))
    grad_gain = gain_sum / gain_vals
    inner_low = exchange(inner_low, SEQ).reshape(seqs, slab, MODS, channels)
    more_low = more_low.reshape(seqs, slab, 2, MODS, channels)
    grad_gate = more_low[:, :, 0].transpose(2, 1, 0, 3)
    grad_out = more_low[:, :, 1].transpose(2, 0, 3, 1)
    grad_out = grad_out.reshape(MODS, seqs * channels, slab).astype(f32)
    step_grad_low, feat_late = held_back((step_grad_low, feat_grad), sent)
    sent = normed_sums.stage(("y", "x"))
    branch.hold(sent)
    branch.stage(("zh", "zh"))
    output = (token_vals + branch.result()).astype(bf16)
    grad_in = jnp.stack([inner_low.transpose(2, 1, 0, 3), grad_gate], axis=2)
    grad_in = grad_in.reshape(MODS, slab, 2, seqs * channels).astype(f32)
    normed_sums.merge()
    normed_sums.stage(("zl", "zl"))
    normed_sums.hold([grad_in])
    normed_sums.stage(("zh", "zh"))
    normed_grad = normed_sums.result()
    step_t = feats[:, :, :, :R].transpose(3, 1, 0, 2, 4).reshape(R, -1)
    grad_step = dot(step_t, masked(step_grad_low, ids))
    grad_step = grad_step.reshape(R, MODS, channels).transpose(1, 0, 2)
    feat_late = feat_late.transpose(3, 1, 0, 2, 4).reshape(features, -1)
    feat_late = [
        jnp.where(ids_rows.reshape(1, -1) == m, feat_late, jnp.zeros_like(feat_late))
        for m in range(MODS)
    ]
    grad_param = dot(jnp.concatenate(feat_late, axis=0), act_low)
    grad_param = grad_param.reshape(MODS, features, channels).transpose(0, 2, 1)
    hat_grad = normed_grad * gain_vals[None, :]
    token_grad = cotangent.astype(f32) + inverse * (
        hat_grad - normal_rows * jnp.mean(hat_grad * normal_rows, axis=1, keepdims=True)
    )
    return (
        output,
        token_grad,
        grad_gain,
        grad_in,
        grad_param,
        grad_step,
        grad_out,
        tap_sums[:KW],
        tap_sums[KW],
        rate_sum[:, :N].T * decay_rate,
        sums[MODS],
        sums[:MODS],
    )


def placed(spec, axes):
    entries = [
        sum((axes[name] for name in ((entry,) if isinstance(entry, str) else entry or ())), ())
        for entry in spec
    ]
    return P(*[entry or None for entry in entries])


def solution(mesh):
    token_rows = P(("seq", "mod"), None)
    in_weight = P(None, "seq", None, "mod")
    out_weight = P(None, "mod", "seq")
    row, column, depth = P(("mod", "seq")), P(None, ("mod", "seq")), P(None, None, ("mod", "seq"))
    middle = P(None, ("mod", "seq"), None)
    ins = (token_rows, P("seq"), P(), P(), in_weight, middle, depth, column, out_weight)
    ins += (column, row, column, row, token_rows)
    outs = (token_rows, token_rows, P(), in_weight, middle, depth, out_weight)
    outs += (column, row, column, row, column)

    def run(*args):
        sizes = (mesh.shape["seq"], mesh.shape["mod"])
        share_of_channels = args[12].shape[0] // (sizes[0] * sizes[1])
        if share_of_channels == LANES and sizes == (8, 4):
            part, over = channel_layout, jax.sharding.Mesh(
                mesh.devices.reshape(sizes[0] // 2, 2, sizes[1]), ("z", "core", "mod")
            )
            axes = {"seq": SEQ, "mod": ("mod",)}
        else:
            part, over = local, mesh
            axes = {"seq": ("seq",), "mod": ("mod",)}
        return jax.shard_map(
            part,
            mesh=over,
            in_specs=tuple(placed(spec, axes) for spec in ins),
            out_specs=tuple(placed(spec, axes) for spec in outs),
            check_vma=False,
        )(*args)

    return run
```

```python
import functools
import math

import jax
import jax.numpy as jnp
from jax import lax
from jax.experimental import pallas as pl
from jax.experimental.pallas import tpu as pltpu
from jax.sharding import PartitionSpec as P

N = 16
KW = 4
R = 128
MODS = 3
TOK_DEV = 128
CAPD = 48


EPSILON = 1e-05
SCAN_ROWS = 512

LANES = 128
SUB = 8
STEPS = 4
UNROLL = 4
COLUMNS = 4
FAR = 1e9
VMEM_BYTES = 60 * 1024 * 1024
f32 = jnp.float32
bf16 = jnp.bfloat16


def shifted_2(value, axis, by):
    size = lax.axis_size(axis)
    pairs = [(i, i + by) for i in range(size) if 0 <= i + by < size]
    return lax.ppermute(value, axis, pairs)


def carried_in(value, axis, combine, identity):
    size, here = (lax.axis_size(axis), lax.axis_index(axis))
    everything = jax.tree.map(
        lambda part, kind: lax.all_gather(part.astype(kind), axis),
        value,
        (jnp.bfloat16, jnp.bfloat16),
    )
    start = jax.tree.map(
        lambda part, zero: jnp.broadcast_to(jnp.asarray(zero, part.dtype), part.shape),
        value,
        identity,
    )

    def carried_hop(k, before):
        reached = k < here
        new = combine(
            before, jax.tree.map(lambda part, own: part[k].astype(own.dtype), everything, value)
        )
        return jax.tree.map(lambda a, b: jnp.where(reached, a, b), new, before)

    return lax.fori_loop(0, size, carried_hop, start)


def prefix(value, axis, combine, identity):
    size, here = (lax.axis_size(axis), lax.axis_index(axis))
    everything = jax.tree.map(lambda part: lax.all_gather(part, axis), value)
    start = jax.tree.map(
        lambda part, zero: jnp.broadcast_to(jnp.asarray(zero, part.dtype), part.shape),
        value,
        identity,
    )

    def prefix_hop(k, before):
        at = size - 1 - k
        reached = at > here
        new = combine(before, jax.tree.map(lambda part: part[at], everything))
        return jax.tree.map(lambda a, b: jnp.where(reached, a, b), new, before)

    return lax.fori_loop(0, size, prefix_hop, start)


def split_rows(count_rows):
    return (count_rows // TOK_DEV, TOK_DEV)


def slot_tables(modal_ids, capacity):
    sub_rows = modal_ids.shape[1]
    marked = (modal_ids[:, :, None] == jnp.arange(MODS, dtype=jnp.int32)[None, None, :]).astype(
        jnp.int32
    )
    ranking = jnp.sum((jnp.cumsum(marked, axis=1) - 1) * marked, axis=2)
    slot_ids = modal_ids * capacity + ranking
    positions = jnp.broadcast_to(jnp.arange(sub_rows, dtype=jnp.int32)[None, :], modal_ids.shape)
    unfilled = jnp.full((modal_ids.shape[0], MODS * capacity), sub_rows, jnp.int32)
    tables = jax.vmap(lambda table_row, slot_row, place_row: table_row.at[slot_row].set(place_row))(
        unfilled, slot_ids, positions
    )
    return (tables, slot_ids)


def group_rows(values, tables, capacity):
    padded = jnp.concatenate([values, jnp.zeros_like(values[:, :1])], axis=1)
    picked = jax.vmap(lambda block_values, block_table: block_values[block_table])(padded, tables)
    return picked.reshape(values.shape[0], MODS, capacity, values.shape[2])


def ungroup_rows(grouped, slot_ids):
    flattened = grouped.reshape(grouped.shape[0], MODS * grouped.shape[2], grouped.shape[3])
    return jax.vmap(lambda block_values, block_slots: block_values[block_slots])(
        flattened, slot_ids
    )


def modal_product(values, modal_ids, weight, transpose):
    count_rows = values.shape[0]
    sub_count, sub_rows = split_rows(count_rows)
    capacity = min(CAPD, sub_rows)
    tables, slot_ids = slot_tables(modal_ids.reshape(sub_count, sub_rows), capacity)
    grouped = group_rows(values.reshape(sub_count, sub_rows, values.shape[1]), tables, capacity)
    if transpose:
        result = jnp.einsum("gmcn,mkn->gmck", grouped, weight, preferred_element_type=jnp.float32)
    else:
        result = jnp.einsum("gmck,mkn->gmcn", grouped, weight, preferred_element_type=jnp.float32)
    return ungroup_rows(result, slot_ids).reshape(count_rows, result.shape[3])


def modal_outer(left, right, modal_ids):
    count_rows = left.shape[0]
    sub_count, sub_rows = split_rows(count_rows)
    capacity = min(CAPD, sub_rows)
    tables, slot_ids = slot_tables(modal_ids.reshape(sub_count, sub_rows), capacity)
    left_grouped = group_rows(left.reshape(sub_count, sub_rows, left.shape[1]), tables, capacity)
    right_grouped = group_rows(right.reshape(sub_count, sub_rows, right.shape[1]), tables, capacity)
    return jnp.einsum(
        "gmcl,gmcr->mlr", left_grouped, right_grouped, preferred_element_type=jnp.float32
    )


def modal_table(table, modal_ids):
    picked = jnp.zeros((modal_ids.shape[0], table.shape[1]), jnp.float32)
    for modal_index in range(MODS):
        picked = (
            picked
            + (modal_ids == modal_index).astype(jnp.float32)[:, None] * table[modal_index][None, :]
        )
    return picked


def modal_sums(values, modal_ids):
    return jnp.stack(
        [
            jnp.sum(values * (modal_ids == modal_index).astype(jnp.float32)[:, None], axis=0)
            for modal_index in range(MODS)
        ]
    )


def pair_combine(earlier, later):
    return (earlier[0] * later[0], later[0] * earlier[1] + later[1])


def back_combine(earlier, later):
    return (earlier[0] * later[0], later[1] + later[0] * earlier[1])


def silu_slope(values):
    sigmoid_part = jax.nn.sigmoid(values)
    return sigmoid_part * (1.0 + values * (1.0 - sigmoid_part))


def local(
    tokens,
    modality,
    lengths,
    norm_gain,
    input_weight,
    param_weight,
    step_weight,
    step_bias,
    output_weight,
    conv_weight,
    conv_bias,
    decay_log,
    skip_gain,
    cotangent,
):
    block_rows = modality.shape[0]
    gathered = (
        lax.all_gather(input_weight, "seq", axis=1, tiled=True),
        lax.all_gather(param_weight, "seq", axis=1, tiled=True),
        lax.all_gather(step_weight, "seq", axis=2, tiled=True),
        lax.all_gather(output_weight, "seq", axis=2, tiled=True),
        lax.all_gather(conv_weight, "seq", axis=1, tiled=True),
        lax.all_gather(conv_bias, "seq", axis=0, tiled=True),
        lax.all_gather(decay_log, "seq", axis=1, tiled=True),
        lax.all_gather(skip_gain, "seq", axis=0, tiled=True),
        lax.all_gather(step_bias, "seq", axis=1, tiled=True),
    )
    in_local = gathered[0]
    param_local = gathered[1]
    step_local = gathered[2]
    out_local = gathered[3]
    tap_weights = gathered[4].astype(jnp.float32)
    tap_bias = gathered[5].astype(jnp.float32)
    decay_rate = -jnp.exp(gathered[6].astype(jnp.float32))
    skip_local = gathered[7].astype(jnp.float32)
    bias_local = gathered[8].astype(jnp.float32)
    channels = in_local.shape[3]
    model_width = in_local.shape[1]
    in_flat = in_local.reshape(MODS, model_width, 2 * channels)
    token_vals = tokens.astype(jnp.float32)
    inverse = lax.rsqrt(jnp.mean(token_vals * token_vals, axis=1, keepdims=True) + EPSILON)
    normal_rows = token_vals * inverse
    gain_vals = norm_gain.astype(jnp.float32)
    normed = (normal_rows * gain_vals[None, :]).astype(jnp.bfloat16)
    piece = lax.all_gather(normed, "mod", axis=0, tiled=True)
    piece_ids = modality
    product = modal_product(piece, piece_ids, in_flat, False)
    filled = product
    folded = (filled, piece)
    expanded = folded[0].reshape(block_rows, 2, channels)
    inner = expanded[:, 0]
    gate_pre = expanded[:, 1]
    first_place = lax.axis_index("seq") * block_rows
    places = first_place + jnp.arange(block_rows, dtype=jnp.int32)
    split_place = lengths[0]
    begins = jnp.where(places >= split_place, split_place, 0)
    keeping = (places != begins).astype(jnp.float32)
    inherit = (begins < first_place).astype(jnp.float32)
    halo_rows = shifted_2(inner[block_rows - KW + 1 :], "seq", 1)
    extended = jnp.concatenate([halo_rows, inner], axis=0)
    valid_taps = [
        (places - (KW - 1 - tap_index) >= begins).astype(jnp.float32)[:, None]
        for tap_index in range(KW)
    ]
    conv_pre = jnp.broadcast_to(tap_bias[None, :], inner.shape)
    for tap_index in range(KW):
        conv_pre = (
            conv_pre
            + tap_weights[tap_index][None, :]
            * extended[tap_index : tap_index + block_rows]
            * valid_taps[tap_index]
        )
    activated = jax.nn.silu(conv_pre)
    act_low = activated.astype(jnp.bfloat16)
    feature_part = modal_product(act_low, modality, param_local, False)
    features = lax.psum(feature_part, "mod")
    step_low = features[:, :R].astype(jnp.bfloat16)
    input_mix = features[:, R : R + N]
    output_mix = features[:, R + N :]
    step_pre = modal_product(step_low, modality, step_local, False) + modal_table(
        bias_local, modality
    )
    step_size = jax.nn.softplus(step_pre)
    scan_rows = math.gcd(block_rows, SCAN_ROWS)
    scan_count = block_rows // scan_rows

    def blocked(values):
        return values.reshape((scan_count, scan_rows) + values.shape[1:])

    def block_mult(keep_block, step_block):
        return keep_block[:, None, None] * jnp.exp(step_block[:, None, :] * decay_rate[None])

    def local_step(state_now, inputs):
        keep_block, step_block, act_block, input_block, output_block = inputs
        multiplier = block_mult(keep_block, step_block)
        addition = (step_block * act_block)[:, None, :] * input_block[:, :, None]
        running = lax.associative_scan(pair_combine, (multiplier, addition), axis=0)
        states = running[0] * state_now[None] + running[1]
        return (
            states[-1],
            (jnp.sum(output_block[:, :, None] * states, axis=1), state_now, running[0], running[1]),
        )

    scan_inputs = (
        blocked(keeping),
        blocked(step_size),
        blocked(activated),
        blocked(input_mix),
        blocked(output_mix),
    )
    end_state, (local_out, local_starts, run_mult, run_add) = lax.scan(
        local_step, jnp.zeros((N, channels), jnp.float32), scan_inputs
    )
    device_decay = jnp.exp(decay_rate * jnp.sum(step_size, axis=0)[None, :]) * jnp.min(keeping)
    chained = carried_in(
        (device_decay, end_state),
        "seq",
        pair_combine,
        (jnp.ones_like(device_decay), jnp.zeros_like(end_state)),
    )
    state_in = chained[1]

    def fix_step(carried, inputs):
        total_step, alive = carried
        inherit_block, step_block, output_block = inputs
        start_factor = alive * jnp.exp(decay_rate * total_step[None, :])
        running_step = total_step[None, :] + jnp.cumsum(step_block, axis=0)
        reach = inherit_block[:, None, None] * jnp.exp(running_step[:, None, :] * decay_rate[None])
        extra = jnp.sum(output_block[:, :, None] * reach * state_in[None], axis=1)
        return ((running_step[-1], inherit_block[-1]), (extra, start_factor))

    reach_inputs = (blocked(inherit), blocked(step_size), blocked(output_mix))
    _, (extra_out, start_factors) = lax.scan(
        fix_step, (jnp.zeros((channels,), jnp.float32), jnp.float32(1.0)), reach_inputs
    )
    start_states = local_starts + start_factors * state_in[None]
    scan_out = (local_out + extra_out).reshape(block_rows, channels) + skip_local[
        None, :
    ] * activated
    gate_act = jax.nn.silu(gate_pre)
    gated = (scan_out * gate_act).astype(jnp.bfloat16)
    piece = gated
    piece_ids = modality
    branch = lax.psum_scatter(
        modal_product(piece, piece_ids, out_local, False), "mod", scatter_dimension=0, tiled=True
    )
    output = (token_vals + branch).astype(jnp.bfloat16)
    back_rows = cotangent.astype(jnp.float32)
    piece = lax.all_gather(cotangent, "mod", axis=0, tiled=True)
    piece_ids = modality
    product = modal_product(piece, piece_ids, out_local, True)
    grad_out = modal_outer(gated, piece, piece_ids)
    grad_scan = product * gate_act
    grad_gate = product * scan_out * silu_slope(gate_pre)
    grad_skip = jnp.sum(grad_scan * activated, axis=0)
    grad_act = grad_scan * skip_local[None, :]

    def lead_step(carried, inputs):
        total_step, lead_sum = carried
        inherit_block, step_block, output_block, grad_block = inputs
        running_step = total_step[None, :] + jnp.cumsum(step_block, axis=0)
        reach = inherit_block[:, None, None] * jnp.exp(running_step[:, None, :] * decay_rate[None])
        lead_sum = lead_sum + jnp.sum(
            reach * output_block[:, :, None] * grad_block[:, None, :], axis=0
        )
        return ((running_step[-1], lead_sum), None)

    (_, lead_local), _ = lax.scan(
        lead_step,
        (jnp.zeros((channels,), jnp.float32), jnp.zeros((N, channels), jnp.float32)),
        reach_inputs + (blocked(grad_scan),),
    )
    incoming = prefix(
        (device_decay, lead_local),
        "seq",
        back_combine,
        (jnp.ones_like(device_decay), jnp.zeros_like(lead_local)),
    )[1]

    def back_step(carried, inputs):
        after_block, rate_grad = carried
        (
            keep_block,
            step_block,
            act_block,
            input_block,
            output_block,
            grad_block,
            start_state,
            mult_block,
            add_block,
        ) = inputs
        multiplier = block_mult(keep_block, step_block)
        states = mult_block * start_state[None] + add_block
        previous = jnp.concatenate([start_state[None], states[:-1]], axis=0)
        pushed = output_block[:, :, None] * grad_block[:, None, :]
        pushed = pushed.at[-1].add(after_block)
        shifted = jnp.concatenate([multiplier[1:], jnp.ones_like(multiplier[:1])], axis=0)
        flipped = lax.associative_scan(pair_combine, (shifted[::-1], pushed[::-1]), axis=0)
        grad_state = flipped[1][::-1]
        mult_grad = grad_state * previous * multiplier
        state_input = jnp.sum(grad_state * input_block[:, :, None], axis=1)
        step_grad = jnp.sum(mult_grad * decay_rate[None], axis=1) + state_input * act_block
        rate_grad = rate_grad + jnp.sum(mult_grad * step_block[:, None, :], axis=0)
        input_grad = jnp.sum(grad_state * (step_block * act_block)[:, None, :], axis=2)
        act_grad = state_input * step_block
        output_grad = jnp.sum(states * grad_block[:, None, :], axis=2)
        return (
            (multiplier[0] * grad_state[0], rate_grad),
            (step_grad, input_grad, act_grad, output_grad),
        )

    back_inputs = scan_inputs[:5] + (blocked(grad_scan), start_states, run_mult, run_add)
    (_, rate_total), (step_grads, input_grads, act_grads, output_grads) = lax.scan(
        back_step, (incoming, jnp.zeros((N, channels), jnp.float32)), back_inputs, reverse=True
    )
    step_pre_grad = step_grads.reshape(block_rows, channels) * jax.nn.sigmoid(step_pre)
    grad_bias = modal_sums(step_pre_grad, modality)
    step_grad_low = step_pre_grad.astype(jnp.bfloat16)
    step_in_part = modal_product(step_grad_low, modality, step_local, True)
    grad_step = modal_outer(step_low, step_grad_low, modality)
    summed = lax.psum(
        (step_in_part, input_grads.reshape(block_rows, N), output_grads.reshape(block_rows, N)),
        "mod",
    )
    feature_grad = jnp.concatenate(summed, axis=1).astype(jnp.bfloat16)
    grad_param = modal_outer(act_low, feature_grad, modality)
    act_total = (
        grad_act
        + act_grads.reshape(block_rows, channels)
        + modal_product(feature_grad, modality, param_local, True)
    )
    conv_grad = act_total * silu_slope(conv_pre)
    tap_grads = []
    ext_grad = jnp.zeros((block_rows + KW - 1, channels), jnp.float32)
    for tap_index in range(KW):
        masked = conv_grad * valid_taps[tap_index]
        tap_grads.append(jnp.sum(masked * extended[tap_index : tap_index + block_rows], axis=0))
        ext_grad = ext_grad.at[tap_index : tap_index + block_rows].add(
            masked * tap_weights[tap_index][None, :]
        )
    grad_taps = jnp.stack(tap_grads)
    grad_tap_bias = jnp.sum(conv_grad, axis=0)
    spill = shifted_2(ext_grad[: KW - 1], "seq", -1)
    inner_grad = ext_grad[KW - 1 :].at[block_rows - KW + 1 :].add(spill)
    both_grad = (
        jnp.stack([inner_grad, grad_gate], axis=1)
        .astype(jnp.bfloat16)
        .reshape(block_rows, 2 * channels)
    )
    piece = both_grad
    piece_ids = modality
    normed_grad = lax.psum_scatter(
        modal_product(piece, piece_ids, in_flat, True), "mod", scatter_dimension=0, tiled=True
    )
    grad_in = modal_outer(folded[1], both_grad, modality)
    gain_part = jnp.sum(normed_grad * normal_rows, axis=0)
    hat_grad = normed_grad * gain_vals[None, :]
    token_grad = back_rows + inverse * (
        hat_grad - normal_rows * jnp.mean(hat_grad * normal_rows, axis=1, keepdims=True)
    )
    grad_gain = lax.psum(gain_part, ("seq", "mod"))
    grad_decay = rate_total * decay_rate
    weight_grads = (
        lax.psum_scatter(
            grad_in.reshape(MODS, model_width, 2, channels), "seq", scatter_dimension=1, tiled=True
        ),
        lax.psum_scatter(grad_param, "seq", scatter_dimension=1, tiled=True),
        lax.psum_scatter(grad_step, "seq", scatter_dimension=2, tiled=True),
        lax.psum_scatter(grad_out, "seq", scatter_dimension=2, tiled=True),
        lax.psum_scatter(grad_taps, "seq", scatter_dimension=1, tiled=True),
        lax.psum_scatter(grad_tap_bias, "seq", scatter_dimension=0, tiled=True),
        lax.psum_scatter(grad_decay, "seq", scatter_dimension=1, tiled=True),
        lax.psum_scatter(grad_skip, "seq", scatter_dimension=0, tiled=True),
        lax.psum_scatter(grad_bias, "seq", scatter_dimension=1, tiled=True),
    )
    return (
        output,
        token_grad,
        grad_gain,
        weight_grads[0],
        weight_grads[1],
        weight_grads[2],
        weight_grads[3],
        weight_grads[4],
        weight_grads[5],
        weight_grads[6],
        weight_grads[7],
        weight_grads[8],
    )


def pick(ids, parts):
    return jnp.where(ids == 0, parts[0], jnp.where(ids == 1, parts[1], parts[2]))


def silu(values):
    return values * jax.nn.sigmoid(values)


def softplus(values):
    small = jnp.exp(-jnp.abs(values))
    series = small * (
        1.0 + small * (-1 / 2 + small * (1 / 3 + small * (-1 / 4 + small * (1 / 5 - small / 6))))
    )
    return jnp.maximum(values, 0.0) + jnp.where(small < 0.05, series, jnp.log(1.0 + small))


def dot(left, right, left_dim=1, right_dim=0):
    return lax.dot_general(
        left, right, (((left_dim,), (right_dim,)), ((), ())), preferred_element_type=f32
    )


def row_places(first, rows):
    return first + lax.broadcasted_iota(jnp.int32, (rows, 1), 0)


def whole(shape):
    return pl.BlockSpec(shape, lambda *_: (0,) * len(shape), pipeline_mode=pl.Buffered(1))


def cost(micros, flops=0):
    return pl.CostEstimate(flops=flops, bytes_accessed=int(micros * 3.69e6), transcendentals=0)


def modal_dot(values, ids, weight):
    part = values[0].shape[1]
    wide = sum(dot(v[...], weight[i * part : (i + 1) * part, :]) for i, v in enumerate(values))
    channels = wide.shape[1] // MODS
    return pick(ids, [wide[:, m * channels : (m + 1) * channels] for m in range(MODS)])


def modal_rows_of(weight, values, ids_row):
    stacked = dot(weight, values, 1, 1)
    height = stacked.shape[0] // MODS
    return pick(ids_row, [stacked[m * height : (m + 1) * height] for m in range(MODS)])


def put_masked(ref, rows, ids, values):
    channels = values.shape[1]
    for m in range(MODS):
        ref[rows, m * channels : (m + 1) * channels] = jnp.where(ids == m, values, 0.0).astype(
            ref.dtype
        )


def arrange(blocks, first, out):
    slab = out.shape[0] // blocks.shape[0]
    channels = blocks.shape[2]
    for at in range(blocks.shape[0]):
        for m in range(MODS):
            out[at * slab : (at + 1) * slab, m * channels : (m + 1) * channels] = blocks[
                at, (first + m) * slab : (first + m + 1) * slab, :
            ]


def project_kernel(lengths, place, *refs):
    pieces, refs = refs[: 4 * COLUMNS], refs[4 * COLUMNS :]
    ids_ref, ids_rows, blocks, taps, bias, param_t = refs[:6]
    xs, refs = refs[6 : 6 + COLUMNS], refs[6 + COLUMNS :]
    w, w_gate, inner_ref, pre_ref, low_ref, feats, ext = refs
    step = pl.program_id(0)

    @pl.when(step == 0)
    def _():
        arrange(blocks, 0, w)
        arrange(blocks, MODS, w_gate)

    block_rows = pieces[0].shape[3]
    for which in (0, 1):

        @pl.when((place[0] == step % 2) == (which == 0))
        def _():
            for at in range(COLUMNS):
                own_line, other_line = pieces[4 * at + 2 * which : 4 * at + 2 * which + 2]
                here = place[1] if at % 2 == 0 else place[2]
                for near in (0, 1):
                    for line, value in ((here, own_line), (1 - here, other_line)):
                        block = line * 2 + near if at % 2 == 0 else near * 2 + line
                        row = pl.multiple_of(block * block_rows, block_rows)
                        xs[at][pl.ds(row, block_rows), :] = value[near, 0, 0]

    rows = xs[0].shape[0]
    channels = inner_ref.shape[1]
    ids = ids_ref[...]
    inner = modal_dot(xs, ids, w)
    inner_ref[...] = inner

    @pl.when(step == 0)
    def _():
        ext[0:8, :] = jnp.zeros((8, channels), f32)

    @pl.when(step > 0)
    def _():
        ext[0:8, :] = ext[rows : rows + 8, :]

    ext[8 : 8 + rows, :] = inner
    places = row_places(step * rows, rows)
    split = lengths[0]
    begins = jnp.where(places >= split, split, 0)
    pre = jnp.broadcast_to(bias[...], (rows, channels))
    for tap in range(KW):
        lag = KW - 1 - tap
        shifted = ext[8 - lag : 8 - lag + rows, :]
        pre = pre + taps[tap : tap + 1, :] * jnp.where(places - lag >= begins, shifted, 0.0)
    pre_ref[...] = pre
    low = silu(pre).astype(bf16)
    low_ref[...] = low
    across = feats.shape[2]
    ours = jnp.where(place[0] == step % 2, 1, 0)
    for j in range(across):
        block = low[j * block_rows : (j + 1) * block_rows]
        feats[ours, step // 2, j] = modal_rows_of(
            param_t[...], block, ids_rows[pl.ds(step * across + j, 1), :]
        )


def project(lengths, place, pieces, ids, ids_rows, blocks, taps, bias, param_t):
    total = ids.shape[0]
    channels = taps.shape[1]
    chips, across = lax.axis_size("z"), lax.axis_size("mod")
    rows = total // (2 * chips)
    width = pieces[0].shape[4]
    by_rows = lambda i: (i, 0)
    feats = (2, chips, across, param_t.shape[0] // MODS, rows // across)
    smem = pl.BlockSpec(memory_space=pltpu.SMEM)
    return pl.pallas_call(
        project_kernel,
        grid=(total // rows,),
        in_specs=[
            smem,
            smem,
            *[
                pl.BlockSpec((2, 1, 1) + piece.shape[3:], lambda i: (0, i // 2 % 2, i // 4, 0, 0))
                for piece in pieces
            ],
            pl.BlockSpec((rows, 1), by_rows),
            whole(ids_rows.shape),
            whole(blocks.shape),
            whole(taps.shape),
            whole(bias.shape),
            whole(param_t.shape),
        ],
        out_specs=[pl.BlockSpec((rows, width), by_rows)] * COLUMNS
        + [whole((COLUMNS * width, MODS * channels))] * 2
        + [pl.BlockSpec((rows, channels), by_rows)] * 3
        + [whole(feats)],
        out_shape=[jax.ShapeDtypeStruct((total, width), bf16)] * COLUMNS
        + [jax.ShapeDtypeStruct((COLUMNS * width, MODS * channels), bf16)] * 2
        + [jax.ShapeDtypeStruct((total, channels), f32)] * 2
        + [jax.ShapeDtypeStruct((total, channels), bf16)]
        + [jax.ShapeDtypeStruct(feats, f32)],
        scratch_shapes=[pltpu.VMEM((rows + 8, channels), f32)],
        compiler_params=pltpu.CompilerParams(vmem_limit_bytes=VMEM_BYTES),
        cost_estimate=cost(1),
        name="project",
    )(lengths, place, *pieces, ids, ids_rows, blocks, taps, bias, param_t)


def modal_kernel(*refs):
    *xs, ids_ref, w, out = refs
    out[...] = modal_dot(xs, ids_ref[...], w)


def modal_rows(values, ids, weight):
    total = values[0].shape[0]
    channels = weight.shape[1] // MODS
    rows = math.gcd(total, 512)
    by_rows = lambda i: (i, 0)
    return pl.pallas_call(
        modal_kernel,
        grid=(total // rows,),
        in_specs=[
            *[pl.BlockSpec((rows, part.shape[1]), by_rows) for part in values],
            pl.BlockSpec((rows, 1), by_rows),
            whole(weight.shape),
        ],
        out_specs=pl.BlockSpec((rows, channels), by_rows),
        out_shape=jax.ShapeDtypeStruct((total, channels), f32),
        compiler_params=pltpu.CompilerParams(vmem_limit_bytes=VMEM_BYTES),
        cost_estimate=cost(1),
        name="modal_rows",
    )(*values, ids, weight)


def side_kernel(*refs):
    out, columns = refs[-1], refs[0].shape[1]
    for at, part in enumerate(refs[:-1]):
        out[:, at * columns : (at + 1) * columns] = part[...]


def side_by_side(*parts):
    rows, columns = parts[0].shape
    step = math.gcd(rows, 512)
    by_rows = lambda i: (i, 0)
    return pl.pallas_call(
        side_kernel,
        grid=(rows // step,),
        in_specs=[pl.BlockSpec((step, columns), by_rows)] * len(parts),
        out_specs=pl.BlockSpec((step, columns * len(parts)), by_rows),
        out_shape=jax.ShapeDtypeStruct((rows, columns * len(parts)), parts[0].dtype),
        cost_estimate=cost(1),
        name="side_by_side",
    )(*parts)


def gates_kernel(
    cot, ids_ref, blocks, pre, out, w_out, grad_scan, gate_wide, gated_wide, gate_low, gated_low
):
    @pl.when(pl.program_id(0) == 0)
    def _():
        arrange(blocks, 0, w_out)

    ids = ids_ref[...]
    here = pre[...]
    grad = modal_dot([cot], ids, w_out)
    sig = jax.nn.sigmoid(here)
    scanned = out[...]
    grad_scan[...] = grad * (here * sig)
    gate_grad = grad * scanned * (sig * (1.0 + here * (1.0 - sig)))
    gated = scanned * (here * sig)
    gate_low[...] = gate_grad.astype(bf16)
    gated_low[...] = gated.astype(bf16)
    put_masked(gate_wide, slice(None), ids, gate_grad)
    put_masked(gated_wide, slice(None), ids, gated)


def gates(cotangents, ids, blocks, pre, out):
    total, channels = out.shape
    width = cotangents.shape[1]
    rows = total // size_of(SEQ)
    by_rows = lambda i: (i, 0)
    block = pl.BlockSpec((rows, channels), by_rows)
    wide = pl.BlockSpec((rows, MODS * channels), by_rows)
    return pl.pallas_call(
        gates_kernel,
        grid=(total // rows,),
        in_specs=[
            pl.BlockSpec((rows, width), by_rows),
            pl.BlockSpec((rows, 1), by_rows),
            whole(blocks.shape),
            block,
            block,
        ],
        out_specs=[whole((width, MODS * channels)), block, wide, wide, block, block],
        out_shape=[
            jax.ShapeDtypeStruct((width, MODS * channels), bf16),
            jax.ShapeDtypeStruct((total, channels), f32),
            jax.ShapeDtypeStruct((total, MODS * channels), bf16),
            jax.ShapeDtypeStruct((total, MODS * channels), bf16),
            jax.ShapeDtypeStruct((total, channels), bf16),
            jax.ShapeDtypeStruct((total, channels), bf16),
        ],
        compiler_params=pltpu.CompilerParams(vmem_limit_bytes=VMEM_BYTES),
        cost_estimate=cost(1),
        name="gates",
    )(cotangents, ids, blocks, pre, out)


def spread_rates(rate_t, out):
    for group in range(rate_t.shape[0] // SUB):
        rows = rate_t[group * SUB : (group + 1) * SUB, :]
        for n in range(N):
            at = (group * N + n) * SUB
            out[at : at + SUB, :] = jnp.broadcast_to(rows[:, n : n + 1], (SUB, LANES))


def spread_mix(mixed, out, tau):
    spread = [jnp.broadcast_to(mixed[n : n + 1, :], (SUB, LANES)) for n in range(2 * N)]
    out[step_rows(tau, 2 * N * SUB), :] = jnp.concatenate(spread, axis=0)


def turned_rows(tau, length):
    return pl.ds(tau, LANES, stride=length)


def step_rows(tau, rows=LANES):
    return pl.ds(pl.multiple_of(tau * rows, rows), rows)


def over_segments(spent, ends, rates, backward):
    at = lax.broadcasted_iota(jnp.int32, (SUB, LANES), 1)
    ends = list(ends)
    reach = 1
    while reach < LANES:
        shift = LANES - reach if backward else reach
        inside = at < LANES - reach if backward else at >= reach
        for n in range(N):
            earlier = jnp.where(inside, pltpu.roll(ends[n], shift, 1), 0.0)
            ends[n] = ends[n] + jnp.exp(spent * rates[n]) * earlier
        spent = spent + jnp.where(inside, pltpu.roll(spent, shift, 1), 0.0)
        reach *= 2
    shift = LANES - 1 if backward else 1
    inside = at < LANES - 1 if backward else at >= 1
    return [jnp.where(inside, pltpu.roll(end, shift, 1), 0.0) for end in ends]


def row_of(at):
    return slice(at * SUB, (at + 1) * SUB)


def group_view(ref, first, count, group):
    start = pl.multiple_of(first * (count * LANES) + group * SUB, SUB)
    return ref.at[pl.ds(start, (count - 1) * LANES + SUB)]


def pieces_of(values, count):
    return [values[n * SUB : (n + 1) * SUB] for n in range(count)]


def scan_kernel(
    lengths,
    ids_ref,
    feats,
    pre,
    step_w,
    step_b,
    rate_t,
    skip,
    states,
    enter,
    step_pre,
    s_turn,
    u_turn,
    mix_rows,
    scan_out,
    s_flat,
    u_flat,
    mix_flat,
    y_turn,
    held,
    rates,
    mix_turn,
):
    chunk = pl.program_id(0)
    total, channels = pre.shape
    length = total // LANES
    steps = states.shape[0]
    groups = channels // SUB
    split = lengths[0]
    wide = N * SUB

    @pl.when(chunk == 0)
    def _():
        spread_rates(rate_t, rates)
        across = feats.shape[2]
        block_rows = feats.shape[4]
        for seq in range(2 * feats.shape[1]):
            for j in range(across):
                first = (seq * across + j) * block_rows
                block = pl.ds(first, block_rows)
                block_ids = ids_ref[block, :]
                low = feats[seq % 2, seq // 2, j, 0:R, :]
                stacked = dot(low, step_w[...], 0, 0) + step_b[...]
                here = pick(
                    block_ids, [stacked[:, m * channels : (m + 1) * channels] for m in range(MODS)]
                )
                step_pre[block, :] = here
                step = softplus(here)
                places = row_places(first, block_rows)
                start = (places == 0) | (places == split)
                s_flat[block, :] = jnp.where(start, FAR, step)
                u_flat[block, :] = step * silu(pre[block, :])
                mixed = feats[seq % 2, seq // 2, j, R : R + 2 * N, :].astype(f32)
                mixed = mixed + feats[seq % 2, seq // 2, j, R + 2 * N :, :].astype(f32)
                blank = jnp.zeros((LANES - 2 * N, block_rows), f32)
                mix_flat[block, :] = jnp.transpose(jnp.concatenate([mixed, blank], axis=0))

        def turn(tau, carried):
            rows = turned_rows(tau, length)
            s_turn[step_rows(tau), :] = jnp.transpose(s_flat[rows, :])
            u_turn[step_rows(tau), :] = jnp.transpose(u_flat[rows, :])
            mixed = jnp.transpose(mix_flat[rows, :])[: 2 * N]
            mix_rows[step_rows(tau, 2 * N), :] = mixed
            spread_mix(mixed, mix_turn, tau)
            return carried

        lax.fori_loop(0, length, turn, 0)

        def ahead(group, carried):
            rate = pieces_of(rates[step_rows(group, wide), :], N)

            def some(i, carried):
                hidden, spent = list(carried[0]), carried[1]
                s_here, u_here = [group_view(v, i, UNROLL, group) for v in (s_turn, u_turn)]
                mix_here = mix_turn.at[step_rows(i, UNROLL * 2 * wide)]
                for j in range(UNROLL):
                    s, u = s_here[row_of(j * groups), :], u_here[row_of(j * groups), :]
                    for n in range(N):
                        b = mix_here[row_of(j * 2 * N + n), :]
                        hidden[n] = jnp.exp(s * rate[n]) * hidden[n] + u * b
                    spent = spent + s
                return hidden, spent

            zero = jnp.zeros((SUB, LANES), f32)
            ends, spent = lax.fori_loop(0, length // UNROLL, some, ([zero] * N, zero))
            inside = jnp.concatenate(over_segments(spent, ends, rate, False), axis=0)
            held[step_rows(group, wide), :] = inside
            enter[step_rows(group, wide), :] = inside
            return carried

        lax.fori_loop(0, groups, ahead, 0)

    def advance(group, carried):
        own = step_rows(group, wide)
        rate = pieces_of(rates[own, :], N)
        hidden = pieces_of(held[own, :], N)
        s_here, u_here, y_here = [
            group_view(v, chunk, steps, group) for v in (s_turn, u_turn, y_turn)
        ]
        mix_here = mix_turn.at[step_rows(chunk, steps * 2 * wide)]
        for j in range(steps):
            s, u = s_here[row_of(j * groups), :], u_here[row_of(j * groups), :]
            out = states.at[j, own]
            terms = []
            for n in range(N):
                b = mix_here[row_of(j * 2 * N + n), :]
                hidden[n] = jnp.exp(s * rate[n]) * hidden[n] + u * b
                out[row_of(n), :] = hidden[n]
                terms.append(hidden[n] * mix_here[row_of(j * 2 * N + N + n), :])
            while len(terms) > 1:
                terms = [a + b for a, b in zip(terms[::2], terms[1::2])]
            y_here[row_of(j * groups), :] = terms[0]
        held[own, :] = jnp.concatenate(hidden, axis=0)
        return carried

    lax.fori_loop(0, groups, advance, 0)

    @pl.when(chunk == pl.num_programs(0) - 1)
    def _():
        def turn_back(tau, carried):
            s_flat[turned_rows(tau, length), :] = jnp.transpose(y_turn[step_rows(tau), :])
            return carried

        lax.fori_loop(0, length, turn_back, 0)
        for block in range(total // 512):
            rows = pl.ds(block * 512, 512)
            scan_out[rows, :] = s_flat[rows, :] + skip[...] * silu(pre[rows, :])


def scan(lengths, ids, feats, pre, step_w, step_b, rate_t, skip):
    total, channels = pre.shape
    length = total // LANES
    steps = math.gcd(length, STEPS)
    wide = N * channels
    flat = pltpu.VMEM((total, channels), f32)
    ins = (ids, feats, pre, step_w, step_b, rate_t, skip)
    shapes = [
        (wide, LANES),
        (total, channels),
        (length * channels, LANES),
        (length * channels, LANES),
        (length * 2 * N, LANES),
        (total, channels),
    ]
    return pl.pallas_call(
        scan_kernel,
        grid=(length // steps,),
        in_specs=[pl.BlockSpec(memory_space=pltpu.SMEM)] + [whole(a.shape) for a in ins],
        out_specs=[pl.BlockSpec((steps, wide, LANES), lambda i: (i, 0, 0))]
        + [whole(shape) for shape in shapes],
        out_shape=[jax.ShapeDtypeStruct((length, wide, LANES), f32)]
        + [jax.ShapeDtypeStruct(shape, f32) for shape in shapes],
        scratch_shapes=[flat, flat, flat, pltpu.VMEM((length * channels, LANES), f32)]
        + [pltpu.VMEM((wide, LANES), f32)] * 2
        + [pltpu.VMEM((length * 2 * N * SUB, LANES), f32)],
        compiler_params=pltpu.CompilerParams(vmem_limit_bytes=VMEM_BYTES),
        cost_estimate=cost(1),
        name="scan",
    )(lengths, *ins)


def back_kernel(
    core,
    ids_ref,
    ids_rows,
    s_turn,
    u_turn,
    mix_rows,
    pre,
    step_pre,
    grad,
    states,
    before,
    enter,
    step_w,
    rate_t,
    skip,
    act_part,
    step_grad_low,
    feat_part,
    sums,
    rate_out,
    g_turn,
    step_turn,
    in_turn,
    mix_grad,
    step_flat,
    in_flat,
    mix_flat,
    in_terms,
    out_terms,
    held,
    rate_sum,
    rates,
    mix_turn,
):
    turn_at = pl.program_id(0)
    chunks = pl.num_programs(0)
    chunk = chunks - 1 - turn_at
    total, channels = pre.shape
    length = total // LANES
    steps = states.shape[0]
    groups = channels // SUB
    wide = N * SUB

    @pl.when(turn_at == 0)
    def _():
        spread_rates(rate_t, rates)
        rate_sum[...] = jnp.zeros(rate_sum.shape, f32)

        def turn(tau, carried):
            g_turn[step_rows(tau), :] = jnp.transpose(grad[turned_rows(tau, length), :])
            spread_mix(mix_rows[step_rows(tau, 2 * N), :], mix_turn, tau)
            return carried

        lax.fori_loop(0, length, turn, 0)

        def ahead(group, carried):
            rate = pieces_of(rates[step_rows(group, wide), :], N)

            def some(i, carried):
                pulled, spent = list(carried[0]), carried[1]
                block = length // UNROLL - 1 - i
                s_here, g_here = [group_view(v, block, UNROLL, group) for v in (s_turn, g_turn)]
                mix_here = mix_turn.at[step_rows(block, UNROLL * 2 * wide)]
                for j in reversed(range(UNROLL)):
                    s, g = s_here[row_of(j * groups), :], g_here[row_of(j * groups), :]
                    for n in range(N):
                        c = mix_here[row_of(j * 2 * N + N + n), :]
                        pulled[n] = jnp.exp(s * rate[n]) * (pulled[n] + g * c)
                    spent = spent + s
                return pulled, spent

            zero = jnp.zeros((SUB, LANES), f32)
            ends, spent = lax.fori_loop(0, length // UNROLL, some, ([zero] * N, zero))
            inside = jnp.concatenate(over_segments(spent, ends, rate, True), axis=0)
            held[step_rows(group, wide), :] = inside
            return carried

        lax.fori_loop(0, groups, ahead, 0)

    in_terms[...] = jnp.zeros(in_terms.shape, f32)
    out_terms[...] = jnp.zeros(out_terms.shape, f32)

    def retreat(group, carried):
        own = step_rows(group, wide)
        views = [
            group_view(v, chunk, steps, group)
            for v in (s_turn, u_turn, g_turn, step_turn, in_turn)
        ]
        s, u, g = [[view[row_of(j * groups), :] for j in range(steps)] for view in views[:3]]
        mix_here = mix_turn.at[step_rows(chunk, steps * 2 * wide)]
        states_here = [states.at[j, own] for j in range(steps)]
        enter_here, before_here = enter.at[own], before.at[0, own]
        rate_here, held_here, sum_here = rates.at[own], held.at[own], rate_sum.at[own]
        step_sum, in_sum = [0.0] * steps, [0.0] * steps
        for n in range(N):
            at = row_of(n)
            rate, pull, rate_acc = rate_here[at, :], held_here[at, :], sum_here[at, :]
            first = jnp.where(chunk == 0, enter_here[at, :], before_here[at, :])
            state = [first] + [view[at, :] for view in states_here]
            for j in reversed(range(steps)):
                term = row_of(j * N + n)
                grad_state = g[j] * mix_here[row_of(j * 2 * N + N + n), :] + pull
                pull = jnp.exp(s[j] * rate) * grad_state
                mult = pull * state[j]
                step_sum[j] = step_sum[j] + mult * rate
                rate_acc = rate_acc + mult * s[j]
                in_sum[j] = in_sum[j] + grad_state * mix_here[row_of(j * 2 * N + n), :]
                in_terms[term, :] += grad_state * u[j]
                out_terms[term, :] += state[j + 1] * g[j]
            held_here[at, :] = pull
            sum_here[at, :] = rate_acc
        for j in range(steps):
            views[3][row_of(j * groups), :] = step_sum[j]
            views[4][row_of(j * groups), :] = in_sum[j]
        return carried

    lax.fori_loop(0, groups, retreat, 0)
    for j in range(steps):
        rows = []
        for terms in (in_terms, out_terms):
            for n in range(N):
                at = (j * N + n) * SUB
                rows.append(jnp.sum(terms[at : at + SUB, :], axis=0, keepdims=True))
        mix_grad[step_rows(chunk * steps + j, 2 * N), :] = jnp.concatenate(rows, axis=0)

    @pl.when(turn_at == chunks - 1)
    def _():
        def turn_back(tau, carried):
            rows = turned_rows(tau, length)
            step_flat[rows, :] = jnp.transpose(step_turn[step_rows(tau), :])
            in_flat[rows, :] = jnp.transpose(in_turn[step_rows(tau), :])
            mixed = mix_grad[step_rows(tau, 2 * N), :]
            blank = jnp.zeros((LANES - 2 * N, LANES), f32)
            mix_flat[rows, :] = jnp.transpose(jnp.concatenate([mixed, blank], axis=0))
            return carried

        lax.fori_loop(0, length, turn_back, 0)
        sums[...] = jnp.zeros(sums.shape, f32)
        across, block_rows = feat_part.shape[2], feat_part.shape[4]
        for seq in range(2 * feat_part.shape[1]):
            rows = pl.ds(seq * across * block_rows, across * block_rows)
            ids = ids_ref[rows, :]
            act = silu(pre[rows, :])
            step_in = step_pre[rows, :]
            state_in = in_flat[rows, :]
            grad_here = grad[rows, :]
            step_grad = step_flat[rows, :] + state_in * act
            pre_grad = step_grad * jax.nn.sigmoid(step_in)
            low = pre_grad.astype(bf16)
            step_grad_low[rows, :] = low
            act_part[rows, :] = grad_here * skip[...] + state_in * softplus(step_in)
            ours = jnp.where(core[0] == seq % 2, 1, 0)
            for j in range(across):
                block = seq * across + j
                block_low = low[j * block_rows : (j + 1) * block_rows]
                feat_part[ours, seq // 2, j, 0:R, :] = modal_rows_of(
                    step_w[...], block_low, ids_rows[block : block + 1, :]
                )
                turned = jnp.transpose(mix_flat[pl.ds(block * block_rows, block_rows), :])
                feat_part[ours, seq // 2, j, R : R + 2 * N, :] = turned[: 2 * N]
            for m in range(MODS):
                sums[m : m + 1, :] += jnp.sum(
                    jnp.where(ids == m, pre_grad, 0.0), axis=0, keepdims=True
                )
            sums[MODS : MODS + 1, :] += jnp.sum(grad_here * act, axis=0, keepdims=True)
        lane_at = lax.broadcasted_iota(jnp.int32, (SUB, LANES), 1)
        for group in range(groups):
            found = jnp.zeros((SUB, LANES), f32)
            for n in range(N):
                at = (group * N + n) * SUB
                total_rate = jnp.sum(rate_sum[at : at + SUB, :], axis=1, keepdims=True)
                found = jnp.where(lane_at == n, total_rate, found)
            rate_out[group * SUB : (group + 1) * SUB, :] = found


def scan_back(
    core, ids, ids_rows, turned, pre, step_pre, grad, states, enter, step_w, rate_t, skip
):
    total, channels = pre.shape
    length = total // LANES
    steps = math.gcd(length, STEPS)
    chunks = length // steps
    wide = N * channels
    feats = (2, lax.axis_size("z"), lax.axis_size("mod"), R + 2 * N, ids_rows.shape[1])
    first = (ids, ids_rows) + turned + (pre, step_pre, grad)
    second = (enter, step_w, rate_t, skip)
    turn = pltpu.VMEM((length * channels, LANES), f32)
    flat = pltpu.VMEM((total, channels), f32)
    terms = pltpu.VMEM((steps * N * SUB, LANES), f32)
    states_row = pltpu.VMEM((wide, LANES), f32)
    return pl.pallas_call(
        back_kernel,
        grid=(chunks,),
        in_specs=[pl.BlockSpec(memory_space=pltpu.SMEM)]
        + [whole(a.shape) for a in first]
        + [
            pl.BlockSpec((steps, wide, LANES), lambda i: (chunks - 1 - i, 0, 0)),
            pl.BlockSpec(
                (1, wide, LANES), lambda i: (jnp.maximum((chunks - 1 - i) * steps - 1, 0), 0, 0)
            ),
        ]
        + [whole(a.shape) for a in second],
        out_specs=[
            whole((total, channels)),
            whole((total, channels)),
            whole(feats),
            whole((SUB, channels)),
            whole((channels, LANES)),
        ],
        out_shape=[
            jax.ShapeDtypeStruct((total, channels), f32),
            jax.ShapeDtypeStruct((total, channels), bf16),
            jax.ShapeDtypeStruct(feats, f32),
            jax.ShapeDtypeStruct((SUB, channels), f32),
            jax.ShapeDtypeStruct((channels, LANES), f32),
        ],
        scratch_shapes=[turn, turn, turn, pltpu.VMEM((length * 2 * N, LANES), f32)]
        + [flat, flat, flat, terms, terms, states_row, states_row, states_row]
        + [pltpu.VMEM((length * 2 * N * SUB, LANES), f32)],
        compiler_params=pltpu.CompilerParams(vmem_limit_bytes=VMEM_BYTES),
        cost_estimate=cost(1),
        name="scan_back",
    )(core, *first, states, states, *second)


def conv_back_kernel(
    seqs,
    lengths,
    ids_ref,
    feat_grad,
    act_part,
    pre,
    inner,
    taps,
    param_w,
    inner_wide,
    inner_low,
    sums,
    ext,
):
    total, channels = pre.shape
    rows = total // seqs
    split = lengths[0]
    ext[total : total + 8, :] = jnp.zeros((8, channels), f32)
    sums[...] = jnp.zeros(sums.shape, f32)

    def through_silu(i, carried):
        at = pl.ds(pl.multiple_of(i * rows, rows), rows)
        for j in range(feat_grad.shape[2]):
            block_rows = feat_grad.shape[4]
            block = pl.ds(pl.multiple_of(i * rows + j * block_rows, block_rows), block_rows)
            low = feat_grad[i % 2, i // 2, j]
            stacked = dot(low, param_w[...], 0, 0)
            ext[block, :] = pick(
                ids_ref[block, :], [stacked[:, m * channels : (m + 1) * channels] for m in range(MODS)]
            )
        act_grad = act_part[at, :] + ext[at, :]
        here = pre[at, :]
        sig = jax.nn.sigmoid(here)
        conv_grad = act_grad * (sig * (1.0 + here * (1.0 - sig)))
        ext[at, :] = conv_grad
        sums[KW : KW + 1, :] += jnp.sum(conv_grad, axis=0, keepdims=True)
        return carried

    lax.fori_loop(0, total // rows, through_silu, 0)

    for block in range(total // rows):
        first = block * rows
        at = pl.ds(first, rows)
        places = row_places(first, rows)
        here = inner[at, :]
        grad = jnp.zeros((rows, channels), f32)
        for tap in range(KW):
            lag = KW - 1 - tap
            kept = (places >= split) | (places + lag < split)
            later = jnp.where(kept, ext[pl.ds(first + lag, rows), :], 0.0)
            grad = grad + taps[tap : tap + 1, :] * later
            sums[tap : tap + 1, :] += jnp.sum(later * here, axis=0, keepdims=True)
        put_masked(inner_wide, at, ids_ref[at, :], grad)
        inner_low[at, :] = grad.astype(bf16)


def conv_back(seqs, lengths, ids, feat_grad, act_part, pre, inner, taps, param_w):
    total, channels = pre.shape
    ins = (ids, feat_grad, act_part, pre, inner, taps, param_w)
    vmem = pl.BlockSpec(memory_space=pltpu.VMEM)
    return pl.pallas_call(
        functools.partial(conv_back_kernel, seqs),
        in_specs=[pl.BlockSpec(memory_space=pltpu.SMEM)] + [vmem] * len(ins),
        out_specs=[vmem, vmem, vmem],
        out_shape=[
            jax.ShapeDtypeStruct((total, MODS * channels), bf16),
            jax.ShapeDtypeStruct((total, channels), bf16),
            jax.ShapeDtypeStruct((8, channels), f32),
        ],
        scratch_shapes=[pltpu.VMEM((total + 8, channels), f32)],
        compiler_params=pltpu.CompilerParams(vmem_limit_bytes=VMEM_BYTES),
        cost_estimate=cost(1),
        name="conv_back",
    )(lengths, *ins)


def flip(axis, bit):
    size = lax.axis_size(axis)
    return lambda value: lax.ppermute(value, axis, [(i, i ^ bit) for i in range(size)])


def taken(values, at, dim):
    return lax.dynamic_index_in_dim(values, at, dim, keepdims=False)


SEQ = ("z", "core")
SAME_CORE = ("z", "mod")


def size_of(axes):
    return math.prod(lax.axis_size(axis) for axis in axes)


def share(values, axes):
    size = size_of(axes)
    return lax.all_to_all(jnp.broadcast_to(values, (size,) + values.shape), axes, 0, 0)


def exchange(blocks, axes):
    return lax.all_to_all(blocks, axes, 0, 0)


def held_back(value, until):
    return lax.optimization_barrier((value, tuple(until)))[0] if until else value


def flip(axis, bit):
    size = lax.axis_size(axis)
    return lambda value: lax.ppermute(value, axis, [(i, i ^ bit) for i in range(size)])


def taken(values, at, dim):
    return lax.dynamic_index_in_dim(values, at, dim, keepdims=False)


def two(bit, mine, got):
    return jnp.where(bit == 0, jnp.stack([mine, got]), jnp.stack([got, mine]))


Z_HIGH, Z_LOW, CORE = ("z", 2), ("z", 1), ("core", 1)
Y, X = ("mod", 2), ("mod", 1)


def place_bit(place):
    axis, bit = place
    return lax.axis_index(axis) // bit % 2


def summed_features(feats, kind=f32):
    feats = (feats[1] + flip(*CORE)(feats[0])).astype(kind)
    feats = feats.reshape((-1,) + feats.shape[2:])
    return jnp.sum(exchange(feats, SAME_CORE).astype(f32), axis=0), feats


def shared_features(block, until=()):
    mine = share(block, SAME_CORE)
    every = two(place_bit(CORE), mine, flip(*CORE)(held_back(mine, until)))
    return every.reshape((2, lax.axis_size("z"), lax.axis_size("mod")) + block.shape)


def core_rows(values, which):
    blocks = values.reshape(lax.axis_size("z"), 2, -1, values.shape[1])
    return taken(blocks, which, 1).reshape(-1, values.shape[1])


def both_cores(low, ids_ours):
    core = place_bit(CORE)
    got = flip(*CORE)(core_rows(low, 1 - core))
    return [masked(core_rows(low, core), ids_ours), masked(got, ids_ours)]


def gathered_columns(shard, between):
    width = shard.shape[1] // COLUMNS
    lines, far = [], []
    for at in range(COLUMNS):
        part = shard[:, at * width : (at + 1) * width]
        far.append(flip(*Z_HIGH)(held_back(part, far[at - 1 : at] if at else ())))
        line = two(place_bit(Z_HIGH), part, far[at])
        given = held_back(line, lines[at - 1 : at] if at else ())
        lines.append(two(place_bit(Z_LOW), line, flip(*Z_LOW)(given)))
    until = between(lines[-1])
    pieces, arrived, halfway = [], [], []
    for at, line in enumerate(lines):
        near, next_ = (X, Y) if at % 2 == 0 else (Y, X)
        halfway.append(flip(*near)(held_back(line, halfway[at - 2 : at - 1] if at > 1 else ())))
        pair = two(place_bit(near), line, halfway[at])
        got = flip(*next_)(held_back(pair, until if at > 1 else ()))
        arrived.append(got)
        pieces += [pair, got, flip(*CORE)(pair), flip(*CORE)(got)]
    return pieces, arrived


def row_parts(left, right, count):
    width = right.shape[0] // count
    return [
        dot(left, right[at * width : (at + 1) * width], 1, 1)
        .astype(bf16)
        .reshape(2, 2, 2, 2, -1, width)
        for at in range(count)
    ]


class SummedRows:
    def __init__(self, parts):
        self.dims = [["zh", "zl", "y", "x"] for _ in parts]
        self.parts = [[part] for part in parts]

    def give(self, at, name, place):
        dim = self.dims[at].index(name)
        bit = place_bit(place)
        away = sum(taken(p, 1 - bit, dim).astype(f32) for p in self.parts[at]).astype(bf16)
        self.parts[at] = [taken(p, bit, dim) for p in self.parts[at]]
        self.dims[at].remove(name)
        return away

    def stage(self, names):
        places = {"x": X, "y": Y, "zl": Z_LOW, "zh": Z_HIGH}
        sent = []
        for at in range(len(self.parts)):
            name = names[at % 2]
            away = self.give(at, name, places[name])
            sent.append(away)
            self.parts[at].append(flip(*places[name])(away))
        return sent

    def merge(self):
        pairs = list(zip(self.parts[::2], self.parts[1::2]))
        self.parts = [
            [jnp.concatenate(both, axis=-1) for both in zip(even, odd)] for even, odd in pairs
        ]
        self.dims = self.dims[::2]

    def arrived(self):
        return [parts[-1] for parts in self.parts]

    def hold(self, until):
        for parts in self.parts:
            parts[-1] = held_back(parts[-1], until)

    def result(self):
        return jnp.concatenate([sum(p.astype(f32) for p in parts) for parts in self.parts], axis=1)


def masked(values, ids):
    return jnp.concatenate(
        [jnp.where(ids == m, values, jnp.zeros_like(values)) for m in range(MODS)], axis=1
    )


def channel_layout(
    tokens,
    modality,
    lengths,
    norm_gain,
    input_weight,
    param_weight,
    step_weight,
    step_bias,
    output_weight,
    conv_weight,
    conv_bias,
    decay_log,
    skip_gain,
    cotangent,
):
    seqs = size_of(SEQ)
    channels = conv_weight.shape[1]
    width = tokens.shape[1]
    features = param_weight.shape[2]
    slab = input_weight.shape[1]

    token_vals = tokens.astype(f32)
    inverse = lax.rsqrt(jnp.mean(token_vals * token_vals, axis=1, keepdims=True) + EPSILON)
    normal_rows = token_vals * inverse
    gain_vals = norm_gain.astype(f32)

    send_in = input_weight.reshape(MODS, slab, 2, seqs, channels)
    send_in = send_in.transpose(3, 2, 0, 1, 4).reshape(seqs, 2 * MODS * slab, channels)
    id_rows = 16
    send_ids = jnp.pad(modality.astype(bf16), (0, id_rows * channels - modality.shape[0]))
    send_ids = jnp.broadcast_to(send_ids.reshape(id_rows, channels), (seqs, id_rows, channels))
    send_in = jnp.concatenate([send_in, send_ids], axis=1)
    made = []

    def send(line):
        made.append(exchange(held_back(send_in, [line]), SEQ))
        return made

    pieces, arrived = gathered_columns((normal_rows * gain_vals[None, :]).astype(bf16), send)
    inner_blocks = made[0]
    ids = inner_blocks[:, 2 * MODS * slab :].reshape(seqs, -1)[:, : modality.shape[0]].astype(jnp.int32)
    ids_rows = ids.reshape(-1, tokens.shape[0])
    ids = ids.reshape(-1, 1)
    send_out = output_weight.reshape(MODS, seqs, channels, slab).transpose(1, 0, 3, 2)
    send_out = send_out.reshape(seqs, MODS * slab, channels)
    param_rows = param_weight.transpose(0, 2, 1).reshape(MODS * features, channels)
    param_columns = param_weight.transpose(2, 0, 1).reshape(features, MODS * channels)
    step_rows_w = step_weight.reshape(MODS * R, channels)
    step_columns = step_weight.transpose(1, 0, 2).reshape(R, MODS * channels)
    core = place_bit(CORE)
    place = jnp.stack([place_bit(at) for at in (CORE, Y, X)]).astype(jnp.int32)
    taps = conv_weight.astype(f32)
    skip = skip_gain.astype(f32)[None, :]
    decay_rate = -jnp.exp(decay_log.astype(f32))
    rate_t = jnp.pad(decay_rate.T, ((0, 0), (0, LANES - N)))

    *normed, own_inner, own_gate, inner, conv_pre, act_low, feats = project(
        lengths,
        place,
        pieces,
        ids,
        ids_rows,
        inner_blocks,
        taps,
        conv_bias.astype(f32)[None, :],
        param_rows,
    )
    cotangents = lax.all_gather(
        held_back(cotangent, [inner]), SEQ + ("mod",), axis=0, tiled=True
    )
    feats, sent = summed_features(feats)
    gate_pre = modal_rows(normed, held_back(ids, [sent]), own_gate)
    pair_in = side_by_side(own_inner, flip(*CORE)(own_inner), own_gate, flip(*CORE)(own_gate))
    feats = held_back(feats, [gate_pre, pair_in])
    mix_high = feats[R:].astype(bf16)
    mix_rest = (feats[R:] - mix_high.astype(f32)).astype(bf16)
    feats = jnp.concatenate([feats[:R].astype(bf16), mix_high, mix_rest], axis=0)
    feats = shared_features(feats)

    out_blocks = exchange(held_back(send_out, [feats]), SEQ)
    states, enter, step_pre, *turned, scan_out = scan(
        lengths,
        ids,
        feats,
        conv_pre,
        step_columns,
        step_bias.astype(f32).reshape(1, MODS * channels),
        rate_t,
        skip,
    )
    out_blocks, scan_out = lax.optimization_barrier((out_blocks, scan_out))
    own_out, grad_scan, gate_wide, gated_wide, gate_rows, gated_rows = gates(
        cotangents, ids, out_blocks, gate_pre, scan_out
    )

    def token_sums(wide, weight):
        lows, gains = [], []
        for at, part in enumerate(normed):
            rows = part.shape[1]
            grad = dot(part, wide, 0, 0)
            lows.append(grad.astype(bf16))
            gains.append(jnp.sum(grad * weight[at * rows : (at + 1) * rows].astype(f32), axis=1))
        return jnp.concatenate(lows, axis=0), jnp.concatenate(gains, axis=0)

    def by_holder(low):
        return low.reshape(seqs, slab, MODS * channels)

    ids_ours = core_rows(ids, core)
    gated_both = jnp.concatenate(both_cores(gated_rows, ids_ours), axis=1)
    pair_out = side_by_side(own_out, flip(*CORE)(own_out))
    branch = SummedRows(row_parts(gated_both, pair_out, 2))
    branch_sent = branch.stage(("x", "y"))
    grad_scan = held_back(grad_scan, branch_sent)

    act_part, step_grad_low, feat_grad, sums, rate_sum = scan_back(
        place,
        ids,
        ids_rows,
        tuple(turned),
        conv_pre,
        step_pre,
        grad_scan,
        states,
        enter,
        step_rows_w,
        rate_t,
        skip,
    )
    feat_grad = held_back(feat_grad, branch.arrived())
    gate_rows, gate_wide, gated_wide = held_back((gate_rows, gate_wide, gated_wide), [feat_grad])
    gate_both = both_cores(gate_rows, ids_ours)
    feat_grad, sent = summed_features(feat_grad, bf16)
    feat_grad = held_back(feat_grad.astype(bf16), branch.stage(("y", "x")))
    gate_wide, gated_wide = held_back((gate_wide, gated_wide), [sent])
    gate_low, gate_gain = token_sums(gate_wide, own_gate)
    out_low = dot(cotangents, gated_wide, 0, 0).astype(bf16)
    more_low = jnp.concatenate([by_holder(gate_low), by_holder(out_low)], axis=2)
    feat_grad = shared_features(feat_grad, [more_low])
    more_low = exchange(held_back(more_low, [feat_grad]), SEQ)
    branch.hold([feat_grad])
    branch.merge()

    inner_wide, inner_rows, tap_sums = conv_back(
        seqs,
        lengths,
        ids,
        feat_grad,
        act_part,
        conv_pre,
        inner,
        taps,
        param_columns,
    )
    both_wide = jnp.concatenate(both_cores(inner_rows, ids_ours) + gate_both, axis=1)
    products = row_parts(both_wide, pair_in, COLUMNS)
    normed_sums = SummedRows(products)
    sent = normed_sums.stage(("x", "y"))
    branch.hold(sent)
    branch.stage(("zl", "zl"))
    inner_low, inner_gain = token_sums(held_back(inner_wide, sent), own_inner)
    inner_low, more_low = lax.optimization_barrier((by_holder(inner_low), more_low))
    inner_low = exchange(inner_low, SEQ)
    step_grad_low = held_back(step_grad_low, sent)
    sent = normed_sums.stage(("y", "x"))
    branch.hold(sent)
    branch.stage(("zh", "zh"))
    output = (token_vals + branch.result()).astype(bf16)
    gain_sum = held_back(inner_gain + gate_gain, sent)
    gain_sum, inner_low = lax.optimization_barrier((gain_sum, inner_low))
    grad_gain = jnp.sum(share(gain_sum, SEQ + ("mod",)), axis=0) / gain_vals
    inner_low = inner_low.reshape(seqs, slab, MODS, channels)
    more_low = more_low.reshape(seqs, slab, 2, MODS, channels)
    grad_gate = more_low[:, :, 0].transpose(2, 1, 0, 3)
    grad_in = jnp.stack([inner_low.transpose(2, 1, 0, 3), grad_gate], axis=2)
    grad_in = grad_in.reshape(MODS, slab, 2, seqs * channels).astype(f32)
    normed_sums.merge()
    sent = normed_sums.stage(("zl", "zl"))
    feat_late, out_low = held_back((feat_grad, more_low[:, :, 1]), sent)
    grad_out = out_low.transpose(2, 0, 3, 1)
    grad_out = grad_out.reshape(MODS, seqs * channels, slab).astype(f32)
    normed_sums.hold([grad_in, grad_gain])
    normed_sums.stage(("zh", "zh"))
    normed_grad = normed_sums.result()
    step_t = feats[:, :, :, :R].transpose(3, 1, 0, 2, 4).reshape(R, -1)
    grad_step = dot(step_t, masked(step_grad_low, ids))
    grad_step = grad_step.reshape(R, MODS, channels).transpose(1, 0, 2)
    feat_late = feat_late.transpose(3, 1, 0, 2, 4).reshape(features, -1)
    feat_late = [
        jnp.where(ids_rows.reshape(1, -1) == m, feat_late, jnp.zeros_like(feat_late))
        for m in range(MODS)
    ]
    grad_param = dot(jnp.concatenate(feat_late, axis=0), act_low)
    grad_param = grad_param.reshape(MODS, features, channels).transpose(0, 2, 1)
    hat_grad = normed_grad * gain_vals[None, :]
    token_grad = cotangent.astype(f32) + inverse * (
        hat_grad - normal_rows * jnp.mean(hat_grad * normal_rows, axis=1, keepdims=True)
    )
    return (
        output,
        token_grad,
        grad_gain,
        grad_in,
        grad_param,
        grad_step,
        grad_out,
        tap_sums[:KW],
        tap_sums[KW],
        rate_sum[:, :N].T * decay_rate,
        sums[MODS],
        sums[:MODS],
    )


def placed(spec, axes):
    entries = [
        sum((axes[name] for name in ((entry,) if isinstance(entry, str) else entry or ())), ())
        for entry in spec
    ]
    return P(*[entry or None for entry in entries])


def solution(mesh):
    token_rows = P(("seq", "mod"), None)
    in_weight = P(None, "seq", None, "mod")
    out_weight = P(None, "mod", "seq")
    row, column, depth = P(("mod", "seq")), P(None, ("mod", "seq")), P(None, None, ("mod", "seq"))
    middle = P(None, ("mod", "seq"), None)
    ins = (token_rows, P("seq"), P(), P(), in_weight, middle, depth, column, out_weight)
    ins += (column, row, column, row, token_rows)
    outs = (token_rows, token_rows, P(), in_weight, middle, depth, out_weight)
    outs += (column, row, column, row, column)

    def run(*args):
        sizes = (mesh.shape["seq"], mesh.shape["mod"])
        share_of_channels = args[12].shape[0] // (sizes[0] * sizes[1])
        if share_of_channels == LANES and sizes == (8, 4):
            part, over = channel_layout, jax.sharding.Mesh(
                mesh.devices.reshape(sizes[0] // 2, 2, sizes[1]), ("z", "core", "mod")
            )
            axes = {"seq": SEQ, "mod": ("mod",)}
        else:
            part, over = local, mesh
            axes = {"seq": ("seq",), "mod": ("mod",)}
        return jax.shard_map(
            part,
            mesh=over,
            in_specs=tuple(placed(spec, axes) for spec in ins),
            out_specs=tuple(placed(spec, axes) for spec in outs),
            check_vma=False,
        )(*args)

    return run
```

```python
import functools
import math

import jax
import jax.numpy as jnp
from jax import lax
from jax.experimental import pallas as pl
from jax.experimental.pallas import tpu as pltpu
from jax.sharding import PartitionSpec as P

N = 16
KW = 4
R = 128
MODS = 3
TOK_DEV = 128
CAPD = 48


EPSILON = 1e-05
SCAN_ROWS = 512

LANES = 128
SUB = 8
STEPS = 4
UNROLL = 4
COLUMNS = 4
FAR = 1e9
VMEM_BYTES = 60 * 1024 * 1024
f32 = jnp.float32
bf16 = jnp.bfloat16


def shifted_2(value, axis, by):
    size = lax.axis_size(axis)
    pairs = [(i, i + by) for i in range(size) if 0 <= i + by < size]
    return lax.ppermute(value, axis, pairs)


def carried_in(value, axis, combine, identity):
    size, here = (lax.axis_size(axis), lax.axis_index(axis))
    everything = jax.tree.map(
        lambda part, kind: lax.all_gather(part.astype(kind), axis),
        value,
        (jnp.bfloat16, jnp.bfloat16),
    )
    start = jax.tree.map(
        lambda part, zero: jnp.broadcast_to(jnp.asarray(zero, part.dtype), part.shape),
        value,
        identity,
    )

    def carried_hop(k, before):
        reached = k < here
        new = combine(
            before, jax.tree.map(lambda part, own: part[k].astype(own.dtype), everything, value)
        )
        return jax.tree.map(lambda a, b: jnp.where(reached, a, b), new, before)

    return lax.fori_loop(0, size, carried_hop, start)


def prefix(value, axis, combine, identity):
    size, here = (lax.axis_size(axis), lax.axis_index(axis))
    everything = jax.tree.map(lambda part: lax.all_gather(part, axis), value)
    start = jax.tree.map(
        lambda part, zero: jnp.broadcast_to(jnp.asarray(zero, part.dtype), part.shape),
        value,
        identity,
    )

    def prefix_hop(k, before):
        at = size - 1 - k
        reached = at > here
        new = combine(before, jax.tree.map(lambda part: part[at], everything))
        return jax.tree.map(lambda a, b: jnp.where(reached, a, b), new, before)

    return lax.fori_loop(0, size, prefix_hop, start)


def split_rows(count_rows):
    return (count_rows // TOK_DEV, TOK_DEV)


def slot_tables(modal_ids, capacity):
    sub_rows = modal_ids.shape[1]
    marked = (modal_ids[:, :, None] == jnp.arange(MODS, dtype=jnp.int32)[None, None, :]).astype(
        jnp.int32
    )
    ranking = jnp.sum((jnp.cumsum(marked, axis=1) - 1) * marked, axis=2)
    slot_ids = modal_ids * capacity + ranking
    positions = jnp.broadcast_to(jnp.arange(sub_rows, dtype=jnp.int32)[None, :], modal_ids.shape)
    unfilled = jnp.full((modal_ids.shape[0], MODS * capacity), sub_rows, jnp.int32)
    tables = jax.vmap(lambda table_row, slot_row, place_row: table_row.at[slot_row].set(place_row))(
        unfilled, slot_ids, positions
    )
    return (tables, slot_ids)


def group_rows(values, tables, capacity):
    padded = jnp.concatenate([values, jnp.zeros_like(values[:, :1])], axis=1)
    picked = jax.vmap(lambda block_values, block_table: block_values[block_table])(padded, tables)
    return picked.reshape(values.shape[0], MODS, capacity, values.shape[2])


def ungroup_rows(grouped, slot_ids):
    flattened = grouped.reshape(grouped.shape[0], MODS * grouped.shape[2], grouped.shape[3])
    return jax.vmap(lambda block_values, block_slots: block_values[block_slots])(
        flattened, slot_ids
    )


def modal_product(values, modal_ids, weight, transpose):
    count_rows = values.shape[0]
    sub_count, sub_rows = split_rows(count_rows)
    capacity = min(CAPD, sub_rows)
    tables, slot_ids = slot_tables(modal_ids.reshape(sub_count, sub_rows), capacity)
    grouped = group_rows(values.reshape(sub_count, sub_rows, values.shape[1]), tables, capacity)
    if transpose:
        result = jnp.einsum("gmcn,mkn->gmck", grouped, weight, preferred_element_type=jnp.float32)
    else:
        result = jnp.einsum("gmck,mkn->gmcn", grouped, weight, preferred_element_type=jnp.float32)
    return ungroup_rows(result, slot_ids).reshape(count_rows, result.shape[3])


def modal_outer(left, right, modal_ids):
    count_rows = left.shape[0]
    sub_count, sub_rows = split_rows(count_rows)
    capacity = min(CAPD, sub_rows)
    tables, slot_ids = slot_tables(modal_ids.reshape(sub_count, sub_rows), capacity)
    left_grouped = group_rows(left.reshape(sub_count, sub_rows, left.shape[1]), tables, capacity)
    right_grouped = group_rows(right.reshape(sub_count, sub_rows, right.shape[1]), tables, capacity)
    return jnp.einsum(
        "gmcl,gmcr->mlr", left_grouped, right_grouped, preferred_element_type=jnp.float32
    )


def modal_table(table, modal_ids):
    picked = jnp.zeros((modal_ids.shape[0], table.shape[1]), jnp.float32)
    for modal_index in range(MODS):
        picked = (
            picked
            + (modal_ids == modal_index).astype(jnp.float32)[:, None] * table[modal_index][None, :]
        )
    return picked


def modal_sums(values, modal_ids):
    return jnp.stack(
        [
            jnp.sum(values * (modal_ids == modal_index).astype(jnp.float32)[:, None], axis=0)
            for modal_index in range(MODS)
        ]
    )


def pair_combine(earlier, later):
    return (earlier[0] * later[0], later[0] * earlier[1] + later[1])


def back_combine(earlier, later):
    return (earlier[0] * later[0], later[1] + later[0] * earlier[1])


def silu_slope(values):
    sigmoid_part = jax.nn.sigmoid(values)
    return sigmoid_part * (1.0 + values * (1.0 - sigmoid_part))


def local(
    tokens,
    modality,
    lengths,
    norm_gain,
    input_weight,
    param_weight,
    step_weight,
    step_bias,
    output_weight,
    conv_weight,
    conv_bias,
    decay_log,
    skip_gain,
    cotangent,
):
    block_rows = modality.shape[0]
    gathered = (
        lax.all_gather(input_weight, "seq", axis=1, tiled=True),
        lax.all_gather(param_weight, "seq", axis=1, tiled=True),
        lax.all_gather(step_weight, "seq", axis=2, tiled=True),
        lax.all_gather(output_weight, "seq", axis=2, tiled=True),
        lax.all_gather(conv_weight, "seq", axis=1, tiled=True),
        lax.all_gather(conv_bias, "seq", axis=0, tiled=True),
        lax.all_gather(decay_log, "seq", axis=1, tiled=True),
        lax.all_gather(skip_gain, "seq", axis=0, tiled=True),
        lax.all_gather(step_bias, "seq", axis=1, tiled=True),
    )
    in_local = gathered[0]
    param_local = gathered[1]
    step_local = gathered[2]
    out_local = gathered[3]
    tap_weights = gathered[4].astype(jnp.float32)
    tap_bias = gathered[5].astype(jnp.float32)
    decay_rate = -jnp.exp(gathered[6].astype(jnp.float32))
    skip_local = gathered[7].astype(jnp.float32)
    bias_local = gathered[8].astype(jnp.float32)
    channels = in_local.shape[3]
    model_width = in_local.shape[1]
    in_flat = in_local.reshape(MODS, model_width, 2 * channels)
    token_vals = tokens.astype(jnp.float32)
    inverse = lax.rsqrt(jnp.mean(token_vals * token_vals, axis=1, keepdims=True) + EPSILON)
    normal_rows = token_vals * inverse
    gain_vals = norm_gain.astype(jnp.float32)
    normed = (normal_rows * gain_vals[None, :]).astype(jnp.bfloat16)
    piece = lax.all_gather(normed, "mod", axis=0, tiled=True)
    piece_ids = modality
    product = modal_product(piece, piece_ids, in_flat, False)
    filled = product
    folded = (filled, piece)
    expanded = folded[0].reshape(block_rows, 2, channels)
    inner = expanded[:, 0]
    gate_pre = expanded[:, 1]
    first_place = lax.axis_index("seq") * block_rows
    places = first_place + jnp.arange(block_rows, dtype=jnp.int32)
    split_place = lengths[0]
    begins = jnp.where(places >= split_place, split_place, 0)
    keeping = (places != begins).astype(jnp.float32)
    inherit = (begins < first_place).astype(jnp.float32)
    halo_rows = shifted_2(inner[block_rows - KW + 1 :], "seq", 1)
    extended = jnp.concatenate([halo_rows, inner], axis=0)
    valid_taps = [
        (places - (KW - 1 - tap_index) >= begins).astype(jnp.float32)[:, None]
        for tap_index in range(KW)
    ]
    conv_pre = jnp.broadcast_to(tap_bias[None, :], inner.shape)
    for tap_index in range(KW):
        conv_pre = (
            conv_pre
            + tap_weights[tap_index][None, :]
            * extended[tap_index : tap_index + block_rows]
            * valid_taps[tap_index]
        )
    activated = jax.nn.silu(conv_pre)
    act_low = activated.astype(jnp.bfloat16)
    feature_part = modal_product(act_low, modality, param_local, False)
    features = lax.psum(feature_part, "mod")
    step_low = features[:, :R].astype(jnp.bfloat16)
    input_mix = features[:, R : R + N]
    output_mix = features[:, R + N :]
    step_pre = modal_product(step_low, modality, step_local, False) + modal_table(
        bias_local, modality
    )
    step_size = jax.nn.softplus(step_pre)
    scan_rows = math.gcd(block_rows, SCAN_ROWS)
    scan_count = block_rows // scan_rows

    def blocked(values):
        return values.reshape((scan_count, scan_rows) + values.shape[1:])

    def block_mult(keep_block, step_block):
        return keep_block[:, None, None] * jnp.exp(step_block[:, None, :] * decay_rate[None])

    def local_step(state_now, inputs):
        keep_block, step_block, act_block, input_block, output_block = inputs
        multiplier = block_mult(keep_block, step_block)
        addition = (step_block * act_block)[:, None, :] * input_block[:, :, None]
        running = lax.associative_scan(pair_combine, (multiplier, addition), axis=0)
        states = running[0] * state_now[None] + running[1]
        return (
            states[-1],
            (jnp.sum(output_block[:, :, None] * states, axis=1), state_now, running[0], running[1]),
        )

    scan_inputs = (
        blocked(keeping),
        blocked(step_size),
        blocked(activated),
        blocked(input_mix),
        blocked(output_mix),
    )
    end_state, (local_out, local_starts, run_mult, run_add) = lax.scan(
        local_step, jnp.zeros((N, channels), jnp.float32), scan_inputs
    )
    device_decay = jnp.exp(decay_rate * jnp.sum(step_size, axis=0)[None, :]) * jnp.min(keeping)
    chained = carried_in(
        (device_decay, end_state),
        "seq",
        pair_combine,
        (jnp.ones_like(device_decay), jnp.zeros_like(end_state)),
    )
    state_in = chained[1]

    def fix_step(carried, inputs):
        total_step, alive = carried
        inherit_block, step_block, output_block = inputs
        start_factor = alive * jnp.exp(decay_rate * total_step[None, :])
        running_step = total_step[None, :] + jnp.cumsum(step_block, axis=0)
        reach = inherit_block[:, None, None] * jnp.exp(running_step[:, None, :] * decay_rate[None])
        extra = jnp.sum(output_block[:, :, None] * reach * state_in[None], axis=1)
        return ((running_step[-1], inherit_block[-1]), (extra, start_factor))

    reach_inputs = (blocked(inherit), blocked(step_size), blocked(output_mix))
    _, (extra_out, start_factors) = lax.scan(
        fix_step, (jnp.zeros((channels,), jnp.float32), jnp.float32(1.0)), reach_inputs
    )
    start_states = local_starts + start_factors * state_in[None]
    scan_out = (local_out + extra_out).reshape(block_rows, channels) + skip_local[
        None, :
    ] * activated
    gate_act = jax.nn.silu(gate_pre)
    gated = (scan_out * gate_act).astype(jnp.bfloat16)
    piece = gated
    piece_ids = modality
    branch = lax.psum_scatter(
        modal_product(piece, piece_ids, out_local, False), "mod", scatter_dimension=0, tiled=True
    )
    output = (token_vals + branch).astype(jnp.bfloat16)
    back_rows = cotangent.astype(jnp.float32)
    piece = lax.all_gather(cotangent, "mod", axis=0, tiled=True)
    piece_ids = modality
    product = modal_product(piece, piece_ids, out_local, True)
    grad_out = modal_outer(gated, piece, piece_ids)
    grad_scan = product * gate_act
    grad_gate = product * scan_out * silu_slope(gate_pre)
    grad_skip = jnp.sum(grad_scan * activated, axis=0)
    grad_act = grad_scan * skip_local[None, :]

    def lead_step(carried, inputs):
        total_step, lead_sum = carried
        inherit_block, step_block, output_block, grad_block = inputs
        running_step = total_step[None, :] + jnp.cumsum(step_block, axis=0)
        reach = inherit_block[:, None, None] * jnp.exp(running_step[:, None, :] * decay_rate[None])
        lead_sum = lead_sum + jnp.sum(
            reach * output_block[:, :, None] * grad_block[:, None, :], axis=0
        )
        return ((running_step[-1], lead_sum), None)

    (_, lead_local), _ = lax.scan(
        lead_step,
        (jnp.zeros((channels,), jnp.float32), jnp.zeros((N, channels), jnp.float32)),
        reach_inputs + (blocked(grad_scan),),
    )
    incoming = prefix(
        (device_decay, lead_local),
        "seq",
        back_combine,
        (jnp.ones_like(device_decay), jnp.zeros_like(lead_local)),
    )[1]

    def back_step(carried, inputs):
        after_block, rate_grad = carried
        (
            keep_block,
            step_block,
            act_block,
            input_block,
            output_block,
            grad_block,
            start_state,
            mult_block,
            add_block,
        ) = inputs
        multiplier = block_mult(keep_block, step_block)
        states = mult_block * start_state[None] + add_block
        previous = jnp.concatenate([start_state[None], states[:-1]], axis=0)
        pushed = output_block[:, :, None] * grad_block[:, None, :]
        pushed = pushed.at[-1].add(after_block)
        shifted = jnp.concatenate([multiplier[1:], jnp.ones_like(multiplier[:1])], axis=0)
        flipped = lax.associative_scan(pair_combine, (shifted[::-1], pushed[::-1]), axis=0)
        grad_state = flipped[1][::-1]
        mult_grad = grad_state * previous * multiplier
        state_input = jnp.sum(grad_state * input_block[:, :, None], axis=1)
        step_grad = jnp.sum(mult_grad * decay_rate[None], axis=1) + state_input * act_block
        rate_grad = rate_grad + jnp.sum(mult_grad * step_block[:, None, :], axis=0)
        input_grad = jnp.sum(grad_state * (step_block * act_block)[:, None, :], axis=2)
        act_grad = state_input * step_block
        output_grad = jnp.sum(states * grad_block[:, None, :], axis=2)
        return (
            (multiplier[0] * grad_state[0], rate_grad),
            (step_grad, input_grad, act_grad, output_grad),
        )

    back_inputs = scan_inputs[:5] + (blocked(grad_scan), start_states, run_mult, run_add)
    (_, rate_total), (step_grads, input_grads, act_grads, output_grads) = lax.scan(
        back_step, (incoming, jnp.zeros((N, channels), jnp.float32)), back_inputs, reverse=True
    )
    step_pre_grad = step_grads.reshape(block_rows, channels) * jax.nn.sigmoid(step_pre)
    grad_bias = modal_sums(step_pre_grad, modality)
    step_grad_low = step_pre_grad.astype(jnp.bfloat16)
    step_in_part = modal_product(step_grad_low, modality, step_local, True)
    grad_step = modal_outer(step_low, step_grad_low, modality)
    summed = lax.psum(
        (step_in_part, input_grads.reshape(block_rows, N), output_grads.reshape(block_rows, N)),
        "mod",
    )
    feature_grad = jnp.concatenate(summed, axis=1).astype(jnp.bfloat16)
    grad_param = modal_outer(act_low, feature_grad, modality)
    act_total = (
        grad_act
        + act_grads.reshape(block_rows, channels)
        + modal_product(feature_grad, modality, param_local, True)
    )
    conv_grad = act_total * silu_slope(conv_pre)
    tap_grads = []
    ext_grad = jnp.zeros((block_rows + KW - 1, channels), jnp.float32)
    for tap_index in range(KW):
        masked = conv_grad * valid_taps[tap_index]
        tap_grads.append(jnp.sum(masked * extended[tap_index : tap_index + block_rows], axis=0))
        ext_grad = ext_grad.at[tap_index : tap_index + block_rows].add(
            masked * tap_weights[tap_index][None, :]
        )
    grad_taps = jnp.stack(tap_grads)
    grad_tap_bias = jnp.sum(conv_grad, axis=0)
    spill = shifted_2(ext_grad[: KW - 1], "seq", -1)
    inner_grad = ext_grad[KW - 1 :].at[block_rows - KW + 1 :].add(spill)
    both_grad = (
        jnp.stack([inner_grad, grad_gate], axis=1)
        .astype(jnp.bfloat16)
        .reshape(block_rows, 2 * channels)
    )
    piece = both_grad
    piece_ids = modality
    normed_grad = lax.psum_scatter(
        modal_product(piece, piece_ids, in_flat, True), "mod", scatter_dimension=0, tiled=True
    )
    grad_in = modal_outer(folded[1], both_grad, modality)
    gain_part = jnp.sum(normed_grad * normal_rows, axis=0)
    hat_grad = normed_grad * gain_vals[None, :]
    token_grad = back_rows + inverse * (
        hat_grad - normal_rows * jnp.mean(hat_grad * normal_rows, axis=1, keepdims=True)
    )
    grad_gain = lax.psum(gain_part, ("seq", "mod"))
    grad_decay = rate_total * decay_rate
    weight_grads = (
        lax.psum_scatter(
            grad_in.reshape(MODS, model_width, 2, channels), "seq", scatter_dimension=1, tiled=True
        ),
        lax.psum_scatter(grad_param, "seq", scatter_dimension=1, tiled=True),
        lax.psum_scatter(grad_step, "seq", scatter_dimension=2, tiled=True),
        lax.psum_scatter(grad_out, "seq", scatter_dimension=2, tiled=True),
        lax.psum_scatter(grad_taps, "seq", scatter_dimension=1, tiled=True),
        lax.psum_scatter(grad_tap_bias, "seq", scatter_dimension=0, tiled=True),
        lax.psum_scatter(grad_decay, "seq", scatter_dimension=1, tiled=True),
        lax.psum_scatter(grad_skip, "seq", scatter_dimension=0, tiled=True),
        lax.psum_scatter(grad_bias, "seq", scatter_dimension=1, tiled=True),
    )
    return (
        output,
        token_grad,
        grad_gain,
        weight_grads[0],
        weight_grads[1],
        weight_grads[2],
        weight_grads[3],
        weight_grads[4],
        weight_grads[5],
        weight_grads[6],
        weight_grads[7],
        weight_grads[8],
    )


def pick(ids, parts):
    return jnp.where(ids == 0, parts[0], jnp.where(ids == 1, parts[1], parts[2]))


def silu(values):
    return values * jax.nn.sigmoid(values)


def softplus(values):
    small = jnp.exp(-jnp.abs(values))
    series = small * (
        1.0 + small * (-1 / 2 + small * (1 / 3 + small * (-1 / 4 + small * (1 / 5 - small / 6))))
    )
    return jnp.maximum(values, 0.0) + jnp.where(small < 0.05, series, jnp.log(1.0 + small))


def dot(left, right, left_dim=1, right_dim=0):
    return lax.dot_general(
        left, right, (((left_dim,), (right_dim,)), ((), ())), preferred_element_type=f32
    )


def row_places(first, rows):
    return first + lax.broadcasted_iota(jnp.int32, (rows, 1), 0)


def whole(shape):
    return pl.BlockSpec(shape, lambda *_: (0,) * len(shape), pipeline_mode=pl.Buffered(1))


def cost(micros, flops=0):
    return pl.CostEstimate(flops=flops, bytes_accessed=int(micros * 3.69e6), transcendentals=0)


def modal_dot(values, ids, weight):
    part = values[0].shape[1]
    wide = sum(dot(v[...], weight[i * part : (i + 1) * part, :]) for i, v in enumerate(values))
    channels = wide.shape[1] // MODS
    return pick(ids, [wide[:, m * channels : (m + 1) * channels] for m in range(MODS)])


def modal_rows_of(weight, values, ids_row):
    stacked = dot(weight, values, 1, 1)
    height = stacked.shape[0] // MODS
    return pick(ids_row, [stacked[m * height : (m + 1) * height] for m in range(MODS)])


def put_masked(ref, rows, ids, values):
    channels = values.shape[1]
    for m in range(MODS):
        ref[rows, m * channels : (m + 1) * channels] = jnp.where(ids == m, values, 0.0).astype(
            ref.dtype
        )


def arrange(blocks, first, out):
    slab = out.shape[0] // blocks.shape[0]
    channels = blocks.shape[2]
    for at in range(blocks.shape[0]):
        for m in range(MODS):
            out[at * slab : (at + 1) * slab, m * channels : (m + 1) * channels] = blocks[
                at, (first + m) * slab : (first + m + 1) * slab, :
            ]


def project_kernel(lengths, place, *refs):
    pieces, refs = refs[: 4 * COLUMNS], refs[4 * COLUMNS :]
    ids_ref, ids_rows, blocks, taps, bias, param_t = refs[:6]
    xs, refs = refs[6 : 6 + COLUMNS], refs[6 + COLUMNS :]
    w, w_gate, inner_ref, pre_ref, low_ref, feats, ext = refs
    step = pl.program_id(0)

    @pl.when(step == 0)
    def _():
        arrange(blocks, 0, w)
        arrange(blocks, MODS, w_gate)

    block_rows = pieces[0].shape[3]
    for which in (0, 1):

        @pl.when((place[0] == step % 2) == (which == 0))
        def _():
            for at in range(COLUMNS):
                own_line, other_line = pieces[4 * at + 2 * which : 4 * at + 2 * which + 2]
                here = place[1] if at % 2 == 0 else place[2]
                for near in (0, 1):
                    for line, value in ((here, own_line), (1 - here, other_line)):
                        block = line * 2 + near if at % 2 == 0 else near * 2 + line
                        row = pl.multiple_of(block * block_rows, block_rows)
                        xs[at][pl.ds(row, block_rows), :] = value[near, 0, 0]

    rows = xs[0].shape[0]
    channels = inner_ref.shape[1]
    ids = ids_ref[...]
    inner = modal_dot(xs, ids, w)
    inner_ref[...] = inner

    @pl.when(step == 0)
    def _():
        ext[0:8, :] = jnp.zeros((8, channels), f32)

    @pl.when(step > 0)
    def _():
        ext[0:8, :] = ext[rows : rows + 8, :]

    ext[8 : 8 + rows, :] = inner
    places = row_places(step * rows, rows)
    split = lengths[0]
    begins = jnp.where(places >= split, split, 0)
    pre = jnp.broadcast_to(bias[...], (rows, channels))
    for tap in range(KW):
        lag = KW - 1 - tap
        shifted = ext[8 - lag : 8 - lag + rows, :]
        pre = pre + taps[tap : tap + 1, :] * jnp.where(places - lag >= begins, shifted, 0.0)
    pre_ref[...] = pre
    low = silu(pre).astype(bf16)
    low_ref[...] = low
    across = feats.shape[2]
    ours = jnp.where(place[0] == step % 2, 1, 0)
    for j in range(across):
        block = low[j * block_rows : (j + 1) * block_rows]
        feats[ours, step // 2, j] = modal_rows_of(
            param_t[...], block, ids_rows[pl.ds(step * across + j, 1), :]
        )


def project(lengths, place, pieces, ids, ids_rows, blocks, taps, bias, param_t):
    total = ids.shape[0]
    channels = taps.shape[1]
    chips, across = lax.axis_size("z"), lax.axis_size("mod")
    rows = total // (2 * chips)
    width = pieces[0].shape[4]
    by_rows = lambda i: (i, 0)
    feats = (2, chips, across, param_t.shape[0] // MODS, rows // across)
    smem = pl.BlockSpec(memory_space=pltpu.SMEM)
    return pl.pallas_call(
        project_kernel,
        grid=(total // rows,),
        in_specs=[
            smem,
            smem,
            *[
                pl.BlockSpec((2, 1, 1) + piece.shape[3:], lambda i: (0, i // 2 % 2, i // 4, 0, 0))
                for piece in pieces
            ],
            pl.BlockSpec((rows, 1), by_rows),
            whole(ids_rows.shape),
            whole(blocks.shape),
            whole(taps.shape),
            whole(bias.shape),
            whole(param_t.shape),
        ],
        out_specs=[pl.BlockSpec((rows, width), by_rows)] * COLUMNS
        + [whole((COLUMNS * width, MODS * channels))] * 2
        + [pl.BlockSpec((rows, channels), by_rows)] * 3
        + [whole(feats)],
        out_shape=[jax.ShapeDtypeStruct((total, width), bf16)] * COLUMNS
        + [jax.ShapeDtypeStruct((COLUMNS * width, MODS * channels), bf16)] * 2
        + [jax.ShapeDtypeStruct((total, channels), f32)] * 2
        + [jax.ShapeDtypeStruct((total, channels), bf16)]
        + [jax.ShapeDtypeStruct(feats, f32)],
        scratch_shapes=[pltpu.VMEM((rows + 8, channels), f32)],
        compiler_params=pltpu.CompilerParams(vmem_limit_bytes=VMEM_BYTES),
        cost_estimate=cost(1),
        name="project",
    )(lengths, place, *pieces, ids, ids_rows, blocks, taps, bias, param_t)


def modal_kernel(*refs):
    *xs, ids_ref, w, out = refs
    out[...] = modal_dot(xs, ids_ref[...], w)


def modal_rows(values, ids, weight):
    total = values[0].shape[0]
    channels = weight.shape[1] // MODS
    rows = math.gcd(total, 512)
    by_rows = lambda i: (i, 0)
    return pl.pallas_call(
        modal_kernel,
        grid=(total // rows,),
        in_specs=[
            *[pl.BlockSpec((rows, part.shape[1]), by_rows) for part in values],
            pl.BlockSpec((rows, 1), by_rows),
            whole(weight.shape),
        ],
        out_specs=pl.BlockSpec((rows, channels), by_rows),
        out_shape=jax.ShapeDtypeStruct((total, channels), f32),
        compiler_params=pltpu.CompilerParams(vmem_limit_bytes=VMEM_BYTES),
        cost_estimate=cost(1),
        name="modal_rows",
    )(*values, ids, weight)


def side_kernel(*refs):
    out, columns = refs[-1], refs[0].shape[1]
    for at, part in enumerate(refs[:-1]):
        out[:, at * columns : (at + 1) * columns] = part[...]


def side_by_side(*parts):
    rows, columns = parts[0].shape
    step = math.gcd(rows, 512)
    by_rows = lambda i: (i, 0)
    return pl.pallas_call(
        side_kernel,
        grid=(rows // step,),
        in_specs=[pl.BlockSpec((step, columns), by_rows)] * len(parts),
        out_specs=pl.BlockSpec((step, columns * len(parts)), by_rows),
        out_shape=jax.ShapeDtypeStruct((rows, columns * len(parts)), parts[0].dtype),
        cost_estimate=cost(1),
        name="side_by_side",
    )(*parts)


def gates_kernel(
    cot, ids_ref, blocks, pre, out, w_out, grad_scan, gate_wide, gated_wide, gate_low, gated_low
):
    @pl.when(pl.program_id(0) == 0)
    def _():
        arrange(blocks, 0, w_out)

    ids = ids_ref[...]
    here = pre[...]
    grad = modal_dot([cot], ids, w_out)
    sig = jax.nn.sigmoid(here)
    scanned = out[...]
    grad_scan[...] = grad * (here * sig)
    gate_grad = grad * scanned * (sig * (1.0 + here * (1.0 - sig)))
    gated = scanned * (here * sig)
    gate_low[...] = gate_grad.astype(bf16)
    gated_low[...] = gated.astype(bf16)
    put_masked(gate_wide, slice(None), ids, gate_grad)
    put_masked(gated_wide, slice(None), ids, gated)


def gates(cotangents, ids, blocks, pre, out):
    total, channels = out.shape
    width = cotangents.shape[1]
    rows = total // size_of(SEQ)
    by_rows = lambda i: (i, 0)
    block = pl.BlockSpec((rows, channels), by_rows)
    wide = pl.BlockSpec((rows, MODS * channels), by_rows)
    return pl.pallas_call(
        gates_kernel,
        grid=(total // rows,),
        in_specs=[
            pl.BlockSpec((rows, width), by_rows),
            pl.BlockSpec((rows, 1), by_rows),
            whole(blocks.shape),
            block,
            block,
        ],
        out_specs=[whole((width, MODS * channels)), block, wide, wide, block, block],
        out_shape=[
            jax.ShapeDtypeStruct((width, MODS * channels), bf16),
            jax.ShapeDtypeStruct((total, channels), f32),
            jax.ShapeDtypeStruct((total, MODS * channels), bf16),
            jax.ShapeDtypeStruct((total, MODS * channels), bf16),
            jax.ShapeDtypeStruct((total, channels), bf16),
            jax.ShapeDtypeStruct((total, channels), bf16),
        ],
        compiler_params=pltpu.CompilerParams(vmem_limit_bytes=VMEM_BYTES),
        cost_estimate=cost(1),
        name="gates",
    )(cotangents, ids, blocks, pre, out)


def spread_rates(rate_t, out):
    for group in range(rate_t.shape[0] // SUB):
        rows = rate_t[group * SUB : (group + 1) * SUB, :]
        for n in range(N):
            at = (group * N + n) * SUB
            out[at : at + SUB, :] = jnp.broadcast_to(rows[:, n : n + 1], (SUB, LANES))


def spread_mix(mixed, out, tau):
    spread = [jnp.broadcast_to(mixed[n : n + 1, :], (SUB, LANES)) for n in range(2 * N)]
    out[step_rows(tau, 2 * N * SUB), :] = jnp.concatenate(spread, axis=0)


def turned_rows(tau, length):
    return pl.ds(tau, LANES, stride=length)


def step_rows(tau, rows=LANES):
    return pl.ds(pl.multiple_of(tau * rows, rows), rows)


def over_segments(spent, ends, rates, backward):
    at = lax.broadcasted_iota(jnp.int32, (SUB, LANES), 1)
    ends = list(ends)
    reach = 1
    while reach < LANES:
        shift = LANES - reach if backward else reach
        inside = at < LANES - reach if backward else at >= reach
        for n in range(N):
            earlier = jnp.where(inside, pltpu.roll(ends[n], shift, 1), 0.0)
            ends[n] = ends[n] + jnp.exp(spent * rates[n]) * earlier
        spent = spent + jnp.where(inside, pltpu.roll(spent, shift, 1), 0.0)
        reach *= 2
    shift = LANES - 1 if backward else 1
    inside = at < LANES - 1 if backward else at >= 1
    return [jnp.where(inside, pltpu.roll(end, shift, 1), 0.0) for end in ends]


def row_of(at):
    return slice(at * SUB, (at + 1) * SUB)


def group_view(ref, first, count, group):
    start = pl.multiple_of(first * (count * LANES) + group * SUB, SUB)
    return ref.at[pl.ds(start, (count - 1) * LANES + SUB)]


def pieces_of(values, count):
    return [values[n * SUB : (n + 1) * SUB] for n in range(count)]


def scan_kernel(
    lengths,
    ids_ref,
    feats,
    pre,
    step_w,
    step_b,
    rate_t,
    skip,
    states,
    enter,
    step_pre,
    s_turn,
    u_turn,
    mix_rows,
    scan_out,
    s_flat,
    u_flat,
    mix_flat,
    y_turn,
    held,
    rates,
    mix_turn,
):
    chunk = pl.program_id(0)
    total, channels = pre.shape
    length = total // LANES
    steps = states.shape[0]
    groups = channels // SUB
    split = lengths[0]
    wide = N * SUB

    @pl.when(chunk == 0)
    def _():
        spread_rates(rate_t, rates)
        across = feats.shape[2]
        block_rows = feats.shape[4]
        for seq in range(2 * feats.shape[1]):
            for j in range(across):
                first = (seq * across + j) * block_rows
                block = pl.ds(first, block_rows)
                block_ids = ids_ref[block, :]
                low = feats[seq % 2, seq // 2, j, 0:R, :]
                stacked = dot(low, step_w[...], 0, 0) + step_b[...]
                here = pick(
                    block_ids, [stacked[:, m * channels : (m + 1) * channels] for m in range(MODS)]
                )
                step_pre[block, :] = here
                step = softplus(here)
                places = row_places(first, block_rows)
                start = (places == 0) | (places == split)
                s_flat[block, :] = jnp.where(start, FAR, step)
                u_flat[block, :] = step * silu(pre[block, :])
                mixed = feats[seq % 2, seq // 2, j, R : R + 2 * N, :].astype(f32)
                mixed = mixed + feats[seq % 2, seq // 2, j, R + 2 * N :, :].astype(f32)
                blank = jnp.zeros((LANES - 2 * N, block_rows), f32)
                mix_flat[block, :] = jnp.transpose(jnp.concatenate([mixed, blank], axis=0))

        def turn(tau, carried):
            rows = turned_rows(tau, length)
            s_turn[step_rows(tau), :] = jnp.transpose(s_flat[rows, :])
            u_turn[step_rows(tau), :] = jnp.transpose(u_flat[rows, :])
            mixed = jnp.transpose(mix_flat[rows, :])[: 2 * N]
            mix_rows[step_rows(tau, 2 * N), :] = mixed
            spread_mix(mixed, mix_turn, tau)
            return carried

        lax.fori_loop(0, length, turn, 0)

        def ahead(group, carried):
            rate = pieces_of(rates[step_rows(group, wide), :], N)

            def some(i, carried):
                hidden, spent = list(carried[0]), carried[1]
                s_here, u_here = [group_view(v, i, UNROLL, group) for v in (s_turn, u_turn)]
                mix_here = mix_turn.at[step_rows(i, UNROLL * 2 * wide)]
                for j in range(UNROLL):
                    s, u = s_here[row_of(j * groups), :], u_here[row_of(j * groups), :]
                    for n in range(N):
                        b = mix_here[row_of(j * 2 * N + n), :]
                        hidden[n] = jnp.exp(s * rate[n]) * hidden[n] + u * b
                    spent = spent + s
                return hidden, spent

            zero = jnp.zeros((SUB, LANES), f32)
            ends, spent = lax.fori_loop(0, length // UNROLL, some, ([zero] * N, zero))
            inside = jnp.concatenate(over_segments(spent, ends, rate, False), axis=0)
            held[step_rows(group, wide), :] = inside
            enter[step_rows(group, wide), :] = inside
            return carried

        lax.fori_loop(0, groups, ahead, 0)

    def advance(group, carried):
        own = step_rows(group, wide)
        rate = pieces_of(rates[own, :], N)
        hidden = pieces_of(held[own, :], N)
        s_here, u_here, y_here = [
            group_view(v, chunk, steps, group) for v in (s_turn, u_turn, y_turn)
        ]
        mix_here = mix_turn.at[step_rows(chunk, steps * 2 * wide)]
        for j in range(steps):
            s, u = s_here[row_of(j * groups), :], u_here[row_of(j * groups), :]
            out = states.at[j, own]
            terms = []
            for n in range(N):
                b = mix_here[row_of(j * 2 * N + n), :]
                hidden[n] = jnp.exp(s * rate[n]) * hidden[n] + u * b
                out[row_of(n), :] = hidden[n]
                terms.append(hidden[n] * mix_here[row_of(j * 2 * N + N + n), :])
            while len(terms) > 1:
                terms = [a + b for a, b in zip(terms[::2], terms[1::2])]
            y_here[row_of(j * groups), :] = terms[0]
        held[own, :] = jnp.concatenate(hidden, axis=0)
        return carried

    lax.fori_loop(0, groups, advance, 0)

    @pl.when(chunk == pl.num_programs(0) - 1)
    def _():
        def turn_back(tau, carried):
            s_flat[turned_rows(tau, length), :] = jnp.transpose(y_turn[step_rows(tau), :])
            return carried

        lax.fori_loop(0, length, turn_back, 0)
        for block in range(total // 512):
            rows = pl.ds(block * 512, 512)
            scan_out[rows, :] = s_flat[rows, :] + skip[...] * silu(pre[rows, :])


def scan(lengths, ids, feats, pre, step_w, step_b, rate_t, skip):
    total, channels = pre.shape
    length = total // LANES
    steps = math.gcd(length, STEPS)
    wide = N * channels
    flat = pltpu.VMEM((total, channels), f32)
    ins = (ids, feats, pre, step_w, step_b, rate_t, skip)
    shapes = [
        (wide, LANES),
        (total, channels),
        (length * channels, LANES),
        (length * channels, LANES),
        (length * 2 * N, LANES),
        (total, channels),
    ]
    return pl.pallas_call(
        scan_kernel,
        grid=(length // steps,),
        in_specs=[pl.BlockSpec(memory_space=pltpu.SMEM)] + [whole(a.shape) for a in ins],
        out_specs=[pl.BlockSpec((steps, wide, LANES), lambda i: (i, 0, 0))]
        + [whole(shape) for shape in shapes],
        out_shape=[jax.ShapeDtypeStruct((length, wide, LANES), f32)]
        + [jax.ShapeDtypeStruct(shape, f32) for shape in shapes],
        scratch_shapes=[flat, flat, flat, pltpu.VMEM((length * channels, LANES), f32)]
        + [pltpu.VMEM((wide, LANES), f32)] * 2
        + [pltpu.VMEM((length * 2 * N * SUB, LANES), f32)],
        compiler_params=pltpu.CompilerParams(vmem_limit_bytes=VMEM_BYTES),
        cost_estimate=cost(1),
        name="scan",
    )(lengths, *ins)


def back_kernel(
    core,
    ids_ref,
    ids_rows,
    s_turn,
    u_turn,
    mix_rows,
    pre,
    step_pre,
    grad,
    states,
    before,
    enter,
    step_w,
    rate_t,
    skip,
    act_part,
    step_grad_low,
    feat_part,
    sums,
    rate_out,
    g_turn,
    step_turn,
    in_turn,
    mix_grad,
    step_flat,
    in_flat,
    mix_flat,
    in_terms,
    out_terms,
    held,
    rate_sum,
    rates,
    mix_turn,
):
    turn_at = pl.program_id(0)
    chunks = pl.num_programs(0)
    chunk = chunks - 1 - turn_at
    total, channels = pre.shape
    length = total // LANES
    steps = states.shape[0]
    groups = channels // SUB
    wide = N * SUB

    @pl.when(turn_at == 0)
    def _():
        spread_rates(rate_t, rates)
        rate_sum[...] = jnp.zeros(rate_sum.shape, f32)

        def turn(tau, carried):
            g_turn[step_rows(tau), :] = jnp.transpose(grad[turned_rows(tau, length), :])
            spread_mix(mix_rows[step_rows(tau, 2 * N), :], mix_turn, tau)
            return carried

        lax.fori_loop(0, length, turn, 0)

        def ahead(group, carried):
            rate = pieces_of(rates[step_rows(group, wide), :], N)

            def some(i, carried):
                pulled, spent = list(carried[0]), carried[1]
                block = length // UNROLL - 1 - i
                s_here, g_here = [group_view(v, block, UNROLL, group) for v in (s_turn, g_turn)]
                mix_here = mix_turn.at[step_rows(block, UNROLL * 2 * wide)]
                for j in reversed(range(UNROLL)):
                    s, g = s_here[row_of(j * groups), :], g_here[row_of(j * groups), :]
                    for n in range(N):
                        c = mix_here[row_of(j * 2 * N + N + n), :]
                        pulled[n] = jnp.exp(s * rate[n]) * (pulled[n] + g * c)
                    spent = spent + s
                return pulled, spent

            zero = jnp.zeros((SUB, LANES), f32)
            ends, spent = lax.fori_loop(0, length // UNROLL, some, ([zero] * N, zero))
            inside = jnp.concatenate(over_segments(spent, ends, rate, True), axis=0)
            held[step_rows(group, wide), :] = inside
            return carried

        lax.fori_loop(0, groups, ahead, 0)

    in_terms[...] = jnp.zeros(in_terms.shape, f32)
    out_terms[...] = jnp.zeros(out_terms.shape, f32)

    def retreat(group, carried):
        own = step_rows(group, wide)
        views = [
            group_view(v, chunk, steps, group)
            for v in (s_turn, u_turn, g_turn, step_turn, in_turn)
        ]
        s, u, g = [[view[row_of(j * groups), :] for j in range(steps)] for view in views[:3]]
        mix_here = mix_turn.at[step_rows(chunk, steps * 2 * wide)]
        states_here = [states.at[j, own] for j in range(steps)]
        enter_here, before_here = enter.at[own], before.at[0, own]
        rate_here, held_here, sum_here = rates.at[own], held.at[own], rate_sum.at[own]
        step_sum, in_sum = [0.0] * steps, [0.0] * steps
        for n in range(N):
            at = row_of(n)
            rate, pull, rate_acc = rate_here[at, :], held_here[at, :], sum_here[at, :]
            first = jnp.where(chunk == 0, enter_here[at, :], before_here[at, :])
            state = [first] + [view[at, :] for view in states_here]
            for j in reversed(range(steps)):
                term = row_of(j * N + n)
                grad_state = g[j] * mix_here[row_of(j * 2 * N + N + n), :] + pull
                pull = jnp.exp(s[j] * rate) * grad_state
                mult = pull * state[j]
                step_sum[j] = step_sum[j] + mult * rate
                rate_acc = rate_acc + mult * s[j]
                in_sum[j] = in_sum[j] + grad_state * mix_here[row_of(j * 2 * N + n), :]
                in_terms[term, :] += grad_state * u[j]
                out_terms[term, :] += state[j + 1] * g[j]
            held_here[at, :] = pull
            sum_here[at, :] = rate_acc
        for j in range(steps):
            views[3][row_of(j * groups), :] = step_sum[j]
            views[4][row_of(j * groups), :] = in_sum[j]
        return carried

    lax.fori_loop(0, groups, retreat, 0)
    for j in range(steps):
        rows = []
        for terms in (in_terms, out_terms):
            for n in range(N):
                at = (j * N + n) * SUB
                rows.append(jnp.sum(terms[at : at + SUB, :], axis=0, keepdims=True))
        mix_grad[step_rows(chunk * steps + j, 2 * N), :] = jnp.concatenate(rows, axis=0)

    @pl.when(turn_at == chunks - 1)
    def _():
        def turn_back(tau, carried):
            rows = turned_rows(tau, length)
            step_flat[rows, :] = jnp.transpose(step_turn[step_rows(tau), :])
            in_flat[rows, :] = jnp.transpose(in_turn[step_rows(tau), :])
            mixed = mix_grad[step_rows(tau, 2 * N), :]
            blank = jnp.zeros((LANES - 2 * N, LANES), f32)
            mix_flat[rows, :] = jnp.transpose(jnp.concatenate([mixed, blank], axis=0))
            return carried

        lax.fori_loop(0, length, turn_back, 0)
        sums[...] = jnp.zeros(sums.shape, f32)
        across, block_rows = feat_part.shape[2], feat_part.shape[4]
        for seq in range(2 * feat_part.shape[1]):
            rows = pl.ds(seq * across * block_rows, across * block_rows)
            ids = ids_ref[rows, :]
            act = silu(pre[rows, :])
            step_in = step_pre[rows, :]
            state_in = in_flat[rows, :]
            grad_here = grad[rows, :]
            step_grad = step_flat[rows, :] + state_in * act
            pre_grad = step_grad * jax.nn.sigmoid(step_in)
            low = pre_grad.astype(bf16)
            step_grad_low[rows, :] = low
            act_part[rows, :] = grad_here * skip[...] + state_in * softplus(step_in)
            ours = jnp.where(core[0] == seq % 2, 1, 0)
            for j in range(across):
                block = seq * across + j
                block_low = low[j * block_rows : (j + 1) * block_rows]
                feat_part[ours, seq // 2, j, 0:R, :] = modal_rows_of(
                    step_w[...], block_low, ids_rows[block : block + 1, :]
                )
                turned = jnp.transpose(mix_flat[pl.ds(block * block_rows, block_rows), :])
                feat_part[ours, seq // 2, j, R : R + 2 * N, :] = turned[: 2 * N]
            for m in range(MODS):
                sums[m : m + 1, :] += jnp.sum(
                    jnp.where(ids == m, pre_grad, 0.0), axis=0, keepdims=True
                )
            sums[MODS : MODS + 1, :] += jnp.sum(grad_here * act, axis=0, keepdims=True)
        lane_at = lax.broadcasted_iota(jnp.int32, (SUB, LANES), 1)
        for group in range(groups):
            found = jnp.zeros((SUB, LANES), f32)
            for n in range(N):
                at = (group * N + n) * SUB
                total_rate = jnp.sum(rate_sum[at : at + SUB, :], axis=1, keepdims=True)
                found = jnp.where(lane_at == n, total_rate, found)
            rate_out[group * SUB : (group + 1) * SUB, :] = found


def scan_back(
    core, ids, ids_rows, turned, pre, step_pre, grad, states, enter, step_w, rate_t, skip
):
    total, channels = pre.shape
    length = total // LANES
    steps = math.gcd(length, STEPS)
    chunks = length // steps
    wide = N * channels
    feats = (2, lax.axis_size("z"), lax.axis_size("mod"), R + 2 * N, ids_rows.shape[1])
    first = (ids, ids_rows) + turned + (pre, step_pre, grad)
    second = (enter, step_w, rate_t, skip)
    turn = pltpu.VMEM((length * channels, LANES), f32)
    flat = pltpu.VMEM((total, channels), f32)
    terms = pltpu.VMEM((steps * N * SUB, LANES), f32)
    states_row = pltpu.VMEM((wide, LANES), f32)
    return pl.pallas_call(
        back_kernel,
        grid=(chunks,),
        in_specs=[pl.BlockSpec(memory_space=pltpu.SMEM)]
        + [whole(a.shape) for a in first]
        + [
            pl.BlockSpec((steps, wide, LANES), lambda i: (chunks - 1 - i, 0, 0)),
            pl.BlockSpec(
                (1, wide, LANES), lambda i: (jnp.maximum((chunks - 1 - i) * steps - 1, 0), 0, 0)
            ),
        ]
        + [whole(a.shape) for a in second],
        out_specs=[
            whole((total, channels)),
            whole((total, channels)),
            whole(feats),
            whole((SUB, channels)),
            whole((channels, LANES)),
        ],
        out_shape=[
            jax.ShapeDtypeStruct((total, channels), f32),
            jax.ShapeDtypeStruct((total, channels), bf16),
            jax.ShapeDtypeStruct(feats, f32),
            jax.ShapeDtypeStruct((SUB, channels), f32),
            jax.ShapeDtypeStruct((channels, LANES), f32),
        ],
        scratch_shapes=[turn, turn, turn, pltpu.VMEM((length * 2 * N, LANES), f32)]
        + [flat, flat, flat, terms, terms, states_row, states_row, states_row]
        + [pltpu.VMEM((length * 2 * N * SUB, LANES), f32)],
        compiler_params=pltpu.CompilerParams(vmem_limit_bytes=VMEM_BYTES),
        cost_estimate=cost(1),
        name="scan_back",
    )(core, *first, states, states, *second)


def conv_back_kernel(
    seqs,
    lengths,
    ids_ref,
    feat_grad,
    act_part,
    pre,
    inner,
    taps,
    param_w,
    inner_wide,
    inner_low,
    sums,
    ext,
):
    total, channels = pre.shape
    rows = total // seqs
    split = lengths[0]
    ext[total : total + 8, :] = jnp.zeros((8, channels), f32)
    sums[...] = jnp.zeros(sums.shape, f32)

    def through_silu(i, carried):
        at = pl.ds(pl.multiple_of(i * rows, rows), rows)
        for j in range(feat_grad.shape[2]):
            block_rows = feat_grad.shape[4]
            block = pl.ds(pl.multiple_of(i * rows + j * block_rows, block_rows), block_rows)
            low = feat_grad[i % 2, i // 2, j]
            stacked = dot(low, param_w[...], 0, 0)
            ext[block, :] = pick(
                ids_ref[block, :], [stacked[:, m * channels : (m + 1) * channels] for m in range(MODS)]
            )
        act_grad = act_part[at, :] + ext[at, :]
        here = pre[at, :]
        sig = jax.nn.sigmoid(here)
        conv_grad = act_grad * (sig * (1.0 + here * (1.0 - sig)))
        ext[at, :] = conv_grad
        sums[KW : KW + 1, :] += jnp.sum(conv_grad, axis=0, keepdims=True)
        return carried

    lax.fori_loop(0, total // rows, through_silu, 0)

    for block in range(total // rows):
        first = block * rows
        at = pl.ds(first, rows)
        places = row_places(first, rows)
        here = inner[at, :]
        grad = jnp.zeros((rows, channels), f32)
        for tap in range(KW):
            lag = KW - 1 - tap
            kept = (places >= split) | (places + lag < split)
            later = jnp.where(kept, ext[pl.ds(first + lag, rows), :], 0.0)
            grad = grad + taps[tap : tap + 1, :] * later
            sums[tap : tap + 1, :] += jnp.sum(later * here, axis=0, keepdims=True)
        put_masked(inner_wide, at, ids_ref[at, :], grad)
        inner_low[at, :] = grad.astype(bf16)


def conv_back(seqs, lengths, ids, feat_grad, act_part, pre, inner, taps, param_w):
    total, channels = pre.shape
    ins = (ids, feat_grad, act_part, pre, inner, taps, param_w)
    vmem = pl.BlockSpec(memory_space=pltpu.VMEM)
    return pl.pallas_call(
        functools.partial(conv_back_kernel, seqs),
        in_specs=[pl.BlockSpec(memory_space=pltpu.SMEM)] + [vmem] * len(ins),
        out_specs=[vmem, vmem, vmem],
        out_shape=[
            jax.ShapeDtypeStruct((total, MODS * channels), bf16),
            jax.ShapeDtypeStruct((total, channels), bf16),
            jax.ShapeDtypeStruct((8, channels), f32),
        ],
        scratch_shapes=[pltpu.VMEM((total + 8, channels), f32)],
        compiler_params=pltpu.CompilerParams(vmem_limit_bytes=VMEM_BYTES),
        cost_estimate=cost(1),
        name="conv_back",
    )(lengths, *ins)


def flip(axis, bit):
    size = lax.axis_size(axis)
    return lambda value: lax.ppermute(value, axis, [(i, i ^ bit) for i in range(size)])


def taken(values, at, dim):
    return lax.dynamic_index_in_dim(values, at, dim, keepdims=False)


SEQ = ("z", "core")
SAME_CORE = ("z", "mod")


def size_of(axes):
    return math.prod(lax.axis_size(axis) for axis in axes)


def share(values, axes):
    size = size_of(axes)
    return lax.all_to_all(jnp.broadcast_to(values, (size,) + values.shape), axes, 0, 0)


def exchange(blocks, axes):
    return lax.all_to_all(blocks, axes, 0, 0)


def held_back(value, until):
    return lax.optimization_barrier((value, tuple(until)))[0] if until else value


def flip(axis, bit):
    size = lax.axis_size(axis)
    return lambda value: lax.ppermute(value, axis, [(i, i ^ bit) for i in range(size)])


def taken(values, at, dim):
    return lax.dynamic_index_in_dim(values, at, dim, keepdims=False)


def two(bit, mine, got):
    return jnp.where(bit == 0, jnp.stack([mine, got]), jnp.stack([got, mine]))


Z_HIGH, Z_LOW, CORE = ("z", 2), ("z", 1), ("core", 1)
Y, X = ("mod", 2), ("mod", 1)


def place_bit(place):
    axis, bit = place
    return lax.axis_index(axis) // bit % 2


def summed_features(feats, kind=f32):
    feats = (feats[1] + flip(*CORE)(feats[0])).astype(kind)
    feats = feats.reshape((-1,) + feats.shape[2:])
    return jnp.sum(exchange(feats, SAME_CORE).astype(f32), axis=0), feats


def shared_features(block, until=()):
    mine = share(block, SAME_CORE)
    every = two(place_bit(CORE), mine, flip(*CORE)(held_back(mine, until)))
    return every.reshape((2, lax.axis_size("z"), lax.axis_size("mod")) + block.shape)


def core_rows(values, which):
    blocks = values.reshape(lax.axis_size("z"), 2, -1, values.shape[1])
    return taken(blocks, which, 1).reshape(-1, values.shape[1])


def both_cores(low, ids_ours):
    core = place_bit(CORE)
    got = flip(*CORE)(core_rows(low, 1 - core))
    return [masked(core_rows(low, core), ids_ours), masked(got, ids_ours)]


def gathered_columns(shard, between):
    width = shard.shape[1] // COLUMNS
    lines, far = [], []
    for at in range(COLUMNS):
        part = shard[:, at * width : (at + 1) * width]
        far.append(flip(*Z_HIGH)(held_back(part, far[at - 1 : at] if at else ())))
        line = two(place_bit(Z_HIGH), part, far[at])
        given = held_back(line, lines[at - 1 : at] if at else ())
        lines.append(two(place_bit(Z_LOW), line, flip(*Z_LOW)(given)))
    until = between(lines[-1])
    pieces, arrived, halfway = [], [], []
    for at, line in enumerate(lines):
        near, next_ = (X, Y) if at % 2 == 0 else (Y, X)
        halfway.append(flip(*near)(held_back(line, halfway[at - 2 : at - 1] if at > 1 else ())))
        pair = two(place_bit(near), line, halfway[at])
        got = flip(*next_)(held_back(pair, until if at > 1 else ()))
        arrived.append(got)
        pieces += [pair, got, flip(*CORE)(pair), flip(*CORE)(got)]
    return pieces, arrived


def row_parts(left, right, count):
    width = right.shape[0] // count
    return [
        dot(left, right[at * width : (at + 1) * width], 1, 1)
        .astype(bf16)
        .reshape(2, 2, 2, 2, -1, width)
        for at in range(count)
    ]


class SummedRows:
    def __init__(self, parts):
        self.dims = [["zh", "zl", "y", "x"] for _ in parts]
        self.parts = [[part] for part in parts]

    def give(self, at, name, place):
        dim = self.dims[at].index(name)
        bit = place_bit(place)
        away = sum(taken(p, 1 - bit, dim).astype(f32) for p in self.parts[at]).astype(bf16)
        self.parts[at] = [taken(p, bit, dim) for p in self.parts[at]]
        self.dims[at].remove(name)
        return away

    def stage(self, names):
        places = {"x": X, "y": Y, "zl": Z_LOW, "zh": Z_HIGH}
        sent = []
        for at in range(len(self.parts)):
            name = names[at % 2]
            away = self.give(at, name, places[name])
            sent.append(away)
            self.parts[at].append(flip(*places[name])(away))
        return sent

    def merge(self):
        pairs = list(zip(self.parts[::2], self.parts[1::2]))
        self.parts = [
            [jnp.concatenate(both, axis=-1) for both in zip(even, odd)] for even, odd in pairs
        ]
        self.dims = self.dims[::2]

    def arrived(self):
        return [parts[-1] for parts in self.parts]

    def hold(self, until):
        for parts in self.parts:
            parts[-1] = held_back(parts[-1], until)

    def result(self):
        return jnp.concatenate([sum(p.astype(f32) for p in parts) for parts in self.parts], axis=1)


def masked(values, ids):
    return jnp.concatenate(
        [jnp.where(ids == m, values, jnp.zeros_like(values)) for m in range(MODS)], axis=1
    )


def channel_layout(
    tokens,
    modality,
    lengths,
    norm_gain,
    input_weight,
    param_weight,
    step_weight,
    step_bias,
    output_weight,
    conv_weight,
    conv_bias,
    decay_log,
    skip_gain,
    cotangent,
):
    seqs = size_of(SEQ)
    channels = conv_weight.shape[1]
    width = tokens.shape[1]
    features = param_weight.shape[2]
    slab = input_weight.shape[1]

    token_vals = tokens.astype(f32)
    inverse = lax.rsqrt(jnp.mean(token_vals * token_vals, axis=1, keepdims=True) + EPSILON)
    normal_rows = token_vals * inverse
    gain_vals = norm_gain.astype(f32)

    send_in = input_weight.reshape(MODS, slab, 2, seqs, channels)
    send_in = send_in.transpose(3, 2, 0, 1, 4).reshape(seqs, 2 * MODS * slab, channels)
    id_rows = 16
    send_ids = jnp.pad(modality.astype(bf16), (0, id_rows * channels - modality.shape[0]))
    send_ids = jnp.broadcast_to(send_ids.reshape(id_rows, channels), (seqs, id_rows, channels))
    send_in = jnp.concatenate([send_in, send_ids], axis=1)
    made = []

    def send(line):
        made.append(exchange(held_back(send_in, [line]), SEQ))
        return made

    pieces, arrived = gathered_columns((normal_rows * gain_vals[None, :]).astype(bf16), send)
    inner_blocks = made[0]
    ids = inner_blocks[:, 2 * MODS * slab :].reshape(seqs, -1)[:, : modality.shape[0]].astype(jnp.int32)
    ids_rows = ids.reshape(-1, tokens.shape[0])
    ids = ids.reshape(-1, 1)
    send_out = output_weight.reshape(MODS, seqs, channels, slab).transpose(1, 0, 3, 2)
    send_out = send_out.reshape(seqs, MODS * slab, channels)
    param_rows = param_weight.transpose(0, 2, 1).reshape(MODS * features, channels)
    param_columns = param_weight.transpose(2, 0, 1).reshape(features, MODS * channels)
    step_rows_w = step_weight.reshape(MODS * R, channels)
    step_columns = step_weight.transpose(1, 0, 2).reshape(R, MODS * channels)
    core = place_bit(CORE)
    place = jnp.stack([place_bit(at) for at in (CORE, Y, X)]).astype(jnp.int32)
    taps = conv_weight.astype(f32)
    skip = skip_gain.astype(f32)[None, :]
    decay_rate = -jnp.exp(decay_log.astype(f32))
    rate_t = jnp.pad(decay_rate.T, ((0, 0), (0, LANES - N)))

    *normed, own_inner, own_gate, inner, conv_pre, act_low, feats = project(
        lengths,
        place,
        pieces,
        ids,
        ids_rows,
        inner_blocks,
        taps,
        conv_bias.astype(f32)[None, :],
        param_rows,
    )
    cotangents = lax.all_gather(
        held_back(cotangent, [inner]), SEQ + ("mod",), axis=0, tiled=True
    )
    feats, sent = summed_features(feats)
    gate_pre = modal_rows(normed, held_back(ids, [sent]), own_gate)
    pair_in = side_by_side(own_inner, flip(*CORE)(own_inner), own_gate, flip(*CORE)(own_gate))
    feats = held_back(feats, [gate_pre, pair_in])
    mix_high = feats[R:].astype(bf16)
    mix_rest = (feats[R:] - mix_high.astype(f32)).astype(bf16)
    feats = jnp.concatenate([feats[:R].astype(bf16), mix_high, mix_rest], axis=0)
    feats = shared_features(feats)

    out_blocks = exchange(held_back(send_out, [feats]), SEQ)
    states, enter, step_pre, *turned, scan_out = scan(
        lengths,
        ids,
        feats,
        conv_pre,
        step_columns,
        step_bias.astype(f32).reshape(1, MODS * channels),
        rate_t,
        skip,
    )
    out_blocks, scan_out = lax.optimization_barrier((out_blocks, scan_out))
    own_out, grad_scan, gate_wide, gated_wide, gate_rows, gated_rows = gates(
        cotangents, ids, out_blocks, gate_pre, scan_out
    )

    def token_sums(wide, weight):
        lows, gains = [], []
        for at, part in enumerate(normed):
            rows = part.shape[1]
            grad = dot(part, wide, 0, 0)
            lows.append(grad.astype(bf16))
            gains.append(jnp.sum(grad * weight[at * rows : (at + 1) * rows].astype(f32), axis=1))
        return jnp.concatenate(lows, axis=0), jnp.concatenate(gains, axis=0)

    def by_holder(low):
        return low.reshape(seqs, slab, MODS * channels)

    ids_ours = core_rows(ids, core)
    gated_both = jnp.concatenate(both_cores(gated_rows, ids_ours), axis=1)
    pair_out = side_by_side(own_out, flip(*CORE)(own_out))
    branch = SummedRows(row_parts(gated_both, pair_out, 2))
    branch_sent = branch.stage(("x", "y"))
    grad_scan = held_back(grad_scan, branch_sent)

    act_part, step_grad_low, feat_grad, sums, rate_sum = scan_back(
        place,
        ids,
        ids_rows,
        tuple(turned),
        conv_pre,
        step_pre,
        grad_scan,
        states,
        enter,
        step_rows_w,
        rate_t,
        skip,
    )
    feat_grad = held_back(feat_grad, branch.arrived())
    gate_rows, gate_wide, gated_wide = held_back((gate_rows, gate_wide, gated_wide), [feat_grad])
    gate_both = both_cores(gate_rows, ids_ours)
    feat_grad, sent = summed_features(feat_grad, bf16)
    feat_grad = held_back(feat_grad.astype(bf16), branch.stage(("y", "x")))
    gate_wide, gated_wide = held_back((gate_wide, gated_wide), [sent])
    gate_low, gate_gain = token_sums(gate_wide, own_gate)
    out_low = dot(cotangents, gated_wide, 0, 0).astype(bf16)
    more_low = jnp.concatenate([by_holder(gate_low), by_holder(out_low)], axis=2)
    feat_grad = shared_features(feat_grad, [more_low])
    more_low = exchange(held_back(more_low, [feat_grad]), SEQ)
    branch.hold([feat_grad])
    branch.merge()

    inner_wide, inner_rows, tap_sums = conv_back(
        seqs,
        lengths,
        ids,
        feat_grad,
        act_part,
        conv_pre,
        inner,
        taps,
        param_columns,
    )
    both_wide = jnp.concatenate(both_cores(inner_rows, ids_ours) + gate_both, axis=1)
    products = row_parts(both_wide, pair_in, COLUMNS)
    normed_sums = SummedRows(products)
    sent = normed_sums.stage(("x", "y"))
    branch.hold(sent)
    branch.stage(("zl", "zl"))
    inner_low, inner_gain = token_sums(held_back(inner_wide, sent), own_inner)
    inner_low, more_low = lax.optimization_barrier((by_holder(inner_low), more_low))
    inner_low = exchange(inner_low, SEQ)
    step_grad_low = held_back(step_grad_low, sent)
    for parts in normed_sums.parts[2:]:
        parts[-1] = held_back(parts[-1], [more_low])
    sent = normed_sums.stage(("y", "x"))
    branch.hold(sent)
    branch.stage(("zh", "zh"))
    output = (token_vals + branch.result()).astype(bf16)
    inner_low = inner_low.reshape(seqs, slab, MODS, channels)
    more_low = more_low.reshape(seqs, slab, 2, MODS, channels)
    grad_gate = more_low[:, :, 0].transpose(2, 1, 0, 3)
    grad_in = jnp.stack([inner_low.transpose(2, 1, 0, 3), grad_gate], axis=2)
    grad_in = grad_in.reshape(MODS, slab, 2, seqs * channels).astype(f32)
    normed_sums.merge()
    sent = normed_sums.stage(("zl", "zl"))
    feat_late, out_low = held_back((feat_grad, more_low[:, :, 1]), sent)
    grad_out = out_low.transpose(2, 0, 3, 1)
    grad_out = grad_out.reshape(MODS, seqs * channels, slab).astype(f32)
    step_t = feats[:, :, :, :R].transpose(3, 1, 0, 2, 4).reshape(R, -1)
    grad_step = dot(step_t, masked(step_grad_low, ids))
    grad_step = grad_step.reshape(R, MODS, channels).transpose(1, 0, 2)
    feat_late = feat_late.transpose(3, 1, 0, 2, 4).reshape(features, -1)
    feat_late = [
        jnp.where(ids_rows.reshape(1, -1) == m, feat_late, jnp.zeros_like(feat_late))
        for m in range(MODS)
    ]
    grad_param = dot(jnp.concatenate(feat_late, axis=0), act_low)
    grad_param = grad_param.reshape(MODS, features, channels).transpose(0, 2, 1)
    normed_sums.hold([grad_out, grad_param])
    normed_sums.stage(("zh", "zh"))
    gain_sum, grad_in = lax.optimization_barrier((inner_gain + gate_gain, grad_in))
    grad_gain = jnp.sum(share(gain_sum, SEQ + ("mod",)), axis=0) / gain_vals
    normed_grad, grad_gain = lax.optimization_barrier((normed_sums.result(), grad_gain))
    hat_grad = normed_grad * gain_vals[None, :]
    token_grad = cotangent.astype(f32) + inverse * (
        hat_grad - normal_rows * jnp.mean(hat_grad * normal_rows, axis=1, keepdims=True)
    )
    return (
        output,
        token_grad,
        grad_gain,
        grad_in,
        grad_param,
        grad_step,
        grad_out,
        tap_sums[:KW],
        tap_sums[KW],
        rate_sum[:, :N].T * decay_rate,
        sums[MODS],
        sums[:MODS],
    )


def placed(spec, axes):
    entries = [
        sum((axes[name] for name in ((entry,) if isinstance(entry, str) else entry or ())), ())
        for entry in spec
    ]
    return P(*[entry or None for entry in entries])


def solution(mesh):
    token_rows = P(("seq", "mod"), None)
    in_weight = P(None, "seq", None, "mod")
    out_weight = P(None, "mod", "seq")
    row, column, depth = P(("mod", "seq")), P(None, ("mod", "seq")), P(None, None, ("mod", "seq"))
    middle = P(None, ("mod", "seq"), None)
    ins = (token_rows, P("seq"), P(), P(), in_weight, middle, depth, column, out_weight)
    ins += (column, row, column, row, token_rows)
    outs = (token_rows, token_rows, P(), in_weight, middle, depth, out_weight)
    outs += (column, row, column, row, column)

    def run(*args):
        sizes = (mesh.shape["seq"], mesh.shape["mod"])
        share_of_channels = args[12].shape[0] // (sizes[0] * sizes[1])
        if share_of_channels == LANES and sizes == (8, 4):
            part, over = channel_layout, jax.sharding.Mesh(
                mesh.devices.reshape(sizes[0] // 2, 2, sizes[1]), ("z", "core", "mod")
            )
            axes = {"seq": SEQ, "mod": ("mod",)}
        else:
            part, over = local, mesh
            axes = {"seq": ("seq",), "mod": ("mod",)}
        return jax.shard_map(
            part,
            mesh=over,
            in_specs=tuple(placed(spec, axes) for spec in ins),
            out_specs=tuple(placed(spec, axes) for spec in outs),
            check_vma=False,
        )(*args)

    return run
```
